32 devices in a mesh: comp: 4 (over x, core), dom: 8 (over z, y).
Axes of the slice: x: 2, y: 2, z: 4, core: 2. Of those that a mesh axis runs over, the one named last changes fastest.
Arguments:
- air_warmth: float32 [16, 64, 4096], P(None, None, ('comp', 'dom')), may hold values from -6 to 6
- eastern_breeze: bfloat16 [16, 64, 4096], P(None, None, ('comp', 'dom')), may hold values from -6 to 6
- northern_breeze: bfloat16 [16, 64, 4096], P(None, None, ('comp', 'dom')), may hold values from -6 to 6
- reciprocal_breadth: float32 [4096], P(('comp', 'dom')), may hold values from 0.5 to 2
- panel_neighbours: int32 [4, 4096], P(None, ('comp', 'dom')), may hold values from 0 to 4095, as said below
- transfer_coefficients: bfloat16 [1024, 128, 128], P(('comp', 'dom')), may hold values from -0.375 to 0.375
- transfer_across_tile: int32 [1024], P(('comp', 'dom')), may hold values from 0 to 15, as said below
- transfer_holder: int32 [1024, 1], P(('comp', 'dom')), may hold values from 0 to 31; in each aligned block of 32 rows (0 to 31, 32 to 63, ...) at most 2 rows name the same one
- transfer_down_tile: int32 [1024], P(('comp', 'dom')), may hold values from 0 to 31
- water_elevation: float32 [131072], P(('comp', 'dom')), may hold values from -6 to 6
- depth_mean_current: float32 [2, 131072], P(None, ('comp', 'dom')), may hold values from -6 to 6
- marine_skin_warmth: float32 [131072], P(('comp', 'dom')), may hold values from -6 to 6
- patch_neighbours: int32 [6, 131072], P(None, ('comp', 'dom')), may hold values from -1 to 4607, as said below
- interface_span: float32 [6, 131072], P(None, ('comp', 'dom')), may hold values from 0.5 to 2
Outputs:
- closing_air_warmth: float32 [16, 64, 4096], P(None, None, ('comp', 'dom'))
- level_out: float32 [131072], P(('comp', 'dom'))
- velocity_out: float32 [2, 131072], P(None, ('comp', 'dom'))
- updated_sea_warmth: float32 [131072], P(('comp', 'dom'))
The draws below stay inside these ranges and needn't reach their ends.
Inputs may be any that keep to these rules, and one draw needn't show every extreme that they name: `panel_neighbours`: entry [k, e] is the element across side k (south, east, north, west) of e, whose side (k + 2) mod 4 faces e with the points in the same order; the relation is symmetric. It lies in e's aligned block of 128 elements, or for k = 1 in the next block and for k = 3 in the previous one, cyclically. In each block exactly 32 elements have their east partner in the next block and exactly 32 their west partner in the previous one. `transfer_across_tile`: in each aligned block of 32 entries every value 0 .. 15 appears exactly 2 times. `transfer_holder`: in each aligned block of 32 rows no owner is named more than 2 times, a bound that some block reaches. `patch_neighbours`: with cells in aligned blocks of 4096, a cell's extended positions are the last 256 cells of the previous block (0 .. 255), its own block (256 .. 4351) and the first 256 cells of the next block, cyclically. Entry [k, i] is -1 or the position of a cell j whose slot (k + 3) mod 6 names i; only cells among the first 256 of a block have neighbours in the previous block, and only cells among the last 256 in the next one.
All inputs are finite; a program needn't handle non-finite values.
Results may differ from the reference program's by a relative error of at most 0.0026.
Values may be sent and summed in bfloat16 or wider, within the bound.
No kernel may reach another device: no remote copies, remote signals or barrier semaphores. Data moves between devices by JAX's collectives and lax.ppermute only.
A program may use at most 64 MiB of HBM per device.

```python
import math
import jax
import jax.numpy as jnp
import numpy as np
from jax import lax

NODES_PER_SIDE = 4
LEV = 64
EX = 4
EY = 32
LOCAL_PANELS = 128
PROCESSOR_COUNT = 32
MESH_PANEL_COUNT = 4096
NF = 3
BC = 128
PATCHES_PER_TILE = 128
NBPC = 2
CB_DEV = 16
NB_DEV = 32
BLOCKS = 1024
CAP = 2
OX = 16
OY = 256
C_DEV = 4096
LOCAL_TILE_COUNT = 32
GRID_PATCH_COUNT = 131072
NSUB = 4


def draw_panel_neighbours(key, part):
    shard_keys = jax.random.split(jax.random.fold_in(key, 11), PROCESSOR_COUNT)
    numbering = jax.vmap(lambda single: jax.random.permutation(single, EX * EY))(shard_keys).astype(jnp.int32)
    shard_base = (jnp.arange(PROCESSOR_COUNT, dtype=jnp.int32) * (EX * EY))[:, None]
    global_ids = (numbering + shard_base).reshape(PROCESSOR_COUNT * EX, EY)
    south = jnp.roll(global_ids, 1, 1)
    east = jnp.roll(global_ids, -1, 0)
    north = jnp.roll(global_ids, -1, 1)
    west = jnp.roll(global_ids, 1, 0)
    stacked = jnp.stack([south, east, north, west]).reshape(4, -1)
    return jnp.zeros((4, PROCESSOR_COUNT * EX * EY), jnp.int32).at[:, global_ids.reshape(-1)].set(stacked)


def draw_transfer_across_tile(key, part):
    shard_keys = jax.random.split(jax.random.fold_in(key, 23), PROCESSOR_COUNT)
    repeated = jnp.tile(jnp.arange(CB_DEV, dtype=jnp.int32), NBPC)
    shuffled = jax.vmap(lambda single: jax.random.permutation(single, repeated))(shard_keys)
    return shuffled.reshape(-1).astype(jnp.int32)


def draw_patch_neighbours(key, part):
    column_total = OX * PROCESSOR_COUNT
    column_keys = jax.random.split(jax.random.fold_in(key, 31), column_total)
    column_order = jax.vmap(lambda single: jax.random.permutation(single, OY))(column_keys).astype(jnp.int32)
    global_ids = jnp.arange(column_total, dtype=jnp.int32)[:, None] * OY + column_order
    kept_edges = jax.random.randint(jax.random.fold_in(key, 37), (3, column_total, OY), 0, 100) < 85
    step_cols = (1, 0, -1, -1, 0, 1)
    step_rows = (0, 1, 1, 0, -1, -1)
    targets = jnp.stack([jnp.roll(global_ids, (-step_cols[direction], -step_rows[direction]), (0, 1)) for direction in range(6)])
    kept_all = jnp.stack([kept_edges[0], kept_edges[1], kept_edges[2], jnp.roll(kept_edges[0], 1, 0), jnp.roll(kept_edges[1], 1, 1), jnp.roll(jnp.roll(kept_edges[2], -1, 0), 1, 1)])
    linked = jnp.where(kept_all, targets, -1).reshape(6, -1)
    global_links = jnp.full((6, GRID_PATCH_COUNT), -1, jnp.int32).at[:, global_ids.reshape(-1)].set(linked)
    own_block = (jnp.arange(GRID_PATCH_COUNT, dtype=jnp.int32) // C_DEV)[None, :]
    safe_global = jnp.maximum(global_links, 0)
    block_gap = (safe_global // C_DEV - own_block) % PROCESSOR_COUNT
    relative = safe_global % C_DEV + OY + jnp.where(block_gap == 1, C_DEV, jnp.where(block_gap == PROCESSOR_COUNT - 1, -C_DEV, 0))
    return jnp.where(global_links >= 0, relative, -1).astype(jnp.int32)


def set_ends(values, key, low, largest):
    dims = values.shape
    spot = [jax.random.randint(jax.random.fold_in(key, axis), (), 0, dims[axis]) for axis in range(len(dims))]
    values = values.at[tuple(spot)].set(low)
    longest = dims.index(max(dims))
    spot[longest] = (spot[longest] + 1) % dims[longest]
    return values.at[tuple(spot)].set(largest)


def block_levels(own_key, dims, shards, least, top_value):
    gain, own = 1.0, jax.random.fold_in(own_key, 6)
    for axis_at, blocks in shards:
        draws = jnp.exp(jax.random.uniform(jax.random.fold_in(own, axis_at), (blocks,), jnp.float32, least / len(shards), top_value / len(shards)))
        gain = gain * jnp.repeat(draws, dims[axis_at] // blocks).reshape([-1 if axis == axis_at else 1 for axis in range(len(dims))])
    return gain


def assign_block(stream_key, own, number, rows, number_of, top, reach, lean):
    order = jax.random.permutation(stream_key, number_of)
    heavy_load, common = load_shares(number_of, rows * top, reach, lean, True), load_shares(number_of, rows * top, reach, lean, False)
    places = jnp.arange(number_of)

    def named(lengths, rotation):
        used = int((lengths > 0).sum())
        fixed = max(1, used // 4)
        passed = fixed + (places - fixed + rotation * (used - fixed)) % max(1, number_of - fixed)
        return jnp.zeros((number_of,), jnp.int32).at[order[jnp.where(places < fixed, places, passed)]].set(jnp.asarray(lengths, jnp.int32))

    lengths = jnp.where(number % 4 == 0, named(heavy_load, number // 4), named(common, number - number // 4 - 1))
    mixed = jax.random.permutation(jax.random.fold_in(own, 3), number_of)
    source_of, taker = mixed[0:number_of // 2 * 2:2], mixed[1:number_of // 2 * 2:2]
    room = jnp.minimum(lengths[source_of] - 1, reach - lengths[taker]) // 2
    room = jnp.where((source_of == order[0]) | (taker == order[0]) | (lengths[taker] == 0), 0, jnp.maximum(room, 0))
    passed = jax.random.randint(jax.random.fold_in(own, 4), (number_of // 2,), 0, 1 << 20) % (room + 1)
    lengths = lengths.at[source_of].add(-passed).at[taker].add(passed)
    labels = jnp.searchsorted(jnp.cumsum(lengths), jnp.arange(rows * top), side="right").astype(jnp.int32)
    table = labels.reshape(top, rows).T
    table = table[jax.random.permutation(jax.random.fold_in(own, 1), rows)]
    rotation = jax.random.randint(jax.random.fold_in(own, 2), (rows, 1), 0, top)
    return jnp.take_along_axis(table, (jnp.arange(top)[None, :] + rotation) % top, axis=1)


def load_shares(count, total, reach, slope, full):
    weights = [(1 << 20) // math.isqrt(rank ** slope) + 1 for rank in range(1, count + 1)]
    largest = reach if full else min(reach, max(-(-total // count), total * weights[0] // sum(weights)))
    least = 1 if total - largest >= count - 1 else 0
    given, rest = [largest] + [least] * (count - 1), total - largest - least * (count - 1)
    while rest > 0:
        movable = [i for i in range(1, count) if given[i] < largest] or [i for i in range(1, count) if given[i] < reach]
        pool, left = sum([weights[i] for i in movable]), rest
        for i in movable:
            more = min(reach - given[i], max(1, left * weights[i] // pool), rest)
            given[i] = given[i] + more
            rest = rest - more
    return np.array(given)


def noise(stream_key, dims, scale, reach, pieces=(), kind=jnp.bfloat16):
    values = jax.random.normal(stream_key, dims, jnp.float32) * scale
    if len(pieces) > 0:
        values = block_levels(stream_key, dims, pieces, -0.22, 0.18) * values
    return jnp.clip(values, min=-reach, max=reach).astype(kind)


def setup_inputs(seed: int = 0) -> dict:
    key_list = jax.random.split(jax.random.key(seed), 15)
    air_warmth = noise(key_list[0], (NODES_PER_SIDE * NODES_PER_SIDE, LEV, MESH_PANEL_COUNT), 1.0, 6.0, ((2, 32),), jnp.float32)
    eastern_breeze = noise(key_list[1], (NODES_PER_SIDE * NODES_PER_SIDE, LEV, MESH_PANEL_COUNT), 1.0, 6.0, ((2, 32),))
    northern_breeze = noise(key_list[2], (NODES_PER_SIDE * NODES_PER_SIDE, LEV, MESH_PANEL_COUNT), 1.0, 6.0, ((2, 32),))
    reciprocal_breadth = jnp.clip(jnp.exp(math.log(2.0) - 1.3862944 * jax.random.uniform(key_list[3], (MESH_PANEL_COUNT,), jnp.float32) ** block_levels(key_list[3], (MESH_PANEL_COUNT,), ((0, 32),), -0.2, 0.2)), 0.5, 2.0)
    panel_neighbours = draw_panel_neighbours(jax.random.fold_in(key_list[14], 71), 0)
    transfer_coefficients = noise(key_list[5], (BLOCKS, BC, PATCHES_PER_TILE), (PATCHES_PER_TILE * NBPC) ** -0.5, 0.375, ((0, 32),))
    transfer_across_tile = draw_transfer_across_tile(jax.random.fold_in(key_list[14], 71), 0)
    transfer_holder_keys = jax.random.split(jax.random.fold_in(key_list[7], 1), BLOCKS // NB_DEV)
    transfer_holder_turns = jax.random.permutation(jax.random.fold_in(key_list[7], 3), BLOCKS // NB_DEV)
    transfer_holder = jax.vmap(lambda own, number: assign_block(jax.random.fold_in(key_list[7], 2), own, number, NB_DEV, PROCESSOR_COUNT, 1, CAP, 2))(transfer_holder_keys, transfer_holder_turns).reshape((BLOCKS, 1))
    transfer_down_tile = set_ends(jax.random.randint(key_list[8], (BLOCKS,), 0, LOCAL_TILE_COUNT), jax.random.fold_in(key_list[8], 1), 0, LOCAL_TILE_COUNT - 1).astype(jnp.int32)
    water_elevation = noise(key_list[9], (GRID_PATCH_COUNT,), 1.0, 6.0, ((0, 32),), jnp.float32)
    depth_mean_current = noise(key_list[10], (2, GRID_PATCH_COUNT), 1.0, 6.0, ((1, 32),), jnp.float32)
    marine_skin_warmth = noise(key_list[11], (GRID_PATCH_COUNT,), 1.0, 6.0, ((0, 32),), jnp.float32)
    patch_neighbours = draw_patch_neighbours(jax.random.fold_in(key_list[14], 71), 0)
    interface_span = jnp.clip(jnp.exp(math.log(2.0) - 1.3862944 * jax.random.uniform(key_list[13], (6, GRID_PATCH_COUNT), jnp.float32) ** block_levels(key_list[13], (6, GRID_PATCH_COUNT), ((1, 32),), -0.2, 0.2)), 0.5, 2.0)
    return {"air_warmth": air_warmth, "eastern_breeze": eastern_breeze, "northern_breeze": northern_breeze, "reciprocal_breadth": reciprocal_breadth, "panel_neighbours": panel_neighbours, "transfer_coefficients": transfer_coefficients, "transfer_across_tile": transfer_across_tile, "transfer_holder": transfer_holder, "transfer_down_tile": transfer_down_tile, "water_elevation": water_elevation, "depth_mean_current": depth_mean_current, "marine_skin_warmth": marine_skin_warmth, "patch_neighbours": patch_neighbours, "interface_span": interface_span}


STEP_SIZE = 0.05
JUMP_WEIGHT = 4.0
NUDGING_SPEED = 0.5
DAMPING = 0.9
GRAVITY = 0.3
WIND_GAIN = 0.3
DEPTH_RATE = 0.3
WARMING_COEFF = 0.3
SPREADING_COEFF = 0.5

def derivative_tables():
    points = np.array([-1.0, -1.0 / np.sqrt(5.0), 1.0 / np.sqrt(5.0), 1.0])
    barycentric = np.array([1.0 / np.prod([points[source] - points[other] for other in range(4) if other != source]) for source in range(4)])
    lagrange = np.zeros((4, 4))
    for target in range(4):
        for source in range(4):
            if target != source:
                lagrange[target, source] = barycentric[source] / barycentric[target] / (points[target] - points[source])
        lagrange[target, target] = -np.sum(lagrange[target])
    identity = np.eye(4)
    return (jnp.asarray(np.kron(identity, lagrange), jnp.float32), jnp.asarray(np.kron(lagrange, identity), jnp.float32))

def edge_trace(state_now, side_index):
    if side_index == 0:
        return state_now[0:4]
    if side_index == 1:
        return state_now[3::4]
    if side_index == 2:
        return state_now[12:16]
    return state_now[0::4]

def add_side(penalty, side_index, values):
    if side_index == 0:
        return penalty.at[0:4].add(values)
    if side_index == 1:
        return penalty.at[3::4].add(values)
    if side_index == 2:
        return penalty.at[12:16].add(values)
    return penalty.at[0::4].add(values)

def atmos_step(state_now, eastern_breeze, northern_breeze, reciprocal_breadth, panel_neighbours):
    diff_x, diff_y = derivative_tables()
    grad_x = jnp.einsum('pq,qle->ple', diff_x, state_now, precision=lax.Precision.HIGHEST)
    grad_y = jnp.einsum('pq,qle->ple', diff_y, state_now, precision=lax.Precision.HIGHEST)
    advect = -(eastern_breeze.astype(jnp.float32) * grad_x + northern_breeze.astype(jnp.float32) * grad_y)
    penalty = jnp.zeros_like(state_now)
    for side_index in range(4):
        facing = jnp.take(edge_trace(state_now, (side_index + 2) % 4), panel_neighbours[side_index], axis=2)
        penalty = add_side(penalty, side_index, facing - edge_trace(state_now, side_index))
    return state_now + STEP_SIZE * reciprocal_breadth * (advect + JUMP_WEIGHT * penalty)

def surface_fluxes(state_now, eastern_breeze, northern_breeze):
    lower_u = eastern_breeze[:, 0, :].astype(jnp.float32)
    lower_v = northern_breeze[:, 0, :].astype(jnp.float32)
    wind_speed = jnp.sqrt(lower_u * lower_u + lower_v * lower_v + 1.0)
    return jnp.stack([wind_speed * state_now[:, 0, :], wind_speed * lower_u, wind_speed * lower_v]).astype(jnp.bfloat16)

def cell_weights(patch_neighbours, interface_span):
    present = patch_neighbours >= 0
    angles = jnp.arange(6, dtype=jnp.float32)[:, None] * (math.pi / 3.0)
    weight_x = jnp.where(present, jnp.cos(angles) * interface_span / 3.0, 0.0)
    weight_y = jnp.where(present, jnp.sin(angles) * interface_span / 3.0, 0.0)
    central_coefficient = jnp.where(present, interface_span / 6.0, 0.0)
    return (weight_x, weight_y, central_coefficient)

def reference(air_warmth, eastern_breeze, northern_breeze, reciprocal_breadth, panel_neighbours, transfer_coefficients, transfer_across_tile, transfer_holder, transfer_down_tile, water_elevation, depth_mean_current, marine_skin_warmth, patch_neighbours, interface_span):
    after_first = atmos_step(air_warmth, eastern_breeze, northern_breeze, reciprocal_breadth, panel_neighbours)
    fluxes = surface_fluxes(after_first, eastern_breeze, northern_breeze)
    sources = fluxes.reshape(NF, NODES_PER_SIDE * NODES_PER_SIDE, PROCESSOR_COUNT, LOCAL_PANELS).transpose(2, 0, 1, 3).reshape(PROCESSOR_COUNT, NF, CB_DEV, BC)
    weights = transfer_coefficients.reshape(PROCESSOR_COUNT, NB_DEV, BC, PATCHES_PER_TILE)
    columns = transfer_across_tile.reshape(PROCESSOR_COUNT, NB_DEV)

    def shard_partial(inputs):
        source_blocks, weight_blocks, column_index = inputs
        picked_data = jnp.take(source_blocks, column_index, axis=1)
        return jnp.einsum('fbc,bcr->bfr', picked_data.astype(jnp.float32), weight_blocks.astype(jnp.float32))
    partial_sums = lax.map(shard_partial, (sources, weights, columns))
    destination = (transfer_holder[:, 0] * LOCAL_TILE_COUNT + transfer_down_tile).astype(jnp.int32)
    summed = jax.ops.segment_sum(partial_sums.reshape(BLOCKS, NF * PATCHES_PER_TILE), destination, PROCESSOR_COUNT * LOCAL_TILE_COUNT)
    thermal_driver = summed.reshape(PROCESSOR_COUNT * LOCAL_TILE_COUNT, NF, PATCHES_PER_TILE).transpose(1, 0, 2).reshape(NF, GRID_PATCH_COUNT)
    weight_x, weight_y, central_coefficient = cell_weights(patch_neighbours, interface_span)
    cell_base = jnp.arange(GRID_PATCH_COUNT, dtype=jnp.int32) // C_DEV * C_DEV
    global_links = (cell_base[None, :] + patch_neighbours - OY) % GRID_PATCH_COUNT
    bounded_neighbours = jnp.where(patch_neighbours >= 0, global_links, 0).astype(jnp.int32)
    water_rise = water_elevation
    eastern_current = depth_mean_current[0]
    northern_current = depth_mean_current[1]
    for substep in range(NSUB):
        nearby = water_rise[bounded_neighbours]
        slope_x = lax.optimization_barrier(jnp.sum(weight_x * (nearby - water_rise), axis=0))
        slope_y = lax.optimization_barrier(jnp.sum(weight_y * (nearby - water_rise), axis=0))
        eastern_current = DAMPING * eastern_current - GRAVITY * slope_x + WIND_GAIN * thermal_driver[1]
        northern_current = DAMPING * northern_current - GRAVITY * slope_y + WIND_GAIN * thermal_driver[2]
        spread_sum = lax.optimization_barrier(jnp.sum(weight_x * (eastern_current[bounded_neighbours] - eastern_current) + weight_y * (northern_current[bounded_neighbours] - northern_current), axis=0))
        water_rise = water_rise - DEPTH_RATE * spread_sum
    updated_sea_warmth = marine_skin_warmth + WARMING_COEFF * thermal_driver[0] + SPREADING_COEFF * lax.optimization_barrier(jnp.sum(central_coefficient * (marine_skin_warmth[bounded_neighbours] - marine_skin_warmth), axis=0))
    halfway_sea_warmth = updated_sea_warmth.astype(jnp.bfloat16)
    sea_warmth_tiles = halfway_sea_warmth.reshape(PROCESSOR_COUNT * LOCAL_TILE_COUNT, PATCHES_PER_TILE)
    owners = transfer_holder[:, 0].reshape(PROCESSOR_COUNT, NB_DEV)
    row_index = transfer_down_tile.reshape(PROCESSOR_COUNT, NB_DEV)

    def shard_back(inputs):
        weight_blocks, column_index, holder_partition, line_fraction = inputs
        picked_data = sea_warmth_tiles[(holder_partition * LOCAL_TILE_COUNT + line_fraction).astype(jnp.int32)]
        contribution = jnp.einsum('bcr,br->bc', weight_blocks.astype(jnp.float32), picked_data.astype(jnp.float32))
        return jax.ops.segment_sum(contribution, column_index, CB_DEV)
    incoming_data = lax.map(shard_back, (weights, columns, owners, row_index))
    joined_sea_warmth = incoming_data.reshape(PROCESSOR_COUNT, NODES_PER_SIDE * NODES_PER_SIDE, LOCAL_PANELS).transpose(1, 0, 2).reshape(NODES_PER_SIDE * NODES_PER_SIDE, MESH_PANEL_COUNT)
    later_advance = atmos_step(after_first, eastern_breeze, northern_breeze, reciprocal_breadth, panel_neighbours)
    lowest_layer = later_advance[:, 0, :]
    closing_air_warmth = later_advance.at[:, 0, :].set(lowest_layer + NUDGING_SPEED * (joined_sea_warmth - lowest_layer))
    return (closing_air_warmth, water_rise, jnp.stack([eastern_current, northern_current]), updated_sea_warmth)
```

```python
import math

import jax
import jax.numpy as jnp
import numpy as np
from jax import lax
from jax.experimental import pallas as pl
from jax.experimental.pallas import tpu as pltpu
from jax.sharding import PartitionSpec as P

OY = 256
NSUB = 4
CAP = 2

STEP_SIZE = 0.05
JUMP_WEIGHT = 4.0
NUDGING_SPEED = 0.5
DAMPING = 0.9
GRAVITY = 0.3
WIND_GAIN = 0.3
DEPTH_RATE = 0.3
WARMING_COEFF = 0.3
SPREADING_COEFF = 0.5

RING = ("comp", "dom")
LANES = 128
HALO = OY // LANES
COS = [math.cos(k * math.pi / 3.0) for k in range(6)]
SIN = [0.0 if k % 3 == 0 else math.sin(k * math.pi / 3.0) for k in range(6)]

ROW_EDGE, ROW_BREADTH, ROW_ETA, ROW_U, ROW_V, ROW_SST = 0, 4, 8, 10, 12, 14
ROW_PX, ROW_PY, ROW_IDX, ROW_W, ROWS_FIRST = 16, 18, 24, 40, 56
PER_DEST, ROW_IDS = 16, 14


def shifted(value, steps):
    count = lax.axis_size(RING)
    return lax.ppermute(value, RING, [(i, (i + steps) % count) for i in range(count)])


def exchange(value):
    return lax.all_to_all(value, RING, split_axis=0, concat_axis=0, tiled=True)


def gll_matrix():
    points = np.array([-1.0, -1.0 / np.sqrt(5.0), 1.0 / np.sqrt(5.0), 1.0])
    barycentric = [
        1.0 / np.prod([points[s] - points[o] for o in range(4) if o != s]) for s in range(4)
    ]
    table = np.zeros((4, 4))
    for t in range(4):
        for s in range(4):
            if t != s:
                table[t, s] = barycentric[s] / barycentric[t] / (points[t] - points[s])
    for t in (0, 3):
        table[t, t] = -np.sum(table[t])
    return [[float(np.float32(value)) for value in line] for line in table]


GLL = gll_matrix()


def vmem(count):
    return [pl.BlockSpec(memory_space=pltpu.VMEM)] * count


def smem(count):
    return [pl.BlockSpec(memory_space=pltpu.SMEM)] * count


def shape_of(*dims, dtype=jnp.float32):
    return jax.ShapeDtypeStruct(dims, dtype)


PARAMS = pltpu.CompilerParams(vmem_limit_bytes=24 * 1024 * 1024)


def lane_take(rows, ids):
    return jnp.take_along_axis(rows, ids, axis=1, mode="promise_in_bounds")


def wide(row, lines):
    return jnp.broadcast_to(row, (lines, row.shape[1]))


def side_ids(pn):
    count = pn.shape[1]
    bits = count.bit_length() - 1
    table = pn[...]
    ids = [table[k : k + 1] & (count - 1) for k in range(4)]
    home = lax.shift_right_logical(table[0:1], bits)
    near = [lax.shift_right_logical(table[k : k + 1], bits) == home for k in range(4)]
    return ids, near


def element_step(state, east_wind, north_wind, scale, facing):
    jumps = [None] * 16
    sides = (
        (0, 1, 2, 3),
        (3, 7, 11, 15),
        (12, 13, 14, 15),
        (0, 4, 8, 12),
    )
    for k in range(4):
        for n, p in enumerate(sides[k]):
            term = facing[k][n] - state[p]
            jumps[p] = term if jumps[p] is None else jumps[p] + term
    result = []
    for p in range(16):
        i, j = p % 4, p // 4
        grad_x = grad_y = None
        for m in range(4):
            if GLL[i][m] != 0.0:
                term = GLL[i][m] * state[m + 4 * j]
                grad_x = term if grad_x is None else grad_x + term
            if GLL[j][m] != 0.0:
                term = GLL[j][m] * state[i + 4 * m]
                grad_y = term if grad_y is None else grad_y + term
        change = -(east_wind(p) * grad_x + north_wind(p) * grad_y)
        if jumps[p] is not None:
            change = change + JUMP_WEIGHT * jumps[p]
        result.append(state[p] + scale * change)
    return result


def local_step_kernel(air, eastern, northern, breadth, pn, loc, east, west):
    ids, near = side_ids(pn)
    lines = air.shape[1]
    state = [air[p] for p in range(16)]
    scale = STEP_SIZE * breadth[...]
    ids = [wide(line, lines) for line in ids]
    facing = [
        [lane_take(state[12 + n], ids[0]) for n in range(4)],
        [jnp.where(near[1], lane_take(state[4 * n], ids[1]), 0.0) for n in range(4)],
        [lane_take(state[n], ids[2]) for n in range(4)],
        [jnp.where(near[3], lane_take(state[3 + 4 * n], ids[3]), 0.0) for n in range(4)],
    ]
    result = element_step(
        state,
        lambda p: eastern[p].astype(jnp.float32),
        lambda p: northern[p].astype(jnp.float32),
        scale,
        facing,
    )
    for p in range(16):
        loc[p] = result[p]
    for n in range(4):
        east[0, n] = state[3 + 4 * n].astype(jnp.bfloat16)
        east[1, n] = result[3 + 4 * n].astype(jnp.bfloat16)
        west[0, n] = state[4 * n].astype(jnp.bfloat16)
        west[1, n] = result[4 * n].astype(jnp.bfloat16)


def second_step_kernel(
    loc, eastern, northern, breadth, pn, east, west, next_west, prev_east, first_prev, first_next, out
):
    ids, near = side_ids(pn)
    lines = loc.shape[1]
    scale = STEP_SIZE * breadth[...]
    jump = JUMP_WEIGHT * scale
    ids = [wide(line, lines) for line in ids]
    state = [loc[p] for p in range(16)]

    def across(table, side, breadth_row):
        own = [table[0, n].astype(jnp.float32) for n in range(4)]
        there = next_west if side == 1 else prev_east
        factor = JUMP_WEIGHT * STEP_SIZE * lane_take(wide(breadth_row, lines), ids[side])
        values, beyond = [], []
        for n in range(4):
            values.append(
                jnp.where(near[side], 0.0, lane_take(there[0, n].astype(jnp.float32), ids[side]))
            )
            beyond.append(
                lane_take(there[1, n].astype(jnp.float32), ids[side]) + factor * own[n]
            )
        return values, beyond

    east_now, east_beyond = across(east, 1, first_next[ROW_BREADTH : ROW_BREADTH + 1])
    west_now, west_beyond = across(west, 3, first_prev[ROW_BREADTH : ROW_BREADTH + 1])
    for n in range(4):
        state[3 + 4 * n] = state[3 + 4 * n] + jump * east_now[n]
        state[4 * n] = state[4 * n] + jump * west_now[n]
    facing = [
        [lane_take(state[12 + n], ids[0]) for n in range(4)],
        [jnp.where(near[1], lane_take(state[4 * n], ids[1]), east_beyond[n]) for n in range(4)],
        [lane_take(state[n], ids[2]) for n in range(4)],
        [jnp.where(near[3], lane_take(state[3 + 4 * n], ids[3]), west_beyond[n]) for n in range(4)],
    ]
    result = element_step(
        state,
        lambda p: eastern[p].astype(jnp.float32),
        lambda p: northern[p].astype(jnp.float32),
        scale,
        facing,
    )
    for p in range(16):
        out[p] = result[p]


def forward_kernel(
    holder, down, across, loc, eastern, northern, breadth, pn, from_prev, from_next, weights,
    out, taken, flux, parts, *, devices, tiles
):
    ids, near = side_ids(pn)
    jump = (JUMP_WEIGHT * STEP_SIZE) * breadth[...]
    from_east = lane_take(from_next[0:8], wide(ids[1], 8))
    from_west = lane_take(from_prev[0:8], wide(ids[3], 8))
    from_east = jnp.where(near[1], 0.0, jump * from_east)
    from_west = jnp.where(near[3], 0.0, jump * from_west)
    flux[...] = jnp.zeros_like(flux)
    for p in range(16):
        value = loc[p, 0:1]
        if p % 4 == 3:
            value = value + from_east[p // 4 : p // 4 + 1]
        if p % 4 == 0:
            value = value + from_west[p // 4 : p // 4 + 1]
        u = eastern[p].astype(jnp.float32)[0:1]
        v = northern[p].astype(jnp.float32)[0:1]
        speed = jnp.sqrt(u * u + v * v + 1.0)
        flux[p, 0:1] = speed * value
        flux[p, 1:2] = speed * u
        flux[p, 2:3] = speed * v
    parts[...] = jnp.zeros_like(parts)
    parts[:, ROW_IDS : ROW_IDS + 1, :] = jnp.full((devices, 1, LANES), -1.0, jnp.float32)
    for owner in range(devices):
        taken[owner] = 0
    lane = lax.broadcasted_iota(jnp.int32, (1, LANES), 1)

    def mark(owner, slot, number):
        ids_row = parts[owner, ROW_IDS : ROW_IDS + 1, :]
        parts[owner, ROW_IDS : ROW_IDS + 1, :] = jnp.where(
            lane == slot, jnp.full((1, LANES), number, jnp.int32).astype(jnp.float32), ids_row
        )

    for b in range(weights.shape[0]):
        owner = holder[b, 0]
        rank = jnp.minimum(taken[owner], CAP - 1)
        taken[owner] = taken[owner] + 1
        tile = down[b]
        sums = jnp.dot(
            flux[across[b]].astype(jnp.bfloat16), weights[b], preferred_element_type=jnp.float32
        )
        for f in range(3):
            parts[owner, pl.ds(3 * rank + f, 1), :] = sums[f : f + 1]
        mark(owner, rank, tile)
        after = jnp.where(owner + 1 == devices, 0, owner + 1)
        before = jnp.where(owner == 0, devices - 1, owner - 1)
        for f in range(2):
            parts[after, pl.ds(6 + 2 * rank + f, 1), :] = sums[1 + f : 2 + f]
            parts[before, pl.ds(10 + 2 * rank + f, 1), :] = sums[1 + f : 2 + f]
        last = tile - (tiles - HALO)
        mark(after, 2 + rank, jnp.where(last >= 0, tiles + last, -1))
        mark(before, 4 + rank, jnp.where(tile < HALO, tiles + HALO + tile, -1))
    out[...] = parts[...].astype(jnp.bfloat16)


def back_kernel(holder, across, arrived, weights, second, out, taken, surface, *, devices):
    for owner in range(devices):
        taken[owner] = 0
    surface[...] = jnp.zeros_like(surface)
    for b in range(weights.shape[0]):
        owner = holder[b, 0]
        rank = jnp.minimum(taken[owner], CAP - 1)
        taken[owner] = taken[owner] + 1
        line = arrived[owner, pl.ds(rank, 1), :]
        share = lax.dot_general(
            wide(line, 8).astype(jnp.bfloat16),
            weights[b],
            (((1,), (1,)), ((), ())),
            preferred_element_type=jnp.float32,
        )
        column = across[b]
        surface[column, 0:1] = surface[column, 0:1] + share[0:1]
    out[...] = second[...]
    for p in range(16):
        lowest = second[p, 0:1]
        out[p, 0:1] = lowest + NUDGING_SPEED * (surface[p, 0:1] - lowest)


def split_index(idx):
    return lax.shift_right_arithmetic(idx, 7), idx & (LANES - 1)


def pick(idx, sources):
    high, low = split_index(idx)
    result = jnp.zeros(idx.shape, jnp.float32)
    for number, line in sources:
        result = jnp.where(high == number, lane_take(wide(line, idx.shape[0]), low), result)
    return result


def own_sources(ref):
    return [(HALO + r, ref[r : r + 1]) for r in range(ref.shape[0])]


def combine(terms, factors):
    total = None
    for term, factor in zip(terms, factors):
        if factor != 0.0:
            total = factor * term if total is None else total + factor * term
    return total


def pair_sums(table):
    terms = [table[HALO * k : HALO * (k + 1)] for k in range(6)]
    return combine(terms, COS), combine(terms, SIN)


def rim_partial(rim_idx, rim_w, eta, first):
    rows = rim_idx.shape[0]
    found = pick(rim_idx, own_sources(eta))
    centre = eta[first : first + HALO]
    centre = jnp.concatenate([centre] * (rows // HALO), axis=0)
    return pair_sums(rim_w * (found - centre))


def prepare_kernel(
    air, breadth, eta, sst, flow, nb, span, idx, w, rim_idx, rim_w, u, v, up, dn
):
    tiles = eta.shape[0]
    for r in range(tiles):
        cut = slice(r * LANES, (r + 1) * LANES)
        links = nb[:, cut]
        factors = jnp.where(links >= 0, span[:, cut] * (1.0 / 3.0), 0.0)
        for k in range(6):
            idx[k * tiles + r : k * tiles + r + 1] = links[k : k + 1]
            w[k * tiles + r : k * tiles + r + 1] = factors[k : k + 1]
        u[r : r + 1] = flow[0:1, cut]
        v[r : r + 1] = flow[1:2, cut]
    for side, first in ((0, 0), (1, tiles - HALO)):
        rim_idx[side, 12:16] = jnp.full((4, LANES), -1, jnp.int32)
        rim_w[side, 12:16] = jnp.zeros((4, LANES), jnp.float32)
        for k in range(6):
            cut = slice(k * tiles + first, k * tiles + first + HALO)
            rim_idx[side, HALO * k : HALO * (k + 1)] = idx[cut]
            rim_w[side, HALO * k : HALO * (k + 1)] = w[cut]
    for side, first, target in ((0, 0, dn), (1, tiles - HALO, up)):
        target[...] = jnp.zeros_like(target)
        for n in range(4):
            p = 4 * n if side == 0 else 3 + 4 * n
            target[ROW_EDGE + n : ROW_EDGE + n + 1] = air[p, 0:1]
        target[ROW_BREADTH : ROW_BREADTH + 1] = breadth[...]
        part_x, part_y = rim_partial(rim_idx[side], rim_w[side], eta, first)
        cut = slice(first, first + HALO)
        target[ROW_ETA : ROW_ETA + HALO] = eta[cut]
        target[ROW_U : ROW_U + HALO] = u[cut]
        target[ROW_V : ROW_V + HALO] = v[cut]
        target[ROW_SST : ROW_SST + HALO] = sst[cut]
        target[ROW_PX : ROW_PX + HALO] = part_x
        target[ROW_PY : ROW_PY + HALO] = part_y
        target[ROW_IDX : ROW_IDX + 16] = rim_idx[side].astype(jnp.float32)
        target[ROW_W : ROW_W + 16] = rim_w[side]


def own_gradient(idx, w, eta, gx, gy):
    tiles = eta.shape[0]

    def chunk(c, carry):
        at = pl.multiple_of(c * 8, 8)
        centre = eta[pl.ds(at, 8)]
        terms = []
        for k in range(6):
            found = pick(idx[pl.ds(k * tiles + at, 8)], own_sources(eta))
            terms.append(w[pl.ds(k * tiles + at, 8)] * (found - centre))
        gx[pl.ds(at, 8)] = combine(terms, COS)
        gy[pl.ds(at, 8)] = combine(terms, SIN)
        return carry

    lax.fori_loop(0, tiles // 8, chunk, 0)


def gradient_kernel(idx, w, eta, gx, gy):
    own_gradient(idx, w, eta, gx, gy)


def first_gradient_kernel(idx, w, eta, sst, gx, gy, spread):
    own_gradient(idx, w, eta, gx, gy)
    tiles = eta.shape[0]

    def chunk(c, carry):
        at = pl.multiple_of(c * 8, 8)
        centre = sst[pl.ds(at, 8)]
        total = jnp.zeros_like(centre)
        for k in range(6):
            found = pick(idx[pl.ds(k * tiles + at, 8)], own_sources(sst))
            total = total + w[pl.ds(k * tiles + at, 8)] * (found - centre)
        spread[pl.ds(at, 8)] = total
        return carry

    lax.fori_loop(0, tiles // 8, chunk, 0)


def outer_terms(idx, w, outer, tiles):
    result = []
    for at, offset, base in ((0, 0, 0), (tiles - 8, tiles + HALO, HALO)):
        sources = [(offset + q, outer[base + q : base + q + 1]) for q in range(HALO)]
        terms = []
        for k in range(6):
            rows = slice(k * tiles + at, k * tiles + at + 8)
            terms.append(w[rows] * pick(idx[rows], sources))
        result.append((at, terms))
    return result


def subcycle(
    gx, gy, eta, u, v, sides, fu, fv, fside, before, after, idx, w, side_idx, side_w,
    rim_idx, rim_w, flow, flow_outer, eta_new, u_new, v_new, sides_new, up, dn
):
    tiles = eta.shape[0]
    outer = jnp.concatenate([before[0], after[0]], axis=0)
    u_new[...] = DAMPING * u[...] - GRAVITY * gx[...] + WIND_GAIN * fu[...]
    v_new[...] = DAMPING * v[...] - GRAVITY * gy[...] + WIND_GAIN * fv[...]
    for at, terms in outer_terms(idx, w, outer, tiles):
        u_new[at : at + 8] = u_new[at : at + 8] - GRAVITY * combine(terms, COS)
        v_new[at : at + 8] = v_new[at : at + 8] - GRAVITY * combine(terms, SIN)
    slopes = []
    for side, offset, first, part in (
        (0, tiles + HALO, 0, before),
        (1, 0, tiles - HALO, after),
    ):
        sources = [(offset + q, eta[first + q : first + q + 1]) for q in range(HALO)]
        add_x, add_y = pair_sums(side_w[side] * pick(side_idx[side], sources))
        slopes.append((part[1] + add_x, part[2] + add_y))
    slope = jnp.concatenate([slopes[0][0], slopes[1][0], slopes[0][1], slopes[1][1]], axis=0)
    sides_next = DAMPING * sides[...] - GRAVITY * slope + WIND_GAIN * fside[...]
    u_all, v_all = u_new[...], v_new[...]
    u_side, v_side = sides_next[0 : 2 * HALO], sides_next[2 * HALO : 4 * HALO]
    for kk in range(3):
        if kk == 0:
            flow[kk] = u_all
            flow_outer[kk, 0 : 2 * HALO] = u_side
        else:
            flow[kk] = COS[kk] * u_all + SIN[kk] * v_all
            flow_outer[kk, 0 : 2 * HALO] = COS[kk] * u_side + SIN[kk] * v_side

    def chunk(c, carry):
        at = pl.multiple_of(c * 8, 8)
        total = jnp.zeros((8, LANES), jnp.float32)
        for kk in range(3):
            sources = [(HALO + r, flow[kk, r : r + 1]) for r in range(tiles)]
            sources += [(q, flow_outer[kk, q : q + 1]) for q in range(HALO)]
            sources += [
                (tiles + HALO + q, flow_outer[kk, HALO + q : HALO + q + 1]) for q in range(HALO)
            ]
            centre = flow[kk, pl.ds(at, 8)]
            one = pick(idx[pl.ds(kk * tiles + at, 8)], sources) - centre
            two = pick(idx[pl.ds((kk + 3) * tiles + at, 8)], sources) - centre
            total = (
                total
                + w[pl.ds(kk * tiles + at, 8)] * one
                - w[pl.ds((kk + 3) * tiles + at, 8)] * two
            )
        eta_new[pl.ds(at, 8)] = eta[pl.ds(at, 8)] - DEPTH_RATE * total
        return carry

    lax.fori_loop(0, tiles // 8, chunk, 0)
    if up is None:
        return
    sides_new[...] = sides_next
    for side, first, target in ((0, 0, dn), (1, tiles - HALO, up)):
        part_x, part_y = rim_partial(rim_idx[side], rim_w[side], eta_new, first)
        target[0:HALO] = eta_new[first : first + HALO]
        target[HALO : 2 * HALO] = part_x
        target[2 * HALO : 3 * HALO] = part_y
        target[3 * HALO : 4 * HALO] = jnp.zeros((HALO, LANES), jnp.float32)


def rim_of(ref, rows):
    return tuple(ref[row : row + HALO] for row in rows)


def first_ocean_kernel(
    arrived, first_prev, first_next, gx, gy, eta, u, v, sst, spread, idx, w, rim_idx, rim_w,
    eta_new, u_new, v_new, sides_new, up, dn, fu, fv, fside, side_idx, side_w, warm, answers,
    flow, flow_outer, sides
):
    tiles = eta.shape[0]
    devices = arrived.shape[0]
    parts = arrived[...].astype(jnp.float32)
    ids = parts[:, ROW_IDS, :]
    number = lax.broadcasted_iota(jnp.int32, (devices, LANES), 1).astype(jnp.float32)
    chosen = [
        jnp.where(ids[:, j : j + 1] == number, 1.0, 0.0).astype(jnp.bfloat16) for j in range(6)
    ]
    nothing = jnp.zeros((devices, LANES), jnp.float32)
    lines = []
    for j in range(6):
        rows = [3 * j, 3 * j + 1, 3 * j + 2] if j < 2 else [None, 2 * j + 2, 2 * j + 3]
        lines.append(
            jnp.concatenate([nothing if r is None else parts[:, r, :] for r in rows], axis=1)
        )
    forcing = lax.dot_general(
        jnp.concatenate(chosen, axis=0),
        jnp.concatenate(lines, axis=0).astype(jnp.bfloat16),
        (((0,), (0,)), ((), ())),
        preferred_element_type=jnp.float32,
    )
    fu[...] = forcing[0:tiles, LANES : 2 * LANES]
    fv[...] = forcing[0:tiles, 2 * LANES : 3 * LANES]
    fside[0 : 2 * HALO] = forcing[tiles : tiles + 2 * HALO, LANES : 2 * LANES]
    fside[2 * HALO : 4 * HALO] = forcing[tiles : tiles + 2 * HALO, 2 * LANES : 3 * LANES]

    outer = jnp.concatenate(
        [first_prev[ROW_SST : ROW_SST + HALO], first_next[ROW_SST : ROW_SST + HALO]], axis=0
    )
    warm[...] = (
        sst[...]
        + WARMING_COEFF * forcing[0:tiles, 0:LANES]
        + (0.5 * SPREADING_COEFF) * spread[...]
    )
    for at, terms in outer_terms(idx, w, outer, tiles):
        warm[at : at + 8] = warm[at : at + 8] + (0.5 * SPREADING_COEFF) * combine(
            terms, [1.0] * 6
        )
    half = warm[...].astype(jnp.bfloat16)
    for j in range(CAP):
        answers[:, j, :] = jnp.dot(
            chosen[j][:, 0:tiles], half, preferred_element_type=jnp.float32
        )
    answers[:, CAP:8, :] = jnp.zeros((devices, 8 - CAP, LANES), jnp.float32)

    for side, ref in ((0, first_prev), (1, first_next)):
        side_idx[side] = ref[ROW_IDX : ROW_IDX + 16].astype(jnp.int32)
        side_w[side] = ref[ROW_W : ROW_W + 16]
        for n, row in ((0, ROW_U), (1, ROW_V)):
            at = HALO * (2 * n + side)
            sides[at : at + HALO] = ref[row : row + HALO]
    rows = (ROW_ETA, ROW_PX, ROW_PY)
    subcycle(
        gx, gy, eta, u, v, sides, fu, fv, fside, rim_of(first_prev, rows), rim_of(first_next, rows),
        idx, w, side_idx, side_w, rim_idx, rim_w, flow, flow_outer,
        eta_new, u_new, v_new, sides_new, up, dn
    )


def ocean_kernel(
    from_prev, from_next, gx, gy, eta, u, v, sides, fu, fv, fside, idx, w, side_idx, side_w,
    rim_idx, rim_w, eta_new, u_new, v_new, sides_new, up, dn, flow, flow_outer
):
    rows = (0, HALO, 2 * HALO)
    subcycle(
        gx, gy, eta, u, v, sides, fu, fv, fside, rim_of(from_prev, rows), rim_of(from_next, rows),
        idx, w, side_idx, side_w, rim_idx, rim_w, flow, flow_outer,
        eta_new, u_new, v_new, sides_new, up, dn
    )


def last_ocean_kernel(
    from_prev, from_next, gx, gy, eta, u, v, sides, fu, fv, fside, idx, w, side_idx, side_w,
    rim_idx, rim_w, eta_new, velocity, u_new, v_new, flow, flow_outer
):
    rows = (0, HALO, 2 * HALO)
    subcycle(
        gx, gy, eta, u, v, sides, fu, fv, fside, rim_of(from_prev, rows), rim_of(from_next, rows),
        idx, w, side_idx, side_w, rim_idx, rim_w, flow, flow_outer,
        eta_new, u_new, v_new, None, None, None
    )
    for r in range(eta.shape[0]):
        cut = slice(r * LANES, (r + 1) * LANES)
        velocity[0:1, cut] = u_new[r : r + 1]
        velocity[1:2, cut] = v_new[r : r + 1]


def shards(
    air_warmth,
    eastern_breeze,
    northern_breeze,
    reciprocal_breadth,
    panel_neighbours,
    transfer_coefficients,
    transfer_across_tile,
    transfer_holder,
    transfer_down_tile,
    water_elevation,
    depth_mean_current,
    marine_skin_warmth,
    patch_neighbours,
    interface_span,
):
    devices = lax.axis_size(RING)
    points, levels, elements = air_warmth.shape
    cells = water_elevation.shape[0]
    tiles = cells // LANES
    breadth = reciprocal_breadth.reshape(1, elements)
    eta = water_elevation.reshape(tiles, LANES)
    sst = marine_skin_warmth.reshape(tiles, LANES)
    cell_rows = shape_of(tiles, LANES)
    rim_rows = shape_of(4 * HALO, LANES)

    lowest = pl.BlockSpec((points, 8, elements), lambda i: (0, 0, 0))
    lowest_wind = pl.BlockSpec((points, 16, elements), lambda i: (0, 0, 0))

    idx, w, rim_idx, rim_w, u, v, up, dn = pl.pallas_call(
        prepare_kernel,
        grid=(1,),
        in_specs=[lowest] + vmem(6),
        out_specs=vmem(8),
        out_shape=(
            shape_of(6 * tiles, LANES, dtype=jnp.int32),
            shape_of(6 * tiles, LANES),
            shape_of(2, 16, LANES, dtype=jnp.int32),
            shape_of(2, 16, LANES),
            cell_rows,
            cell_rows,
            shape_of(ROWS_FIRST, LANES),
            shape_of(ROWS_FIRST, LANES),
        ),
        compiler_params=PARAMS,
        name="prepare",
    )(air_warmth, breadth, eta, sst, depth_mean_current, patch_neighbours, interface_span)
    first_prev, first_next = shifted(up, 1), shifted(dn, -1)

    block = pl.BlockSpec((points, 16, elements), lambda i: (0, i, 0))
    edge_block = pl.BlockSpec((2, 4, 16, elements), lambda i: (0, 0, i, 0))
    whole = [
        pl.BlockSpec((1, elements), lambda i: (0, 0)),
        pl.BlockSpec((4, elements), lambda i: (0, 0)),
    ]
    edge_shape = shape_of(2, 4, levels, elements, dtype=jnp.bfloat16)
    loc, east, west = pl.pallas_call(
        local_step_kernel,
        grid=(levels // 16,),
        in_specs=[block, block, block] + whole,
        out_specs=[block, edge_block, edge_block],
        out_shape=(shape_of(points, levels, elements), edge_shape, edge_shape),
        compiler_params=PARAMS,
        name="local_step",
    )(air_warmth, eastern_breeze, northern_breeze, breadth, panel_neighbours)
    prev_east, next_west = shifted(east, 1), shifted(west, -1)

    gx, gy, spread = pl.pallas_call(
        first_gradient_kernel,
        in_specs=vmem(4),
        out_specs=vmem(3),
        out_shape=(cell_rows,) * 3,
        compiler_params=PARAMS,
        name="first_gradient",
    )(idx, w, eta, sst)

    outgoing = pl.pallas_call(
        lambda *refs: forward_kernel(*refs, devices=devices, tiles=tiles),
        grid=(1,),
        in_specs=smem(3) + [lowest, lowest_wind, lowest_wind] + vmem(5),
        out_specs=pl.BlockSpec(memory_space=pltpu.VMEM),
        out_shape=shape_of(devices, PER_DEST, LANES, dtype=jnp.bfloat16),
        scratch_shapes=[
            pltpu.SMEM((devices,), jnp.int32),
            pltpu.VMEM((points, 8, elements), jnp.float32),
            pltpu.VMEM((devices, PER_DEST, LANES), jnp.float32),
        ],
        compiler_params=PARAMS,
        name="forward_remap",
    )(
        transfer_holder, transfer_down_tile, transfer_across_tile, loc, eastern_breeze,
        northern_breeze, breadth, panel_neighbours, first_prev, first_next, transfer_coefficients
    )
    arrived = exchange(outgoing)

    flow_scratch = [
        pltpu.VMEM((3, tiles, LANES), jnp.float32),
        pltpu.VMEM((3, 8, LANES), jnp.float32),
    ]
    tables = (idx, w)
    (
        eta, u, v, sides, up, dn, fu, fv, fside, side_idx, side_w, warm, answers
    ) = pl.pallas_call(
        first_ocean_kernel,
        in_specs=vmem(14),
        out_specs=vmem(13),
        out_shape=(
            cell_rows, cell_rows, cell_rows, rim_rows, rim_rows, rim_rows,
            cell_rows, cell_rows, rim_rows,
            shape_of(2, 16, LANES, dtype=jnp.int32), shape_of(2, 16, LANES),
            cell_rows, shape_of(devices, 8, LANES),
        ),
        scratch_shapes=flow_scratch + [pltpu.VMEM((4 * HALO, LANES), jnp.float32)],
        compiler_params=PARAMS,
        name="first_ocean",
    )(
        arrived, first_prev, first_next, gx, gy, eta, u, v, sst, spread, idx, w, rim_idx, rim_w
    )
    from_prev, from_next = shifted(up, 1), shifted(dn, -1)
    answered = exchange(answers)

    for substep in range(1, NSUB):
        gx, gy = pl.pallas_call(
            gradient_kernel,
            in_specs=vmem(3),
            out_specs=vmem(2),
            out_shape=(cell_rows,) * 2,
            compiler_params=PARAMS,
            name="gradient",
        )(idx, w, eta)
        operands = (
            from_prev, from_next, gx, gy, eta, u, v, sides, fu, fv, fside, idx, w,
            side_idx, side_w, rim_idx, rim_w
        )
        if substep + 1 < NSUB:
            eta, u, v, sides, up, dn = pl.pallas_call(
                ocean_kernel,
                in_specs=vmem(17),
                out_specs=vmem(6),
                out_shape=(cell_rows,) * 3 + (rim_rows,) * 3,
                scratch_shapes=flow_scratch,
                compiler_params=PARAMS,
                name="ocean",
            )(*operands)
            from_prev, from_next = shifted(up, 1), shifted(dn, -1)
        else:
            eta, velocity = pl.pallas_call(
                last_ocean_kernel,
                in_specs=vmem(17),
                out_specs=vmem(2),
                out_shape=(cell_rows, shape_of(2, cells)),
                scratch_shapes=[pltpu.VMEM((tiles, LANES), jnp.float32)] * 2 + flow_scratch,
                compiler_params=PARAMS,
                name="last_ocean",
            )(*operands)

    second = pl.pallas_call(
        second_step_kernel,
        grid=(levels // 16,),
        in_specs=[block, block, block] + whole + [edge_block] * 4 + [
            pl.BlockSpec((ROWS_FIRST, LANES), lambda i: (0, 0))
        ] * 2,
        out_specs=block,
        out_shape=shape_of(points, levels, elements),
        compiler_params=PARAMS,
        name="second_step",
    )(
        loc, eastern_breeze, northern_breeze, breadth, panel_neighbours, east, west,
        next_west, prev_east, first_prev, first_next
    )

    closing = pl.pallas_call(
        lambda *refs: back_kernel(*refs, devices=devices),
        grid=(1,),
        in_specs=smem(2) + vmem(2) + [lowest],
        out_specs=lowest,
        out_shape=shape_of(points, levels, elements),
        scratch_shapes=[
            pltpu.SMEM((devices,), jnp.int32),
            pltpu.VMEM((points, 8, elements), jnp.float32),
        ],
        input_output_aliases={4: 0},
        compiler_params=PARAMS,
        name="back_remap",
    )(transfer_holder, transfer_across_tile, answered, transfer_coefficients, second)
    return closing, eta.reshape(cells), velocity, warm.reshape(cells)


def solution(mesh):
    split = P(RING)
    last = P(None, RING)
    field = P(None, None, RING)
    return jax.shard_map(
        shards,
        mesh=mesh,
        in_specs=(
            field,
            field,
            field,
            split,
            last,
            P(RING, None, None),
            split,
            P(RING, None),
            split,
            split,
            last,
            split,
            last,
            last,
        ),
        out_specs=(field, split, last, split),
        check_vma=False,
    )
```

```python
import math

import jax
import jax.numpy as jnp
import numpy as np
from jax import lax
from jax.experimental import pallas as pl
from jax.experimental.pallas import tpu as pltpu
from jax.sharding import PartitionSpec as P

OY = 256
NSUB = 4
CAP = 2

STEP_SIZE = 0.05
JUMP_WEIGHT = 4.0
NUDGING_SPEED = 0.5
DAMPING = 0.9
GRAVITY = 0.3
WIND_GAIN = 0.3
DEPTH_RATE = 0.3
WARMING_COEFF = 0.3
SPREADING_COEFF = 0.5

RING = ("comp", "dom")
LANES = 128
HALO = OY // LANES
COS = [math.cos(k * math.pi / 3.0) for k in range(6)]
SIN = [0.0 if k % 3 == 0 else math.sin(k * math.pi / 3.0) for k in range(6)]

ROW_EDGE, ROW_BREADTH, ROW_ETA, ROW_U, ROW_V, ROW_SST = 0, 4, 8, 10, 12, 14
ROW_PX, ROW_PY, ROW_IDX, ROW_W, ROWS_FIRST = 16, 18, 24, 40, 56
PER_DEST, ROW_HEAT, ROW_IDS = 16, 12, 14


def swapped(value, first):
    count = lax.axis_size(RING)
    pairs = []
    for i in range(first, count + first, 2):
        pairs += [(i % count, (i + 1) % count), ((i + 1) % count, i % count)]
    return lax.ppermute(value, RING, pairs)


def swap_both(far, near):
    got_far = swapped(far, 1)
    return got_far, swapped(near, 0)


class Received:
    def __init__(self, far, near, odd):
        self.far, self.near, self.odd = far, near, odd

    def flag(self, rows):
        return jnp.broadcast_to(self.odd[0:1], rows.shape) > 0

    def prev(self, *cut):
        far, near = self.far[cut], self.near[cut]
        return jnp.where(self.flag(far), near, far)

    def next(self, *cut):
        far, near = self.far[cut], self.near[cut]
        return jnp.where(self.flag(far), far, near)

    def rim(self, side, row):
        cut = slice(row, row + HALO)
        return self.prev(cut) if side == 0 else self.next(cut)

    def rims(self, side, rows):
        return tuple(self.rim(side, row) for row in rows)


def arrange(up, dn, odd, far, near):
    flag = jnp.broadcast_to(odd[0:1], up.shape) > 0
    far[...] = jnp.where(flag, up[...], dn[...])
    near[...] = jnp.where(flag, dn[...], up[...])


def exchange(value):
    return lax.all_to_all(value, RING, split_axis=0, concat_axis=0, tiled=True)


def gll_matrix():
    points = np.array([-1.0, -1.0 / np.sqrt(5.0), 1.0 / np.sqrt(5.0), 1.0])
    barycentric = [
        1.0 / np.prod([points[s] - points[o] for o in range(4) if o != s]) for s in range(4)
    ]
    table = np.zeros((4, 4))
    for t in range(4):
        for s in range(4):
            if t != s:
                table[t, s] = barycentric[s] / barycentric[t] / (points[t] - points[s])
    for t in (0, 3):
        table[t, t] = -np.sum(table[t])
    return [[float(np.float32(value)) for value in line] for line in table]


GLL = gll_matrix()


def vmem(count):
    return [pl.BlockSpec(memory_space=pltpu.VMEM)] * count


def hbm(count):
    return [pl.BlockSpec(memory_space=pltpu.HBM)] * count


def in_hbm(*arrays):
    return [pltpu.with_memory_space_constraint(array, pltpu.HBM) for array in arrays]


def smem(count):
    return [pl.BlockSpec(memory_space=pltpu.SMEM)] * count


def shape_of(*dims, dtype=jnp.float32):
    return jax.ShapeDtypeStruct(dims, dtype)


PARAMS = pltpu.CompilerParams(vmem_limit_bytes=24 * 1024 * 1024)


def lane_take(rows, ids):
    return jnp.take_along_axis(rows, ids, axis=1, mode="promise_in_bounds")


def wide(row, lines):
    return jnp.broadcast_to(row, (lines, row.shape[1]))


def side_ids(pn):
    count = pn.shape[1]
    bits = count.bit_length() - 1
    table = pn[...]
    ids = [table[k : k + 1] & (count - 1) for k in range(4)]
    home = lax.shift_right_logical(table[0:1], bits)
    near = [lax.shift_right_logical(table[k : k + 1], bits) == home for k in range(4)]
    return ids, near


def element_step(state, east_wind, north_wind, scale, facing):
    jumps = [None] * 16
    sides = (
        (0, 1, 2, 3),
        (3, 7, 11, 15),
        (12, 13, 14, 15),
        (0, 4, 8, 12),
    )
    for k in range(4):
        for n, p in enumerate(sides[k]):
            term = facing[k][n] - state[p]
            jumps[p] = term if jumps[p] is None else jumps[p] + term
    result = []
    for p in range(16):
        i, j = p % 4, p // 4
        grad_x = grad_y = None
        for m in range(4):
            if GLL[i][m] != 0.0:
                term = GLL[i][m] * state[m + 4 * j]
                grad_x = term if grad_x is None else grad_x + term
            if GLL[j][m] != 0.0:
                term = GLL[j][m] * state[i + 4 * m]
                grad_y = term if grad_y is None else grad_y + term
        change = -(east_wind(p) * grad_x + north_wind(p) * grad_y)
        if jumps[p] is not None:
            change = change + JUMP_WEIGHT * jumps[p]
        result.append(state[p] + scale * change)
    return result


def load(pairs, sems):
    copies = [
        pltpu.make_async_copy(source, target, sems.at[n])
        for n, (source, target) in enumerate(pairs)
    ]
    for copy in copies:
        copy.start()
    return copies


def as_column(row):
    count = row.shape[1]
    return jnp.transpose(jnp.broadcast_to(row, (count, count)))


def edge_tables(partner, remote):
    count = partner.shape[1]
    pack = count // 4
    lane = lax.broadcasted_iota(jnp.int32, (count, count), 1)
    line = lax.broadcasted_iota(jnp.int32, (count, count), 0)
    flag = jnp.where(remote, 1.0, 0.0)
    rank = jnp.sum(jnp.where(line < lane, as_column(flag), 0.0), axis=0, keepdims=True)
    rank = as_column(jnp.where(remote, rank, -1.0))
    slot = (lane & (pack - 1)).astype(jnp.float32)
    chosen = jnp.sum(
        jnp.where(rank == slot, line.astype(jnp.float32), 0.0), axis=0, keepdims=True
    ).astype(jnp.int32)
    key = jnp.where(remote, partner, 2 * count).astype(jnp.float32)
    before = jnp.where(as_column(key) < key, 1.0, 0.0)
    place = jnp.sum(before, axis=0, keepdims=True).astype(jnp.int32)
    return chosen, jnp.minimum(place, pack - 1)


def slot_rows(holder_row, down_row, devices, tiles):
    blocks = holder_row.shape[1]
    earlier = lax.broadcasted_iota(jnp.int32, (blocks, blocks), 0) < lax.broadcasted_iota(
        jnp.int32, (blocks, blocks), 1
    )
    number = holder_row.astype(jnp.float32)
    same = as_column(number) == number
    rank = jnp.sum(jnp.where(same & earlier, 1, 0), axis=0, keepdims=True)
    rank = jnp.minimum(rank, CAP - 1)
    target = lax.broadcasted_iota(jnp.int32, (devices, blocks), 0)
    after = jnp.where(holder_row + 1 == devices, 0, holder_row + 1)
    before = jnp.where(holder_row == 0, devices - 1, holder_row - 1)
    last = down_row - (tiles - HALO)
    lane = lax.broadcasted_iota(jnp.int32, (devices, LANES), 1)
    result = jnp.full((devices, LANES), -1.0, jnp.float32)
    for n, (owner, number) in enumerate(
        (
            (holder_row, down_row),
            (after, jnp.where(last >= 0, tiles + last, -1)),
            (before, jnp.where(down_row < HALO, tiles + HALO + down_row, -1)),
        )
    ):
        for slot in range(CAP):
            named = (target == owner) & (rank == slot)
            value = jnp.sum(
                jnp.where(named, (number + 1).astype(jnp.float32), 0.0), axis=1, keepdims=True
            )
            result = jnp.where(lane == CAP * n + slot, value - 1.0, result)
    return result


def home_facing(state, ids, near):
    return [
        [lane_take(state[12 + n], ids[0]) for n in range(4)],
        [jnp.where(near[1], lane_take(state[4 * n], ids[1]), 0.0) for n in range(4)],
        [lane_take(state[n], ids[2]) for n in range(4)],
        [jnp.where(near[3], lane_take(state[3 + 4 * n], ids[3]), 0.0) for n in range(4)],
    ]


def plan_kernel(
    air_hbm, eastern_hbm, northern_hbm, breadth_hbm, pn_hbm, holder_hbm, across_hbm, down_hbm,
    flux, slots, breadth, pn, holder, across, air, eastern, northern, down, sems,
    *, devices, tiles
):
    copies = load(
        (
            (air_hbm.at[:, pl.ds(0, 8), :], air),
            (eastern_hbm.at[:, pl.ds(0, 16), :], eastern),
            (northern_hbm.at[:, pl.ds(0, 16), :], northern),
            (breadth_hbm, breadth),
            (pn_hbm, pn),
            (holder_hbm, holder),
            (across_hbm, across),
            (down_hbm, down),
        ),
        sems,
    )
    for copy in copies:
        copy.wait()
    lines, count = air.shape[1], air.shape[2]
    ids, near = side_ids(pn)
    ids = [wide(line, lines) for line in ids]
    state = [air[p] for p in range(16)]
    u = [eastern[p].astype(jnp.float32)[0:lines] for p in range(16)]
    v = [northern[p].astype(jnp.float32)[0:lines] for p in range(16)]
    result = element_step(
        state, lambda p: u[p], lambda p: v[p], STEP_SIZE * breadth[...],
        home_facing(state, ids, near)
    )
    for p in range(16):
        speed = jnp.sqrt(u[p] * u[p] + v[p] * v[p] + 1.0)
        flux[p, 0:1] = result[p][0:1]
        flux[p, 1:2] = (speed * u[p])[0:1]
        flux[p, 2:3] = (speed * v[p])[0:1]
        flux[p, 3:4] = speed[0:1]
        flux[p, 4:8] = jnp.zeros((4, count), jnp.float32)
    slots[...] = slot_rows(holder[...], down[...], devices, tiles)


def local_step_kernel(
    air_hbm, eastern_hbm, northern_hbm, breadth, pn, loc, eastern, northern, east, west,
    east_pack, west_pack, places, air, sems
):
    copies = load(((air_hbm, air), (eastern_hbm, eastern), (northern_hbm, northern)), sems)
    count = breadth.shape[1]
    lines = 16
    ids, near = side_ids(pn)
    chosen_east, place_east = edge_tables(ids[1], jnp.logical_not(near[1]))
    chosen_west, place_west = edge_tables(ids[3], jnp.logical_not(near[3]))
    places[...] = jnp.zeros_like(places)
    places[0:1] = place_east
    places[1:2] = place_west
    chosen_east, chosen_west = wide(chosen_east, lines), wide(chosen_west, lines)
    group = lax.broadcasted_iota(jnp.int32, (lines, count), 1) // (count // 4)
    scale = STEP_SIZE * breadth[...]
    ids = [wide(line, lines) for line in ids]

    def packed(values, chosen):
        result = jnp.zeros((lines, count), jnp.float32)
        for n in range(4):
            result = jnp.where(group == n, lane_take(values[n], chosen), result)
        return result

    for copy in copies:
        copy.wait()
    levels = air.shape[1]

    def chunk(c, carry):
        at = pl.multiple_of(c * lines, lines)
        rows = pl.ds(at, lines)
        state = [air[p, rows] for p in range(16)]
        result = element_step(
            state,
            lambda p: eastern[p, rows].astype(jnp.float32),
            lambda p: northern[p, rows].astype(jnp.float32),
            scale,
            home_facing(state, ids, near),
        )
        for p in range(16):
            loc[p, rows] = result[p]
        beyond = pl.ds(pl.multiple_of(levels + at, lines), lines)
        for own, pack, chosen, first in (
            (east, east_pack, chosen_east, 3),
            (west, west_pack, chosen_west, 0),
        ):
            for n in range(4):
                own[n, rows] = state[first + 4 * n].astype(jnp.bfloat16)
            pack[rows] = packed([state[first + 4 * n] for n in range(4)], chosen)
            pack[beyond] = packed([result[first + 4 * n] for n in range(4)], chosen)
        return carry

    lax.fori_loop(0, levels // lines, chunk, 0)


def second_step_kernel(
    loc, eastern, northern, breadth, pn, east, west, far, near_swap, places, first_far,
    first_near, odd, surface, out_hbm, out, sems
):
    ids, near = side_ids(pn)
    levels, count = loc.shape[1], loc.shape[2]
    lines = 16
    pack = count // 4
    scale = STEP_SIZE * breadth[...]
    jump = JUMP_WEIGHT * scale
    ids = [wide(line, lines) for line in ids]
    got = Received(far, near_swap, odd)
    first = Received(first_far, first_near, odd)
    row = slice(ROW_BREADTH, ROW_BREADTH + 1)
    factors = [
        JUMP_WEIGHT * STEP_SIZE * lane_take(wide(line, lines), ids[side])
        for side, line in ((1, first.next(row)), (3, first.prev(row)))
    ]
    spots = [
        [wide(places[n : n + 1] + m * pack, lines) for m in range(4)] for n in (0, 1)
    ]

    def copy_out(c):
        rows = pl.ds(pl.multiple_of(c * lines, lines), lines)
        return pltpu.make_async_copy(out.at[:, rows, :], out_hbm.at[:, rows, :], sems.at[c])

    def chunk(c, carry):
        at = pl.multiple_of(c * lines, lines)
        rows = pl.ds(at, lines)
        now = pl.ds(pl.multiple_of(4 * HALO + at, 8), lines)
        later = pl.ds(pl.multiple_of(4 * HALO + levels + at, 8), lines)
        state = [loc[p, rows] for p in range(16)]

        def across(own, there_now, there_next, side, factor, spot):
            values, beyond = [], []
            for n in range(4):
                values.append(jnp.where(near[side], 0.0, lane_take(there_now, spot[n])))
                beyond.append(
                    lane_take(there_next, spot[n]) + factor * own[n, rows].astype(jnp.float32)
                )
            return values, beyond

        east_now, east_beyond = across(
            east, got.next(now), got.next(later), 1, factors[0], spots[0]
        )
        west_now, west_beyond = across(
            west, got.prev(now), got.prev(later), 3, factors[1], spots[1]
        )
        for n in range(4):
            state[3 + 4 * n] = state[3 + 4 * n] + jump * east_now[n]
            state[4 * n] = state[4 * n] + jump * west_now[n]
        facing = home_facing(state, ids, near)
        facing[1] = [jnp.where(near[1], facing[1][n], east_beyond[n]) for n in range(4)]
        facing[3] = [jnp.where(near[3], facing[3][n], west_beyond[n]) for n in range(4)]
        result = element_step(
            state,
            lambda p: eastern[p, rows].astype(jnp.float32),
            lambda p: northern[p, rows].astype(jnp.float32),
            scale,
            facing,
        )
        for p in range(16):
            out[p, rows] = result[p]

        @pl.when(c == 0)
        def _():
            for p in range(16):
                lowest = out[p, 0:1]
                out[p, 0:1] = lowest + NUDGING_SPEED * (surface[p : p + 1] - lowest)

        copy_out(c).start()
        return carry

    lax.fori_loop(0, levels // lines, chunk, 0)

    def finish(c, carry):
        copy_out(c).wait()
        return carry

    lax.fori_loop(0, levels // lines, finish, 0)


def forward_kernel(
    holder, across, flux, slots, breadth, pn, first_far, first_near, odd, weights,
    out, taken, source, own, *, devices
):
    ids, near = side_ids(pn)
    jump = (JUMP_WEIGHT * STEP_SIZE) * breadth[...]
    first = Received(first_far, first_near, odd)
    from_east = lane_take(first.next(slice(0, 8)), wide(ids[1], 8))
    from_west = lane_take(first.prev(slice(0, 8)), wide(ids[3], 8))
    from_east = jnp.where(near[1], 0.0, jump * from_east)
    from_west = jnp.where(near[3], 0.0, jump * from_west)
    for p in range(16):
        value = flux[p, 0:1]
        if p % 4 == 3:
            value = value + from_east[p // 4 : p // 4 + 1]
        if p % 4 == 0:
            value = value + from_west[p // 4 : p // 4 + 1]
        source[p] = flux[p]
        source[p, 0:1] = flux[p, 3:4] * value
    own[...] = jnp.zeros_like(own)
    for owner in range(devices):
        taken[owner] = 0
    for b in range(weights.shape[0]):
        owner = holder[0, b]
        rank = jnp.minimum(taken[owner], CAP - 1)
        taken[owner] = taken[owner] + 1
        sums = jnp.dot(
            source[across[0, b]].astype(jnp.bfloat16), weights[b], preferred_element_type=jnp.float32
        )
        own[owner, pl.ds(2 * rank, 1), :] = sums[1:2]
        own[owner, pl.ds(2 * rank + 1, 1), :] = sums[2:3]
        own[owner, pl.ds(4 + rank, 1), :] = sums[0:1]
    line = lax.broadcasted_iota(jnp.int32, (8, LANES), 0)
    for d in range(devices):
        mine = own[d]
        prev = own[(d - 1) % devices]
        following = own[(d + 1) % devices]
        top = jnp.concatenate([mine[0:4], prev[0:4]], axis=0)
        bottom = jnp.where(line < 4, following, mine)
        bottom = jnp.where(line == ROW_IDS - 8, wide(slots[d : d + 1], 8), bottom)
        out[d] = jnp.concatenate([top, bottom], axis=0).astype(jnp.bfloat16)


def back_kernel(holder, across, arrived, weights, surface, taken, places, share, *, devices):
    for owner in range(devices):
        taken[owner] = 0
    blocks = weights.shape[0]
    points = surface.shape[0]
    for column in range(points):
        taken[devices + column] = 0
    for b in range(blocks):
        owner = holder[0, b]
        rank = jnp.minimum(taken[owner], CAP - 1)
        taken[owner] = taken[owner] + 1
        column = across[0, b]
        seen = jnp.minimum(taken[devices + column], 1)
        taken[devices + column] = taken[devices + column] + 1
        places[2 * column + seen] = b
        line = arrived[owner, pl.ds(rank, 1), :]
        share[b] = lax.dot_general(
            wide(line, 8).astype(jnp.bfloat16),
            weights[b],
            (((1,), (1,)), ((), ())),
            preferred_element_type=jnp.float32,
        )
    for p in range(points):
        surface[p : p + 1] = share[places[2 * p], 0:1] + share[places[2 * p + 1], 0:1]


def split_index(idx):
    return lax.shift_right_arithmetic(idx, 7), idx & (LANES - 1)


def pick(idx, sources):
    high, low = split_index(idx)
    result = jnp.zeros(idx.shape, jnp.float32)
    for number, line in sources:
        result = jnp.where(high == number, lane_take(wide(line, idx.shape[0]), low), result)
    return result


def own_sources(ref):
    return [(HALO + r, ref[r : r + 1]) for r in range(ref.shape[0])]


def combine(terms, factors):
    total = None
    for term, factor in zip(terms, factors):
        if factor != 0.0:
            total = factor * term if total is None else total + factor * term
    return total


def pair_sums(table):
    terms = [table[HALO * k : HALO * (k + 1)] for k in range(6)]
    return combine(terms, COS), combine(terms, SIN)


def rim_partial(rim_idx, rim_w, eta, first):
    rows = rim_idx.shape[0]
    found = pick(rim_idx, own_sources(eta))
    centre = eta[first : first + HALO]
    centre = jnp.concatenate([centre] * (rows // HALO), axis=0)
    return pair_sums(rim_w * (found - centre))


def prepare_kernel(
    air_hbm, breadth_hbm, pn_hbm, eta_hbm, sst_hbm, flow_hbm, nb_hbm, span_hbm,
    idx, w, rim_idx, rim_w, u, v, eta, sst, far, near, odd, up, dn, air, breadth, pn, flow, nb,
    span, sems
):
    copies = load(
        (
            (nb_hbm, nb),
            (span_hbm, span),
            (flow_hbm, flow),
            (eta_hbm, eta),
            (sst_hbm, sst),
            (breadth_hbm, breadth),
            (pn_hbm, pn),
            (air_hbm.at[:, pl.ds(0, 8), :], air),
        ),
        sems,
    )
    for copy in copies:
        copy.wait()
    shard = lax.shift_right_logical(pn[0:1], pn.shape[1].bit_length() - 1)
    odd[...] = wide(shard & 1, 8)
    tiles = eta.shape[0]
    for r in range(tiles):
        cut = slice(r * LANES, (r + 1) * LANES)
        links = nb[:, cut]
        factors = jnp.where(links >= 0, span[:, cut] * (1.0 / 3.0), 0.0)
        for k in range(6):
            idx[k * tiles + r : k * tiles + r + 1] = links[k : k + 1]
            w[k * tiles + r : k * tiles + r + 1] = factors[k : k + 1]
        u[r : r + 1] = flow[0:1, cut]
        v[r : r + 1] = flow[1:2, cut]
    for side, first in ((0, 0), (1, tiles - HALO)):
        rim_idx[side, 12:16] = jnp.full((4, LANES), -1, jnp.int32)
        rim_w[side, 12:16] = jnp.zeros((4, LANES), jnp.float32)
        for k in range(6):
            cut = slice(k * tiles + first, k * tiles + first + HALO)
            rim_idx[side, HALO * k : HALO * (k + 1)] = idx[cut]
            rim_w[side, HALO * k : HALO * (k + 1)] = w[cut]
    for side, first, target in ((0, 0, dn), (1, tiles - HALO, up)):
        target[...] = jnp.zeros_like(target)
        for n in range(4):
            p = 4 * n if side == 0 else 3 + 4 * n
            target[ROW_EDGE + n : ROW_EDGE + n + 1] = air[p, 0:1]
        target[ROW_BREADTH : ROW_BREADTH + 1] = breadth[...]
        part_x, part_y = rim_partial(rim_idx[side], rim_w[side], eta, first)
        cut = slice(first, first + HALO)
        target[ROW_ETA : ROW_ETA + HALO] = eta[cut]
        target[ROW_U : ROW_U + HALO] = u[cut]
        target[ROW_V : ROW_V + HALO] = v[cut]
        target[ROW_SST : ROW_SST + HALO] = sst[cut]
        target[ROW_PX : ROW_PX + HALO] = part_x
        target[ROW_PY : ROW_PY + HALO] = part_y
        target[ROW_IDX : ROW_IDX + 16] = rim_idx[side].astype(jnp.float32)
        target[ROW_W : ROW_W + 16] = rim_w[side]
    arrange(up, dn, odd, far, near)


def own_gradient(idx, w, eta, gx, gy):
    tiles = eta.shape[0]

    def chunk(c, carry):
        at = pl.multiple_of(c * 8, 8)
        centre = eta[pl.ds(at, 8)]
        terms = []
        for k in range(6):
            found = pick(idx[pl.ds(k * tiles + at, 8)], own_sources(eta))
            terms.append(w[pl.ds(k * tiles + at, 8)] * (found - centre))
        gx[pl.ds(at, 8)] = combine(terms, COS)
        gy[pl.ds(at, 8)] = combine(terms, SIN)
        return carry

    lax.fori_loop(0, tiles // 8, chunk, 0)


def inner_kernel(idx, w, eta, u, v, fu, fv, eta_part, u_part, v_part, flow):
    own_gradient(idx, w, eta, u_part, v_part)
    tiles = eta.shape[0]
    u_part[...] = DAMPING * u[...] - GRAVITY * u_part[...] + WIND_GAIN * fu[...]
    v_part[...] = DAMPING * v[...] - GRAVITY * v_part[...] + WIND_GAIN * fv[...]
    fill_flow(flow, u_part[...], v_part[...])

    def chunk(c, carry):
        at = pl.multiple_of(c * 8, 8)
        total = jnp.zeros((8, LANES), jnp.float32)
        for kk in range(3):
            sources = [(HALO + r, flow[kk, r : r + 1]) for r in range(tiles)]
            centre = flow[kk, pl.ds(at, 8)]
            one = pick(idx[pl.ds(kk * tiles + at, 8)], sources) - centre
            two = pick(idx[pl.ds((kk + 3) * tiles + at, 8)], sources) - centre
            total = (
                total
                + w[pl.ds(kk * tiles + at, 8)] * one
                - w[pl.ds((kk + 3) * tiles + at, 8)] * two
            )
        eta_part[pl.ds(at, 8)] = eta[pl.ds(at, 8)] - DEPTH_RATE * total
        return carry

    lax.fori_loop(0, tiles // 8, chunk, 0)


def first_gradient_kernel(idx, w, eta, sst, gx, gy, spread):
    own_gradient(idx, w, eta, gx, gy)
    tiles = eta.shape[0]

    def chunk(c, carry):
        at = pl.multiple_of(c * 8, 8)
        centre = sst[pl.ds(at, 8)]
        total = jnp.zeros_like(centre)
        for k in range(6):
            found = pick(idx[pl.ds(k * tiles + at, 8)], own_sources(sst))
            total = total + w[pl.ds(k * tiles + at, 8)] * (found - centre)
        spread[pl.ds(at, 8)] = total
        return carry

    lax.fori_loop(0, tiles // 8, chunk, 0)


def fill_flow(flow, u, v):
    flow[0] = u
    for kk in (1, 2):
        flow[kk] = COS[kk] * u + SIN[kk] * v


def side_currents(eta, sides, fside, before, after, side_idx, side_w):
    tiles = eta.shape[0]
    slopes = []
    for side, offset, first, part in (
        (0, tiles + HALO, 0, before),
        (1, 0, tiles - HALO, after),
    ):
        sources = [(offset + q, eta[first + q : first + q + 1]) for q in range(HALO)]
        add_x, add_y = pair_sums(side_w[side] * pick(side_idx[side], sources))
        slopes.append((part[1] + add_x, part[2] + add_y))
    slope = jnp.concatenate([slopes[0][0], slopes[1][0], slopes[0][1], slopes[1][1]], axis=0)
    return DAMPING * sides[...] - GRAVITY * slope + WIND_GAIN * fside[...]


def rim_slopes(rim_idx, rim_w, before, after, tiles):
    result = []
    for side, offset, part in ((0, 0, before), (1, tiles + HALO, after)):
        sources = [(offset + q, part[0][q : q + 1]) for q in range(HALO)]
        result.append(pair_sums(rim_w[side] * pick(rim_idx[side], sources)))
    return result


def send_rims(eta, rim_idx, rim_w, odd, far, near, up, dn):
    tiles = eta.shape[0]
    for side, first, target in ((0, 0, dn), (1, tiles - HALO, up)):
        part_x, part_y = rim_partial(rim_idx[side], rim_w[side], eta, first)
        target[0:HALO] = eta[first : first + HALO]
        target[HALO : 2 * HALO] = part_x
        target[2 * HALO : 3 * HALO] = part_y
        target[3 * HALO : 4 * HALO] = jnp.zeros((HALO, LANES), jnp.float32)
    rows = pl.ds(0, 4 * HALO)
    arrange(up, dn, odd, far.at[rows], near.at[rows])


def first_subcycle(
    gx, gy, eta, u, v, sides, fu, fv, fside, before, after, idx, w, side_idx, side_w,
    rim_idx, rim_w, flow, flow_outer, eta_new, u_new, v_new, sides_new
):
    tiles = eta.shape[0]
    u_new[...] = DAMPING * u[...] - GRAVITY * gx[...] + WIND_GAIN * fu[...]
    v_new[...] = DAMPING * v[...] - GRAVITY * gy[...] + WIND_GAIN * fv[...]
    slopes = rim_slopes(rim_idx, rim_w, before, after, tiles)
    for first, (add_x, add_y) in zip((0, tiles - HALO), slopes):
        rows = slice(first, first + HALO)
        u_new[rows] = u_new[rows] - GRAVITY * add_x
        v_new[rows] = v_new[rows] - GRAVITY * add_y
    sides_next = side_currents(eta, sides, fside, before, after, side_idx, side_w)
    sides_new[...] = sides_next
    fill_flow(flow, u_new[...], v_new[...])
    fill_flow(flow_outer, sides_next[0 : 2 * HALO], sides_next[2 * HALO : 4 * HALO])

    def chunk(c, carry):
        at = pl.multiple_of(c * 8, 8)
        total = jnp.zeros((8, LANES), jnp.float32)
        for kk in range(3):
            sources = [(HALO + r, flow[kk, r : r + 1]) for r in range(tiles)]
            sources += [(q, flow_outer[kk, q : q + 1]) for q in range(HALO)]
            sources += [
                (tiles + HALO + q, flow_outer[kk, HALO + q : HALO + q + 1]) for q in range(HALO)
            ]
            centre = flow[kk, pl.ds(at, 8)]
            one = pick(idx[pl.ds(kk * tiles + at, 8)], sources) - centre
            two = pick(idx[pl.ds((kk + 3) * tiles + at, 8)], sources) - centre
            total = (
                total
                + w[pl.ds(kk * tiles + at, 8)] * one
                - w[pl.ds((kk + 3) * tiles + at, 8)] * two
            )
        eta_new[pl.ds(at, 8)] = eta[pl.ds(at, 8)] - DEPTH_RATE * total
        return carry

    lax.fori_loop(0, tiles // 8, chunk, 0)


def outer_subcycle(
    eta, eta_part, u_part, v_part, sides, fside, before, after, idx, w, side_idx, side_w,
    rim_idx, rim_w, flow_outer, eta_new, u_new, v_new
):
    tiles = eta.shape[0]
    slopes = rim_slopes(rim_idx, rim_w, before, after, tiles)
    sides_next = side_currents(eta, sides, fside, before, after, side_idx, side_w)
    u_new[...] = u_part[...]
    v_new[...] = v_part[...]
    changes_u = [-GRAVITY * slopes[side][0] for side in (0, 1)]
    changes_v = [-GRAVITY * slopes[side][1] for side in (0, 1)]
    for side, first in ((0, 0), (1, tiles - HALO)):
        rows = slice(first, first + HALO)
        u_new[rows] = u_new[rows] + changes_u[side]
        v_new[rows] = v_new[rows] + changes_v[side]
    fill_flow(
        flow_outer,
        jnp.concatenate([sides_next[0 : 2 * HALO]] + changes_u, axis=0),
        jnp.concatenate([sides_next[2 * HALO : 4 * HALO]] + changes_v, axis=0),
    )
    for c in range(tiles // 8):
        at = c * 8
        total = jnp.zeros((8, LANES), jnp.float32)
        for kk in range(3):
            line = lambda n: flow_outer[kk, n : n + 1]
            sources = [(HALO + q, line(2 * HALO + q)) for q in range(HALO)]
            sources += [(tiles + q, line(3 * HALO + q)) for q in range(HALO)]
            if at == 0:
                sources += [(q, line(q)) for q in range(HALO)]
            if at + 8 == tiles:
                sources += [(tiles + HALO + q, line(HALO + q)) for q in range(HALO)]
            total = (
                total
                + w[kk * tiles + at : kk * tiles + at + 8]
                * pick(idx[kk * tiles + at : kk * tiles + at + 8], sources)
                - w[(kk + 3) * tiles + at : (kk + 3) * tiles + at + 8]
                * pick(idx[(kk + 3) * tiles + at : (kk + 3) * tiles + at + 8], sources)
            )
        eta_new[at : at + 8] = eta_part[at : at + 8] - DEPTH_RATE * total
    for side, first in ((0, 0), (1, tiles - HALO)):
        centre = jnp.zeros((HALO, LANES), jnp.float32)
        for kk in range(3):
            factor = (
                rim_w[side, HALO * kk : HALO * (kk + 1)]
                - rim_w[side, HALO * (kk + 3) : HALO * (kk + 4)]
            )
            start = (2 + side) * HALO
            centre = centre + factor * flow_outer[kk, start : start + HALO]
        rows = slice(first, first + HALO)
        eta_new[rows] = eta_new[rows] + DEPTH_RATE * centre
    return sides_next


def first_ocean_kernel(
    arrived, first_far, first_near, odd, gx, gy, eta, u, v, idx, w, rim_idx, rim_w,
    east_pack, west_pack, eta_new, u_new, v_new, sides_new, far, near, fu, fv, fside, side_idx,
    side_w, heat, ids, flow, flow_outer, sides, up, dn
):
    tiles = eta.shape[0]
    devices = arrived.shape[0]
    parts = arrived[...].astype(jnp.float32)
    ids[...] = parts[:, ROW_IDS, :]
    number = lax.broadcasted_iota(jnp.int32, (devices, LANES), 1).astype(jnp.float32)
    nothing = jnp.zeros((devices, LANES), jnp.float32)
    chosen, lines = [], []
    for j in range(3 * CAP):
        chosen.append(jnp.where(ids[:, j : j + 1] == number, 1.0, 0.0))
        first = parts[:, ROW_HEAT + j, :] if j < CAP else nothing
        lines.append(
            jnp.concatenate([first, parts[:, 2 * j, :], parts[:, 2 * j + 1, :]], axis=1)
        )
    forcing = lax.dot_general(
        jnp.concatenate(chosen, axis=0).astype(jnp.bfloat16),
        jnp.concatenate(lines, axis=0).astype(jnp.bfloat16),
        (((0,), (0,)), ((), ())),
        preferred_element_type=jnp.float32,
    )
    heat[...] = forcing[0:tiles, 0:LANES]
    fu[...] = forcing[0:tiles, LANES : 2 * LANES]
    fv[...] = forcing[0:tiles, 2 * LANES : 3 * LANES]
    fside[0 : 2 * HALO] = forcing[tiles : tiles + 2 * HALO, LANES : 2 * LANES]
    fside[2 * HALO : 4 * HALO] = forcing[tiles : tiles + 2 * HALO, 2 * LANES : 3 * LANES]
    first = Received(first_far, first_near, odd)
    for side, part in ((0, first.prev), (1, first.next)):
        side_idx[side] = part(slice(ROW_IDX, ROW_IDX + 16)).astype(jnp.int32)
        side_w[side] = part(slice(ROW_W, ROW_W + 16))
        for n, row in ((0, ROW_U), (1, ROW_V)):
            at = HALO * (2 * n + side)
            sides[at : at + HALO] = first.rim(side, row)
    rows = (ROW_ETA, ROW_PX, ROW_PY)
    first_subcycle(
        gx, gy, eta, u, v, sides, fu, fv, fside, first.rims(0, rows), first.rims(1, rows), idx, w, side_idx, side_w, rim_idx, rim_w, flow, flow_outer,
        eta_new, u_new, v_new, sides_new
    )
    send_rims(eta_new, rim_idx, rim_w, odd, far, near, up, dn)
    flag = jnp.broadcast_to(odd[0:1], east_pack.shape) > 0
    far[4 * HALO :] = jnp.where(flag, east_pack[...], west_pack[...])
    near[4 * HALO :] = jnp.where(flag, west_pack[...], east_pack[...])


def sea_kernel(
    first_far, first_near, odd, sst, heat, spread, ids, rim_idx, rim_w, warm, answers
):
    first = Received(first_far, first_near, odd)
    tiles = sst.shape[0]
    devices = ids.shape[0]
    warm[...] = (
        sst[...] + WARMING_COEFF * heat[...] + (0.5 * SPREADING_COEFF) * spread[...]
    )
    for side, start, offset in ((0, 0, 0), (1, tiles - HALO, tiles + HALO)):
        rim = first.rim(side, ROW_SST)
        sources = [(offset + q, rim[q : q + 1]) for q in range(HALO)]
        found = rim_w[side] * pick(rim_idx[side], sources)
        total = combine([found[HALO * k : HALO * (k + 1)] for k in range(6)], [1.0] * 6)
        rows = slice(start, start + HALO)
        warm[rows] = warm[rows] + (0.5 * SPREADING_COEFF) * total
    half = warm[...].astype(jnp.bfloat16)
    number = lax.broadcasted_iota(jnp.int32, (devices, tiles), 1).astype(jnp.float32)
    for j in range(CAP):
        chosen = jnp.where(ids[:, j : j + 1] == number, 1.0, 0.0).astype(jnp.bfloat16)
        answers[:, j, :] = jnp.dot(chosen, half, preferred_element_type=jnp.float32)


def ocean_kernel(
    far, near, odd, eta, eta_part, u_part, v_part, sides, fside, idx, w, side_idx, side_w,
    rim_idx, rim_w, eta_new, u_new, v_new, sides_new, far_new, near_new, flow_outer, up, dn
):
    rows = (0, HALO, 2 * HALO)
    got = Received(far, near, odd)
    sides_new[...] = outer_subcycle(
        eta, eta_part, u_part, v_part, sides, fside, got.rims(0, rows), got.rims(1, rows), idx, w, side_idx, side_w, rim_idx, rim_w, flow_outer,
        eta_new, u_new, v_new
    )
    send_rims(eta_new, rim_idx, rim_w, odd, far_new, near_new, up, dn)


def last_ocean_kernel(
    far, near, odd, eta, eta_part, u_part, v_part, sides, fside, idx, w, side_idx, side_w,
    rim_idx, rim_w, eta_new, velocity, u_new, v_new, flow_outer
):
    rows = (0, HALO, 2 * HALO)
    got = Received(far, near, odd)
    outer_subcycle(
        eta, eta_part, u_part, v_part, sides, fside, got.rims(0, rows), got.rims(1, rows), idx, w, side_idx, side_w, rim_idx, rim_w, flow_outer,
        eta_new, u_new, v_new
    )
    for r in range(eta.shape[0]):
        cut = slice(r * LANES, (r + 1) * LANES)
        velocity[0:1, cut] = u_new[r : r + 1]
        velocity[1:2, cut] = v_new[r : r + 1]


def shards(
    air_warmth,
    eastern_breeze,
    northern_breeze,
    reciprocal_breadth,
    panel_neighbours,
    transfer_coefficients,
    transfer_across_tile,
    transfer_holder,
    transfer_down_tile,
    water_elevation,
    depth_mean_current,
    marine_skin_warmth,
    patch_neighbours,
    interface_span,
):
    devices = lax.axis_size(RING)
    points, levels, elements = air_warmth.shape
    cells = water_elevation.shape[0]
    tiles = cells // LANES
    blocks = transfer_holder.shape[0]
    cell_rows = shape_of(tiles, LANES)
    rim_rows = shape_of(4 * HALO, LANES)
    dma = pltpu.SemaphoreType.DMA
    air, eastern, northern, breadth_hbm, pn_hbm = in_hbm(
        air_warmth, eastern_breeze, northern_breeze, reciprocal_breadth.reshape(1, elements),
        panel_neighbours
    )

    idx, w, rim_idx, rim_w, u, v, eta, sst, far, near, odd = pl.pallas_call(
        prepare_kernel,
        in_specs=hbm(8),
        out_specs=vmem(11),
        out_shape=(
            shape_of(6 * tiles, LANES, dtype=jnp.int32),
            shape_of(6 * tiles, LANES),
            shape_of(2, 16, LANES, dtype=jnp.int32),
            shape_of(2, 16, LANES),
            cell_rows,
            cell_rows,
            cell_rows,
            cell_rows,
            shape_of(ROWS_FIRST, LANES),
            shape_of(ROWS_FIRST, LANES),
            shape_of(8, elements, dtype=jnp.int32),
        ),
        scratch_shapes=[
            pltpu.VMEM((ROWS_FIRST, LANES), jnp.float32),
            pltpu.VMEM((ROWS_FIRST, LANES), jnp.float32),
            pltpu.VMEM((points, 8, elements), jnp.float32),
            pltpu.VMEM((1, elements), jnp.float32),
            pltpu.VMEM((4, elements), jnp.int32),
            pltpu.VMEM((2, cells), jnp.float32),
            pltpu.VMEM((6, cells), jnp.int32),
            pltpu.VMEM((6, cells), jnp.float32),
            dma((8,)),
        ],
        compiler_params=PARAMS,
        name="prepare",
    )(
        air,
        breadth_hbm,
        pn_hbm,
        *in_hbm(
            water_elevation.reshape(tiles, LANES),
            marine_skin_warmth.reshape(tiles, LANES),
            depth_mean_current,
            patch_neighbours,
            interface_span,
        ),
    )
    first_far, first_near = swap_both(far, near)

    one_row = shape_of(1, blocks, dtype=jnp.int32)
    low_wind = pltpu.VMEM((points, 16, elements), jnp.bfloat16)
    flux, slots, breadth, pn, holder, across = pl.pallas_call(
        lambda *refs: plan_kernel(*refs, devices=devices, tiles=tiles),
        in_specs=hbm(8),
        out_specs=vmem(6),
        out_shape=(
            shape_of(points, 8, elements), shape_of(devices, LANES), shape_of(1, elements),
            shape_of(4, elements, dtype=jnp.int32), one_row, one_row
        ),
        scratch_shapes=[
            pltpu.VMEM((points, 8, elements), jnp.float32), low_wind, low_wind,
            pltpu.VMEM((1, blocks), jnp.int32), dma((8,))
        ],
        compiler_params=PARAMS,
        name="plan",
    )(
        air,
        eastern,
        northern,
        breadth_hbm,
        pn_hbm,
        *in_hbm(
            transfer_holder.reshape(1, blocks),
            transfer_across_tile.reshape(1, blocks),
            transfer_down_tile.reshape(1, blocks),
        ),
    )

    outgoing = pl.pallas_call(
        lambda *refs: forward_kernel(*refs, devices=devices),
        in_specs=smem(2) + vmem(8),
        out_specs=pl.BlockSpec(memory_space=pltpu.VMEM),
        out_shape=shape_of(devices, PER_DEST, LANES, dtype=jnp.bfloat16),
        scratch_shapes=[
            pltpu.SMEM((devices,), jnp.int32),
            pltpu.VMEM((points, 8, elements), jnp.float32),
            pltpu.VMEM((devices, 8, LANES), jnp.float32),
        ],
        compiler_params=PARAMS,
        name="forward_remap",
    )(
        holder, across, flux, slots, breadth, pn, first_far, first_near, odd,
        transfer_coefficients
    )
    outgoing, pn, gradient_eta = lax.optimization_barrier((outgoing, pn, eta))
    arrived = exchange(outgoing)
    gx, gy, spread = pl.pallas_call(
        first_gradient_kernel,
        in_specs=vmem(4),
        out_specs=vmem(3),
        out_shape=(cell_rows,) * 3,
        compiler_params=PARAMS,
        name="first_gradient",
    )(idx, w, gradient_eta, sst)

    field = shape_of(points, levels, elements)
    edge = shape_of(4, levels, elements, dtype=jnp.bfloat16)
    pack = shape_of(2 * levels, elements)
    wind = shape_of(points, levels, elements, dtype=jnp.bfloat16)
    loc, eastern, northern, east, west, east_pack, west_pack, places = pl.pallas_call(
        local_step_kernel,
        in_specs=hbm(3) + vmem(2),
        out_specs=vmem(8),
        out_shape=(
            field, wind, wind, edge, edge, pack, pack, shape_of(8, elements, dtype=jnp.int32)
        ),
        scratch_shapes=[pltpu.VMEM((points, levels, elements), jnp.float32), dma((3,))],
        compiler_params=PARAMS,
        name="local_step",
    )(air, eastern, northern, breadth, pn)

    rim_scratch = pltpu.VMEM((4 * HALO, LANES), jnp.float32)
    second_rows = shape_of(4 * HALO + 2 * levels, elements)
    flow_scratch = [
        pltpu.VMEM((3, tiles, LANES), jnp.float32),
        pltpu.VMEM((3, 2 * HALO, LANES), jnp.float32),
    ]
    (
        eta, u, v, sides, far, near, fu, fv, fside, side_idx, side_w, heat, ids
    ) = pl.pallas_call(
        first_ocean_kernel,
        in_specs=vmem(15),
        out_specs=vmem(13),
        out_shape=(
            cell_rows, cell_rows, cell_rows, rim_rows, second_rows, second_rows,
            cell_rows, cell_rows, rim_rows,
            shape_of(2, 16, LANES, dtype=jnp.int32), shape_of(2, 16, LANES),
            cell_rows, shape_of(devices, LANES),
        ),
        scratch_shapes=flow_scratch + [rim_scratch] * 3,
        compiler_params=PARAMS,
        name="first_ocean",
    )(
        arrived, first_far, first_near, odd, gx, gy, eta, u, v, idx, w, rim_idx, rim_w,
        east_pack, west_pack
    )
    far, near = swap_both(far, near)
    edges_far, edges_near = far, near

    for substep in range(1, NSUB):
        eta_part, u_part, v_part = pl.pallas_call(
            inner_kernel,
            in_specs=vmem(7),
            out_specs=vmem(3),
            out_shape=(cell_rows,) * 3,
            scratch_shapes=flow_scratch[:1],
            compiler_params=PARAMS,
            name="inner",
        )(idx, w, eta, u, v, fu, fv)
        if substep == 1:
            eta_part, heat = lax.optimization_barrier((eta_part, heat))
            warm, answers = pl.pallas_call(
                sea_kernel,
                in_specs=vmem(9),
                out_specs=vmem(2),
                out_shape=(cell_rows, shape_of(devices, CAP, LANES)),
                compiler_params=PARAMS,
                name="sea",
            )(first_far, first_near, odd, sst, heat, spread, ids, rim_idx, rim_w)
            answered = exchange(answers)
        operands = (
            far, near, odd, eta, eta_part, u_part, v_part, sides, fside, idx, w, side_idx, side_w, rim_idx, rim_w
        )
        outer_scratch = [pltpu.VMEM((3, 4 * HALO, LANES), jnp.float32)]
        if substep + 1 < NSUB:
            eta, u, v, sides, far, near = pl.pallas_call(
                ocean_kernel,
                in_specs=vmem(15),
                out_specs=vmem(6),
                out_shape=(cell_rows,) * 3 + (rim_rows,) * 3,
                scratch_shapes=outer_scratch + [rim_scratch] * 2,
                compiler_params=PARAMS,
                name="ocean",
            )(*operands)
            far, near = swap_both(far, near)
        else:
            eta, velocity = pl.pallas_call(
                last_ocean_kernel,
                in_specs=vmem(15),
                out_specs=vmem(2),
                out_shape=(cell_rows, shape_of(2, cells)),
                scratch_shapes=[pltpu.VMEM((tiles, LANES), jnp.float32)] * 2 + outer_scratch,
                compiler_params=PARAMS,
                name="last_ocean",
            )(*operands)

    surface = pl.pallas_call(
        lambda *refs: back_kernel(*refs, devices=devices),
        in_specs=smem(2) + vmem(2),
        out_specs=pl.BlockSpec(memory_space=pltpu.VMEM),
        out_shape=shape_of(points, LANES),
        scratch_shapes=[
            pltpu.SMEM((devices + points,), jnp.int32),
            pltpu.SMEM((2 * points,), jnp.int32),
            pltpu.VMEM((blocks, 8, LANES), jnp.float32),
        ],
        compiler_params=PARAMS,
        name="back_remap",
    )(holder, across, answered, transfer_coefficients)

    closing = pl.pallas_call(
        second_step_kernel,
        in_specs=vmem(14),
        out_specs=pl.BlockSpec(memory_space=pltpu.HBM),
        out_shape=pltpu.HBM((points, levels, elements), jnp.float32),
        scratch_shapes=[
            pltpu.VMEM((points, levels, elements), jnp.float32), dma((levels // 16,))
        ],
        compiler_params=PARAMS,
        name="second_step",
    )(
        loc, eastern, northern, breadth, pn, east, west, edges_far, edges_near, places,
        first_far, first_near, odd, surface
    )
    return closing, eta.reshape(cells), velocity, warm.reshape(cells)


def solution(mesh):
    split = P(RING)
    last = P(None, RING)
    field = P(None, None, RING)
    return jax.shard_map(
        shards,
        mesh=mesh,
        in_specs=(
            field,
            field,
            field,
            split,
            last,
            P(RING, None, None),
            split,
            P(RING, None),
            split,
            split,
            last,
            split,
            last,
            last,
        ),
        out_specs=(field, split, last, split),
        check_vma=False,
    )
```

```python
import math

import jax
import jax.numpy as jnp
import numpy as np
from jax import lax
from jax.experimental import pallas as pl
from jax.experimental.pallas import tpu as pltpu
from jax.sharding import PartitionSpec as P

OY = 256
NSUB = 4
CAP = 2

STEP_SIZE = 0.05
JUMP_WEIGHT = 4.0
NUDGING_SPEED = 0.5
DAMPING = 0.9
GRAVITY = 0.3
WIND_GAIN = 0.3
DEPTH_RATE = 0.3
WARMING_COEFF = 0.3
SPREADING_COEFF = 0.5

RING = ("comp", "dom")
LANES = 128
HALO = OY // LANES
COS = [math.cos(k * math.pi / 3.0) for k in range(6)]
SIN = [0.0 if k % 3 == 0 else math.sin(k * math.pi / 3.0) for k in range(6)]

ROW_EDGE, ROW_BREADTH, ROW_ETA, ROW_U, ROW_V, ROW_SST = 0, 4, 8, 10, 12, 14
ROW_PX, ROW_PY, ROW_IDX, ROW_W, ROWS_FIRST = 16, 18, 24, 40, 56
PER_DEST, ROW_HEAT, ROW_IDS = 16, 12, 14


def swapped(value, first):
    count = lax.axis_size(RING)
    pairs = []
    for i in range(first, count + first, 2):
        pairs += [(i % count, (i + 1) % count), ((i + 1) % count, i % count)]
    return lax.ppermute(value, RING, pairs)


def swap_both(far, near):
    got_far = swapped(far, 1)
    return got_far, swapped(near, 0)


class Received:
    def __init__(self, far, near, odd):
        self.far, self.near, self.odd = far, near, odd

    def flag(self, rows):
        return jnp.broadcast_to(self.odd[0:1], rows.shape) > 0

    def prev(self, *cut):
        far, near = self.far[cut], self.near[cut]
        return jnp.where(self.flag(far), near, far)

    def next(self, *cut):
        far, near = self.far[cut], self.near[cut]
        return jnp.where(self.flag(far), far, near)

    def rim(self, side, row):
        cut = slice(row, row + HALO)
        return self.prev(cut) if side == 0 else self.next(cut)

    def rims(self, side, rows):
        return tuple(self.rim(side, row) for row in rows)


def arrange(up, dn, odd, far, near):
    flag = jnp.broadcast_to(odd[0:1], up.shape) > 0
    far[...] = jnp.where(flag, up[...], dn[...])
    near[...] = jnp.where(flag, dn[...], up[...])


def exchange(value):
    return lax.all_to_all(value, RING, split_axis=0, concat_axis=0, tiled=True)


def gll_matrix():
    points = np.array([-1.0, -1.0 / np.sqrt(5.0), 1.0 / np.sqrt(5.0), 1.0])
    barycentric = [
        1.0 / np.prod([points[s] - points[o] for o in range(4) if o != s]) for s in range(4)
    ]
    table = np.zeros((4, 4))
    for t in range(4):
        for s in range(4):
            if t != s:
                table[t, s] = barycentric[s] / barycentric[t] / (points[t] - points[s])
    for t in (0, 3):
        table[t, t] = -np.sum(table[t])
    return [[float(np.float32(value)) for value in line] for line in table]


GLL = gll_matrix()


def vmem(count):
    return [pl.BlockSpec(memory_space=pltpu.VMEM)] * count


def hbm(count):
    return [pl.BlockSpec(memory_space=pltpu.HBM)] * count


def in_hbm(*arrays):
    return [pltpu.with_memory_space_constraint(array, pltpu.HBM) for array in arrays]


def smem(count):
    return [pl.BlockSpec(memory_space=pltpu.SMEM)] * count


def shape_of(*dims, dtype=jnp.float32):
    return jax.ShapeDtypeStruct(dims, dtype)


PARAMS = pltpu.CompilerParams(vmem_limit_bytes=24 * 1024 * 1024)


def lane_take(rows, ids):
    return jnp.take_along_axis(rows, ids, axis=1, mode="promise_in_bounds")


def wide(row, lines):
    return jnp.broadcast_to(row, (lines, row.shape[1]))


def side_ids(pn):
    count = pn.shape[1]
    bits = count.bit_length() - 1
    table = pn[...]
    ids = [table[k : k + 1] & (count - 1) for k in range(4)]
    home = lax.shift_right_logical(table[0:1], bits)
    near = [lax.shift_right_logical(table[k : k + 1], bits) == home for k in range(4)]
    return ids, near


def element_step(state, east_wind, north_wind, scale, facing):
    jumps = [None] * 16
    sides = (
        (0, 1, 2, 3),
        (3, 7, 11, 15),
        (12, 13, 14, 15),
        (0, 4, 8, 12),
    )
    for k in range(4):
        for n, p in enumerate(sides[k]):
            term = facing[k][n] - state[p]
            jumps[p] = term if jumps[p] is None else jumps[p] + term
    result = []
    for p in range(16):
        i, j = p % 4, p // 4
        grad_x = grad_y = None
        for m in range(4):
            if GLL[i][m] != 0.0:
                term = GLL[i][m] * state[m + 4 * j]
                grad_x = term if grad_x is None else grad_x + term
            if GLL[j][m] != 0.0:
                term = GLL[j][m] * state[i + 4 * m]
                grad_y = term if grad_y is None else grad_y + term
        change = -(east_wind(p) * grad_x + north_wind(p) * grad_y)
        if jumps[p] is not None:
            change = change + JUMP_WEIGHT * jumps[p]
        result.append(state[p] + scale * change)
    return result


def load(pairs, sems):
    copies = [
        pltpu.make_async_copy(source, target, sems.at[n])
        for n, (source, target) in enumerate(pairs)
    ]
    for copy in copies:
        copy.start()
    return copies


def as_column(row):
    count = row.shape[1]
    return jnp.transpose(jnp.broadcast_to(row, (count, count)))


def edge_tables(partner, remote):
    count = partner.shape[1]
    pack = count // 4
    lane = lax.broadcasted_iota(jnp.int32, (count, count), 1)
    line = lax.broadcasted_iota(jnp.int32, (count, count), 0)
    flag = jnp.where(remote, 1.0, 0.0)
    rank = jnp.sum(jnp.where(line < lane, as_column(flag), 0.0), axis=0, keepdims=True)
    rank = as_column(jnp.where(remote, rank, -1.0))
    slot = (lane & (pack - 1)).astype(jnp.float32)
    chosen = jnp.sum(
        jnp.where(rank == slot, line.astype(jnp.float32), 0.0), axis=0, keepdims=True
    ).astype(jnp.int32)
    key = jnp.where(remote, partner, 2 * count).astype(jnp.float32)
    before = jnp.where(as_column(key) < key, 1.0, 0.0)
    place = jnp.sum(before, axis=0, keepdims=True).astype(jnp.int32)
    return chosen, jnp.minimum(place, pack - 1)


def rank_among_equals(row, most):
    count = row.shape[1]
    earlier = lax.broadcasted_iota(jnp.int32, (count, count), 0) < lax.broadcasted_iota(
        jnp.int32, (count, count), 1
    )
    number = row.astype(jnp.float32)
    same = as_column(number) == number
    return jnp.minimum(jnp.sum(jnp.where(same & earlier, 1, 0), axis=0, keepdims=True), most)


def slot_rows(holder_row, rank, down_row, devices, tiles):
    blocks = holder_row.shape[1]
    target = lax.broadcasted_iota(jnp.int32, (devices, blocks), 0)
    after = jnp.where(holder_row + 1 == devices, 0, holder_row + 1)
    before = jnp.where(holder_row == 0, devices - 1, holder_row - 1)
    last = down_row - (tiles - HALO)
    lane = lax.broadcasted_iota(jnp.int32, (devices, LANES), 1)
    result = jnp.full((devices, LANES), -1.0, jnp.float32)
    for n, (owner, number) in enumerate(
        (
            (holder_row, down_row),
            (after, jnp.where(last >= 0, tiles + last, -1)),
            (before, jnp.where(down_row < HALO, tiles + HALO + down_row, -1)),
        )
    ):
        for slot in range(CAP):
            named = (target == owner) & (rank == slot)
            value = jnp.sum(
                jnp.where(named, (number + 1).astype(jnp.float32), 0.0), axis=1, keepdims=True
            )
            result = jnp.where(lane == CAP * n + slot, value - 1.0, result)
    return result


def home_facing(state, ids, near):
    return [
        [lane_take(state[12 + n], ids[0]) for n in range(4)],
        [jnp.where(near[1], lane_take(state[4 * n], ids[1]), 0.0) for n in range(4)],
        [lane_take(state[n], ids[2]) for n in range(4)],
        [jnp.where(near[3], lane_take(state[3 + 4 * n], ids[3]), 0.0) for n in range(4)],
    ]


def plan_kernel(
    air_hbm, eastern_hbm, northern_hbm, breadth_hbm, pn_hbm, holder_hbm, across_hbm, down_hbm,
    nb, span, flow, flux, slots, breadth, pn, across, own_rows, heat_rows, answer_rows, places,
    idx, w, u, v, air, eastern, northern, holder, down, sems, *, devices, tiles
):
    copies = load(
        (
            (air_hbm.at[:, pl.ds(0, 8), :], air),
            (eastern_hbm.at[:, pl.ds(0, 16), :], eastern),
            (northern_hbm.at[:, pl.ds(0, 16), :], northern),
            (breadth_hbm, breadth),
            (pn_hbm, pn),
            (holder_hbm, holder),
            (across_hbm, across),
            (down_hbm, down),
        ),
        sems,
    )
    fill_tables(nb, span, flow, idx, w, u, v)
    for copy in copies:
        copy.wait()
    lines, count = air.shape[1], air.shape[2]
    ids, near = side_ids(pn)
    ids = [wide(line, lines) for line in ids]
    state = [air[p] for p in range(16)]
    u = [eastern[p].astype(jnp.float32)[0:lines] for p in range(16)]
    v = [northern[p].astype(jnp.float32)[0:lines] for p in range(16)]
    result = element_step(
        state, lambda p: u[p], lambda p: v[p], STEP_SIZE * breadth[...],
        home_facing(state, ids, near)
    )
    for p in range(16):
        speed = jnp.sqrt(u[p] * u[p] + v[p] * v[p] + 1.0)
        flux[p, 0:1] = result[p][0:1]
        flux[p, 1:2] = (speed * u[p])[0:1]
        flux[p, 2:3] = (speed * v[p])[0:1]
        flux[p, 3:4] = speed[0:1]
        flux[p, 4:8] = jnp.zeros((4, count), jnp.float32)
    rank = rank_among_equals(holder[...], CAP - 1)
    slots[...] = slot_rows(holder[...], rank, down[...], devices, tiles)
    own_rows[...] = holder[...] * 8 + 2 * rank
    heat_rows[...] = holder[...] * 8 + 4 + rank
    answer_rows[...] = holder[...] * CAP + rank
    places[...] = across[...] * 2 + rank_among_equals(across[...], 1)


def local_step_kernel(
    air_hbm, eastern_hbm, northern_hbm, breadth, pn, loc, eastern, northern, east, west,
    east_pack, west_pack, places, air, sems
):
    copies = load(((air_hbm, air), (eastern_hbm, eastern), (northern_hbm, northern)), sems)
    count = breadth.shape[1]
    lines = 16
    ids, near = side_ids(pn)
    chosen_east, place_east = edge_tables(ids[1], jnp.logical_not(near[1]))
    chosen_west, place_west = edge_tables(ids[3], jnp.logical_not(near[3]))
    places[...] = jnp.zeros_like(places)
    places[0:1] = place_east
    places[1:2] = place_west
    chosen_east, chosen_west = wide(chosen_east, lines), wide(chosen_west, lines)
    group = lax.broadcasted_iota(jnp.int32, (lines, count), 1) // (count // 4)
    scale = STEP_SIZE * breadth[...]
    ids = [wide(line, lines) for line in ids]

    def packed(values, chosen):
        result = jnp.zeros((lines, count), jnp.float32)
        for n in range(4):
            result = jnp.where(group == n, lane_take(values[n], chosen), result)
        return result

    for copy in copies:
        copy.wait()
    levels = air.shape[1]

    def chunk(c, carry):
        at = pl.multiple_of(c * lines, lines)
        rows = pl.ds(at, lines)
        state = [air[p, rows] for p in range(16)]
        result = element_step(
            state,
            lambda p: eastern[p, rows].astype(jnp.float32),
            lambda p: northern[p, rows].astype(jnp.float32),
            scale,
            home_facing(state, ids, near),
        )
        for p in range(16):
            loc[p, rows] = result[p]
        beyond = pl.ds(pl.multiple_of(levels + at, lines), lines)
        for own, pack, chosen, first in (
            (east, east_pack, chosen_east, 3),
            (west, west_pack, chosen_west, 0),
        ):
            for n in range(4):
                own[n, rows] = state[first + 4 * n].astype(jnp.bfloat16)
            pack[rows] = packed([state[first + 4 * n] for n in range(4)], chosen)
            pack[beyond] = packed([result[first + 4 * n] for n in range(4)], chosen)
        return carry

    lax.fori_loop(0, levels // lines, chunk, 0)


def second_step_kernel(
    loc, eastern, northern, breadth, pn, east, west, far, near_swap, places, first_far,
    first_near, odd, surface, out_hbm, out, sems
):
    ids, near = side_ids(pn)
    levels, count = loc.shape[1], loc.shape[2]
    lines = 16
    pack = count // 4
    scale = STEP_SIZE * breadth[...]
    jump = JUMP_WEIGHT * scale
    ids = [wide(line, lines) for line in ids]
    got = Received(far, near_swap, odd)
    first = Received(first_far, first_near, odd)
    row = slice(ROW_BREADTH, ROW_BREADTH + 1)
    factors = [
        JUMP_WEIGHT * STEP_SIZE * lane_take(wide(line, lines), ids[side])
        for side, line in ((1, first.next(row)), (3, first.prev(row)))
    ]
    spots = [
        [wide(places[n : n + 1] + m * pack, lines) for m in range(4)] for n in (0, 1)
    ]

    def copy_out(c):
        rows = pl.ds(pl.multiple_of(c * lines, lines), lines)
        return pltpu.make_async_copy(out.at[:, rows, :], out_hbm.at[:, rows, :], sems.at[c])

    def chunk(c, carry):
        at = pl.multiple_of(c * lines, lines)
        rows = pl.ds(at, lines)
        now = pl.ds(pl.multiple_of(4 * HALO + at, 8), lines)
        later = pl.ds(pl.multiple_of(4 * HALO + levels + at, 8), lines)
        state = [loc[p, rows] for p in range(16)]

        def across(own, there_now, there_next, side, factor, spot):
            values, beyond = [], []
            for n in range(4):
                values.append(jnp.where(near[side], 0.0, lane_take(there_now, spot[n])))
                beyond.append(
                    lane_take(there_next, spot[n]) + factor * own[n, rows].astype(jnp.float32)
                )
            return values, beyond

        east_now, east_beyond = across(
            east, got.next(now), got.next(later), 1, factors[0], spots[0]
        )
        west_now, west_beyond = across(
            west, got.prev(now), got.prev(later), 3, factors[1], spots[1]
        )
        for n in range(4):
            state[3 + 4 * n] = state[3 + 4 * n] + jump * east_now[n]
            state[4 * n] = state[4 * n] + jump * west_now[n]
        facing = home_facing(state, ids, near)
        facing[1] = [jnp.where(near[1], facing[1][n], east_beyond[n]) for n in range(4)]
        facing[3] = [jnp.where(near[3], facing[3][n], west_beyond[n]) for n in range(4)]
        result = element_step(
            state,
            lambda p: eastern[p, rows].astype(jnp.float32),
            lambda p: northern[p, rows].astype(jnp.float32),
            scale,
            facing,
        )
        for p in range(16):
            out[p, rows] = result[p]

        @pl.when(c == 0)
        def _():
            for p in range(16):
                lowest = out[p, 0:1]
                out[p, 0:1] = lowest + NUDGING_SPEED * (surface[p : p + 1] - lowest)

        copy_out(c).start()
        return carry

    lax.fori_loop(0, levels // lines, chunk, 0)

    def finish(c, carry):
        copy_out(c).wait()
        return carry

    lax.fori_loop(0, levels // lines, finish, 0)


def forward_kernel(
    across, own_rows, heat_rows, flux, slots, breadth, pn, first_far, first_near, odd, weights,
    out, source, own, *, devices
):
    ids, near = side_ids(pn)
    jump = (JUMP_WEIGHT * STEP_SIZE) * breadth[...]
    first = Received(first_far, first_near, odd)
    from_east = lane_take(first.next(slice(0, 8)), wide(ids[1], 8))
    from_west = lane_take(first.prev(slice(0, 8)), wide(ids[3], 8))
    from_east = jnp.where(near[1], 0.0, jump * from_east)
    from_west = jnp.where(near[3], 0.0, jump * from_west)
    for p in range(16):
        value = flux[p, 0:1]
        if p % 4 == 3:
            value = value + from_east[p // 4 : p // 4 + 1]
        if p % 4 == 0:
            value = value + from_west[p // 4 : p // 4 + 1]
        source[p] = flux[p]
        source[p, 0:1] = flux[p, 3:4] * value
    own[...] = jnp.zeros_like(own)
    for b in range(weights.shape[0]):
        sums = jnp.dot(
            source[across[0, b]].astype(jnp.bfloat16), weights[b], preferred_element_type=jnp.float32
        )
        row = own_rows[0, b]
        own[pl.ds(row, 1), :] = sums[1:2]
        own[pl.ds(row + 1, 1), :] = sums[2:3]
        own[pl.ds(heat_rows[0, b], 1), :] = sums[0:1]
    line = lax.broadcasted_iota(jnp.int32, (8, LANES), 0)
    for d in range(devices):
        mine, prev, following = (
            own[8 * (n % devices) : 8 * (n % devices) + 8] for n in (d, d - 1, d + 1)
        )
        top = jnp.concatenate([mine[0:4], prev[0:4]], axis=0)
        bottom = jnp.where(line < 4, following, mine)
        bottom = jnp.where(line == ROW_IDS - 8, wide(slots[d : d + 1], 8), bottom)
        out[d] = jnp.concatenate([top, bottom], axis=0).astype(jnp.bfloat16)


def back_kernel(answer_rows, places, arrived, weights, surface, lines, share):
    lines[...] = arrived[...].reshape(lines.shape)
    for b in range(weights.shape[0]):
        line = lines[pl.ds(answer_rows[0, b], 1), :]
        share[places[0, b]] = lax.dot_general(
            wide(line, 8).astype(jnp.bfloat16),
            weights[b],
            (((1,), (1,)), ((), ())),
            preferred_element_type=jnp.float32,
        )
    for p in range(surface.shape[0]):
        surface[p : p + 1] = share[2 * p, 0:1] + share[2 * p + 1, 0:1]


def split_index(idx):
    return lax.shift_right_arithmetic(idx, 7), idx & (LANES - 1)


def pick(idx, sources):
    high, low = split_index(idx)
    result = jnp.zeros(idx.shape, jnp.float32)
    for number, line in sources:
        result = jnp.where(high == number, lane_take(wide(line, idx.shape[0]), low), result)
    return result


def fill_pack(values, packed, scales):
    tiles = values.shape[0]
    half = tiles // 2
    largest = jnp.maximum(jnp.max(jnp.abs(values), axis=1, keepdims=True), 1e-30)
    number = jnp.floor(values * (32767.0 / largest) + 0.5).astype(jnp.int32)
    packed[...] = (number[half:] << 16) | (number[:half] & 0xFFFF)
    lane = lax.broadcasted_iota(jnp.int32, (tiles, LANES), 1)
    line = lax.broadcasted_iota(jnp.int32, (tiles, LANES), 0)
    row = jnp.sum(jnp.where(lane == line, largest * (1.0 / 32767.0), 0.0), axis=0, keepdims=True)
    scales[...] = wide(row, 8)


def pick_own(idx, packed, scales):
    lines = idx.shape[0]
    half = packed.shape[0]
    high, low = split_index(idx)
    own = high - HALO
    row = jnp.where(own >= half, own - half, own)
    words = jnp.zeros(idx.shape, jnp.int32)
    for r in range(half):
        words = jnp.where(row == r, lane_take(wide(packed[r : r + 1], lines), low), words)
    number = jnp.where(own >= half, words >> 16, (words << 16) >> 16)
    return number.astype(jnp.float32) * lane_take(wide(scales[0:1], lines), own & (LANES - 1))


def combine(terms, factors):
    total = None
    for term, factor in zip(terms, factors):
        if factor != 0.0:
            total = factor * term if total is None else total + factor * term
    return total


def pair_sums(table):
    terms = [table[HALO * k : HALO * (k + 1)] for k in range(6)]
    return combine(terms, COS), combine(terms, SIN)


def rim_partial(rim_idx, rim_w, eta, packed, scales, first):
    rows = rim_idx.shape[0]
    found = pick_own(rim_idx, packed, scales)
    centre = eta[first : first + HALO]
    centre = jnp.concatenate([centre] * (rows // HALO), axis=0)
    return pair_sums(rim_w * (found - centre))


def prepare_kernel(
    air_hbm, breadth_hbm, pn_hbm, eta_hbm, sst_hbm, flow_hbm, nb_hbm, span_hbm,
    nb, span, flow, rim_idx, rim_w, eta, eta_pack, eta_scale, sst, far, near, odd,
    up, dn, air, breadth, pn, sems
):
    copies = load(
        (
            (nb_hbm, nb),
            (span_hbm, span),
            (flow_hbm, flow),
            (eta_hbm, eta),
            (sst_hbm, sst),
            (breadth_hbm, breadth),
            (pn_hbm, pn),
            (air_hbm.at[:, pl.ds(0, 8), :], air),
        ),
        sems,
    )
    for copy in copies:
        copy.wait()
    shard = lax.shift_right_logical(pn[0:1], pn.shape[1].bit_length() - 1)
    odd[...] = wide(shard & 1, 8)
    tiles = eta.shape[0]
    fill_pack(eta[...], eta_pack, eta_scale)
    for side, first in ((0, 0), (1, tiles - HALO)):
        rim_idx[side, 12:16] = jnp.full((4, LANES), -1, jnp.int32)
        rim_w[side, 12:16] = jnp.zeros((4, LANES), jnp.float32)
        for j in range(HALO):
            cut = slice((first + j) * LANES, (first + j + 1) * LANES)
            links = nb[:, cut]
            factors = slot_factors(links, span[:, cut])
            for k in range(6):
                at = HALO * k + j
                rim_idx[side, at : at + 1] = links[k : k + 1]
                rim_w[side, at : at + 1] = factors[k : k + 1]
    for side, first, target in ((0, 0, dn), (1, tiles - HALO, up)):
        target[...] = jnp.zeros_like(target)
        for n in range(4):
            p = 4 * n if side == 0 else 3 + 4 * n
            target[ROW_EDGE + n : ROW_EDGE + n + 1] = air[p, 0:1]
        target[ROW_BREADTH : ROW_BREADTH + 1] = breadth[...]
        part_x, part_y = rim_partial(
            rim_idx[side], rim_w[side], eta, eta_pack, eta_scale, first
        )
        cut = slice(first, first + HALO)
        target[ROW_ETA : ROW_ETA + HALO] = eta[cut]
        for j in range(HALO):
            here = slice((first + j) * LANES, (first + j + 1) * LANES)
            target[ROW_U + j : ROW_U + j + 1] = flow[0:1, here]
            target[ROW_V + j : ROW_V + j + 1] = flow[1:2, here]
        target[ROW_SST : ROW_SST + HALO] = sst[cut]
        target[ROW_PX : ROW_PX + HALO] = part_x
        target[ROW_PY : ROW_PY + HALO] = part_y
        target[ROW_IDX : ROW_IDX + 16] = rim_idx[side].astype(jnp.float32)
        target[ROW_W : ROW_W + 16] = rim_w[side]
    arrange(up, dn, odd, far, near)


def slot_factors(links, span):
    return jnp.where(links >= 0, span * (1.0 / 3.0), 0.0)


def fill_tables(nb, span, flow, idx, w, u, v):
    tiles = u.shape[0]
    for r in range(tiles):
        cut = slice(r * LANES, (r + 1) * LANES)
        links = nb[:, cut]
        factors = slot_factors(links, span[:, cut])
        for k in range(6):
            idx[k * tiles + r : k * tiles + r + 1] = links[k : k + 1]
            w[k * tiles + r : k * tiles + r + 1] = factors[k : k + 1]
        u[r : r + 1] = flow[0:1, cut]
        v[r : r + 1] = flow[1:2, cut]


def own_gradient(idx, w, eta, packed, scales, gx, gy):
    tiles = eta.shape[0]

    def chunk(at):
        centre = eta[pl.ds(at, 8)]
        terms = []
        for k in range(6):
            found = pick_own(idx[pl.ds(k * tiles + at, 8)], packed, scales)
            terms.append(w[pl.ds(k * tiles + at, 8)] * (found - centre))
        gx[pl.ds(at, 8)] = combine(terms, COS)
        gy[pl.ds(at, 8)] = combine(terms, SIN)

    for c in range(tiles // 8):
        chunk(c * 8)


def own_spread(at, idx, w, flow, packed, scales):
    tiles = flow.shape[1]
    total = jnp.zeros((8, LANES), jnp.float32)
    for kk in range(3):
        centre = flow[kk, pl.ds(at, 8)]
        for k, sign in ((kk, 1.0), (kk + 3, -1.0)):
            rows = pl.ds(k * tiles + at, 8)
            found = pick_own(idx[rows], packed.at[kk], scales.at[kk])
            total = total + sign * w[rows] * (found - centre)
    return total


def inner_kernel(
    idx, w, eta, eta_pack, eta_scale, u, v, fu, fv, eta_part, u_part, v_part,
    flow, flow_pack, flow_scale
):
    own_gradient(idx, w, eta, eta_pack, eta_scale, u_part, v_part)
    tiles = eta.shape[0]
    u_part[...] = DAMPING * u[...] - GRAVITY * u_part[...] + WIND_GAIN * fu[...]
    v_part[...] = DAMPING * v[...] - GRAVITY * v_part[...] + WIND_GAIN * fv[...]
    fill_flow(flow, u_part[...], v_part[...])
    for kk in range(3):
        fill_pack(flow[kk], flow_pack.at[kk], flow_scale.at[kk])

    def chunk(at):
        total = own_spread(at, idx, w, flow, flow_pack, flow_scale)
        eta_part[pl.ds(at, 8)] = eta[pl.ds(at, 8)] - DEPTH_RATE * total

    for c in range(tiles // 8):
        chunk(c * 8)


def first_gradient_kernel(
    idx, w, eta, eta_pack, eta_scale, sst, first_far, first_near, odd, rim_idx, rim_w,
    gx, gy, base, sst_pack, sst_scale
):
    own_gradient(idx, w, eta, eta_pack, eta_scale, gx, gy)
    tiles = eta.shape[0]
    fill_pack(sst[...], sst_pack, sst_scale)

    def chunk(at):
        centre = sst[pl.ds(at, 8)]
        total = jnp.zeros_like(centre)
        for k in range(6):
            found = pick_own(idx[pl.ds(k * tiles + at, 8)], sst_pack, sst_scale)
            total = total + w[pl.ds(k * tiles + at, 8)] * (found - centre)
        base[pl.ds(at, 8)] = centre + (0.5 * SPREADING_COEFF) * total

    for c in range(tiles // 8):
        chunk(c * 8)
    first = Received(first_far, first_near, odd)
    for side, start, offset in ((0, 0, 0), (1, tiles - HALO, tiles + HALO)):
        rim = first.rim(side, ROW_SST)
        sources = [(offset + q, rim[q : q + 1]) for q in range(HALO)]
        found = rim_w[side] * pick(rim_idx[side], sources)
        total = combine([found[HALO * k : HALO * (k + 1)] for k in range(6)], [1.0] * 6)
        rows = slice(start, start + HALO)
        base[rows] = base[rows] + (0.5 * SPREADING_COEFF) * total


def fill_flow(flow, u, v):
    flow[0] = u
    for kk in (1, 2):
        flow[kk] = COS[kk] * u + SIN[kk] * v


def side_currents(eta, sides, fside, before, after, side_idx, side_w):
    tiles = eta.shape[0]
    slopes = []
    for side, offset, first, part in (
        (0, tiles + HALO, 0, before),
        (1, 0, tiles - HALO, after),
    ):
        sources = [(offset + q, eta[first + q : first + q + 1]) for q in range(HALO)]
        add_x, add_y = pair_sums(side_w[side] * pick(side_idx[side], sources))
        slopes.append((part[1] + add_x, part[2] + add_y))
    slope = jnp.concatenate([slopes[0][0], slopes[1][0], slopes[0][1], slopes[1][1]], axis=0)
    return DAMPING * sides[...] - GRAVITY * slope + WIND_GAIN * fside[...]


def rim_slopes(rim_idx, rim_w, before, after, tiles):
    result = []
    for side, offset, part in ((0, 0, before), (1, tiles + HALO, after)):
        sources = [(offset + q, part[0][q : q + 1]) for q in range(HALO)]
        result.append(pair_sums(rim_w[side] * pick(rim_idx[side], sources)))
    return result


def send_rims(eta, eta_pack, eta_scale, rim_idx, rim_w, odd, far, near, up, dn):
    tiles = eta.shape[0]
    fill_pack(eta[...], eta_pack, eta_scale)
    for side, first, target in ((0, 0, dn), (1, tiles - HALO, up)):
        part_x, part_y = rim_partial(
            rim_idx[side], rim_w[side], eta, eta_pack, eta_scale, first
        )
        target[0:HALO] = eta[first : first + HALO]
        target[HALO : 2 * HALO] = part_x
        target[2 * HALO : 3 * HALO] = part_y
        target[3 * HALO : 4 * HALO] = jnp.zeros((HALO, LANES), jnp.float32)
    rows = pl.ds(0, 4 * HALO)
    arrange(up, dn, odd, far.at[rows], near.at[rows])


def first_subcycle(
    gx, gy, eta, u, v, sides, fu, fv, fside, before, after, idx, w, side_idx, side_w,
    rim_idx, rim_w, flow, flow_pack, flow_scale, flow_outer, eta_new, u_new, v_new, sides_new
):
    tiles = eta.shape[0]
    u_new[...] = DAMPING * u[...] - GRAVITY * gx[...] + WIND_GAIN * fu[...]
    v_new[...] = DAMPING * v[...] - GRAVITY * gy[...] + WIND_GAIN * fv[...]
    slopes = rim_slopes(rim_idx, rim_w, before, after, tiles)
    for first, (add_x, add_y) in zip((0, tiles - HALO), slopes):
        rows = slice(first, first + HALO)
        u_new[rows] = u_new[rows] - GRAVITY * add_x
        v_new[rows] = v_new[rows] - GRAVITY * add_y
    sides_next = side_currents(eta, sides, fside, before, after, side_idx, side_w)
    sides_new[...] = sides_next
    fill_flow(flow, u_new[...], v_new[...])
    fill_flow(flow_outer, sides_next[0 : 2 * HALO], sides_next[2 * HALO : 4 * HALO])
    for kk in range(3):
        fill_pack(flow[kk], flow_pack.at[kk], flow_scale.at[kk])

    def chunk(at):
        total = own_spread(at, idx, w, flow, flow_pack, flow_scale)
        eta_new[pl.ds(at, 8)] = eta[pl.ds(at, 8)] - DEPTH_RATE * total

    for c in range(tiles // 8):
        chunk(c * 8)
    for side, first, offset in ((0, 0, 0), (1, tiles - HALO, tiles + HALO)):
        total = jnp.zeros((HALO, LANES), jnp.float32)
        for kk in range(3):
            at = side * HALO
            sources = [(offset + q, flow_outer[kk, at + q : at + q + 1]) for q in range(HALO)]
            found = rim_w[side] * pick(rim_idx[side], sources)
            total = (
                total
                + found[HALO * kk : HALO * (kk + 1)]
                - found[HALO * (kk + 3) : HALO * (kk + 4)]
            )
        rows = slice(first, first + HALO)
        eta_new[rows] = eta_new[rows] - DEPTH_RATE * total


def outer_subcycle(
    eta, eta_part, u_part, v_part, sides, fside, before, after, idx, w, side_idx, side_w,
    rim_idx, rim_w, flow_outer, eta_new, u_new, v_new
):
    tiles = eta.shape[0]
    slopes = rim_slopes(rim_idx, rim_w, before, after, tiles)
    sides_next = side_currents(eta, sides, fside, before, after, side_idx, side_w)
    u_new[...] = u_part[...]
    v_new[...] = v_part[...]
    changes_u = [-GRAVITY * slopes[side][0] for side in (0, 1)]
    changes_v = [-GRAVITY * slopes[side][1] for side in (0, 1)]
    for side, first in ((0, 0), (1, tiles - HALO)):
        rows = slice(first, first + HALO)
        u_new[rows] = u_new[rows] + changes_u[side]
        v_new[rows] = v_new[rows] + changes_v[side]
    fill_flow(
        flow_outer,
        jnp.concatenate([sides_next[0 : 2 * HALO]] + changes_u, axis=0),
        jnp.concatenate([sides_next[2 * HALO : 4 * HALO]] + changes_v, axis=0),
    )
    for c in range(tiles // 8):
        at = c * 8
        total = jnp.zeros((8, LANES), jnp.float32)
        for kk in range(3):
            line = lambda n: flow_outer[kk, n : n + 1]
            sources = [(HALO + q, line(2 * HALO + q)) for q in range(HALO)]
            sources += [(tiles + q, line(3 * HALO + q)) for q in range(HALO)]
            if at == 0:
                sources += [(q, line(q)) for q in range(HALO)]
            if at + 8 == tiles:
                sources += [(tiles + HALO + q, line(HALO + q)) for q in range(HALO)]
            total = (
                total
                + w[kk * tiles + at : kk * tiles + at + 8]
                * pick(idx[kk * tiles + at : kk * tiles + at + 8], sources)
                - w[(kk + 3) * tiles + at : (kk + 3) * tiles + at + 8]
                * pick(idx[(kk + 3) * tiles + at : (kk + 3) * tiles + at + 8], sources)
            )
        eta_new[at : at + 8] = eta_part[at : at + 8] - DEPTH_RATE * total
    for side, first in ((0, 0), (1, tiles - HALO)):
        centre = jnp.zeros((HALO, LANES), jnp.float32)
        for kk in range(3):
            factor = (
                rim_w[side, HALO * kk : HALO * (kk + 1)]
                - rim_w[side, HALO * (kk + 3) : HALO * (kk + 4)]
            )
            start = (2 + side) * HALO
            centre = centre + factor * flow_outer[kk, start : start + HALO]
        rows = slice(first, first + HALO)
        eta_new[rows] = eta_new[rows] + DEPTH_RATE * centre
    return sides_next


def first_ocean_kernel(
    arrived, first_far, first_near, odd, gx, gy, eta, u, v, idx, w, rim_idx, rim_w,
    east_pack, west_pack, eta_new, eta_pack, eta_scale, u_new, v_new, sides_new, far, near,
    fu, fv, fside, side_idx, side_w, heat, ids,
    flow, flow_pack, flow_scale, flow_outer, sides, up, dn
):
    tiles = eta.shape[0]
    devices = arrived.shape[0]
    parts = arrived[...].astype(jnp.float32)
    ids[...] = parts[:, ROW_IDS, :]
    number = lax.broadcasted_iota(jnp.int32, (devices, LANES), 1).astype(jnp.float32)
    nothing = jnp.zeros((devices, LANES), jnp.float32)
    chosen, lines = [], []
    for j in range(3 * CAP):
        chosen.append(jnp.where(ids[:, j : j + 1] == number, 1.0, 0.0))
        first = parts[:, ROW_HEAT + j, :] if j < CAP else nothing
        lines.append(
            jnp.concatenate([first, parts[:, 2 * j, :], parts[:, 2 * j + 1, :]], axis=1)
        )
    forcing = lax.dot_general(
        jnp.concatenate(chosen, axis=0).astype(jnp.bfloat16),
        jnp.concatenate(lines, axis=0).astype(jnp.bfloat16),
        (((0,), (0,)), ((), ())),
        preferred_element_type=jnp.float32,
    )
    heat[...] = forcing[0:tiles, 0:LANES]
    fu[...] = forcing[0:tiles, LANES : 2 * LANES]
    fv[...] = forcing[0:tiles, 2 * LANES : 3 * LANES]
    fside[0 : 2 * HALO] = forcing[tiles : tiles + 2 * HALO, LANES : 2 * LANES]
    fside[2 * HALO : 4 * HALO] = forcing[tiles : tiles + 2 * HALO, 2 * LANES : 3 * LANES]
    first = Received(first_far, first_near, odd)
    for side, part in ((0, first.prev), (1, first.next)):
        side_idx[side] = part(slice(ROW_IDX, ROW_IDX + 16)).astype(jnp.int32)
        side_w[side] = part(slice(ROW_W, ROW_W + 16))
        for n, row in ((0, ROW_U), (1, ROW_V)):
            at = HALO * (2 * n + side)
            sides[at : at + HALO] = first.rim(side, row)
    rows = (ROW_ETA, ROW_PX, ROW_PY)
    first_subcycle(
        gx, gy, eta, u, v, sides, fu, fv, fside, first.rims(0, rows), first.rims(1, rows), idx, w, side_idx, side_w, rim_idx, rim_w, flow, flow_pack, flow_scale, flow_outer,
        eta_new, u_new, v_new, sides_new
    )
    send_rims(eta_new, eta_pack, eta_scale, rim_idx, rim_w, odd, far, near, up, dn)
    flag = jnp.broadcast_to(odd[0:1], east_pack.shape) > 0
    far[4 * HALO :] = jnp.where(flag, east_pack[...], west_pack[...])
    near[4 * HALO :] = jnp.where(flag, west_pack[...], east_pack[...])


def sea_kernel(base, heat, ids, warm, answers):
    tiles = base.shape[0]
    devices = ids.shape[0]
    warm[...] = base[...] + WARMING_COEFF * heat[...]
    half = warm[...].astype(jnp.bfloat16)
    number = lax.broadcasted_iota(jnp.int32, (devices, tiles), 1).astype(jnp.float32)
    for j in range(CAP):
        chosen = jnp.where(ids[:, j : j + 1] == number, 1.0, 0.0).astype(jnp.bfloat16)
        answers[:, j, :] = jnp.dot(chosen, half, preferred_element_type=jnp.float32)


def ocean_kernel(
    far, near, odd, eta, eta_part, u_part, v_part, sides, fside, idx, w, side_idx, side_w,
    rim_idx, rim_w, eta_new, eta_pack, eta_scale, u_new, v_new, sides_new, far_new, near_new,
    flow_outer, up, dn
):
    rows = (0, HALO, 2 * HALO)
    got = Received(far, near, odd)
    sides_new[...] = outer_subcycle(
        eta, eta_part, u_part, v_part, sides, fside, got.rims(0, rows), got.rims(1, rows), idx, w, side_idx, side_w, rim_idx, rim_w, flow_outer,
        eta_new, u_new, v_new
    )
    send_rims(
        eta_new, eta_pack, eta_scale, rim_idx, rim_w, odd, far_new, near_new, up, dn
    )


def last_ocean_kernel(
    far, near, odd, eta, eta_part, u_part, v_part, sides, fside, idx, w, side_idx, side_w,
    rim_idx, rim_w, eta_new, velocity, u_new, v_new, flow_outer
):
    rows = (0, HALO, 2 * HALO)
    got = Received(far, near, odd)
    outer_subcycle(
        eta, eta_part, u_part, v_part, sides, fside, got.rims(0, rows), got.rims(1, rows), idx, w, side_idx, side_w, rim_idx, rim_w, flow_outer,
        eta_new, u_new, v_new
    )
    for r in range(eta.shape[0]):
        cut = slice(r * LANES, (r + 1) * LANES)
        velocity[0:1, cut] = u_new[r : r + 1]
        velocity[1:2, cut] = v_new[r : r + 1]


def shards(
    air_warmth,
    eastern_breeze,
    northern_breeze,
    reciprocal_breadth,
    panel_neighbours,
    transfer_coefficients,
    transfer_across_tile,
    transfer_holder,
    transfer_down_tile,
    water_elevation,
    depth_mean_current,
    marine_skin_warmth,
    patch_neighbours,
    interface_span,
):
    devices = lax.axis_size(RING)
    points, levels, elements = air_warmth.shape
    cells = water_elevation.shape[0]
    tiles = cells // LANES
    blocks = transfer_holder.shape[0]
    cell_rows = shape_of(tiles, LANES)
    rim_rows = shape_of(4 * HALO, LANES)
    dma = pltpu.SemaphoreType.DMA
    air, eastern, northern, breadth_hbm, pn_hbm = in_hbm(
        air_warmth, eastern_breeze, northern_breeze, reciprocal_breadth.reshape(1, elements),
        panel_neighbours
    )

    pack_rows = shape_of(tiles // 2, LANES, dtype=jnp.int32)
    scale_rows = shape_of(8, LANES)
    nb, span, flow, rim_idx, rim_w, eta, eta_pack, eta_scale, sst, far, near, odd = pl.pallas_call(
        prepare_kernel,
        in_specs=hbm(8),
        out_specs=vmem(12),
        out_shape=(
            shape_of(6, cells, dtype=jnp.int32),
            shape_of(6, cells),
            shape_of(2, cells),
            shape_of(2, 16, LANES, dtype=jnp.int32),
            shape_of(2, 16, LANES),
            cell_rows,
            pack_rows,
            scale_rows,
            cell_rows,
            shape_of(ROWS_FIRST, LANES),
            shape_of(ROWS_FIRST, LANES),
            shape_of(8, elements, dtype=jnp.int32),
        ),
        scratch_shapes=[
            pltpu.VMEM((ROWS_FIRST, LANES), jnp.float32),
            pltpu.VMEM((ROWS_FIRST, LANES), jnp.float32),
            pltpu.VMEM((points, 8, elements), jnp.float32),
            pltpu.VMEM((1, elements), jnp.float32),
            pltpu.VMEM((4, elements), jnp.int32),
            dma((8,)),
        ],
        compiler_params=PARAMS,
        name="prepare",
    )(
        air,
        breadth_hbm,
        pn_hbm,
        *in_hbm(
            water_elevation.reshape(tiles, LANES),
            marine_skin_warmth.reshape(tiles, LANES),
            depth_mean_current,
            patch_neighbours,
            interface_span,
        ),
    )
    first_far, first_near = swap_both(far, near)

    one_row = shape_of(1, blocks, dtype=jnp.int32)
    low_wind = pltpu.VMEM((points, 16, elements), jnp.bfloat16)
    (
        flux, slots, breadth, pn, across, own_rows, heat_rows, answer_rows, places, idx, w, u, v
    ) = pl.pallas_call(
        lambda *refs: plan_kernel(*refs, devices=devices, tiles=tiles),
        in_specs=hbm(8) + vmem(3),
        out_specs=vmem(13),
        out_shape=(
            shape_of(points, 8, elements), shape_of(devices, LANES), shape_of(1, elements),
            shape_of(4, elements, dtype=jnp.int32), one_row, one_row, one_row, one_row, one_row,
            shape_of(6 * tiles, LANES, dtype=jnp.int32), shape_of(6 * tiles, LANES),
            cell_rows, cell_rows
        ),
        scratch_shapes=[
            pltpu.VMEM((points, 8, elements), jnp.float32), low_wind, low_wind,
            pltpu.VMEM((1, blocks), jnp.int32), pltpu.VMEM((1, blocks), jnp.int32), dma((8,))
        ],
        compiler_params=PARAMS,
        name="plan",
    )(
        air,
        eastern,
        northern,
        breadth_hbm,
        pn_hbm,
        *in_hbm(
            transfer_holder.reshape(1, blocks),
            transfer_across_tile.reshape(1, blocks),
            transfer_down_tile.reshape(1, blocks),
        ),
        nb,
        span,
        flow,
    )

    outgoing = pl.pallas_call(
        lambda *refs: forward_kernel(*refs, devices=devices),
        in_specs=smem(3) + vmem(8),
        out_specs=pl.BlockSpec(memory_space=pltpu.VMEM),
        out_shape=shape_of(devices, PER_DEST, LANES, dtype=jnp.bfloat16),
        scratch_shapes=[
            pltpu.VMEM((points, 8, elements), jnp.float32),
            pltpu.VMEM((devices * 8, LANES), jnp.float32),
        ],
        compiler_params=PARAMS,
        name="forward_remap",
    )(
        across, own_rows, heat_rows, flux, slots, breadth, pn, first_far, first_near, odd,
        transfer_coefficients
    )
    outgoing, pn, gradient_eta = lax.optimization_barrier((outgoing, pn, eta))
    arrived = exchange(outgoing)
    gx, gy, base = pl.pallas_call(
        first_gradient_kernel,
        in_specs=vmem(11),
        out_specs=vmem(3),
        out_shape=(cell_rows,) * 3,
        scratch_shapes=[
            pltpu.VMEM((tiles // 2, LANES), jnp.int32), pltpu.VMEM((8, LANES), jnp.float32)
        ],
        compiler_params=PARAMS,
        name="first_gradient",
    )(
        idx, w, gradient_eta, eta_pack, eta_scale, sst, first_far, first_near, odd, rim_idx, rim_w
    )

    field = shape_of(points, levels, elements)
    edge = shape_of(4, levels, elements, dtype=jnp.bfloat16)
    pack = shape_of(2 * levels, elements)
    wind = shape_of(points, levels, elements, dtype=jnp.bfloat16)
    loc, eastern, northern, east, west, east_pack, west_pack, edge_places = pl.pallas_call(
        local_step_kernel,
        in_specs=hbm(3) + vmem(2),
        out_specs=vmem(8),
        out_shape=(
            field, wind, wind, edge, edge, pack, pack, shape_of(8, elements, dtype=jnp.int32)
        ),
        scratch_shapes=[pltpu.VMEM((points, levels, elements), jnp.float32), dma((3,))],
        compiler_params=PARAMS,
        name="local_step",
    )(air, eastern, northern, breadth, pn)

    rim_scratch = pltpu.VMEM((4 * HALO, LANES), jnp.float32)
    second_rows = shape_of(4 * HALO + 2 * levels, elements)
    flow_scratch = [
        pltpu.VMEM((3, tiles, LANES), jnp.float32),
        pltpu.VMEM((3, tiles // 2, LANES), jnp.int32),
        pltpu.VMEM((3, 8, LANES), jnp.float32),
        pltpu.VMEM((3, 2 * HALO, LANES), jnp.float32),
    ]
    (
        eta, eta_pack, eta_scale, u, v, sides, far, near, fu, fv, fside, side_idx, side_w,
        heat, ids
    ) = pl.pallas_call(
        first_ocean_kernel,
        in_specs=vmem(15),
        out_specs=vmem(15),
        out_shape=(
            cell_rows, pack_rows, scale_rows, cell_rows, cell_rows, rim_rows, second_rows, second_rows,
            cell_rows, cell_rows, rim_rows,
            shape_of(2, 16, LANES, dtype=jnp.int32), shape_of(2, 16, LANES),
            cell_rows, shape_of(devices, LANES),
        ),
        scratch_shapes=flow_scratch + [rim_scratch] * 3,
        compiler_params=PARAMS,
        name="first_ocean",
    )(
        arrived, first_far, first_near, odd, gx, gy, eta, u, v, idx, w, rim_idx, rim_w,
        east_pack, west_pack
    )
    far, near = swap_both(far, near)
    edges_far, edges_near = far, near

    for substep in range(1, NSUB):
        eta_part, u_part, v_part = pl.pallas_call(
            inner_kernel,
            in_specs=vmem(9),
            out_specs=vmem(3),
            out_shape=(cell_rows,) * 3,
            scratch_shapes=flow_scratch[:3],
            compiler_params=PARAMS,
            name="inner",
        )(idx, w, eta, eta_pack, eta_scale, u, v, fu, fv)
        if substep == 1:
            eta_part, heat = lax.optimization_barrier((eta_part, heat))
            warm, answers = pl.pallas_call(
                sea_kernel,
                in_specs=vmem(3),
                out_specs=vmem(2),
                out_shape=(cell_rows, shape_of(devices, CAP, LANES)),
                compiler_params=PARAMS,
                name="sea",
            )(base, heat, ids)
            answered = exchange(answers)
        if substep == 2:
            eta_part, answered = lax.optimization_barrier((eta_part, answered))
            surface = pl.pallas_call(
                back_kernel,
                in_specs=smem(2) + vmem(2),
                out_specs=pl.BlockSpec(memory_space=pltpu.VMEM),
                out_shape=shape_of(points, LANES),
                scratch_shapes=[
                    pltpu.VMEM((devices * CAP, LANES), jnp.float32),
                    pltpu.VMEM((blocks, 8, LANES), jnp.float32),
                ],
                compiler_params=PARAMS,
                name="back_remap",
            )(answer_rows, places, answered, transfer_coefficients)
            eta_part, surface = lax.optimization_barrier((eta_part, surface))
        operands = (
            far, near, odd, eta, eta_part, u_part, v_part, sides, fside, idx, w, side_idx, side_w, rim_idx, rim_w
        )
        outer_scratch = [pltpu.VMEM((3, 4 * HALO, LANES), jnp.float32)]
        if substep + 1 < NSUB:
            eta, eta_pack, eta_scale, u, v, sides, far, near = pl.pallas_call(
                ocean_kernel,
                in_specs=vmem(15),
                out_specs=vmem(8),
                out_shape=(cell_rows, pack_rows, scale_rows) + (cell_rows,) * 2 + (rim_rows,) * 3,
                scratch_shapes=outer_scratch + [rim_scratch] * 2,
                compiler_params=PARAMS,
                name="ocean",
            )(*operands)
            far, near = swap_both(far, near)
        else:
            eta, velocity = pl.pallas_call(
                last_ocean_kernel,
                in_specs=vmem(15),
                out_specs=vmem(2),
                out_shape=(cell_rows, shape_of(2, cells)),
                scratch_shapes=[pltpu.VMEM((tiles, LANES), jnp.float32)] * 2 + outer_scratch,
                compiler_params=PARAMS,
                name="last_ocean",
            )(*operands)

    closing = pl.pallas_call(
        second_step_kernel,
        in_specs=vmem(14),
        out_specs=pl.BlockSpec(memory_space=pltpu.HBM),
        out_shape=pltpu.HBM((points, levels, elements), jnp.float32),
        scratch_shapes=[
            pltpu.VMEM((points, levels, elements), jnp.float32), dma((levels // 16,))
        ],
        compiler_params=PARAMS,
        name="second_step",
    )(
        loc, eastern, northern, breadth, pn, east, west, edges_far, edges_near, edge_places,
        first_far, first_near, odd, surface
    )
    return closing, eta.reshape(cells), velocity, warm.reshape(cells)


def solution(mesh):
    split = P(RING)
    last = P(None, RING)
    field = P(None, None, RING)
    return jax.shard_map(
        shards,
        mesh=mesh,
        in_specs=(
            field,
            field,
            field,
            split,
            last,
            P(RING, None, None),
            split,
            P(RING, None),
            split,
            split,
            last,
            split,
            last,
            last,
        ),
        out_specs=(field, split, last, split),
        check_vma=False,
    )
```

```python
import math

import jax
import jax.numpy as jnp
import numpy as np
from jax import lax
from jax.experimental import pallas as pl
from jax.experimental.pallas import tpu as pltpu
from jax.sharding import PartitionSpec as P

OY = 256
NSUB = 4
CAP = 2

STEP_SIZE = 0.05
JUMP_WEIGHT = 4.0
NUDGING_SPEED = 0.5
DAMPING = 0.9
GRAVITY = 0.3
WIND_GAIN = 0.3
DEPTH_RATE = 0.3
WARMING_COEFF = 0.3
SPREADING_COEFF = 0.5

RING = ("comp", "dom")
LANES = 128
HALO = OY // LANES
COS = [math.cos(k * math.pi / 3.0) for k in range(6)]
SIN = [0.0 if k % 3 == 0 else math.sin(k * math.pi / 3.0) for k in range(6)]

ROW_EDGE, ROW_BREADTH, ROW_ETA, ROW_U, ROW_V, ROW_SST = 0, 4, 8, 10, 12, 14
ROW_PX, ROW_PY, ROW_IDX, ROW_W, ROWS_FIRST = 16, 18, 24, 40, 56
MARK_COLUMN, MARK_OWN, MARK_HEAT, MARK_ANSWER, MARK_PLACE, MARK_READER = range(6)
PER_DEST, ROW_HEAT, ROW_IDS = 16, 12, 14


def swapped(value, first):
    count = lax.axis_size(RING)
    pairs = []
    for i in range(first, count + first, 2):
        pairs += [(i % count, (i + 1) % count), ((i + 1) % count, i % count)]
    return lax.ppermute(value, RING, pairs)


def swap_both(far, near):
    got_far = swapped(far, 1)
    return got_far, swapped(near, 0)


class Received:
    def __init__(self, far, near, odd):
        self.far, self.near, self.odd = far, near, odd

    def flag(self, rows):
        return jnp.broadcast_to(self.odd[0:1], rows.shape) > 0

    def prev(self, *cut):
        far, near = self.far[cut], self.near[cut]
        return jnp.where(self.flag(far), near, far)

    def next(self, *cut):
        far, near = self.far[cut], self.near[cut]
        return jnp.where(self.flag(far), far, near)

    def rim(self, side, row):
        cut = slice(row, row + HALO)
        return self.prev(cut) if side == 0 else self.next(cut)

    def rims(self, side, rows):
        return tuple(self.rim(side, row) for row in rows)


def arrange(up, dn, odd, far, near):
    flag = jnp.broadcast_to(odd[0:1], up.shape) > 0
    far[...] = jnp.where(flag, up[...], dn[...])
    near[...] = jnp.where(flag, dn[...], up[...])


def exchange(value):
    return lax.all_to_all(value, RING, split_axis=0, concat_axis=0, tiled=True)


def gll_matrix():
    points = np.array([-1.0, -1.0 / np.sqrt(5.0), 1.0 / np.sqrt(5.0), 1.0])
    barycentric = [
        1.0 / np.prod([points[s] - points[o] for o in range(4) if o != s]) for s in range(4)
    ]
    table = np.zeros((4, 4))
    for t in range(4):
        for s in range(4):
            if t != s:
                table[t, s] = barycentric[s] / barycentric[t] / (points[t] - points[s])
    for t in (0, 3):
        table[t, t] = -np.sum(table[t])
    return [[float(np.float32(value)) for value in line] for line in table]


GLL = gll_matrix()


def vmem(count):
    return [pl.BlockSpec(memory_space=pltpu.VMEM)] * count


def hbm(count):
    return [pl.BlockSpec(memory_space=pltpu.HBM)] * count


def in_hbm(*arrays):
    return [pltpu.with_memory_space_constraint(array, pltpu.HBM) for array in arrays]


def smem(count):
    return [pl.BlockSpec(memory_space=pltpu.SMEM)] * count


def shape_of(*dims, dtype=jnp.float32):
    return jax.ShapeDtypeStruct(dims, dtype)


PARAMS = pltpu.CompilerParams(vmem_limit_bytes=24 * 1024 * 1024)


def lane_take(rows, ids):
    return jnp.take_along_axis(rows, ids, axis=1, mode="promise_in_bounds")


def wide(row, lines):
    return jnp.broadcast_to(row, (lines, row.shape[1]))


def side_ids(pn):
    count = pn.shape[1]
    bits = count.bit_length() - 1
    table = pn[...]
    ids = [table[k : k + 1] & (count - 1) for k in range(4)]
    home = lax.shift_right_logical(table[0:1], bits)
    near = [lax.shift_right_logical(table[k : k + 1], bits) == home for k in range(4)]
    return ids, near


def element_step(state, east_wind, north_wind, scale, facing):
    jumps = [None] * 16
    sides = (
        (0, 1, 2, 3),
        (3, 7, 11, 15),
        (12, 13, 14, 15),
        (0, 4, 8, 12),
    )
    for k in range(4):
        for n, p in enumerate(sides[k]):
            term = facing[k][n] - state[p]
            jumps[p] = term if jumps[p] is None else jumps[p] + term
    result = []
    for p in range(16):
        i, j = p % 4, p // 4
        grad_x = grad_y = None
        for m in range(4):
            if GLL[i][m] != 0.0:
                term = GLL[i][m] * state[m + 4 * j]
                grad_x = term if grad_x is None else grad_x + term
            if GLL[j][m] != 0.0:
                term = GLL[j][m] * state[i + 4 * m]
                grad_y = term if grad_y is None else grad_y + term
        change = -(east_wind(p) * grad_x + north_wind(p) * grad_y)
        if jumps[p] is not None:
            change = change + JUMP_WEIGHT * jumps[p]
        result.append(state[p] + scale * change)
    return result


def load(pairs, sems):
    copies = [
        pltpu.make_async_copy(source, target, sems.at[n])
        for n, (source, target) in enumerate(pairs)
    ]
    for copy in copies:
        copy.start()
    return copies


def as_column(row):
    count = row.shape[1]
    return jnp.transpose(jnp.broadcast_to(row, (count, count)))


def edge_tables(partner, remote):
    count = partner.shape[1]
    pack = count // 4
    lane = lax.broadcasted_iota(jnp.int32, (count, count), 1)
    line = lax.broadcasted_iota(jnp.int32, (count, count), 0)
    flag = jnp.where(remote, 1.0, 0.0)
    rank = jnp.sum(jnp.where(line < lane, as_column(flag), 0.0), axis=0, keepdims=True)
    rank = as_column(jnp.where(remote, rank, -1.0))
    slot = (lane & (pack - 1)).astype(jnp.float32)
    chosen = jnp.sum(
        jnp.where(rank == slot, line.astype(jnp.float32), 0.0), axis=0, keepdims=True
    ).astype(jnp.int32)
    key = jnp.where(remote, partner, 2 * count).astype(jnp.float32)
    before = jnp.where(as_column(key) < key, 1.0, 0.0)
    place = jnp.sum(before, axis=0, keepdims=True).astype(jnp.int32)
    return chosen, jnp.minimum(place, pack - 1)


def rank_among_equals(row, most):
    count = row.shape[1]
    earlier = lax.broadcasted_iota(jnp.int32, (count, count), 0) < lax.broadcasted_iota(
        jnp.int32, (count, count), 1
    )
    number = row.astype(jnp.float32)
    same = as_column(number) == number
    return jnp.minimum(jnp.sum(jnp.where(same & earlier, 1, 0), axis=0, keepdims=True), most)


def slot_rows(holder_row, rank, down_row, devices, tiles):
    blocks = holder_row.shape[1]
    target = lax.broadcasted_iota(jnp.int32, (devices, blocks), 0)
    after = jnp.where(holder_row + 1 == devices, 0, holder_row + 1)
    before = jnp.where(holder_row == 0, devices - 1, holder_row - 1)
    last = down_row - (tiles - HALO)
    lane = lax.broadcasted_iota(jnp.int32, (devices, LANES), 1)
    result = jnp.full((devices, LANES), -1.0, jnp.float32)
    for n, (owner, number) in enumerate(
        (
            (holder_row, down_row),
            (after, jnp.where(last >= 0, tiles + last, -1)),
            (before, jnp.where(down_row < HALO, tiles + HALO + down_row, -1)),
        )
    ):
        for slot in range(CAP):
            named = (target == owner) & (rank == slot)
            value = jnp.sum(
                jnp.where(named, (number + 1).astype(jnp.float32), 0.0), axis=1, keepdims=True
            )
            result = jnp.where(lane == CAP * n + slot, value - 1.0, result)
    return result


def home_facing(state, ids, near):
    return [
        [lane_take(state[12 + n], ids[0]) for n in range(4)],
        [jnp.where(near[1], lane_take(state[4 * n], ids[1]), 0.0) for n in range(4)],
        [lane_take(state[n], ids[2]) for n in range(4)],
        [jnp.where(near[3], lane_take(state[3 + 4 * n], ids[3]), 0.0) for n in range(4)],
    ]


def plan_kernel(
    air_hbm, eastern_hbm, northern_hbm, breadth_hbm, pn_hbm, holder_hbm, across_hbm, down_hbm,
    nb, span, flow, flux, slots, breadth, pn, marks, idx, w, u, v,
    air, eastern, northern, holder, across, down, lists, sems, *, devices, tiles
):
    copies = load(
        (
            (air_hbm.at[:, pl.ds(0, 8), :], air),
            (eastern_hbm.at[:, pl.ds(0, 16), :], eastern),
            (northern_hbm.at[:, pl.ds(0, 16), :], northern),
            (breadth_hbm, breadth),
            (pn_hbm, pn),
            (holder_hbm, holder),
            (across_hbm, across),
            (down_hbm, down),
        ),
        sems,
    )
    fill_tables(nb, span, flow, idx, w, u, v)
    for copy in copies:
        copy.wait()
    rank = rank_among_equals(holder[...], CAP - 1)
    place = across[...] * 2 + rank_among_equals(across[...], 1)
    blocks = place.shape[1]
    line = lax.broadcasted_iota(jnp.int32, (blocks, blocks), 0).astype(jnp.float32)
    lane = lax.broadcasted_iota(jnp.int32, (blocks, blocks), 1).astype(jnp.float32)
    here = as_column(place.astype(jnp.float32)) == lane
    reader = jnp.sum(jnp.where(here, line, 0.0), axis=0, keepdims=True).astype(jnp.int32)
    lists[...] = jnp.zeros_like(lists)
    for mark, row in (
        (MARK_COLUMN, across[...]),
        (MARK_OWN, holder[...] * 8 + 2 * rank),
        (MARK_HEAT, holder[...] * 8 + 4 + rank),
        (MARK_ANSWER, holder[...] * CAP + rank),
        (MARK_PLACE, place),
        (MARK_READER, reader),
    ):
        lists[mark : mark + 1] = row
    copy = pltpu.make_async_copy(lists, marks, sems.at[0])
    copy.start()
    slots[...] = slot_rows(holder[...], rank, down[...], devices, tiles)
    lines, count = air.shape[1], air.shape[2]
    ids, near = side_ids(pn)
    ids = [wide(line, lines) for line in ids]
    state = [air[p] for p in range(16)]
    u = [eastern[p].astype(jnp.float32)[0:lines] for p in range(16)]
    v = [northern[p].astype(jnp.float32)[0:lines] for p in range(16)]
    result = element_step(
        state, lambda p: u[p], lambda p: v[p], STEP_SIZE * breadth[...],
        home_facing(state, ids, near)
    )
    for p in range(16):
        speed = jnp.sqrt(u[p] * u[p] + v[p] * v[p] + 1.0)
        flux[p, 0:1] = (speed * result[p])[0:1]
        flux[p, 1:2] = (speed * u[p])[0:1]
        flux[p, 2:3] = (speed * v[p])[0:1]
        flux[p, 3:4] = speed[0:1]
        flux[p, 4:8] = jnp.zeros((4, count), jnp.float32)
    copy.wait()


def local_step_kernel(
    air_hbm, eastern_hbm, northern_hbm, breadth, pn, loc, eastern, northern, east, west,
    east_pack, west_pack, places, air, sems
):
    copies = load(((air_hbm, air), (eastern_hbm, eastern), (northern_hbm, northern)), sems)
    count = breadth.shape[1]
    lines = 16
    ids, near = side_ids(pn)
    chosen_east, place_east = edge_tables(ids[1], jnp.logical_not(near[1]))
    chosen_west, place_west = edge_tables(ids[3], jnp.logical_not(near[3]))
    places[...] = jnp.zeros_like(places)
    places[0:1] = place_east
    places[1:2] = place_west
    chosen_east, chosen_west = wide(chosen_east, lines), wide(chosen_west, lines)
    group = lax.broadcasted_iota(jnp.int32, (lines, count), 1) // (count // 4)
    scale = STEP_SIZE * breadth[...]
    ids = [wide(line, lines) for line in ids]

    def packed(values, chosen):
        result = jnp.zeros((lines, count), jnp.float32)
        for n in range(4):
            result = jnp.where(group == n, lane_take(values[n], chosen), result)
        return result

    for copy in copies:
        copy.wait()
    levels = air.shape[1]

    def chunk(c, carry):
        at = pl.multiple_of(c * lines, lines)
        rows = pl.ds(at, lines)
        state = [air[p, rows] for p in range(16)]
        result = element_step(
            state,
            lambda p: eastern[p, rows].astype(jnp.float32),
            lambda p: northern[p, rows].astype(jnp.float32),
            scale,
            home_facing(state, ids, near),
        )
        for p in range(16):
            loc[p, rows] = result[p]
        beyond = pl.ds(pl.multiple_of(levels + at, lines), lines)
        for own, pack, chosen, first in (
            (east, east_pack, chosen_east, 3),
            (west, west_pack, chosen_west, 0),
        ):
            for n in range(4):
                own[n, rows] = state[first + 4 * n].astype(jnp.bfloat16)
            pack[rows] = packed([state[first + 4 * n] for n in range(4)], chosen)
            pack[beyond] = packed([result[first + 4 * n] for n in range(4)], chosen)
        return carry

    lax.fori_loop(0, levels // lines, chunk, 0)


def second_step_kernel(
    loc, eastern, northern, breadth, pn, east, west, far, near_swap, places, first_far,
    first_near, odd, surface, out_hbm, out, sems
):
    ids, near = side_ids(pn)
    levels, count = loc.shape[1], loc.shape[2]
    lines = 16
    pack = count // 4
    scale = STEP_SIZE * breadth[...]
    jump = JUMP_WEIGHT * scale
    ids = [wide(line, lines) for line in ids]
    got = Received(far, near_swap, odd)
    first = Received(first_far, first_near, odd)
    row = slice(ROW_BREADTH, ROW_BREADTH + 1)
    factors = [
        JUMP_WEIGHT * STEP_SIZE * lane_take(wide(line, lines), ids[side])
        for side, line in ((1, first.next(row)), (3, first.prev(row)))
    ]
    spots = [
        [wide(places[n : n + 1] + m * pack, lines) for m in range(4)] for n in (0, 1)
    ]

    def copy_out(c):
        rows = pl.ds(pl.multiple_of(c * lines, lines), lines)
        return pltpu.make_async_copy(out.at[:, rows, :], out_hbm.at[:, rows, :], sems.at[c])

    def chunk(c, carry):
        at = pl.multiple_of(c * lines, lines)
        rows = pl.ds(at, lines)
        now = pl.ds(pl.multiple_of(4 * HALO + at, 8), lines)
        later = pl.ds(pl.multiple_of(4 * HALO + levels + at, 8), lines)
        state = [loc[p, rows] for p in range(16)]

        def across(own, there_now, there_next, side, factor, spot):
            values, beyond = [], []
            for n in range(4):
                values.append(jnp.where(near[side], 0.0, lane_take(there_now, spot[n])))
                beyond.append(
                    lane_take(there_next, spot[n]) + factor * own[n, rows].astype(jnp.float32)
                )
            return values, beyond

        east_now, east_beyond = across(
            east, got.next(now), got.next(later), 1, factors[0], spots[0]
        )
        west_now, west_beyond = across(
            west, got.prev(now), got.prev(later), 3, factors[1], spots[1]
        )
        for n in range(4):
            state[3 + 4 * n] = state[3 + 4 * n] + jump * east_now[n]
            state[4 * n] = state[4 * n] + jump * west_now[n]
        facing = home_facing(state, ids, near)
        facing[1] = [jnp.where(near[1], facing[1][n], east_beyond[n]) for n in range(4)]
        facing[3] = [jnp.where(near[3], facing[3][n], west_beyond[n]) for n in range(4)]
        result = element_step(
            state,
            lambda p: eastern[p, rows].astype(jnp.float32),
            lambda p: northern[p, rows].astype(jnp.float32),
            scale,
            facing,
        )
        for p in range(16):
            out[p, rows] = result[p]

        @pl.when(c == 0)
        def _():
            for p in range(16):
                lowest = out[p, 0:1]
                out[p, 0:1] = lowest + NUDGING_SPEED * (surface[p : p + 1] - lowest)

        copy_out(c).start()
        return carry

    lax.fori_loop(0, levels // lines, chunk, 0)

    def finish(c, carry):
        copy_out(c).wait()
        return carry

    lax.fori_loop(0, levels // lines, finish, 0)


def home_sums_kernel(marks, flux, weights, own):
    own[...] = jnp.zeros_like(own)
    for b in range(weights.shape[0]):
        sums = jnp.dot(
            flux[marks[MARK_COLUMN, b]].astype(jnp.bfloat16), weights[b], preferred_element_type=jnp.float32
        )
        row = marks[MARK_OWN, b]
        own[pl.ds(row, 1), :] = sums[1:2]
        own[pl.ds(row + 1, 1), :] = sums[2:3]
        own[pl.ds(marks[MARK_HEAT, b], 1), :] = sums[0:1]


def forward_kernel(
    marks, home, flux, slots, breadth, pn, first_far, first_near, odd, weights, out_hbm, out, extra,
    sems, *, devices
):
    ids, near = side_ids(pn)
    jump = (JUMP_WEIGHT * STEP_SIZE) * breadth[...]
    first = Received(first_far, first_near, odd)
    from_east = lane_take(first.next(slice(0, 8)), wide(ids[1], 8))
    from_west = lane_take(first.prev(slice(0, 8)), wide(ids[3], 8))
    from_east = jnp.where(near[1], 0.0, jump * from_east)
    from_west = jnp.where(near[3], 0.0, jump * from_west)
    extra[...] = jnp.zeros_like(extra)
    for n in range(4):
        for p, change in ((3 + 4 * n, from_east), (4 * n, from_west)):
            line = wide(flux[p, 3:4] * change[n : n + 1], 8).astype(jnp.bfloat16)
            for reader in range(2):
                b = marks[MARK_READER, 2 * p + reader]
                sums = jnp.dot(line, weights[b], preferred_element_type=jnp.float32)
                extra[pl.ds(marks[MARK_HEAT, b], 1), :] = sums[0:1]
    line = lax.broadcasted_iota(jnp.int32, (8, LANES), 0)
    part, copies = devices // 4, []
    for d in range(devices):
        mine, prev, following = (
            home[8 * (n % devices) : 8 * (n % devices) + 8] for n in (d, d - 1, d + 1)
        )
        top = jnp.concatenate([mine[0:4], prev[0:4]], axis=0)
        bottom = jnp.where(line < 4, following, mine + extra[8 * d : 8 * d + 8])
        bottom = jnp.where(line == ROW_IDS - 8, wide(slots[d : d + 1], 8), bottom)
        out[d] = jnp.concatenate([top, bottom], axis=0).astype(jnp.bfloat16)
        if (d + 1) % part == 0:
            copies.append(
                pltpu.make_async_copy(
                    out.at[pl.ds(d + 1 - part, part)],
                    out_hbm.at[pl.ds(d + 1 - part, part)],
                    sems.at[d // part],
                )
            )
            copies[-1].start()
    for copy in copies:
        copy.wait()


def back_kernel(marks, arrived, weights, surface, lines, share):
    lines[...] = arrived[...].reshape(lines.shape)
    for b in range(weights.shape[0]):
        line = lines[pl.ds(marks[MARK_ANSWER, b], 1), :]
        share[marks[MARK_PLACE, b]] = lax.dot_general(
            wide(line, 8).astype(jnp.bfloat16),
            weights[b],
            (((1,), (1,)), ((), ())),
            preferred_element_type=jnp.float32,
        )
    for p in range(surface.shape[0]):
        surface[p : p + 1] = share[2 * p, 0:1] + share[2 * p + 1, 0:1]


def split_index(idx):
    return lax.shift_right_arithmetic(idx, 7), idx & (LANES - 1)


def pick(idx, sources):
    high, low = split_index(idx)
    result = jnp.zeros(idx.shape, jnp.float32)
    for number, line in sources:
        result = jnp.where(high == number, lane_take(wide(line, idx.shape[0]), low), result)
    return result


def fill_pack(values, packed, scales):
    tiles = values.shape[0]
    half = tiles // 2
    largest = jnp.maximum(jnp.max(jnp.abs(values), axis=1, keepdims=True), 1e-30)
    number = jnp.floor(values * (32767.0 / largest) + 0.5).astype(jnp.int32)
    packed[...] = (number[half:] << 16) | (number[:half] & 0xFFFF)
    lane = lax.broadcasted_iota(jnp.int32, (tiles, LANES), 1)
    line = lax.broadcasted_iota(jnp.int32, (tiles, LANES), 0)
    row = jnp.sum(jnp.where(lane == line, largest * (1.0 / 32767.0), 0.0), axis=0, keepdims=True)
    scales[...] = wide(row, 8)


def pick_own(idx, packed, scales):
    lines = idx.shape[0]
    half = packed.shape[0]
    high, low = split_index(idx)
    own = high - HALO
    row = jnp.where(own >= half, own - half, own)
    words = jnp.zeros(idx.shape, jnp.int32)
    for r in range(half):
        words = jnp.where(row == r, lane_take(wide(packed[r : r + 1], lines), low), words)
    number = jnp.where(own >= half, words >> 16, (words << 16) >> 16)
    return number.astype(jnp.float32) * lane_take(wide(scales[0:1], lines), own & (LANES - 1))


def combine(terms, factors):
    total = None
    for term, factor in zip(terms, factors):
        if factor != 0.0:
            total = factor * term if total is None else total + factor * term
    return total


def pair_sums(table):
    terms = [table[HALO * k : HALO * (k + 1)] for k in range(6)]
    return combine(terms, COS), combine(terms, SIN)


def rim_partial(rim_idx, rim_w, eta, packed, scales, first):
    rows = rim_idx.shape[0]
    found = pick_own(rim_idx, packed, scales)
    centre = eta[first : first + HALO]
    centre = jnp.concatenate([centre] * (rows // HALO), axis=0)
    return pair_sums(rim_w * (found - centre))


def prepare_kernel(
    air_hbm, breadth_hbm, pn_hbm, eta_hbm, sst_hbm, flow_hbm, nb_hbm, span_hbm,
    nb, span, flow, rim_idx, rim_w, eta, eta_pack, eta_scale, sst, far, near, odd,
    up, dn, air, breadth, pn, sems
):
    copies = load(
        (
            (nb_hbm, nb),
            (span_hbm, span),
            (flow_hbm, flow),
            (eta_hbm, eta),
            (sst_hbm, sst),
            (breadth_hbm, breadth),
            (pn_hbm, pn),
            (air_hbm.at[:, pl.ds(0, 8), :], air),
        ),
        sems,
    )
    for copy in copies:
        copy.wait()
    shard = lax.shift_right_logical(pn[0:1], pn.shape[1].bit_length() - 1)
    odd[...] = wide(shard & 1, 8)
    tiles = eta.shape[0]
    fill_pack(eta[...], eta_pack, eta_scale)
    for side, first in ((0, 0), (1, tiles - HALO)):
        rim_idx[side, 12:16] = jnp.full((4, LANES), -1, jnp.int32)
        rim_w[side, 12:16] = jnp.zeros((4, LANES), jnp.float32)
        for j in range(HALO):
            cut = slice((first + j) * LANES, (first + j + 1) * LANES)
            links = nb[:, cut]
            factors = slot_factors(links, span[:, cut])
            for k in range(6):
                at = HALO * k + j
                rim_idx[side, at : at + 1] = links[k : k + 1]
                rim_w[side, at : at + 1] = factors[k : k + 1]
    for side, first, target in ((0, 0, dn), (1, tiles - HALO, up)):
        target[...] = jnp.zeros_like(target)
        for n in range(4):
            p = 4 * n if side == 0 else 3 + 4 * n
            target[ROW_EDGE + n : ROW_EDGE + n + 1] = air[p, 0:1]
        target[ROW_BREADTH : ROW_BREADTH + 1] = breadth[...]
        part_x, part_y = rim_partial(
            rim_idx[side], rim_w[side], eta, eta_pack, eta_scale, first
        )
        cut = slice(first, first + HALO)
        target[ROW_ETA : ROW_ETA + HALO] = eta[cut]
        for j in range(HALO):
            here = slice((first + j) * LANES, (first + j + 1) * LANES)
            target[ROW_U + j : ROW_U + j + 1] = flow[0:1, here]
            target[ROW_V + j : ROW_V + j + 1] = flow[1:2, here]
        target[ROW_SST : ROW_SST + HALO] = sst[cut]
        target[ROW_PX : ROW_PX + HALO] = part_x
        target[ROW_PY : ROW_PY + HALO] = part_y
        target[ROW_IDX : ROW_IDX + 16] = rim_idx[side].astype(jnp.float32)
        target[ROW_W : ROW_W + 16] = rim_w[side]
    arrange(up, dn, odd, far, near)


def slot_factors(links, span):
    return jnp.where(links >= 0, span * (1.0 / 3.0), 0.0)


def fill_tables(nb, span, flow, idx, w, u, v):
    tiles = u.shape[0]
    for r in range(tiles):
        cut = slice(r * LANES, (r + 1) * LANES)
        links = nb[:, cut]
        factors = slot_factors(links, span[:, cut])
        for k in range(6):
            idx[k * tiles + r : k * tiles + r + 1] = links[k : k + 1]
            w[k * tiles + r : k * tiles + r + 1] = factors[k : k + 1]
        u[r : r + 1] = flow[0:1, cut]
        v[r : r + 1] = flow[1:2, cut]


def own_gradient(idx, w, eta, packed, scales, gx, gy):
    tiles = eta.shape[0]

    def chunk(at):
        centre = eta[pl.ds(at, 8)]
        terms = []
        for k in range(6):
            found = pick_own(idx[pl.ds(k * tiles + at, 8)], packed, scales)
            terms.append(w[pl.ds(k * tiles + at, 8)] * (found - centre))
        gx[pl.ds(at, 8)] = combine(terms, COS)
        gy[pl.ds(at, 8)] = combine(terms, SIN)

    for c in range(tiles // 8):
        chunk(c * 8)


def own_spread(at, idx, w, flow, packed, scales):
    tiles = flow.shape[1]
    total = jnp.zeros((8, LANES), jnp.float32)
    for kk in range(3):
        centre = flow[kk, pl.ds(at, 8)]
        for k, sign in ((kk, 1.0), (kk + 3, -1.0)):
            rows = pl.ds(k * tiles + at, 8)
            found = pick_own(idx[rows], packed.at[kk], scales.at[kk])
            total = total + sign * w[rows] * (found - centre)
    return total


def inner_kernel(
    idx, w, eta, eta_pack, eta_scale, u, v, fu, fv, eta_part, u_part, v_part,
    flow, flow_pack, flow_scale
):
    current_kernel(idx, w, eta, eta_pack, eta_scale, u, v, fu, fv, u_part, v_part)
    height_kernel(idx, w, eta, u_part, v_part, eta_part, flow, flow_pack, flow_scale)


def current_kernel(idx, w, eta, eta_pack, eta_scale, u, v, fu, fv, u_part, v_part):
    own_gradient(idx, w, eta, eta_pack, eta_scale, u_part, v_part)
    u_part[...] = DAMPING * u[...] - GRAVITY * u_part[...] + WIND_GAIN * fu[...]
    v_part[...] = DAMPING * v[...] - GRAVITY * v_part[...] + WIND_GAIN * fv[...]


def height_kernel(idx, w, eta, u_part, v_part, eta_part, flow, flow_pack, flow_scale):
    tiles = eta.shape[0]
    fill_flow(flow, u_part[...], v_part[...])
    for kk in range(3):
        fill_pack(flow[kk], flow_pack.at[kk], flow_scale.at[kk])

    def chunk(at):
        total = own_spread(at, idx, w, flow, flow_pack, flow_scale)
        eta_part[pl.ds(at, 8)] = eta[pl.ds(at, 8)] - DEPTH_RATE * total

    for c in range(tiles // 8):
        chunk(c * 8)


def first_gradient_kernel(
    idx, w, eta, eta_pack, eta_scale, sst, first_far, first_near, odd, rim_idx, rim_w,
    gx, gy, base, sst_pack, sst_scale
):
    own_gradient(idx, w, eta, eta_pack, eta_scale, gx, gy)
    tiles = eta.shape[0]
    fill_pack(sst[...], sst_pack, sst_scale)

    def chunk(at):
        centre = sst[pl.ds(at, 8)]
        total = jnp.zeros_like(centre)
        for k in range(6):
            found = pick_own(idx[pl.ds(k * tiles + at, 8)], sst_pack, sst_scale)
            total = total + w[pl.ds(k * tiles + at, 8)] * (found - centre)
        base[pl.ds(at, 8)] = centre + (0.5 * SPREADING_COEFF) * total

    for c in range(tiles // 8):
        chunk(c * 8)
    first = Received(first_far, first_near, odd)
    for side, start, offset in ((0, 0, 0), (1, tiles - HALO, tiles + HALO)):
        rim = first.rim(side, ROW_SST)
        sources = [(offset + q, rim[q : q + 1]) for q in range(HALO)]
        found = rim_w[side] * pick(rim_idx[side], sources)
        total = combine([found[HALO * k : HALO * (k + 1)] for k in range(6)], [1.0] * 6)
        rows = slice(start, start + HALO)
        base[rows] = base[rows] + (0.5 * SPREADING_COEFF) * total


def fill_flow(flow, u, v):
    flow[0] = u
    for kk in (1, 2):
        flow[kk] = COS[kk] * u + SIN[kk] * v


def side_currents(eta, sides, fside, before, after, side_idx, side_w):
    tiles = eta.shape[0]
    slopes = []
    for side, offset, first, part in (
        (0, tiles + HALO, 0, before),
        (1, 0, tiles - HALO, after),
    ):
        sources = [(offset + q, eta[first + q : first + q + 1]) for q in range(HALO)]
        add_x, add_y = pair_sums(side_w[side] * pick(side_idx[side], sources))
        slopes.append((part[1] + add_x, part[2] + add_y))
    slope = jnp.concatenate([slopes[0][0], slopes[1][0], slopes[0][1], slopes[1][1]], axis=0)
    return DAMPING * sides[...] - GRAVITY * slope + WIND_GAIN * fside[...]


def rim_slopes(rim_idx, rim_w, before, after, tiles):
    result = []
    for side, offset, part in ((0, 0, before), (1, tiles + HALO, after)):
        sources = [(offset + q, part[0][q : q + 1]) for q in range(HALO)]
        result.append(pair_sums(rim_w[side] * pick(rim_idx[side], sources)))
    return result


def send_rims(eta, eta_pack, eta_scale, rim_idx, rim_w, odd, far, near, up, dn):
    tiles = eta.shape[0]
    fill_pack(eta[...], eta_pack, eta_scale)
    for side, first, target in ((0, 0, dn), (1, tiles - HALO, up)):
        part_x, part_y = rim_partial(
            rim_idx[side], rim_w[side], eta, eta_pack, eta_scale, first
        )
        target[0:HALO] = eta[first : first + HALO]
        target[HALO : 2 * HALO] = part_x
        target[2 * HALO : 3 * HALO] = part_y
        target[3 * HALO : 4 * HALO] = jnp.zeros((HALO, LANES), jnp.float32)
    rows = pl.ds(0, 4 * HALO)
    arrange(up, dn, odd, far.at[rows], near.at[rows])


def first_subcycle(
    gx, gy, eta, u, v, sides, fu, fv, fside, before, after, idx, w, side_idx, side_w,
    rim_idx, rim_w, flow, flow_pack, flow_scale, flow_outer, eta_new, u_new, v_new, sides_new
):
    tiles = eta.shape[0]
    u_new[...] = DAMPING * u[...] - GRAVITY * gx[...] + WIND_GAIN * fu[...]
    v_new[...] = DAMPING * v[...] - GRAVITY * gy[...] + WIND_GAIN * fv[...]
    slopes = rim_slopes(rim_idx, rim_w, before, after, tiles)
    for first, (add_x, add_y) in zip((0, tiles - HALO), slopes):
        rows = slice(first, first + HALO)
        u_new[rows] = u_new[rows] - GRAVITY * add_x
        v_new[rows] = v_new[rows] - GRAVITY * add_y
    sides_next = side_currents(eta, sides, fside, before, after, side_idx, side_w)
    sides_new[...] = sides_next
    fill_flow(flow, u_new[...], v_new[...])
    fill_flow(flow_outer, sides_next[0 : 2 * HALO], sides_next[2 * HALO : 4 * HALO])
    for kk in range(3):
        fill_pack(flow[kk], flow_pack.at[kk], flow_scale.at[kk])

    def chunk(at):
        total = own_spread(at, idx, w, flow, flow_pack, flow_scale)
        eta_new[pl.ds(at, 8)] = eta[pl.ds(at, 8)] - DEPTH_RATE * total

    for c in range(tiles // 8):
        chunk(c * 8)
    for side, first, offset in ((0, 0, 0), (1, tiles - HALO, tiles + HALO)):
        total = jnp.zeros((HALO, LANES), jnp.float32)
        for kk in range(3):
            at = side * HALO
            sources = [(offset + q, flow_outer[kk, at + q : at + q + 1]) for q in range(HALO)]
            found = rim_w[side] * pick(rim_idx[side], sources)
            total = (
                total
                + found[HALO * kk : HALO * (kk + 1)]
                - found[HALO * (kk + 3) : HALO * (kk + 4)]
            )
        rows = slice(first, first + HALO)
        eta_new[rows] = eta_new[rows] - DEPTH_RATE * total


def outer_subcycle(
    eta, eta_part, u_part, v_part, sides, fside, before, after, idx, w, side_idx, side_w,
    rim_idx, rim_w, flow_outer, eta_new, u_new, v_new
):
    tiles = eta.shape[0]
    slopes = rim_slopes(rim_idx, rim_w, before, after, tiles)
    sides_next = side_currents(eta, sides, fside, before, after, side_idx, side_w)
    u_new[...] = u_part[...]
    v_new[...] = v_part[...]
    changes_u = [-GRAVITY * slopes[side][0] for side in (0, 1)]
    changes_v = [-GRAVITY * slopes[side][1] for side in (0, 1)]
    for side, first in ((0, 0), (1, tiles - HALO)):
        rows = slice(first, first + HALO)
        u_new[rows] = u_new[rows] + changes_u[side]
        v_new[rows] = v_new[rows] + changes_v[side]
    fill_flow(
        flow_outer,
        jnp.concatenate([sides_next[0 : 2 * HALO]] + changes_u, axis=0),
        jnp.concatenate([sides_next[2 * HALO : 4 * HALO]] + changes_v, axis=0),
    )
    for c in range(tiles // 8):
        at = c * 8
        total = jnp.zeros((8, LANES), jnp.float32)
        for kk in range(3):
            line = lambda n: flow_outer[kk, n : n + 1]
            sources = [(HALO + q, line(2 * HALO + q)) for q in range(HALO)]
            sources += [(tiles + q, line(3 * HALO + q)) for q in range(HALO)]
            if at == 0:
                sources += [(q, line(q)) for q in range(HALO)]
            if at + 8 == tiles:
                sources += [(tiles + HALO + q, line(HALO + q)) for q in range(HALO)]
            total = (
                total
                + w[kk * tiles + at : kk * tiles + at + 8]
                * pick(idx[kk * tiles + at : kk * tiles + at + 8], sources)
                - w[(kk + 3) * tiles + at : (kk + 3) * tiles + at + 8]
                * pick(idx[(kk + 3) * tiles + at : (kk + 3) * tiles + at + 8], sources)
            )
        eta_new[at : at + 8] = eta_part[at : at + 8] - DEPTH_RATE * total
    for side, first in ((0, 0), (1, tiles - HALO)):
        centre = jnp.zeros((HALO, LANES), jnp.float32)
        for kk in range(3):
            factor = (
                rim_w[side, HALO * kk : HALO * (kk + 1)]
                - rim_w[side, HALO * (kk + 3) : HALO * (kk + 4)]
            )
            start = (2 + side) * HALO
            centre = centre + factor * flow_outer[kk, start : start + HALO]
        rows = slice(first, first + HALO)
        eta_new[rows] = eta_new[rows] + DEPTH_RATE * centre
    return sides_next


def first_ocean_kernel(
    arrived, first_far, first_near, odd, gx, gy, eta, u, v, idx, w, rim_idx, rim_w,
    east_pack, west_pack, base, eta_new, eta_pack, eta_scale, u_new, v_new, sides_new, far, near,
    fu, fv, fside, side_idx, side_w, heat, answers_hbm,
    flow, flow_pack, flow_scale, flow_outer, sides, up, dn, parts, answers, sems
):
    tiles = eta.shape[0]
    devices = arrived.shape[0]
    parts[...] = arrived[...].astype(jnp.float32).reshape(parts.shape)

    def rows_of(r):
        return parts[pl.ds(r, devices, stride=PER_DEST), :]

    ids = rows_of(ROW_IDS)
    number = lax.broadcasted_iota(jnp.int32, (devices, LANES), 1).astype(jnp.float32)
    nothing = jnp.zeros((devices, LANES), jnp.float32)
    chosen, lines = [], []
    for j in range(3 * CAP):
        chosen.append(jnp.where(ids[:, j : j + 1] == number, 1.0, 0.0).astype(jnp.bfloat16))
        first = rows_of(ROW_HEAT + j) if j < CAP else nothing
        lines.append(jnp.concatenate([first, rows_of(2 * j), rows_of(2 * j + 1)], axis=1))
    forcing = lax.dot_general(
        jnp.concatenate(chosen, axis=0),
        jnp.concatenate(lines, axis=0).astype(jnp.bfloat16),
        (((0,), (0,)), ((), ())),
        preferred_element_type=jnp.float32,
    )
    heat[...] = forcing[0:tiles, 0:LANES]
    half = (base[...] + WARMING_COEFF * forcing[0:tiles, 0:LANES]).astype(jnp.bfloat16)
    for j in range(CAP):
        answers[:, j, :] = jnp.dot(
            chosen[j][:, 0:tiles], half, preferred_element_type=jnp.float32
        )
    copy = pltpu.make_async_copy(answers, answers_hbm, sems.at[0])
    copy.start()
    fu[...] = forcing[0:tiles, LANES : 2 * LANES]
    fv[...] = forcing[0:tiles, 2 * LANES : 3 * LANES]
    fside[0 : 2 * HALO] = forcing[tiles : tiles + 2 * HALO, LANES : 2 * LANES]
    fside[2 * HALO : 4 * HALO] = forcing[tiles : tiles + 2 * HALO, 2 * LANES : 3 * LANES]
    first = Received(first_far, first_near, odd)
    for side, part in ((0, first.prev), (1, first.next)):
        side_idx[side] = part(slice(ROW_IDX, ROW_IDX + 16)).astype(jnp.int32)
        side_w[side] = part(slice(ROW_W, ROW_W + 16))
        for n, row in ((0, ROW_U), (1, ROW_V)):
            at = HALO * (2 * n + side)
            sides[at : at + HALO] = first.rim(side, row)
    rows = (ROW_ETA, ROW_PX, ROW_PY)
    first_subcycle(
        gx, gy, eta, u, v, sides, fu, fv, fside, first.rims(0, rows), first.rims(1, rows), idx, w, side_idx, side_w, rim_idx, rim_w, flow, flow_pack, flow_scale, flow_outer,
        eta_new, u_new, v_new, sides_new
    )
    send_rims(eta_new, eta_pack, eta_scale, rim_idx, rim_w, odd, far, near, up, dn)
    flag = jnp.broadcast_to(odd[0:1], east_pack.shape) > 0
    far[4 * HALO :] = jnp.where(flag, east_pack[...], west_pack[...])
    near[4 * HALO :] = jnp.where(flag, west_pack[...], east_pack[...])
    copy.wait()


def ocean_kernel(
    far, near, odd, eta, eta_part, u_part, v_part, sides, fside, idx, w, side_idx, side_w,
    rim_idx, rim_w, eta_new, eta_pack, eta_scale, u_new, v_new, sides_new, far_new, near_new,
    flow_outer, up, dn
):
    rows = (0, HALO, 2 * HALO)
    got = Received(far, near, odd)
    sides_new[...] = outer_subcycle(
        eta, eta_part, u_part, v_part, sides, fside, got.rims(0, rows), got.rims(1, rows), idx, w, side_idx, side_w, rim_idx, rim_w, flow_outer,
        eta_new, u_new, v_new
    )
    send_rims(
        eta_new, eta_pack, eta_scale, rim_idx, rim_w, odd, far_new, near_new, up, dn
    )


def last_ocean_kernel(
    far, near, odd, eta, eta_part, u_part, v_part, sides, fside, idx, w, side_idx, side_w,
    rim_idx, rim_w, base, heat, eta_new, velocity, warm, u_new, v_new, flow_outer
):
    warm[...] = base[...] + WARMING_COEFF * heat[...]
    rows = (0, HALO, 2 * HALO)
    got = Received(far, near, odd)
    outer_subcycle(
        eta, eta_part, u_part, v_part, sides, fside, got.rims(0, rows), got.rims(1, rows), idx, w, side_idx, side_w, rim_idx, rim_w, flow_outer,
        eta_new, u_new, v_new
    )
    for r in range(eta.shape[0]):
        cut = slice(r * LANES, (r + 1) * LANES)
        velocity[0:1, cut] = u_new[r : r + 1]
        velocity[1:2, cut] = v_new[r : r + 1]


def shards(
    air_warmth,
    eastern_breeze,
    northern_breeze,
    reciprocal_breadth,
    panel_neighbours,
    transfer_coefficients,
    transfer_across_tile,
    transfer_holder,
    transfer_down_tile,
    water_elevation,
    depth_mean_current,
    marine_skin_warmth,
    patch_neighbours,
    interface_span,
):
    devices = lax.axis_size(RING)
    points, levels, elements = air_warmth.shape
    cells = water_elevation.shape[0]
    tiles = cells // LANES
    blocks = transfer_holder.shape[0]
    cell_rows = shape_of(tiles, LANES)
    rim_rows = shape_of(4 * HALO, LANES)
    dma = pltpu.SemaphoreType.DMA
    air, eastern, northern, breadth_hbm, pn_hbm = in_hbm(
        air_warmth, eastern_breeze, northern_breeze, reciprocal_breadth.reshape(1, elements),
        panel_neighbours
    )

    pack_rows = shape_of(tiles // 2, LANES, dtype=jnp.int32)
    scale_rows = shape_of(8, LANES)
    nb, span, flow, rim_idx, rim_w, eta, eta_pack, eta_scale, sst, far, near, odd = pl.pallas_call(
        prepare_kernel,
        in_specs=hbm(8),
        out_specs=vmem(12),
        out_shape=(
            shape_of(6, cells, dtype=jnp.int32),
            shape_of(6, cells),
            shape_of(2, cells),
            shape_of(2, 16, LANES, dtype=jnp.int32),
            shape_of(2, 16, LANES),
            cell_rows,
            pack_rows,
            scale_rows,
            cell_rows,
            shape_of(ROWS_FIRST, LANES),
            shape_of(ROWS_FIRST, LANES),
            shape_of(8, elements, dtype=jnp.int32),
        ),
        scratch_shapes=[
            pltpu.VMEM((ROWS_FIRST, LANES), jnp.float32),
            pltpu.VMEM((ROWS_FIRST, LANES), jnp.float32),
            pltpu.VMEM((points, 8, elements), jnp.float32),
            pltpu.VMEM((1, elements), jnp.float32),
            pltpu.VMEM((4, elements), jnp.int32),
            dma((8,)),
        ],
        compiler_params=PARAMS,
        name="prepare",
    )(
        air,
        breadth_hbm,
        pn_hbm,
        *in_hbm(
            water_elevation.reshape(tiles, LANES),
            marine_skin_warmth.reshape(tiles, LANES),
            depth_mean_current,
            patch_neighbours,
            interface_span,
        ),
    )
    first_far, first_near = swap_both(far, near)

    low_wind = pltpu.VMEM((points, 16, elements), jnp.bfloat16)
    low_row = pltpu.VMEM((1, blocks), jnp.int32)
    flux, slots, breadth, pn, marks, idx, w, u, v = pl.pallas_call(
        lambda *refs: plan_kernel(*refs, devices=devices, tiles=tiles),
        in_specs=hbm(8) + vmem(3),
        out_specs=vmem(4) + smem(1) + vmem(4),
        out_shape=(
            shape_of(points, 8, elements), shape_of(devices, LANES), shape_of(1, elements),
            shape_of(4, elements, dtype=jnp.int32), pltpu.SMEM((8, blocks), jnp.int32),
            shape_of(6 * tiles, LANES, dtype=jnp.int32), shape_of(6 * tiles, LANES),
            cell_rows, cell_rows
        ),
        scratch_shapes=[
            pltpu.VMEM((points, 8, elements), jnp.float32), low_wind, low_wind,
            low_row, low_row, low_row, pltpu.VMEM((8, blocks), jnp.int32), dma((8,))
        ],
        compiler_params=PARAMS,
        name="plan",
    )(
        air,
        eastern,
        northern,
        breadth_hbm,
        pn_hbm,
        *in_hbm(
            transfer_holder.reshape(1, blocks),
            transfer_across_tile.reshape(1, blocks),
            transfer_down_tile.reshape(1, blocks),
        ),
        nb,
        span,
        flow,
    )

    home = pl.pallas_call(
        home_sums_kernel,
        in_specs=smem(1) + vmem(2),
        out_specs=pl.BlockSpec(memory_space=pltpu.VMEM),
        out_shape=shape_of(devices * 8, LANES),
        compiler_params=PARAMS,
        name="home_sums",
    )(marks, flux, transfer_coefficients)
    outgoing = pl.pallas_call(
        lambda *refs: forward_kernel(*refs, devices=devices),
        in_specs=smem(1) + vmem(9),
        out_specs=pl.BlockSpec(memory_space=pltpu.HBM),
        out_shape=pltpu.HBM((devices, PER_DEST, LANES), jnp.bfloat16),
        scratch_shapes=[
            pltpu.VMEM((devices, PER_DEST, LANES), jnp.bfloat16),
            pltpu.VMEM((devices * 8, LANES), jnp.float32),
            dma((4,)),
        ],
        compiler_params=PARAMS,
        name="forward_remap",
    )(
        marks, home, flux, slots, breadth, pn, first_far, first_near, odd, transfer_coefficients
    )
    outgoing, pn, gradient_eta = lax.optimization_barrier((outgoing, pn, eta))
    arrived = exchange(outgoing)
    gx, gy, base = pl.pallas_call(
        first_gradient_kernel,
        in_specs=vmem(11),
        out_specs=vmem(3),
        out_shape=(cell_rows,) * 3,
        scratch_shapes=[
            pltpu.VMEM((tiles // 2, LANES), jnp.int32), pltpu.VMEM((8, LANES), jnp.float32)
        ],
        compiler_params=PARAMS,
        name="first_gradient",
    )(
        idx, w, gradient_eta, eta_pack, eta_scale, sst, first_far, first_near, odd, rim_idx, rim_w
    )

    field = shape_of(points, levels, elements)
    edge = shape_of(4, levels, elements, dtype=jnp.bfloat16)
    pack = shape_of(2 * levels, elements)
    wind = shape_of(points, levels, elements, dtype=jnp.bfloat16)
    loc, eastern, northern, east, west, east_pack, west_pack, edge_places = pl.pallas_call(
        local_step_kernel,
        in_specs=hbm(3) + vmem(2),
        out_specs=vmem(8),
        out_shape=(
            field, wind, wind, edge, edge, pack, pack, shape_of(8, elements, dtype=jnp.int32)
        ),
        scratch_shapes=[pltpu.VMEM((points, levels, elements), jnp.float32), dma((3,))],
        compiler_params=PARAMS,
        name="local_step",
    )(air, eastern, northern, breadth, pn)

    rim_scratch = pltpu.VMEM((4 * HALO, LANES), jnp.float32)
    second_rows = shape_of(4 * HALO + 2 * levels, elements)
    flow_scratch = [
        pltpu.VMEM((3, tiles, LANES), jnp.float32),
        pltpu.VMEM((3, tiles // 2, LANES), jnp.int32),
        pltpu.VMEM((3, 8, LANES), jnp.float32),
        pltpu.VMEM((3, 2 * HALO, LANES), jnp.float32),
    ]
    (
        eta, eta_pack, eta_scale, u, v, sides, far, near, fu, fv, fside, side_idx, side_w,
        heat, answers
    ) = pl.pallas_call(
        first_ocean_kernel,
        in_specs=vmem(16),
        out_specs=vmem(14) + hbm(1),
        out_shape=(
            cell_rows, pack_rows, scale_rows, cell_rows, cell_rows, rim_rows, second_rows, second_rows,
            cell_rows, cell_rows, rim_rows,
            shape_of(2, 16, LANES, dtype=jnp.int32), shape_of(2, 16, LANES),
            cell_rows, pltpu.HBM((devices, CAP, LANES), jnp.float32),
        ),
        scratch_shapes=flow_scratch + [rim_scratch] * 3 + [
            pltpu.VMEM((devices * PER_DEST, LANES), jnp.float32),
            pltpu.VMEM((devices, CAP, LANES), jnp.float32),
            dma((1,)),
        ],
        compiler_params=PARAMS,
        name="first_ocean",
    )(
        arrived, first_far, first_near, odd, gx, gy, eta, u, v, idx, w, rim_idx, rim_w,
        east_pack, west_pack, base
    )
    far, near = swap_both(far, near)
    edges_far, edges_near = far, near

    for substep in range(1, NSUB):
        if substep == 1:
            u_part, v_part = pl.pallas_call(
                current_kernel,
                in_specs=vmem(9),
                out_specs=vmem(2),
                out_shape=(cell_rows,) * 2,
                compiler_params=PARAMS,
                name="current",
            )(idx, w, eta, eta_pack, eta_scale, u, v, fu, fv)
            answers, u_part = lax.optimization_barrier((answers, u_part))
            answered = exchange(answers)
            eta_part = pl.pallas_call(
                height_kernel,
                in_specs=vmem(5),
                out_specs=pl.BlockSpec(memory_space=pltpu.VMEM),
                out_shape=cell_rows,
                scratch_shapes=flow_scratch[:3],
                compiler_params=PARAMS,
                name="height",
            )(idx, w, eta, u_part, v_part)
        else:
            eta_part, u_part, v_part = pl.pallas_call(
                inner_kernel,
                in_specs=vmem(9),
                out_specs=vmem(3),
                out_shape=(cell_rows,) * 3,
                scratch_shapes=flow_scratch[:3],
                compiler_params=PARAMS,
                name="inner",
            )(idx, w, eta, eta_pack, eta_scale, u, v, fu, fv)
        if substep == 2:
            eta_part, answered = lax.optimization_barrier((eta_part, answered))
            surface = pl.pallas_call(
                back_kernel,
                in_specs=smem(1) + vmem(2),
                out_specs=pl.BlockSpec(memory_space=pltpu.VMEM),
                out_shape=shape_of(points, LANES),
                scratch_shapes=[
                    pltpu.VMEM((devices * CAP, LANES), jnp.float32),
                    pltpu.VMEM((blocks, 8, LANES), jnp.float32),
                ],
                compiler_params=PARAMS,
                name="back_remap",
            )(marks, answered, transfer_coefficients)
            eta_part, surface = lax.optimization_barrier((eta_part, surface))
        operands = (
            far, near, odd, eta, eta_part, u_part, v_part, sides, fside, idx, w, side_idx, side_w, rim_idx, rim_w
        )
        outer_scratch = [pltpu.VMEM((3, 4 * HALO, LANES), jnp.float32)]
        if substep + 1 < NSUB:
            eta, eta_pack, eta_scale, u, v, sides, far, near = pl.pallas_call(
                ocean_kernel,
                in_specs=vmem(15),
                out_specs=vmem(8),
                out_shape=(cell_rows, pack_rows, scale_rows) + (cell_rows,) * 2 + (rim_rows,) * 3,
                scratch_shapes=outer_scratch + [rim_scratch] * 2,
                compiler_params=PARAMS,
                name="ocean",
            )(*operands)
            far, near = swap_both(far, near)
        else:
            eta, velocity, warm = pl.pallas_call(
                last_ocean_kernel,
                in_specs=vmem(17),
                out_specs=vmem(3),
                out_shape=(cell_rows, shape_of(2, cells), cell_rows),
                scratch_shapes=[pltpu.VMEM((tiles, LANES), jnp.float32)] * 2 + outer_scratch,
                compiler_params=PARAMS,
                name="last_ocean",
            )(*operands, base, heat)

    closing = pl.pallas_call(
        second_step_kernel,
        in_specs=vmem(14),
        out_specs=pl.BlockSpec(memory_space=pltpu.HBM),
        out_shape=pltpu.HBM((points, levels, elements), jnp.float32),
        scratch_shapes=[
            pltpu.VMEM((points, levels, elements), jnp.float32), dma((levels // 16,))
        ],
        compiler_params=PARAMS,
        name="second_step",
    )(
        loc, eastern, northern, breadth, pn, east, west, edges_far, edges_near, edge_places,
        first_far, first_near, odd, surface
    )
    return closing, eta.reshape(cells), velocity, warm.reshape(cells)


def solution(mesh):
    split = P(RING)
    last = P(None, RING)
    field = P(None, None, RING)
    return jax.shard_map(
        shards,
        mesh=mesh,
        in_specs=(
            field,
            field,
            field,
            split,
            last,
            P(RING, None, None),
            split,
            P(RING, None),
            split,
            split,
            last,
            split,
            last,
            last,
        ),
        out_specs=(field, split, last, split),
        check_vma=False,
    )
```

```python
import math

import jax
import jax.numpy as jnp
import numpy as np
from jax import lax
from jax.experimental import pallas as pl
from jax.experimental.pallas import tpu as pltpu
from jax.sharding import PartitionSpec as P

OY = 256
NSUB = 4
CAP = 2

STEP_SIZE = 0.05
JUMP_WEIGHT = 4.0
NUDGING_SPEED = 0.5
DAMPING = 0.9
GRAVITY = 0.3
WIND_GAIN = 0.3
DEPTH_RATE = 0.3
WARMING_COEFF = 0.3
SPREADING_COEFF = 0.5

RING = ("comp", "dom")
LANES = 128
HALO = OY // LANES
COS = [math.cos(k * math.pi / 3.0) for k in range(6)]
SIN = [0.0 if k % 3 == 0 else math.sin(k * math.pi / 3.0) for k in range(6)]

ROW_EDGE, ROW_BREADTH, ROW_ETA, ROW_U, ROW_V, ROW_SST = 0, 4, 8, 10, 12, 14
ROW_PX, ROW_PY, ROW_IDX, ROW_W, ROWS_FIRST = 16, 18, 24, 40, 56
MARK_COLUMN, MARK_OWN, MARK_HEAT, MARK_ANSWER, MARK_PLACE, MARK_READER = range(6)
PER_DEST, ROW_HEAT, ROW_IDS = 16, 12, 14


def swapped(value, first):
    count = lax.axis_size(RING)
    pairs = []
    for i in range(first, count + first, 2):
        pairs += [(i % count, (i + 1) % count), ((i + 1) % count, i % count)]
    return lax.ppermute(value, RING, pairs)


def swap_both(far, near):
    got_far = swapped(far, 1)
    return got_far, swapped(near, 0)


class Received:
    def __init__(self, far, near, odd):
        self.far, self.near, self.odd = far, near, odd

    def flag(self, rows):
        return jnp.broadcast_to(self.odd[0:1], rows.shape) > 0

    def prev(self, *cut):
        far, near = self.far[cut], self.near[cut]
        return jnp.where(self.flag(far), near, far)

    def next(self, *cut):
        far, near = self.far[cut], self.near[cut]
        return jnp.where(self.flag(far), far, near)

    def rim(self, side, row):
        cut = slice(row, row + HALO)
        return self.prev(cut) if side == 0 else self.next(cut)

    def rims(self, side, rows):
        return tuple(self.rim(side, row) for row in rows)


def arrange(up, dn, odd, far, near):
    flag = jnp.broadcast_to(odd[0:1], up.shape) > 0
    far[...] = jnp.where(flag, up[...], dn[...])
    near[...] = jnp.where(flag, dn[...], up[...])


def exchange(value):
    return lax.all_to_all(value, RING, split_axis=0, concat_axis=0, tiled=True)


def gll_matrix():
    points = np.array([-1.0, -1.0 / np.sqrt(5.0), 1.0 / np.sqrt(5.0), 1.0])
    barycentric = [
        1.0 / np.prod([points[s] - points[o] for o in range(4) if o != s]) for s in range(4)
    ]
    table = np.zeros((4, 4))
    for t in range(4):
        for s in range(4):
            if t != s:
                table[t, s] = barycentric[s] / barycentric[t] / (points[t] - points[s])
    for t in (0, 3):
        table[t, t] = -np.sum(table[t])
    return [[float(np.float32(value)) for value in line] for line in table]


GLL = gll_matrix()


def vmem(count):
    return [pl.BlockSpec(memory_space=pltpu.VMEM)] * count


def hbm(count):
    return [pl.BlockSpec(memory_space=pltpu.HBM)] * count


def in_hbm(*arrays):
    return [pltpu.with_memory_space_constraint(array, pltpu.HBM) for array in arrays]


def smem(count):
    return [pl.BlockSpec(memory_space=pltpu.SMEM)] * count


def shape_of(*dims, dtype=jnp.float32):
    return jax.ShapeDtypeStruct(dims, dtype)


PARAMS = pltpu.CompilerParams(vmem_limit_bytes=24 * 1024 * 1024)


def lane_take(rows, ids):
    return jnp.take_along_axis(rows, ids, axis=1, mode="promise_in_bounds")


def wide(row, lines):
    return jnp.broadcast_to(row, (lines, row.shape[1]))


def side_ids(pn):
    count = pn.shape[1]
    bits = count.bit_length() - 1
    table = pn[...]
    ids = [table[k : k + 1] & (count - 1) for k in range(4)]
    home = lax.shift_right_logical(table[0:1], bits)
    near = [lax.shift_right_logical(table[k : k + 1], bits) == home for k in range(4)]
    return ids, near


def element_step(state, east_wind, north_wind, scale, facing):
    jumps = [None] * 16
    sides = (
        (0, 1, 2, 3),
        (3, 7, 11, 15),
        (12, 13, 14, 15),
        (0, 4, 8, 12),
    )
    for k in range(4):
        for n, p in enumerate(sides[k]):
            term = facing[k][n] - state[p]
            jumps[p] = term if jumps[p] is None else jumps[p] + term
    result = []
    for p in range(16):
        i, j = p % 4, p // 4
        grad_x = grad_y = None
        for m in range(4):
            if GLL[i][m] != 0.0:
                term = GLL[i][m] * state[m + 4 * j]
                grad_x = term if grad_x is None else grad_x + term
            if GLL[j][m] != 0.0:
                term = GLL[j][m] * state[i + 4 * m]
                grad_y = term if grad_y is None else grad_y + term
        change = -(east_wind(p) * grad_x + north_wind(p) * grad_y)
        if jumps[p] is not None:
            change = change + JUMP_WEIGHT * jumps[p]
        result.append(state[p] + scale * change)
    return result


def load(pairs, sems):
    copies = [
        pltpu.make_async_copy(source, target, sems.at[n])
        for n, (source, target) in enumerate(pairs)
    ]
    for copy in copies:
        copy.start()
    return copies


def as_column(row):
    count = row.shape[1]
    return jnp.transpose(jnp.broadcast_to(row, (count, count)))


def edge_tables(partner, remote):
    count = partner.shape[1]
    pack = count // 4
    lane = lax.broadcasted_iota(jnp.int32, (count, count), 1)
    line = lax.broadcasted_iota(jnp.int32, (count, count), 0)
    flag = jnp.where(remote, 1.0, 0.0)
    rank = jnp.sum(jnp.where(line < lane, as_column(flag), 0.0), axis=0, keepdims=True)
    rank = as_column(jnp.where(remote, rank, -1.0))
    slot = (lane & (pack - 1)).astype(jnp.float32)
    chosen = jnp.sum(
        jnp.where(rank == slot, line.astype(jnp.float32), 0.0), axis=0, keepdims=True
    ).astype(jnp.int32)
    key = jnp.where(remote, partner, 2 * count).astype(jnp.float32)
    before = jnp.where(as_column(key) < key, 1.0, 0.0)
    place = jnp.sum(before, axis=0, keepdims=True).astype(jnp.int32)
    return chosen, jnp.minimum(place, pack - 1)


def rank_among_equals(row, most):
    count = row.shape[1]
    earlier = lax.broadcasted_iota(jnp.int32, (count, count), 0) < lax.broadcasted_iota(
        jnp.int32, (count, count), 1
    )
    number = row.astype(jnp.float32)
    same = as_column(number) == number
    return jnp.minimum(jnp.sum(jnp.where(same & earlier, 1, 0), axis=0, keepdims=True), most)


def slot_rows(holder_row, rank, down_row, devices, tiles):
    blocks = holder_row.shape[1]
    target = lax.broadcasted_iota(jnp.int32, (devices, blocks), 0)
    after = jnp.where(holder_row + 1 == devices, 0, holder_row + 1)
    before = jnp.where(holder_row == 0, devices - 1, holder_row - 1)
    last = down_row - (tiles - HALO)
    lane = lax.broadcasted_iota(jnp.int32, (devices, LANES), 1)
    result = jnp.full((devices, LANES), -1.0, jnp.float32)
    for n, (owner, number) in enumerate(
        (
            (holder_row, down_row),
            (after, jnp.where(last >= 0, tiles + last, -1)),
            (before, jnp.where(down_row < HALO, tiles + HALO + down_row, -1)),
        )
    ):
        for slot in range(CAP):
            named = (target == owner) & (rank == slot)
            value = jnp.sum(
                jnp.where(named, (number + 1).astype(jnp.float32), 0.0), axis=1, keepdims=True
            )
            result = jnp.where(lane == CAP * n + slot, value - 1.0, result)
    return result


def home_facing(state, ids, near):
    return [
        [lane_take(state[12 + n], ids[0]) for n in range(4)],
        [jnp.where(near[1], lane_take(state[4 * n], ids[1]), 0.0) for n in range(4)],
        [lane_take(state[n], ids[2]) for n in range(4)],
        [jnp.where(near[3], lane_take(state[3 + 4 * n], ids[3]), 0.0) for n in range(4)],
    ]


def plan_kernel(
    air_hbm, eastern_hbm, northern_hbm, breadth_hbm, pn_hbm, holder_hbm, across_hbm, down_hbm,
    nb_hbm, span_hbm, flow_hbm, sst_hbm, flux, slots, breadth, pn, marks, idx, w, u, v, sst,
    air, eastern, northern, holder, across, down, nb, span, flow, lists, sems, *, devices, tiles
):
    copies = load(
        (
            (air_hbm.at[:, pl.ds(0, 8), :], air),
            (eastern_hbm.at[:, pl.ds(0, 16), :], eastern),
            (northern_hbm.at[:, pl.ds(0, 16), :], northern),
            (breadth_hbm, breadth),
            (pn_hbm, pn),
            (holder_hbm, holder),
            (across_hbm, across),
            (down_hbm, down),
            (nb_hbm, nb),
            (span_hbm, span),
            (flow_hbm, flow),
            (sst_hbm, sst),
        ),
        sems,
    )
    for copy in copies:
        copy.wait()
    rank = rank_among_equals(holder[...], CAP - 1)
    place = across[...] * 2 + rank_among_equals(across[...], 1)
    blocks = place.shape[1]
    line = lax.broadcasted_iota(jnp.int32, (blocks, blocks), 0).astype(jnp.float32)
    lane = lax.broadcasted_iota(jnp.int32, (blocks, blocks), 1).astype(jnp.float32)
    here = as_column(place.astype(jnp.float32)) == lane
    reader = jnp.sum(jnp.where(here, line, 0.0), axis=0, keepdims=True).astype(jnp.int32)
    lists[...] = jnp.zeros_like(lists)
    for mark, row in (
        (MARK_COLUMN, across[...]),
        (MARK_OWN, holder[...] * 8 + 2 * rank),
        (MARK_HEAT, holder[...] * 8 + 4 + rank),
        (MARK_ANSWER, holder[...] * CAP + rank),
        (MARK_PLACE, place),
        (MARK_READER, reader),
    ):
        lists[mark : mark + 1] = row
    copy = pltpu.make_async_copy(lists, marks, sems.at[0])
    copy.start()
    slots[...] = slot_rows(holder[...], rank, down[...], devices, tiles)
    fill_tables(nb, span, flow, idx, w, u, v)
    lines, count = air.shape[1], air.shape[2]
    ids, near = side_ids(pn)
    ids = [wide(line, lines) for line in ids]
    state = [air[p] for p in range(16)]
    u = [eastern[p].astype(jnp.float32)[0:lines] for p in range(16)]
    v = [northern[p].astype(jnp.float32)[0:lines] for p in range(16)]
    result = element_step(
        state, lambda p: u[p], lambda p: v[p], STEP_SIZE * breadth[...],
        home_facing(state, ids, near)
    )
    for p in range(16):
        speed = jnp.sqrt(u[p] * u[p] + v[p] * v[p] + 1.0)
        flux[p, 0:1] = (speed * result[p])[0:1]
        flux[p, 1:2] = (speed * u[p])[0:1]
        flux[p, 2:3] = (speed * v[p])[0:1]
        flux[p, 3:4] = speed[0:1]
        flux[p, 4:8] = jnp.zeros((4, count), jnp.float32)
    copy.wait()


def local_step_kernel(
    air_hbm, eastern_hbm, northern_hbm, breadth, pn, odd, loc, eastern, northern, east, west,
    far, near_swap, places, air, sems
):
    copies = load(((air_hbm, air), (eastern_hbm, eastern), (northern_hbm, northern)), sems)
    count = breadth.shape[1]
    lines = 16
    ids, near = side_ids(pn)
    chosen_east, place_east = edge_tables(ids[1], jnp.logical_not(near[1]))
    chosen_west, place_west = edge_tables(ids[3], jnp.logical_not(near[3]))
    places[...] = jnp.zeros_like(places)
    places[0:1] = place_east
    places[1:2] = place_west
    chosen_east, chosen_west = wide(chosen_east, lines), wide(chosen_west, lines)
    group = lax.broadcasted_iota(jnp.int32, (lines, count), 1) // (count // 4)
    scale = STEP_SIZE * breadth[...]
    ids = [wide(line, lines) for line in ids]

    def packed(values, chosen):
        result = jnp.zeros((lines, count), jnp.float32)
        for n in range(4):
            result = jnp.where(group == n, lane_take(values[n], chosen), result)
        return result

    for copy in copies:
        copy.wait()
    levels = air.shape[1]

    def chunk(c, carry):
        at = pl.multiple_of(c * lines, lines)
        rows = pl.ds(at, lines)
        state = [air[p, rows] for p in range(16)]
        result = element_step(
            state,
            lambda p: eastern[p, rows].astype(jnp.float32),
            lambda p: northern[p, rows].astype(jnp.float32),
            scale,
            home_facing(state, ids, near),
        )
        for p in range(16):
            loc[p, rows] = result[p]
        here = pl.ds(pl.multiple_of(4 * HALO + at, 8), lines)
        beyond = pl.ds(pl.multiple_of(4 * HALO + levels + at, 8), lines)
        for n in range(4):
            east[n, rows] = state[3 + 4 * n].astype(jnp.bfloat16)
            west[n, rows] = state[4 * n].astype(jnp.bfloat16)
        flag = jnp.broadcast_to(odd[0:1], (lines, count)) > 0
        for target, values in ((here, state), (beyond, result)):
            to_next = packed([values[3 + 4 * n] for n in range(4)], chosen_east)
            to_prev = packed([values[4 * n] for n in range(4)], chosen_west)
            far[target] = jnp.where(flag, to_next, to_prev)
            near_swap[target] = jnp.where(flag, to_prev, to_next)
        return carry

    lax.fori_loop(0, levels // lines, chunk, 0)


def second_step_kernel(
    loc, eastern, northern, breadth, pn, east, west, far, near_swap, places, first_far,
    first_near, odd, surface, out_hbm, out, sems
):
    ids, near = side_ids(pn)
    levels, count = loc.shape[1], loc.shape[2]
    lines = 16
    pack = count // 4
    scale = STEP_SIZE * breadth[...]
    jump = JUMP_WEIGHT * scale
    ids = [wide(line, lines) for line in ids]
    got = Received(far, near_swap, odd)
    first = Received(first_far, first_near, odd)
    row = slice(ROW_BREADTH, ROW_BREADTH + 1)
    factors = [
        JUMP_WEIGHT * STEP_SIZE * lane_take(wide(line, lines), ids[side])
        for side, line in ((1, first.next(row)), (3, first.prev(row)))
    ]
    spots = [
        [wide(places[n : n + 1] + m * pack, lines) for m in range(4)] for n in (0, 1)
    ]

    def copy_out(c):
        rows = pl.ds(pl.multiple_of(c * lines, lines), lines)
        return pltpu.make_async_copy(out.at[:, rows, :], out_hbm.at[:, rows, :], sems.at[c])

    def chunk(c, carry):
        at = pl.multiple_of(c * lines, lines)
        rows = pl.ds(at, lines)
        now = pl.ds(pl.multiple_of(4 * HALO + at, 8), lines)
        later = pl.ds(pl.multiple_of(4 * HALO + levels + at, 8), lines)
        state = [loc[p, rows] for p in range(16)]

        def across(own, there_now, there_next, side, factor, spot):
            values, beyond = [], []
            for n in range(4):
                values.append(jnp.where(near[side], 0.0, lane_take(there_now, spot[n])))
                beyond.append(
                    lane_take(there_next, spot[n]) + factor * own[n, rows].astype(jnp.float32)
                )
            return values, beyond

        east_now, east_beyond = across(
            east, got.next(now), got.next(later), 1, factors[0], spots[0]
        )
        west_now, west_beyond = across(
            west, got.prev(now), got.prev(later), 3, factors[1], spots[1]
        )
        for n in range(4):
            state[3 + 4 * n] = state[3 + 4 * n] + jump * east_now[n]
            state[4 * n] = state[4 * n] + jump * west_now[n]
        facing = home_facing(state, ids, near)
        facing[1] = [jnp.where(near[1], facing[1][n], east_beyond[n]) for n in range(4)]
        facing[3] = [jnp.where(near[3], facing[3][n], west_beyond[n]) for n in range(4)]
        result = element_step(
            state,
            lambda p: eastern[p, rows].astype(jnp.float32),
            lambda p: northern[p, rows].astype(jnp.float32),
            scale,
            facing,
        )
        for p in range(16):
            out[p, rows] = result[p]

        @pl.when(c == 0)
        def _():
            for p in range(16):
                lowest = out[p, 0:1]
                out[p, 0:1] = lowest + NUDGING_SPEED * (surface[p : p + 1] - lowest)

        copy_out(c).start()
        return carry

    lax.fori_loop(0, levels // lines, chunk, 0)

    def finish(c, carry):
        copy_out(c).wait()
        return carry

    lax.fori_loop(0, levels // lines, finish, 0)


def home_sums_kernel(marks, flux, weights, own):
    own[...] = jnp.zeros_like(own)
    for b in range(weights.shape[0]):
        sums = jnp.dot(
            flux[marks[MARK_COLUMN, b]].astype(jnp.bfloat16), weights[b], preferred_element_type=jnp.float32
        )
        row = marks[MARK_OWN, b]
        own[pl.ds(row, 1), :] = sums[1:2]
        own[pl.ds(row + 1, 1), :] = sums[2:3]
        own[pl.ds(marks[MARK_HEAT, b], 1), :] = sums[0:1]


def forward_kernel(
    marks, home, flux, slots, breadth, pn, first_far, first_near, odd, weights, out_hbm, out, extra,
    sems, *, devices
):
    ids, near = side_ids(pn)
    jump = (JUMP_WEIGHT * STEP_SIZE) * breadth[...]
    first = Received(first_far, first_near, odd)
    from_east = lane_take(first.next(slice(0, 8)), wide(ids[1], 8))
    from_west = lane_take(first.prev(slice(0, 8)), wide(ids[3], 8))
    from_east = jnp.where(near[1], 0.0, jump * from_east)
    from_west = jnp.where(near[3], 0.0, jump * from_west)
    extra[...] = jnp.zeros_like(extra)
    for n in range(4):
        for p, change in ((3 + 4 * n, from_east), (4 * n, from_west)):
            line = wide(flux[p, 3:4] * change[n : n + 1], 8).astype(jnp.bfloat16)
            for reader in range(2):
                b = marks[MARK_READER, 2 * p + reader]
                sums = jnp.dot(line, weights[b], preferred_element_type=jnp.float32)
                extra[pl.ds(marks[MARK_HEAT, b], 1), :] = sums[0:1]
    line = lax.broadcasted_iota(jnp.int32, (8, LANES), 0)
    part, copies = devices // 4, []
    for d in range(devices):
        mine, prev, following = (
            home[8 * (n % devices) : 8 * (n % devices) + 8] for n in (d, d - 1, d + 1)
        )
        top = jnp.concatenate([mine[0:4], prev[0:4]], axis=0)
        bottom = jnp.where(line < 4, following, mine + extra[8 * d : 8 * d + 8])
        bottom = jnp.where(line == ROW_IDS - 8, wide(slots[d : d + 1], 8), bottom)
        out[d] = jnp.concatenate([top, bottom], axis=0).astype(jnp.bfloat16)
        if (d + 1) % part == 0:
            copies.append(
                pltpu.make_async_copy(
                    out.at[pl.ds(d + 1 - part, part)],
                    out_hbm.at[pl.ds(d + 1 - part, part)],
                    sems.at[d // part],
                )
            )
            copies[-1].start()
    for copy in copies:
        copy.wait()


def back_kernel(marks, arrived, weights, surface, lines, share):
    lines[...] = arrived[...].reshape(lines.shape)
    for b in range(weights.shape[0]):
        line = lines[pl.ds(marks[MARK_ANSWER, b], 1), :]
        share[marks[MARK_PLACE, b]] = lax.dot_general(
            wide(line, 8).astype(jnp.bfloat16),
            weights[b],
            (((1,), (1,)), ((), ())),
            preferred_element_type=jnp.float32,
        )
    for p in range(surface.shape[0]):
        surface[p : p + 1] = share[2 * p, 0:1] + share[2 * p + 1, 0:1]


def split_index(idx):
    return lax.shift_right_arithmetic(idx, 7), idx & (LANES - 1)


def by_tiles(function, idx):
    if idx.shape[0] <= 8:
        return function(idx)
    return jnp.concatenate(
        [function(idx[at : at + 8]) for at in range(0, idx.shape[0], 8)], axis=0
    )


def pick(idx, sources):
    def one(idx):
        high, low = split_index(idx)
        result = jnp.zeros(idx.shape, jnp.float32)
        for number, line in sources:
            result = jnp.where(high == number, lane_take(wide(line, idx.shape[0]), low), result)
        return result

    return by_tiles(one, idx)


def fill_pack(values, packed, scales):
    half = values.shape[0] // 2
    numbers = []
    for n, part in enumerate((values[:half], values[half:])):
        largest = jnp.maximum(jnp.max(jnp.abs(part), axis=(0, 1), keepdims=True), 1e-30)
        numbers.append(jnp.floor(part * (32767.0 / largest) + 0.5).astype(jnp.int32))
        scales[n : n + 1] = jnp.broadcast_to(largest * (1.0 / 32767.0), (1, LANES))
    packed[...] = (numbers[1] << 16) | (numbers[0] & 0xFFFF)


def pick_own(idx, packed, scales):
    half = packed.shape[0]

    def one(idx):
        lines = idx.shape[0]
        high, low = split_index(idx)
        own = high - HALO
        upper = own >= half
        row = jnp.where(upper, own - half, own)
        words = jnp.zeros(idx.shape, jnp.int32)
        for r in range(half):
            words = jnp.where(row == r, lane_take(wide(packed[r : r + 1], lines), low), words)
        number = jnp.where(upper, words >> 16, (words << 16) >> 16)
        scale = jnp.where(upper, wide(scales[1:2], lines), wide(scales[0:1], lines))
        return number.astype(jnp.float32) * scale

    return by_tiles(one, idx)


def combine(terms, factors):
    total = None
    for term, factor in zip(terms, factors):
        if factor != 0.0:
            total = factor * term if total is None else total + factor * term
    return total


def pair_sums(table):
    terms = [table[HALO * k : HALO * (k + 1)] for k in range(6)]
    return combine(terms, COS), combine(terms, SIN)


def rim_partial(rim_idx, rim_w, eta, packed, scales, first):
    rows = rim_idx.shape[0]
    found = pick_own(rim_idx, packed, scales)
    centre = eta[first : first + HALO]
    centre = jnp.concatenate([centre] * (rows // HALO), axis=0)
    return pair_sums(rim_w * (found - centre))


def prepare_kernel(
    air_hbm, breadth_hbm, pn_hbm, eta_hbm, sst_hbm, flow_hbm, nb_hbm, span_hbm,
    rim_idx, rim_w, eta, eta_pack, eta_scale, far, near, odd,
    up, dn, air, breadth, pn, sst, flow, nb, span, sems
):
    tiles, cells = eta.shape[0], nb_hbm.shape[1]
    pairs = [(eta_hbm, eta)]
    for side, at in ((0, 0), (1, cells - OY)):
        cut = pl.ds(at, OY)
        pairs.append((nb_hbm.at[:, cut], nb.at[side]))
        pairs.append((span_hbm.at[:, cut], span.at[side]))
        pairs.append((flow_hbm.at[:, cut], flow.at[side]))
    for side, at in ((0, 0), (1, tiles - 8)):
        pairs.append((sst_hbm.at[pl.ds(at, 8)], sst.at[side]))
    pairs.append((breadth_hbm, breadth))
    pairs.append((pn_hbm, pn))
    pairs.append((air_hbm.at[:, pl.ds(0, 8), :], air))
    copies = load(pairs, sems)
    for copy in copies:
        copy.wait()
    shard = lax.shift_right_logical(pn[0:1], pn.shape[1].bit_length() - 1)
    odd[...] = wide(shard & 1, 8)
    fill_pack(eta[...], eta_pack, eta_scale)
    for side, first in ((0, 0), (1, tiles - HALO)):
        rim_idx[side, 12:16] = jnp.full((4, LANES), -1, jnp.int32)
        rim_w[side, 12:16] = jnp.zeros((4, LANES), jnp.float32)
        for j in range(HALO):
            cut = slice(j * LANES, (j + 1) * LANES)
            links = nb[side, :, cut]
            factors = slot_factors(links, span[side, :, cut])
            for k in range(6):
                at = HALO * k + j
                rim_idx[side, at : at + 1] = links[k : k + 1]
                rim_w[side, at : at + 1] = factors[k : k + 1]
    for side, first, target in ((0, 0, dn), (1, tiles - HALO, up)):
        target[...] = jnp.zeros_like(target)
        for n in range(4):
            p = 4 * n if side == 0 else 3 + 4 * n
            target[ROW_EDGE + n : ROW_EDGE + n + 1] = air[p, 0:1]
        target[ROW_BREADTH : ROW_BREADTH + 1] = breadth[...]
        part_x, part_y = rim_partial(
            rim_idx[side], rim_w[side], eta, eta_pack, eta_scale, first
        )
        cut = slice(first, first + HALO)
        target[ROW_ETA : ROW_ETA + HALO] = eta[cut]
        for j in range(HALO):
            here = slice(j * LANES, (j + 1) * LANES)
            target[ROW_U + j : ROW_U + j + 1] = flow[side, 0:1, here]
            target[ROW_V + j : ROW_V + j + 1] = flow[side, 1:2, here]
        start = first % 8
        target[ROW_SST : ROW_SST + HALO] = sst[side, start : start + HALO]
        target[ROW_PX : ROW_PX + HALO] = part_x
        target[ROW_PY : ROW_PY + HALO] = part_y
        target[ROW_IDX : ROW_IDX + 16] = rim_idx[side].astype(jnp.float32)
        target[ROW_W : ROW_W + 16] = rim_w[side]
    arrange(up, dn, odd, far, near)


def slot_factors(links, span):
    return jnp.where(links >= 0, span * (1.0 / 3.0), 0.0)


def fill_tables(nb, span, flow, idx, w, u, v):
    tiles = u.shape[0]
    for r in range(tiles):
        cut = slice(r * LANES, (r + 1) * LANES)
        links = nb[:, cut]
        factors = slot_factors(links, span[:, cut])
        for k in range(6):
            idx[k * tiles + r : k * tiles + r + 1] = links[k : k + 1]
            w[k * tiles + r : k * tiles + r + 1] = factors[k : k + 1]
        u[r : r + 1] = flow[0:1, cut]
        v[r : r + 1] = flow[1:2, cut]


def own_gradient(idx, w, eta, packed, scales, gx, gy):
    tiles = eta.shape[0]

    def chunk(at):
        centre = eta[pl.ds(at, 8)]
        terms = []
        for k in range(6):
            found = pick_own(idx[pl.ds(k * tiles + at, 8)], packed, scales)
            terms.append(w[pl.ds(k * tiles + at, 8)] * (found - centre))
        gx[pl.ds(at, 8)] = combine(terms, COS)
        gy[pl.ds(at, 8)] = combine(terms, SIN)

    for c in range(tiles // 8):
        chunk(c * 8)


def own_spread(at, idx, w, flow, packed, scales):
    tiles = flow.shape[1]
    total = jnp.zeros((8, LANES), jnp.float32)
    for kk in range(3):
        centre = flow[kk, pl.ds(at, 8)]
        for k, sign in ((kk, 1.0), (kk + 3, -1.0)):
            rows = pl.ds(k * tiles + at, 8)
            found = pick_own(idx[rows], packed.at[kk], scales.at[kk])
            total = total + sign * w[rows] * (found - centre)
    return total


def inner_kernel(
    idx, w, eta, eta_pack, eta_scale, u, v, fu, fv, eta_part, u_part, v_part,
    flow, flow_pack, flow_scale
):
    current_kernel(idx, w, eta, eta_pack, eta_scale, u, v, fu, fv, u_part, v_part)
    height_kernel(idx, w, eta, u_part, v_part, eta_part, flow, flow_pack, flow_scale)


def current_kernel(idx, w, eta, eta_pack, eta_scale, u, v, fu, fv, u_part, v_part):
    own_gradient(idx, w, eta, eta_pack, eta_scale, u_part, v_part)
    u_part[...] = DAMPING * u[...] - GRAVITY * u_part[...] + WIND_GAIN * fu[...]
    v_part[...] = DAMPING * v[...] - GRAVITY * v_part[...] + WIND_GAIN * fv[...]


def height_kernel(idx, w, eta, u_part, v_part, eta_part, flow, flow_pack, flow_scale):
    tiles = eta.shape[0]
    fill_flow(flow, u_part[...], v_part[...])
    for kk in range(3):
        fill_pack(flow[kk], flow_pack.at[kk], flow_scale.at[kk])

    def chunk(at):
        total = own_spread(at, idx, w, flow, flow_pack, flow_scale)
        eta_part[pl.ds(at, 8)] = eta[pl.ds(at, 8)] - DEPTH_RATE * total

    for c in range(tiles // 8):
        chunk(c * 8)


def first_gradient_kernel(
    idx, w, eta, eta_pack, eta_scale, sst, first_far, first_near, odd, rim_idx, rim_w,
    gx, gy, base, sst_pack, sst_scale
):
    own_gradient(idx, w, eta, eta_pack, eta_scale, gx, gy)
    tiles = eta.shape[0]
    fill_pack(sst[...], sst_pack, sst_scale)

    def chunk(at):
        centre = sst[pl.ds(at, 8)]
        total = jnp.zeros_like(centre)
        for k in range(6):
            found = pick_own(idx[pl.ds(k * tiles + at, 8)], sst_pack, sst_scale)
            total = total + w[pl.ds(k * tiles + at, 8)] * (found - centre)
        base[pl.ds(at, 8)] = centre + (0.5 * SPREADING_COEFF) * total

    for c in range(tiles // 8):
        chunk(c * 8)
    first = Received(first_far, first_near, odd)
    for side, start, offset in ((0, 0, 0), (1, tiles - HALO, tiles + HALO)):
        rim = first.rim(side, ROW_SST)
        sources = [(offset + q, rim[q : q + 1]) for q in range(HALO)]
        found = rim_w[side] * pick(rim_idx[side], sources)
        total = combine([found[HALO * k : HALO * (k + 1)] for k in range(6)], [1.0] * 6)
        rows = slice(start, start + HALO)
        base[rows] = base[rows] + (0.5 * SPREADING_COEFF) * total


def fill_flow(flow, u, v):
    flow[0] = u
    for kk in (1, 2):
        flow[kk] = COS[kk] * u + SIN[kk] * v


def side_currents(eta, sides, fside, before, after, side_idx, side_w):
    tiles = eta.shape[0]
    slopes = []
    for side, offset, first, part in (
        (0, tiles + HALO, 0, before),
        (1, 0, tiles - HALO, after),
    ):
        sources = [(offset + q, eta[first + q : first + q + 1]) for q in range(HALO)]
        add_x, add_y = pair_sums(side_w[side] * pick(side_idx[side], sources))
        slopes.append((part[1] + add_x, part[2] + add_y))
    slope = jnp.concatenate([slopes[0][0], slopes[1][0], slopes[0][1], slopes[1][1]], axis=0)
    return DAMPING * sides[...] - GRAVITY * slope + WIND_GAIN * fside[...]


def rim_slopes(rim_idx, rim_w, before, after, tiles):
    result = []
    for side, offset, part in ((0, 0, before), (1, tiles + HALO, after)):
        sources = [(offset + q, part[0][q : q + 1]) for q in range(HALO)]
        result.append(pair_sums(rim_w[side] * pick(rim_idx[side], sources)))
    return result


def send_rims(eta, eta_pack, eta_scale, rim_idx, rim_w, odd, far, near, up, dn):
    tiles = eta.shape[0]
    fill_pack(eta[...], eta_pack, eta_scale)
    for side, first, target in ((0, 0, dn), (1, tiles - HALO, up)):
        part_x, part_y = rim_partial(
            rim_idx[side], rim_w[side], eta, eta_pack, eta_scale, first
        )
        target[0:HALO] = eta[first : first + HALO]
        target[HALO : 2 * HALO] = part_x
        target[2 * HALO : 3 * HALO] = part_y
        target[3 * HALO : 4 * HALO] = jnp.zeros((HALO, LANES), jnp.float32)
    rows = pl.ds(0, 4 * HALO)
    arrange(up, dn, odd, far.at[rows], near.at[rows])


def first_subcycle(
    gx, gy, eta, u, v, sides, fu, fv, fside, before, after, idx, w, side_idx, side_w,
    rim_idx, rim_w, flow, flow_pack, flow_scale, flow_outer, eta_new, u_new, v_new, sides_new,
    midway
):
    tiles = eta.shape[0]
    u_new[...] = DAMPING * u[...] - GRAVITY * gx[...] + WIND_GAIN * fu[...]
    v_new[...] = DAMPING * v[...] - GRAVITY * gy[...] + WIND_GAIN * fv[...]
    slopes = rim_slopes(rim_idx, rim_w, before, after, tiles)
    for first, (add_x, add_y) in zip((0, tiles - HALO), slopes):
        rows = slice(first, first + HALO)
        u_new[rows] = u_new[rows] - GRAVITY * add_x
        v_new[rows] = v_new[rows] - GRAVITY * add_y
    sides_next = side_currents(eta, sides, fside, before, after, side_idx, side_w)
    sides_new[...] = sides_next
    fill_flow(flow, u_new[...], v_new[...])
    fill_flow(flow_outer, sides_next[0 : 2 * HALO], sides_next[2 * HALO : 4 * HALO])
    for kk in range(3):
        fill_pack(flow[kk], flow_pack.at[kk], flow_scale.at[kk])

    def chunk(at):
        total = own_spread(at, idx, w, flow, flow_pack, flow_scale)
        eta_new[pl.ds(at, 8)] = eta[pl.ds(at, 8)] - DEPTH_RATE * total

    for c in range(tiles // 8):
        if c == tiles // 16:
            midway()
        chunk(c * 8)
    for side, first, offset in ((0, 0, 0), (1, tiles - HALO, tiles + HALO)):
        total = jnp.zeros((HALO, LANES), jnp.float32)
        for kk in range(3):
            at = side * HALO
            sources = [(offset + q, flow_outer[kk, at + q : at + q + 1]) for q in range(HALO)]
            found = rim_w[side] * pick(rim_idx[side], sources)
            total = (
                total
                + found[HALO * kk : HALO * (kk + 1)]
                - found[HALO * (kk + 3) : HALO * (kk + 4)]
            )
        rows = slice(first, first + HALO)
        eta_new[rows] = eta_new[rows] - DEPTH_RATE * total


def outer_subcycle(
    eta, eta_part, u_part, v_part, sides, fside, before, after, idx, w, side_idx, side_w,
    rim_idx, rim_w, flow_outer, eta_new, u_new, v_new
):
    tiles = eta.shape[0]
    slopes = rim_slopes(rim_idx, rim_w, before, after, tiles)
    sides_next = side_currents(eta, sides, fside, before, after, side_idx, side_w)
    u_new[...] = u_part[...]
    v_new[...] = v_part[...]
    changes_u = [-GRAVITY * slopes[side][0] for side in (0, 1)]
    changes_v = [-GRAVITY * slopes[side][1] for side in (0, 1)]
    for side, first in ((0, 0), (1, tiles - HALO)):
        rows = slice(first, first + HALO)
        u_new[rows] = u_new[rows] + changes_u[side]
        v_new[rows] = v_new[rows] + changes_v[side]
    fill_flow(
        flow_outer,
        jnp.concatenate([sides_next[0 : 2 * HALO]] + changes_u, axis=0),
        jnp.concatenate([sides_next[2 * HALO : 4 * HALO]] + changes_v, axis=0),
    )
    for c in range(tiles // 8):
        at = c * 8
        total = jnp.zeros((8, LANES), jnp.float32)
        for kk in range(3):
            line = lambda n: flow_outer[kk, n : n + 1]
            sources = [(HALO + q, line(2 * HALO + q)) for q in range(HALO)]
            sources += [(tiles + q, line(3 * HALO + q)) for q in range(HALO)]
            if at == 0:
                sources += [(q, line(q)) for q in range(HALO)]
            if at + 8 == tiles:
                sources += [(tiles + HALO + q, line(HALO + q)) for q in range(HALO)]
            total = (
                total
                + w[kk * tiles + at : kk * tiles + at + 8]
                * pick(idx[kk * tiles + at : kk * tiles + at + 8], sources)
                - w[(kk + 3) * tiles + at : (kk + 3) * tiles + at + 8]
                * pick(idx[(kk + 3) * tiles + at : (kk + 3) * tiles + at + 8], sources)
            )
        eta_new[at : at + 8] = eta_part[at : at + 8] - DEPTH_RATE * total
    for side, first in ((0, 0), (1, tiles - HALO)):
        centre = jnp.zeros((HALO, LANES), jnp.float32)
        for kk in range(3):
            factor = (
                rim_w[side, HALO * kk : HALO * (kk + 1)]
                - rim_w[side, HALO * (kk + 3) : HALO * (kk + 4)]
            )
            start = (2 + side) * HALO
            centre = centre + factor * flow_outer[kk, start : start + HALO]
        rows = slice(first, first + HALO)
        eta_new[rows] = eta_new[rows] + DEPTH_RATE * centre
    return sides_next


def first_ocean_kernel(
    arrived, first_far, first_near, odd, gx, gy, eta, u, v, idx, w, rim_idx, rim_w,
    far_old, near_old, base, eta_new, eta_pack, eta_scale, u_new, v_new, sides_new, far, near,
    fu, fv, fside, side_idx, side_w, heat, answers_hbm,
    flow, flow_pack, flow_scale, flow_outer, sides, up, dn, parts, answers, sems
):
    tiles = eta.shape[0]
    devices = arrived.shape[0]
    parts[...] = arrived[...].astype(jnp.float32).reshape(parts.shape)

    def rows_of(r):
        return parts[pl.ds(r, devices, stride=PER_DEST), :]

    ids = rows_of(ROW_IDS)
    number = lax.broadcasted_iota(jnp.int32, (devices, LANES), 1).astype(jnp.float32)
    nothing = jnp.zeros((devices, LANES), jnp.float32)
    chosen, lines = [], []
    for j in range(3 * CAP):
        chosen.append(jnp.where(ids[:, j : j + 1] == number, 1.0, 0.0).astype(jnp.bfloat16))
        first = rows_of(ROW_HEAT + j) if j < CAP else nothing
        lines.append(jnp.concatenate([first, rows_of(2 * j), rows_of(2 * j + 1)], axis=1))
    forcing = lax.dot_general(
        jnp.concatenate(chosen, axis=0),
        jnp.concatenate(lines, axis=0).astype(jnp.bfloat16),
        (((0,), (0,)), ((), ())),
        preferred_element_type=jnp.float32,
    )
    heat[...] = forcing[0:tiles, 0:LANES]
    half = (base[...] + WARMING_COEFF * forcing[0:tiles, 0:LANES]).astype(jnp.bfloat16)
    for j in range(CAP):
        answers[:, j, :] = jnp.dot(
            chosen[j][:, 0:tiles], half, preferred_element_type=jnp.float32
        )
    fu[...] = forcing[0:tiles, LANES : 2 * LANES]
    fv[...] = forcing[0:tiles, 2 * LANES : 3 * LANES]
    fside[0 : 2 * HALO] = forcing[tiles : tiles + 2 * HALO, LANES : 2 * LANES]
    fside[2 * HALO : 4 * HALO] = forcing[tiles : tiles + 2 * HALO, 2 * LANES : 3 * LANES]
    copy = pltpu.make_async_copy(answers, answers_hbm, sems.at[0])
    first = Received(first_far, first_near, odd)
    for side, part in ((0, first.prev), (1, first.next)):
        side_idx[side] = part(slice(ROW_IDX, ROW_IDX + 16)).astype(jnp.int32)
        side_w[side] = part(slice(ROW_W, ROW_W + 16))
        for n, row in ((0, ROW_U), (1, ROW_V)):
            at = HALO * (2 * n + side)
            sides[at : at + HALO] = first.rim(side, row)
    rows = (ROW_ETA, ROW_PX, ROW_PY)
    first_subcycle(
        gx, gy, eta, u, v, sides, fu, fv, fside, first.rims(0, rows), first.rims(1, rows), idx, w, side_idx, side_w, rim_idx, rim_w, flow, flow_pack, flow_scale, flow_outer,
        eta_new, u_new, v_new, sides_new, copy.start
    )
    send_rims(eta_new, eta_pack, eta_scale, rim_idx, rim_w, odd, far, near, up, dn)
    copy.wait()


def ocean_kernel(
    far, near, odd, eta, eta_part, u_part, v_part, sides, fside, idx, w, side_idx, side_w,
    rim_idx, rim_w, eta_new, eta_pack, eta_scale, u_new, v_new, sides_new, far_new, near_new,
    flow_outer, up, dn
):
    rows = (0, HALO, 2 * HALO)
    got = Received(far, near, odd)
    sides_new[...] = outer_subcycle(
        eta, eta_part, u_part, v_part, sides, fside, got.rims(0, rows), got.rims(1, rows), idx, w, side_idx, side_w, rim_idx, rim_w, flow_outer,
        eta_new, u_new, v_new
    )
    send_rims(
        eta_new, eta_pack, eta_scale, rim_idx, rim_w, odd, far_new, near_new, up, dn
    )


def last_ocean_kernel(
    far, near, odd, eta, eta_part, u_part, v_part, sides, fside, idx, w, side_idx, side_w,
    rim_idx, rim_w, base, heat, eta_new, velocity, warm, u_new, v_new, flow_outer
):
    warm[...] = base[...] + WARMING_COEFF * heat[...]
    rows = (0, HALO, 2 * HALO)
    got = Received(far, near, odd)
    outer_subcycle(
        eta, eta_part, u_part, v_part, sides, fside, got.rims(0, rows), got.rims(1, rows), idx, w, side_idx, side_w, rim_idx, rim_w, flow_outer,
        eta_new, u_new, v_new
    )
    for r in range(eta.shape[0]):
        cut = slice(r * LANES, (r + 1) * LANES)
        velocity[0:1, cut] = u_new[r : r + 1]
        velocity[1:2, cut] = v_new[r : r + 1]


def shards(
    air_warmth,
    eastern_breeze,
    northern_breeze,
    reciprocal_breadth,
    panel_neighbours,
    transfer_coefficients,
    transfer_across_tile,
    transfer_holder,
    transfer_down_tile,
    water_elevation,
    depth_mean_current,
    marine_skin_warmth,
    patch_neighbours,
    interface_span,
):
    devices = lax.axis_size(RING)
    points, levels, elements = air_warmth.shape
    cells = water_elevation.shape[0]
    tiles = cells // LANES
    blocks = transfer_holder.shape[0]
    cell_rows = shape_of(tiles, LANES)
    rim_rows = shape_of(4 * HALO, LANES)
    dma = pltpu.SemaphoreType.DMA
    air, eastern, northern, breadth_hbm, pn_hbm = in_hbm(
        air_warmth, eastern_breeze, northern_breeze, reciprocal_breadth.reshape(1, elements),
        panel_neighbours
    )

    pack_rows = shape_of(tiles // 2, LANES, dtype=jnp.int32)
    scale_rows = shape_of(8, LANES)
    cell_tables = in_hbm(
        marine_skin_warmth.reshape(tiles, LANES),
        depth_mean_current,
        patch_neighbours,
        interface_span,
    )
    rim_idx, rim_w, eta, eta_pack, eta_scale, far, near, odd = pl.pallas_call(
        prepare_kernel,
        in_specs=hbm(8),
        out_specs=vmem(8),
        out_shape=(
            shape_of(2, 16, LANES, dtype=jnp.int32),
            shape_of(2, 16, LANES),
            cell_rows,
            pack_rows,
            scale_rows,
            shape_of(ROWS_FIRST, LANES),
            shape_of(ROWS_FIRST, LANES),
            shape_of(8, elements, dtype=jnp.int32),
        ),
        scratch_shapes=[
            pltpu.VMEM((ROWS_FIRST, LANES), jnp.float32),
            pltpu.VMEM((ROWS_FIRST, LANES), jnp.float32),
            pltpu.VMEM((points, 8, elements), jnp.float32),
            pltpu.VMEM((1, elements), jnp.float32),
            pltpu.VMEM((4, elements), jnp.int32),
            pltpu.VMEM((2, 8, LANES), jnp.float32),
            pltpu.VMEM((2, 2, OY), jnp.float32),
            pltpu.VMEM((2, 6, OY), jnp.int32),
            pltpu.VMEM((2, 6, OY), jnp.float32),
            dma((12,)),
        ],
        compiler_params=PARAMS,
        name="prepare",
    )(
        air,
        breadth_hbm,
        pn_hbm,
        *in_hbm(water_elevation.reshape(tiles, LANES)),
        *cell_tables,
    )
    first_far, first_near = swap_both(far, near)

    low_wind = pltpu.VMEM((points, 16, elements), jnp.bfloat16)
    low_row = pltpu.VMEM((1, blocks), jnp.int32)
    flux, slots, breadth, pn, marks, idx, w, u, v, sst = pl.pallas_call(
        lambda *refs: plan_kernel(*refs, devices=devices, tiles=tiles),
        in_specs=hbm(12),
        out_specs=vmem(4) + smem(1) + vmem(5),
        out_shape=(
            shape_of(points, 8, elements), shape_of(devices, LANES), shape_of(1, elements),
            shape_of(4, elements, dtype=jnp.int32), pltpu.SMEM((8, blocks), jnp.int32),
            shape_of(6 * tiles, LANES, dtype=jnp.int32), shape_of(6 * tiles, LANES),
            cell_rows, cell_rows, cell_rows
        ),
        scratch_shapes=[
            pltpu.VMEM((points, 8, elements), jnp.float32), low_wind, low_wind,
            low_row, low_row, low_row, pltpu.VMEM((6, cells), jnp.int32),
            pltpu.VMEM((6, cells), jnp.float32), pltpu.VMEM((2, cells), jnp.float32),
            pltpu.VMEM((8, blocks), jnp.int32), dma((12,))
        ],
        compiler_params=PARAMS,
        name="plan",
    )(
        air,
        eastern,
        northern,
        breadth_hbm,
        pn_hbm,
        *in_hbm(
            transfer_holder.reshape(1, blocks),
            transfer_across_tile.reshape(1, blocks),
            transfer_down_tile.reshape(1, blocks),
        ),
        cell_tables[2],
        cell_tables[3],
        cell_tables[1],
        cell_tables[0],
    )

    home = pl.pallas_call(
        home_sums_kernel,
        in_specs=smem(1) + vmem(2),
        out_specs=pl.BlockSpec(memory_space=pltpu.VMEM),
        out_shape=shape_of(devices * 8, LANES),
        compiler_params=PARAMS,
        name="home_sums",
    )(marks, flux, transfer_coefficients)
    outgoing = pl.pallas_call(
        lambda *refs: forward_kernel(*refs, devices=devices),
        in_specs=smem(1) + vmem(9),
        out_specs=pl.BlockSpec(memory_space=pltpu.HBM),
        out_shape=pltpu.HBM((devices, PER_DEST, LANES), jnp.bfloat16),
        scratch_shapes=[
            pltpu.VMEM((devices, PER_DEST, LANES), jnp.bfloat16),
            pltpu.VMEM((devices * 8, LANES), jnp.float32),
            dma((4,)),
        ],
        compiler_params=PARAMS,
        name="forward_remap",
    )(
        marks, home, flux, slots, breadth, pn, first_far, first_near, odd, transfer_coefficients
    )
    outgoing, pn, gradient_eta = lax.optimization_barrier((outgoing, pn, eta))
    arrived = exchange(outgoing)
    gx, gy, base = pl.pallas_call(
        first_gradient_kernel,
        in_specs=vmem(11),
        out_specs=vmem(3),
        out_shape=(cell_rows,) * 3,
        scratch_shapes=[
            pltpu.VMEM((tiles // 2, LANES), jnp.int32), pltpu.VMEM((8, LANES), jnp.float32)
        ],
        compiler_params=PARAMS,
        name="first_gradient",
    )(
        idx, w, gradient_eta, eta_pack, eta_scale, sst, first_far, first_near, odd, rim_idx, rim_w
    )

    field = shape_of(points, levels, elements)
    edge = shape_of(4, levels, elements, dtype=jnp.bfloat16)
    swap_rows = shape_of(4 * HALO + 2 * levels, elements)
    wind = shape_of(points, levels, elements, dtype=jnp.bfloat16)
    loc, eastern, northern, east, west, far, near, edge_places = pl.pallas_call(
        local_step_kernel,
        in_specs=hbm(3) + vmem(3),
        out_specs=vmem(8),
        out_shape=(
            field, wind, wind, edge, edge, swap_rows, swap_rows,
            shape_of(8, elements, dtype=jnp.int32)
        ),
        scratch_shapes=[pltpu.VMEM((points, levels, elements), jnp.float32), dma((3,))],
        compiler_params=PARAMS,
        name="local_step",
    )(air, eastern, northern, breadth, pn, odd)

    rim_scratch = pltpu.VMEM((4 * HALO, LANES), jnp.float32)
    flow_scratch = [
        pltpu.VMEM((3, tiles, LANES), jnp.float32),
        pltpu.VMEM((3, tiles // 2, LANES), jnp.int32),
        pltpu.VMEM((3, 8, LANES), jnp.float32),
        pltpu.VMEM((3, 2 * HALO, LANES), jnp.float32),
    ]
    (
        eta, eta_pack, eta_scale, u, v, sides, far, near, fu, fv, fside, side_idx, side_w,
        heat, answers
    ) = pl.pallas_call(
        first_ocean_kernel,
        in_specs=vmem(16),
        out_specs=vmem(14) + hbm(1),
        out_shape=(
            cell_rows, pack_rows, scale_rows, cell_rows, cell_rows, rim_rows, swap_rows, swap_rows,
            cell_rows, cell_rows, rim_rows,
            shape_of(2, 16, LANES, dtype=jnp.int32), shape_of(2, 16, LANES),
            cell_rows, pltpu.HBM((devices, CAP, LANES), jnp.float32),
        ),
        scratch_shapes=flow_scratch + [rim_scratch] * 3 + [
            pltpu.VMEM((devices * PER_DEST, LANES), jnp.float32),
            pltpu.VMEM((devices, CAP, LANES), jnp.float32),
            dma((1,)),
        ],
        input_output_aliases={13: 6, 14: 7},
        compiler_params=PARAMS,
        name="first_ocean",
    )(
        arrived, first_far, first_near, odd, gx, gy, eta, u, v, idx, w, rim_idx, rim_w,
        far, near, base
    )
    far, near = swap_both(far, near)
    edges_far, edges_near = far, near

    for substep in range(1, NSUB):
        if substep == 1:
            u_part, v_part = pl.pallas_call(
                current_kernel,
                in_specs=vmem(9),
                out_specs=vmem(2),
                out_shape=(cell_rows,) * 2,
                compiler_params=PARAMS,
                name="current",
            )(idx, w, eta, eta_pack, eta_scale, u, v, fu, fv)
            answers, u_part = lax.optimization_barrier((answers, u_part))
            answered = exchange(answers)
            eta_part = pl.pallas_call(
                height_kernel,
                in_specs=vmem(5),
                out_specs=pl.BlockSpec(memory_space=pltpu.VMEM),
                out_shape=cell_rows,
                scratch_shapes=flow_scratch[:3],
                compiler_params=PARAMS,
                name="height",
            )(idx, w, eta, u_part, v_part)
        else:
            eta_part, u_part, v_part = pl.pallas_call(
                inner_kernel,
                in_specs=vmem(9),
                out_specs=vmem(3),
                out_shape=(cell_rows,) * 3,
                scratch_shapes=flow_scratch[:3],
                compiler_params=PARAMS,
                name="inner",
            )(idx, w, eta, eta_pack, eta_scale, u, v, fu, fv)
        if substep == 2:
            eta_part, answered = lax.optimization_barrier((eta_part, answered))
            surface = pl.pallas_call(
                back_kernel,
                in_specs=smem(1) + vmem(2),
                out_specs=pl.BlockSpec(memory_space=pltpu.VMEM),
                out_shape=shape_of(points, LANES),
                scratch_shapes=[
                    pltpu.VMEM((devices * CAP, LANES), jnp.float32),
                    pltpu.VMEM((blocks, 8, LANES), jnp.float32),
                ],
                compiler_params=PARAMS,
                name="back_remap",
            )(marks, answered, transfer_coefficients)
            eta_part, surface = lax.optimization_barrier((eta_part, surface))
        operands = (
            far, near, odd, eta, eta_part, u_part, v_part, sides, fside, idx, w, side_idx, side_w, rim_idx, rim_w
        )
        outer_scratch = [pltpu.VMEM((3, 4 * HALO, LANES), jnp.float32)]
        if substep + 1 < NSUB:
            eta, eta_pack, eta_scale, u, v, sides, far, near = pl.pallas_call(
                ocean_kernel,
                in_specs=vmem(15),
                out_specs=vmem(8),
                out_shape=(cell_rows, pack_rows, scale_rows) + (cell_rows,) * 2 + (rim_rows,) * 3,
                scratch_shapes=outer_scratch + [rim_scratch] * 2,
                compiler_params=PARAMS,
                name="ocean",
            )(*operands)
            far, near = swap_both(far, near)
        else:
            eta, velocity, warm = pl.pallas_call(
                last_ocean_kernel,
                in_specs=vmem(17),
                out_specs=vmem(3),
                out_shape=(cell_rows, shape_of(2, cells), cell_rows),
                scratch_shapes=[pltpu.VMEM((tiles, LANES), jnp.float32)] * 2 + outer_scratch,
                compiler_params=PARAMS,
                name="last_ocean",
            )(*operands, base, heat)

    closing = pl.pallas_call(
        second_step_kernel,
        in_specs=vmem(14),
        out_specs=pl.BlockSpec(memory_space=pltpu.HBM),
        out_shape=pltpu.HBM((points, levels, elements), jnp.float32),
        scratch_shapes=[
            pltpu.VMEM((points, levels, elements), jnp.float32), dma((levels // 16,))
        ],
        compiler_params=PARAMS,
        name="second_step",
    )(
        loc, eastern, northern, breadth, pn, east, west, edges_far, edges_near, edge_places,
        first_far, first_near, odd, surface
    )
    return closing, eta.reshape(cells), velocity, warm.reshape(cells)


def solution(mesh):
    split = P(RING)
    last = P(None, RING)
    field = P(None, None, RING)
    return jax.shard_map(
        shards,
        mesh=mesh,
        in_specs=(
            field,
            field,
            field,
            split,
            last,
            P(RING, None, None),
            split,
            P(RING, None),
            split,
            split,
            last,
            split,
            last,
            last,
        ),
        out_specs=(field, split, last, split),
        check_vma=False,
    )
```

```python
import math

import jax
import jax.numpy as jnp
import numpy as np
from jax import lax
from jax.experimental import pallas as pl
from jax.experimental.pallas import tpu as pltpu
from jax.sharding import PartitionSpec as P

OY = 256
NSUB = 4
CAP = 2

STEP_SIZE = 0.05
JUMP_WEIGHT = 4.0
NUDGING_SPEED = 0.5
DAMPING = 0.9
GRAVITY = 0.3
WIND_GAIN = 0.3
DEPTH_RATE = 0.3
WARMING_COEFF = 0.3
SPREADING_COEFF = 0.5

RING = ("comp", "dom")
LANES = 128
HALO = OY // LANES
COS = [math.cos(k * math.pi / 3.0) for k in range(6)]
SIN = [0.0 if k % 3 == 0 else math.sin(k * math.pi / 3.0) for k in range(6)]

ROW_EDGE, ROW_BREADTH, ROW_ETA, ROW_U, ROW_V, ROW_SST = 0, 4, 8, 10, 12, 14
ROW_PX, ROW_PY, ROW_IDX, ROW_W, ROWS_FIRST = 16, 18, 24, 40, 56
MARK_COLUMN, MARK_OWN, MARK_HEAT, MARK_ANSWER, MARK_PLACE, MARK_READER = range(6)
PER_DEST, ROW_HEAT, ROW_IDS = 16, 12, 14


def swapped(value, first):
    count = lax.axis_size(RING)
    pairs = []
    for i in range(first, count + first, 2):
        pairs += [(i % count, (i + 1) % count), ((i + 1) % count, i % count)]
    return lax.ppermute(value, RING, pairs)


def swap_both(far, near):
    got_far = swapped(far, 1)
    return got_far, swapped(near, 0)


class Received:
    def __init__(self, far, near, odd):
        self.far, self.near, self.odd = far, near, odd

    def flag(self, rows):
        return jnp.broadcast_to(self.odd[0:1], rows.shape) > 0

    def prev(self, *cut):
        far, near = self.far[cut], self.near[cut]
        return jnp.where(self.flag(far), near, far)

    def next(self, *cut):
        far, near = self.far[cut], self.near[cut]
        return jnp.where(self.flag(far), far, near)

    def rim(self, side, row):
        cut = slice(row, row + HALO)
        return self.prev(cut) if side == 0 else self.next(cut)

    def rims(self, side, rows):
        return tuple(self.rim(side, row) for row in rows)


def arrange(up, dn, odd, far, near):
    flag = jnp.broadcast_to(odd[0:1], up.shape) > 0
    far[...] = jnp.where(flag, up[...], dn[...])
    near[...] = jnp.where(flag, dn[...], up[...])


def exchange(value):
    return lax.all_to_all(value, RING, split_axis=0, concat_axis=0, tiled=True)


def gll_matrix():
    points = np.array([-1.0, -1.0 / np.sqrt(5.0), 1.0 / np.sqrt(5.0), 1.0])
    barycentric = [
        1.0 / np.prod([points[s] - points[o] for o in range(4) if o != s]) for s in range(4)
    ]
    table = np.zeros((4, 4))
    for t in range(4):
        for s in range(4):
            if t != s:
                table[t, s] = barycentric[s] / barycentric[t] / (points[t] - points[s])
    for t in (0, 3):
        table[t, t] = -np.sum(table[t])
    return [[float(np.float32(value)) for value in line] for line in table]


GLL = gll_matrix()


def vmem(count):
    return [pl.BlockSpec(memory_space=pltpu.VMEM)] * count


def hbm(count):
    return [pl.BlockSpec(memory_space=pltpu.HBM)] * count


def in_hbm(*arrays):
    return [pltpu.with_memory_space_constraint(array, pltpu.HBM) for array in arrays]


def smem(count):
    return [pl.BlockSpec(memory_space=pltpu.SMEM)] * count


def shape_of(*dims, dtype=jnp.float32):
    return jax.ShapeDtypeStruct(dims, dtype)


PARAMS = pltpu.CompilerParams(vmem_limit_bytes=24 * 1024 * 1024)


def lane_take(rows, ids):
    return jnp.take_along_axis(rows, ids, axis=1, mode="promise_in_bounds")


def wide(row, lines):
    return jnp.broadcast_to(row, (lines, row.shape[1]))


def side_ids(pn):
    count = pn.shape[1]
    bits = count.bit_length() - 1
    table = pn[...]
    ids = [table[k : k + 1] & (count - 1) for k in range(4)]
    home = lax.shift_right_logical(table[0:1], bits)
    near = [lax.shift_right_logical(table[k : k + 1], bits) == home for k in range(4)]
    return ids, near


def element_step(state, east_wind, north_wind, scale, facing):
    jumps = [None] * 16
    sides = (
        (0, 1, 2, 3),
        (3, 7, 11, 15),
        (12, 13, 14, 15),
        (0, 4, 8, 12),
    )
    for k in range(4):
        for n, p in enumerate(sides[k]):
            term = facing[k][n] - state[p]
            jumps[p] = term if jumps[p] is None else jumps[p] + term
    result = []
    for p in range(16):
        i, j = p % 4, p // 4
        grad_x = grad_y = None
        for m in range(4):
            if GLL[i][m] != 0.0:
                term = GLL[i][m] * state[m + 4 * j]
                grad_x = term if grad_x is None else grad_x + term
            if GLL[j][m] != 0.0:
                term = GLL[j][m] * state[i + 4 * m]
                grad_y = term if grad_y is None else grad_y + term
        change = -(east_wind(p) * grad_x + north_wind(p) * grad_y)
        if jumps[p] is not None:
            change = change + JUMP_WEIGHT * jumps[p]
        result.append(state[p] + scale * change)
    return result


def load(pairs, sems):
    copies = [
        pltpu.make_async_copy(source, target, sems.at[n])
        for n, (source, target) in enumerate(pairs)
    ]
    for copy in copies:
        copy.start()
    return copies


def as_column(row):
    count = row.shape[1]
    return jnp.transpose(jnp.broadcast_to(row, (count, count)))


def edge_tables(partner, remote):
    count = partner.shape[1]
    pack = count // 4
    lane = lax.broadcasted_iota(jnp.int32, (count, count), 1)
    line = lax.broadcasted_iota(jnp.int32, (count, count), 0)
    flag = jnp.where(remote, 1.0, 0.0)
    rank = jnp.sum(jnp.where(line < lane, as_column(flag), 0.0), axis=0, keepdims=True)
    rank = as_column(jnp.where(remote, rank, -1.0))
    slot = (lane & (pack - 1)).astype(jnp.float32)
    chosen = jnp.sum(
        jnp.where(rank == slot, line.astype(jnp.float32), 0.0), axis=0, keepdims=True
    ).astype(jnp.int32)
    key = jnp.where(remote, partner, 2 * count).astype(jnp.float32)
    before = jnp.where(as_column(key) < key, 1.0, 0.0)
    place = jnp.sum(before, axis=0, keepdims=True).astype(jnp.int32)
    return chosen, jnp.minimum(place, pack - 1)


def rank_among_equals(row, most):
    count = row.shape[1]
    earlier = lax.broadcasted_iota(jnp.int32, (count, count), 0) < lax.broadcasted_iota(
        jnp.int32, (count, count), 1
    )
    number = row.astype(jnp.float32)
    same = as_column(number) == number
    return jnp.minimum(jnp.sum(jnp.where(same & earlier, 1, 0), axis=0, keepdims=True), most)


def slot_rows(holder_row, rank, down_row, devices, tiles):
    blocks = holder_row.shape[1]
    target = lax.broadcasted_iota(jnp.int32, (devices, blocks), 0)
    after = jnp.where(holder_row + 1 == devices, 0, holder_row + 1)
    before = jnp.where(holder_row == 0, devices - 1, holder_row - 1)
    last = down_row - (tiles - HALO)
    lane = lax.broadcasted_iota(jnp.int32, (devices, LANES), 1)
    result = jnp.full((devices, LANES), -1.0, jnp.float32)
    for n, (owner, number) in enumerate(
        (
            (holder_row, down_row),
            (after, jnp.where(last >= 0, tiles + last, -1)),
            (before, jnp.where(down_row < HALO, tiles + HALO + down_row, -1)),
        )
    ):
        for slot in range(CAP):
            named = (target == owner) & (rank == slot)
            value = jnp.sum(
                jnp.where(named, (number + 1).astype(jnp.float32), 0.0), axis=1, keepdims=True
            )
            result = jnp.where(lane == CAP * n + slot, value - 1.0, result)
    return result


def home_facing(state, ids, near):
    return [
        [lane_take(state[12 + n], ids[0]) for n in range(4)],
        [jnp.where(near[1], lane_take(state[4 * n], ids[1]), 0.0) for n in range(4)],
        [lane_take(state[n], ids[2]) for n in range(4)],
        [jnp.where(near[3], lane_take(state[3 + 4 * n], ids[3]), 0.0) for n in range(4)],
    ]


def plan_kernel(
    air_hbm, eastern_hbm, northern_hbm, breadth_hbm, pn_hbm, holder_hbm, across_hbm, down_hbm,
    nb_hbm, span_hbm, flow_hbm, sst_hbm, flux, slots, breadth, pn, marks, idx, w, u, v, sst,
    air, eastern, northern, holder, across, down, nb, span, flow, lists, sems, *, devices, tiles
):
    copies = load(
        (
            (air_hbm.at[:, pl.ds(0, 8), :], air),
            (eastern_hbm.at[:, pl.ds(0, 16), :], eastern),
            (northern_hbm.at[:, pl.ds(0, 16), :], northern),
            (breadth_hbm, breadth),
            (pn_hbm, pn),
            (holder_hbm, holder),
            (across_hbm, across),
            (down_hbm, down),
            (nb_hbm, nb),
            (span_hbm, span),
            (flow_hbm, flow),
            (sst_hbm, sst),
        ),
        sems,
    )
    for copy in copies:
        copy.wait()
    rank = rank_among_equals(holder[...], CAP - 1)
    place = across[...] * 2 + rank_among_equals(across[...], 1)
    blocks = place.shape[1]
    line = lax.broadcasted_iota(jnp.int32, (blocks, blocks), 0).astype(jnp.float32)
    lane = lax.broadcasted_iota(jnp.int32, (blocks, blocks), 1).astype(jnp.float32)
    here = as_column(place.astype(jnp.float32)) == lane
    reader = jnp.sum(jnp.where(here, line, 0.0), axis=0, keepdims=True).astype(jnp.int32)
    lists[...] = jnp.zeros_like(lists)
    for mark, row in (
        (MARK_COLUMN, across[...]),
        (MARK_OWN, holder[...] * 8 + 2 * rank),
        (MARK_HEAT, holder[...] * 8 + 4 + rank),
        (MARK_ANSWER, holder[...] * CAP + rank),
        (MARK_PLACE, place),
        (MARK_READER, reader),
    ):
        lists[mark : mark + 1] = row
    copy = pltpu.make_async_copy(lists, marks, sems.at[0])
    copy.start()
    slots[...] = slot_rows(holder[...], rank, down[...], devices, tiles)
    fill_tables(nb, span, flow, idx, w, u, v)
    lines, count = air.shape[1], air.shape[2]
    ids, near = side_ids(pn)
    ids = [wide(line, lines) for line in ids]
    state = [air[p] for p in range(16)]
    u = [eastern[p].astype(jnp.float32)[0:lines] for p in range(16)]
    v = [northern[p].astype(jnp.float32)[0:lines] for p in range(16)]
    result = element_step(
        state, lambda p: u[p], lambda p: v[p], STEP_SIZE * breadth[...],
        home_facing(state, ids, near)
    )
    for p in range(16):
        speed = jnp.sqrt(u[p] * u[p] + v[p] * v[p] + 1.0)
        flux[p, 0:1] = (speed * result[p])[0:1]
        flux[p, 1:2] = (speed * u[p])[0:1]
        flux[p, 2:3] = (speed * v[p])[0:1]
        flux[p, 3:4] = speed[0:1]
        flux[p, 4:8] = jnp.zeros((4, count), jnp.float32)
    copy.wait()


def local_step_kernel(
    air_hbm, eastern_hbm, northern_hbm, breadth, pn, odd, loc, eastern, northern, east, west,
    far, near_swap, places, air, sems
):
    copies = load(((air_hbm, air), (eastern_hbm, eastern), (northern_hbm, northern)), sems)
    count = breadth.shape[1]
    lines = 16
    ids, near = side_ids(pn)
    chosen_east, place_east = edge_tables(ids[1], jnp.logical_not(near[1]))
    chosen_west, place_west = edge_tables(ids[3], jnp.logical_not(near[3]))
    places[...] = jnp.zeros_like(places)
    places[0:1] = place_east
    places[1:2] = place_west
    chosen_east, chosen_west = wide(chosen_east, lines), wide(chosen_west, lines)
    group = lax.broadcasted_iota(jnp.int32, (lines, count), 1) // (count // 4)
    scale = STEP_SIZE * breadth[...]
    ids = [wide(line, lines) for line in ids]

    def packed(values, chosen):
        result = jnp.zeros((lines, count), jnp.float32)
        for n in range(4):
            result = jnp.where(group == n, lane_take(values[n], chosen), result)
        return result

    for copy in copies:
        copy.wait()
    levels = air.shape[1]

    def chunk(c, carry):
        at = pl.multiple_of(c * lines, lines)
        rows = pl.ds(at, lines)
        state = [air[p, rows] for p in range(16)]
        result = element_step(
            state,
            lambda p: eastern[p, rows].astype(jnp.float32),
            lambda p: northern[p, rows].astype(jnp.float32),
            scale,
            home_facing(state, ids, near),
        )
        for p in range(16):
            loc[p, rows] = result[p]
        here = pl.ds(pl.multiple_of(4 * HALO + at, 8), lines)
        beyond = pl.ds(pl.multiple_of(4 * HALO + levels + at, 8), lines)
        for n in range(4):
            east[n, rows] = state[3 + 4 * n].astype(jnp.bfloat16)
            west[n, rows] = state[4 * n].astype(jnp.bfloat16)
        flag = jnp.broadcast_to(odd[0:1], (lines, count)) > 0
        for target, values in ((here, state), (beyond, result)):
            to_next = packed([values[3 + 4 * n] for n in range(4)], chosen_east)
            to_prev = packed([values[4 * n] for n in range(4)], chosen_west)
            far[target] = jnp.where(flag, to_next, to_prev)
            near_swap[target] = jnp.where(flag, to_prev, to_next)
        return carry

    lax.fori_loop(0, levels // lines, chunk, 0)


def second_step_kernel(
    loc, eastern, northern, breadth, pn, east, west, far, near_swap, places, first_far,
    first_near, odd, surface, out_hbm, out, sems
):
    ids, near = side_ids(pn)
    levels, count = loc.shape[1], loc.shape[2]
    lines = 16
    pack = count // 4
    scale = STEP_SIZE * breadth[...]
    jump = JUMP_WEIGHT * scale
    ids = [wide(line, lines) for line in ids]
    got = Received(far, near_swap, odd)
    first = Received(first_far, first_near, odd)
    row = slice(ROW_BREADTH, ROW_BREADTH + 1)
    factors = [
        JUMP_WEIGHT * STEP_SIZE * lane_take(wide(line, lines), ids[side])
        for side, line in ((1, first.next(row)), (3, first.prev(row)))
    ]
    spots = [
        [wide(places[n : n + 1] + m * pack, lines) for m in range(4)] for n in (0, 1)
    ]

    def copy_out(c):
        rows = pl.ds(pl.multiple_of(c * lines, lines), lines)
        return pltpu.make_async_copy(out.at[:, rows, :], out_hbm.at[:, rows, :], sems.at[c])

    def chunk(c, carry):
        at = pl.multiple_of(c * lines, lines)
        rows = pl.ds(at, lines)
        now = pl.ds(pl.multiple_of(4 * HALO + at, 8), lines)
        later = pl.ds(pl.multiple_of(4 * HALO + levels + at, 8), lines)
        state = [loc[p, rows] for p in range(16)]

        def across(own, there_now, there_next, side, factor, spot):
            values, beyond = [], []
            for n in range(4):
                values.append(jnp.where(near[side], 0.0, lane_take(there_now, spot[n])))
                beyond.append(
                    lane_take(there_next, spot[n]) + factor * own[n, rows].astype(jnp.float32)
                )
            return values, beyond

        east_now, east_beyond = across(
            east, got.next(now), got.next(later), 1, factors[0], spots[0]
        )
        west_now, west_beyond = across(
            west, got.prev(now), got.prev(later), 3, factors[1], spots[1]
        )
        for n in range(4):
            state[3 + 4 * n] = state[3 + 4 * n] + jump * east_now[n]
            state[4 * n] = state[4 * n] + jump * west_now[n]
        facing = home_facing(state, ids, near)
        facing[1] = [jnp.where(near[1], facing[1][n], east_beyond[n]) for n in range(4)]
        facing[3] = [jnp.where(near[3], facing[3][n], west_beyond[n]) for n in range(4)]
        result = element_step(
            state,
            lambda p: eastern[p, rows].astype(jnp.float32),
            lambda p: northern[p, rows].astype(jnp.float32),
            scale,
            facing,
        )
        for p in range(16):
            out[p, rows] = result[p]

        @pl.when(c == 0)
        def _():
            for p in range(16):
                lowest = out[p, 0:1]
                out[p, 0:1] = lowest + NUDGING_SPEED * (surface[p : p + 1] - lowest)

        copy_out(c).start()
        return carry

    lax.fori_loop(0, levels // lines, chunk, 0)

    def finish(c, carry):
        copy_out(c).wait()
        return carry

    lax.fori_loop(0, levels // lines, finish, 0)


def home_sums_kernel(marks, flux, weights, own):
    own[...] = jnp.zeros_like(own)
    for b in range(weights.shape[0]):
        sums = jnp.dot(
            flux[marks[MARK_COLUMN, b]].astype(jnp.bfloat16), weights[b], preferred_element_type=jnp.float32
        )
        row = marks[MARK_OWN, b]
        own[pl.ds(row, 1), :] = sums[1:2]
        own[pl.ds(row + 1, 1), :] = sums[2:3]
        own[pl.ds(marks[MARK_HEAT, b], 1), :] = sums[0:1]


def forward_kernel(
    marks, home, flux, slots, breadth, pn, first_far, first_near, odd, weights, out_hbm, out, extra,
    sems, *, devices
):
    ids, near = side_ids(pn)
    jump = (JUMP_WEIGHT * STEP_SIZE) * breadth[...]
    first = Received(first_far, first_near, odd)
    from_east = lane_take(first.next(slice(0, 8)), wide(ids[1], 8))
    from_west = lane_take(first.prev(slice(0, 8)), wide(ids[3], 8))
    from_east = jnp.where(near[1], 0.0, jump * from_east)
    from_west = jnp.where(near[3], 0.0, jump * from_west)
    extra[...] = jnp.zeros_like(extra)
    for n in range(4):
        for p, change in ((3 + 4 * n, from_east), (4 * n, from_west)):
            line = wide(flux[p, 3:4] * change[n : n + 1], 8).astype(jnp.bfloat16)
            for reader in range(2):
                b = marks[MARK_READER, 2 * p + reader]
                sums = jnp.dot(line, weights[b], preferred_element_type=jnp.float32)
                extra[pl.ds(marks[MARK_HEAT, b], 1), :] = sums[0:1]
    line = lax.broadcasted_iota(jnp.int32, (8, LANES), 0)
    part, copies = devices // 4, []
    for d in range(devices):
        mine, prev, following = (
            home[8 * (n % devices) : 8 * (n % devices) + 8] for n in (d, d - 1, d + 1)
        )
        top = jnp.concatenate([mine[0:4], prev[0:4]], axis=0)
        bottom = jnp.where(line < 4, following, mine + extra[8 * d : 8 * d + 8])
        bottom = jnp.where(line == ROW_IDS - 8, wide(slots[d : d + 1], 8), bottom)
        out[d] = jnp.concatenate([top, bottom], axis=0).astype(jnp.bfloat16)
        if (d + 1) % part == 0:
            copies.append(
                pltpu.make_async_copy(
                    out.at[pl.ds(d + 1 - part, part)],
                    out_hbm.at[pl.ds(d + 1 - part, part)],
                    sems.at[d // part],
                )
            )
            copies[-1].start()
    for copy in copies:
        copy.wait()


def back_kernel(marks, arrived, weights, surface, lines, share):
    lines[...] = arrived[...].reshape(lines.shape)
    for b in range(weights.shape[0]):
        line = lines[pl.ds(marks[MARK_ANSWER, b], 1), :]
        share[marks[MARK_PLACE, b]] = lax.dot_general(
            wide(line, 8).astype(jnp.bfloat16),
            weights[b],
            (((1,), (1,)), ((), ())),
            preferred_element_type=jnp.float32,
        )
    for p in range(surface.shape[0]):
        surface[p : p + 1] = share[2 * p, 0:1] + share[2 * p + 1, 0:1]


def split_index(idx):
    return lax.shift_right_arithmetic(idx, 7), idx & (LANES - 1)


def by_tiles(function, idx):
    if idx.shape[0] <= 8:
        return function(idx)
    return jnp.concatenate(
        [function(idx[at : at + 8]) for at in range(0, idx.shape[0], 8)], axis=0
    )


def pick(idx, sources):
    def one(idx):
        high, low = split_index(idx)
        result = jnp.zeros(idx.shape, jnp.float32)
        for number, line in sources:
            result = jnp.where(high == number, lane_take(wide(line, idx.shape[0]), low), result)
        return result

    return by_tiles(one, idx)


def fill_pack(values, packed, scales):
    half = values.shape[0] // 2
    numbers = []
    for n, part in enumerate((values[:half], values[half:])):
        largest = jnp.maximum(jnp.max(jnp.abs(part), axis=(0, 1), keepdims=True), 1e-30)
        numbers.append(jnp.floor(part * (32767.0 / largest) + 0.5).astype(jnp.int32))
        scales[n : n + 1] = jnp.broadcast_to(largest * (1.0 / 32767.0), (1, LANES))
    packed[...] = (numbers[1] << 16) | (numbers[0] & 0xFFFF)


def pick_own(idx, packed, scales):
    half = packed.shape[0]

    def one(idx):
        lines = idx.shape[0]
        high, low = split_index(idx)
        own = high - HALO
        upper = own >= half
        row = jnp.where(upper, own - half, own)
        words = jnp.zeros(idx.shape, jnp.int32)
        for r in range(half):
            words = jnp.where(row == r, lane_take(wide(packed[r : r + 1], lines), low), words)
        number = jnp.where(upper, words >> 16, (words << 16) >> 16)
        scale = jnp.where(upper, wide(scales[1:2], lines), wide(scales[0:1], lines))
        return number.astype(jnp.float32) * scale

    return by_tiles(one, idx)


def combine(terms, factors):
    total = None
    for term, factor in zip(terms, factors):
        if factor != 0.0:
            total = factor * term if total is None else total + factor * term
    return total


def pair_sums(table):
    terms = [table[HALO * k : HALO * (k + 1)] for k in range(6)]
    return combine(terms, COS), combine(terms, SIN)


def rim_partial(rim_idx, rim_w, eta, packed, scales, first):
    rows = rim_idx.shape[0]
    found = pick_own(rim_idx, packed, scales)
    centre = eta[first : first + HALO]
    centre = jnp.concatenate([centre] * (rows // HALO), axis=0)
    return pair_sums(rim_w * (found - centre))


def prepare_kernel(
    air_hbm, breadth_hbm, pn_hbm, eta_hbm, sst_hbm, flow_hbm, nb_hbm, span_hbm,
    rim_idx, rim_w, eta, eta_pack, eta_scale, far, near, odd,
    up, dn, air, breadth, pn, sst, flow, nb, span, sems
):
    tiles, cells = eta.shape[0], nb_hbm.shape[1]
    pairs = [(air_hbm.at[:, 3 * side, pl.ds(0, 8), :], air.at[side]) for side in (0, 1)]
    pairs.append((eta_hbm, eta))
    for side, at in ((0, 0), (1, cells - OY)):
        cut = pl.ds(at, OY)
        pairs.append((nb_hbm.at[:, cut], nb.at[side]))
        pairs.append((span_hbm.at[:, cut], span.at[side]))
        pairs.append((flow_hbm.at[:, cut], flow.at[side]))
    for side, at in ((0, 0), (1, tiles - 8)):
        pairs.append((sst_hbm.at[pl.ds(at, 8)], sst.at[side]))
    pairs.append((breadth_hbm, breadth))
    pairs.append((pn_hbm, pn))
    copies = load(pairs, sems)
    for copy in copies:
        copy.wait()
    shard = lax.shift_right_logical(pn[0:1], pn.shape[1].bit_length() - 1)
    odd[...] = wide(shard & 1, 8)
    fill_pack(eta[...], eta_pack, eta_scale)
    for side, first in ((0, 0), (1, tiles - HALO)):
        rim_idx[side, 12:16] = jnp.full((4, LANES), -1, jnp.int32)
        rim_w[side, 12:16] = jnp.zeros((4, LANES), jnp.float32)
        for j in range(HALO):
            cut = slice(j * LANES, (j + 1) * LANES)
            links = nb[side, :, cut]
            factors = slot_factors(links, span[side, :, cut])
            for k in range(6):
                at = HALO * k + j
                rim_idx[side, at : at + 1] = links[k : k + 1]
                rim_w[side, at : at + 1] = factors[k : k + 1]
    for side, first, target in ((0, 0, dn), (1, tiles - HALO, up)):
        target[...] = jnp.zeros_like(target)
        for n in range(4):
            target[ROW_EDGE + n : ROW_EDGE + n + 1] = air[side, n, 0:1]
        target[ROW_BREADTH : ROW_BREADTH + 1] = breadth[...]
        part_x, part_y = rim_partial(
            rim_idx[side], rim_w[side], eta, eta_pack, eta_scale, first
        )
        cut = slice(first, first + HALO)
        target[ROW_ETA : ROW_ETA + HALO] = eta[cut]
        for j in range(HALO):
            here = slice(j * LANES, (j + 1) * LANES)
            target[ROW_U + j : ROW_U + j + 1] = flow[side, 0:1, here]
            target[ROW_V + j : ROW_V + j + 1] = flow[side, 1:2, here]
        start = first % 8
        target[ROW_SST : ROW_SST + HALO] = sst[side, start : start + HALO]
        target[ROW_PX : ROW_PX + HALO] = part_x
        target[ROW_PY : ROW_PY + HALO] = part_y
        target[ROW_IDX : ROW_IDX + 16] = rim_idx[side].astype(jnp.float32)
        target[ROW_W : ROW_W + 16] = rim_w[side]
    arrange(up, dn, odd, far, near)


def slot_factors(links, span):
    return jnp.where(links >= 0, span * (1.0 / 3.0), 0.0)


def fill_tables(nb, span, flow, idx, w, u, v):
    tiles = u.shape[0]
    for r in range(tiles):
        cut = slice(r * LANES, (r + 1) * LANES)
        links = nb[:, cut]
        factors = slot_factors(links, span[:, cut])
        for k in range(6):
            idx[k * tiles + r : k * tiles + r + 1] = links[k : k + 1]
            w[k * tiles + r : k * tiles + r + 1] = factors[k : k + 1]
        u[r : r + 1] = flow[0:1, cut]
        v[r : r + 1] = flow[1:2, cut]


def own_gradient(idx, w, eta, packed, scales, gx, gy):
    tiles = eta.shape[0]

    def chunk(at):
        centre = eta[pl.ds(at, 8)]
        terms = []
        for k in range(6):
            found = pick_own(idx[pl.ds(k * tiles + at, 8)], packed, scales)
            terms.append(w[pl.ds(k * tiles + at, 8)] * (found - centre))
        gx[pl.ds(at, 8)] = combine(terms, COS)
        gy[pl.ds(at, 8)] = combine(terms, SIN)

    for c in range(tiles // 8):
        chunk(c * 8)


def own_spread(at, idx, w, flow, packed, scales):
    tiles = flow.shape[1]
    total = jnp.zeros((8, LANES), jnp.float32)
    for kk in range(3):
        centre = flow[kk, pl.ds(at, 8)]
        for k, sign in ((kk, 1.0), (kk + 3, -1.0)):
            rows = pl.ds(k * tiles + at, 8)
            found = pick_own(idx[rows], packed.at[kk], scales.at[kk])
            total = total + sign * w[rows] * (found - centre)
    return total


def inner_kernel(
    idx, w, eta, eta_pack, eta_scale, u, v, fu, fv, eta_part, u_part, v_part,
    flow, flow_pack, flow_scale
):
    current_kernel(idx, w, eta, eta_pack, eta_scale, u, v, fu, fv, u_part, v_part)
    height_kernel(idx, w, eta, u_part, v_part, eta_part, flow, flow_pack, flow_scale)


def current_kernel(idx, w, eta, eta_pack, eta_scale, u, v, fu, fv, u_part, v_part):
    own_gradient(idx, w, eta, eta_pack, eta_scale, u_part, v_part)
    u_part[...] = DAMPING * u[...] - GRAVITY * u_part[...] + WIND_GAIN * fu[...]
    v_part[...] = DAMPING * v[...] - GRAVITY * v_part[...] + WIND_GAIN * fv[...]


def height_kernel(idx, w, eta, u_part, v_part, eta_part, flow, flow_pack, flow_scale):
    tiles = eta.shape[0]
    fill_flow(flow, u_part[...], v_part[...])
    for kk in range(3):
        fill_pack(flow[kk], flow_pack.at[kk], flow_scale.at[kk])

    def chunk(at):
        total = own_spread(at, idx, w, flow, flow_pack, flow_scale)
        eta_part[pl.ds(at, 8)] = eta[pl.ds(at, 8)] - DEPTH_RATE * total

    for c in range(tiles // 8):
        chunk(c * 8)


def first_gradient_kernel(
    idx, w, eta, eta_pack, eta_scale, sst, first_far, first_near, odd, rim_idx, rim_w,
    gx, gy, base, sst_pack, sst_scale
):
    own_gradient(idx, w, eta, eta_pack, eta_scale, gx, gy)
    tiles = eta.shape[0]
    fill_pack(sst[...], sst_pack, sst_scale)

    def chunk(at):
        centre = sst[pl.ds(at, 8)]
        total = jnp.zeros_like(centre)
        for k in range(6):
            found = pick_own(idx[pl.ds(k * tiles + at, 8)], sst_pack, sst_scale)
            total = total + w[pl.ds(k * tiles + at, 8)] * (found - centre)
        base[pl.ds(at, 8)] = centre + (0.5 * SPREADING_COEFF) * total

    for c in range(tiles // 8):
        chunk(c * 8)
    first = Received(first_far, first_near, odd)
    for side, start, offset in ((0, 0, 0), (1, tiles - HALO, tiles + HALO)):
        rim = first.rim(side, ROW_SST)
        sources = [(offset + q, rim[q : q + 1]) for q in range(HALO)]
        found = rim_w[side] * pick(rim_idx[side], sources)
        total = combine([found[HALO * k : HALO * (k + 1)] for k in range(6)], [1.0] * 6)
        rows = slice(start, start + HALO)
        base[rows] = base[rows] + (0.5 * SPREADING_COEFF) * total


def fill_flow(flow, u, v):
    flow[0] = u
    for kk in (1, 2):
        flow[kk] = COS[kk] * u + SIN[kk] * v


def side_currents(eta, sides, fside, before, after, side_idx, side_w):
    tiles = eta.shape[0]
    slopes = []
    for side, offset, first, part in (
        (0, tiles + HALO, 0, before),
        (1, 0, tiles - HALO, after),
    ):
        sources = [(offset + q, eta[first + q : first + q + 1]) for q in range(HALO)]
        add_x, add_y = pair_sums(side_w[side] * pick(side_idx[side], sources))
        slopes.append((part[1] + add_x, part[2] + add_y))
    slope = jnp.concatenate([slopes[0][0], slopes[1][0], slopes[0][1], slopes[1][1]], axis=0)
    return DAMPING * sides[...] - GRAVITY * slope + WIND_GAIN * fside[...]


def rim_slopes(rim_idx, rim_w, before, after, tiles):
    result = []
    for side, offset, part in ((0, 0, before), (1, tiles + HALO, after)):
        sources = [(offset + q, part[0][q : q + 1]) for q in range(HALO)]
        result.append(pair_sums(rim_w[side] * pick(rim_idx[side], sources)))
    return result


def send_rims(eta, eta_pack, eta_scale, rim_idx, rim_w, odd, far, near, up, dn):
    tiles = eta.shape[0]
    fill_pack(eta[...], eta_pack, eta_scale)
    for side, first, target in ((0, 0, dn), (1, tiles - HALO, up)):
        part_x, part_y = rim_partial(
            rim_idx[side], rim_w[side], eta, eta_pack, eta_scale, first
        )
        target[0:HALO] = eta[first : first + HALO]
        target[HALO : 2 * HALO] = part_x
        target[2 * HALO : 3 * HALO] = part_y
        target[3 * HALO : 4 * HALO] = jnp.zeros((HALO, LANES), jnp.float32)
    rows = pl.ds(0, 4 * HALO)
    arrange(up, dn, odd, far.at[rows], near.at[rows])


def first_subcycle(
    gx, gy, eta, u, v, sides, fu, fv, fside, before, after, idx, w, side_idx, side_w,
    rim_idx, rim_w, flow, flow_pack, flow_scale, flow_outer, eta_new, u_new, v_new, sides_new,
    midway
):
    tiles = eta.shape[0]
    u_new[...] = DAMPING * u[...] - GRAVITY * gx[...] + WIND_GAIN * fu[...]
    v_new[...] = DAMPING * v[...] - GRAVITY * gy[...] + WIND_GAIN * fv[...]
    slopes = rim_slopes(rim_idx, rim_w, before, after, tiles)
    for first, (add_x, add_y) in zip((0, tiles - HALO), slopes):
        rows = slice(first, first + HALO)
        u_new[rows] = u_new[rows] - GRAVITY * add_x
        v_new[rows] = v_new[rows] - GRAVITY * add_y
    sides_next = side_currents(eta, sides, fside, before, after, side_idx, side_w)
    sides_new[...] = sides_next
    fill_flow(flow, u_new[...], v_new[...])
    fill_flow(flow_outer, sides_next[0 : 2 * HALO], sides_next[2 * HALO : 4 * HALO])
    for kk in range(3):
        fill_pack(flow[kk], flow_pack.at[kk], flow_scale.at[kk])

    def chunk(at):
        total = own_spread(at, idx, w, flow, flow_pack, flow_scale)
        eta_new[pl.ds(at, 8)] = eta[pl.ds(at, 8)] - DEPTH_RATE * total

    for c in range(tiles // 8):
        if c == tiles // 16:
            midway()
        chunk(c * 8)
    for side, first, offset in ((0, 0, 0), (1, tiles - HALO, tiles + HALO)):
        total = jnp.zeros((HALO, LANES), jnp.float32)
        for kk in range(3):
            at = side * HALO
            sources = [(offset + q, flow_outer[kk, at + q : at + q + 1]) for q in range(HALO)]
            found = rim_w[side] * pick(rim_idx[side], sources)
            total = (
                total
                + found[HALO * kk : HALO * (kk + 1)]
                - found[HALO * (kk + 3) : HALO * (kk + 4)]
            )
        rows = slice(first, first + HALO)
        eta_new[rows] = eta_new[rows] - DEPTH_RATE * total


def outer_subcycle(
    eta, eta_part, u_part, v_part, sides, fside, before, after, idx, w, side_idx, side_w,
    rim_idx, rim_w, flow_outer, eta_new, u_new, v_new
):
    tiles = eta.shape[0]
    slopes = rim_slopes(rim_idx, rim_w, before, after, tiles)
    sides_next = side_currents(eta, sides, fside, before, after, side_idx, side_w)
    u_new[...] = u_part[...]
    v_new[...] = v_part[...]
    changes_u = [-GRAVITY * slopes[side][0] for side in (0, 1)]
    changes_v = [-GRAVITY * slopes[side][1] for side in (0, 1)]
    for side, first in ((0, 0), (1, tiles - HALO)):
        rows = slice(first, first + HALO)
        u_new[rows] = u_new[rows] + changes_u[side]
        v_new[rows] = v_new[rows] + changes_v[side]
    fill_flow(
        flow_outer,
        jnp.concatenate([sides_next[0 : 2 * HALO]] + changes_u, axis=0),
        jnp.concatenate([sides_next[2 * HALO : 4 * HALO]] + changes_v, axis=0),
    )
    for c in range(tiles // 8):
        at = c * 8
        total = jnp.zeros((8, LANES), jnp.float32)
        for kk in range(3):
            line = lambda n: flow_outer[kk, n : n + 1]
            sources = [(HALO + q, line(2 * HALO + q)) for q in range(HALO)]
            sources += [(tiles + q, line(3 * HALO + q)) for q in range(HALO)]
            if at == 0:
                sources += [(q, line(q)) for q in range(HALO)]
            if at + 8 == tiles:
                sources += [(tiles + HALO + q, line(HALO + q)) for q in range(HALO)]
            total = (
                total
                + w[kk * tiles + at : kk * tiles + at + 8]
                * pick(idx[kk * tiles + at : kk * tiles + at + 8], sources)
                - w[(kk + 3) * tiles + at : (kk + 3) * tiles + at + 8]
                * pick(idx[(kk + 3) * tiles + at : (kk + 3) * tiles + at + 8], sources)
            )
        eta_new[at : at + 8] = eta_part[at : at + 8] - DEPTH_RATE * total
    for side, first in ((0, 0), (1, tiles - HALO)):
        centre = jnp.zeros((HALO, LANES), jnp.float32)
        for kk in range(3):
            factor = (
                rim_w[side, HALO * kk : HALO * (kk + 1)]
                - rim_w[side, HALO * (kk + 3) : HALO * (kk + 4)]
            )
            start = (2 + side) * HALO
            centre = centre + factor * flow_outer[kk, start : start + HALO]
        rows = slice(first, first + HALO)
        eta_new[rows] = eta_new[rows] + DEPTH_RATE * centre
    return sides_next


def first_ocean_kernel(
    arrived, first_far, first_near, odd, gx, gy, eta, u, v, idx, w, rim_idx, rim_w,
    far_old, near_old, base, eta_new, eta_pack, eta_scale, u_new, v_new, sides_new, far, near,
    fu, fv, fside, side_idx, side_w, heat, answers_hbm,
    flow, flow_pack, flow_scale, flow_outer, sides, up, dn, parts, answers, sems
):
    tiles = eta.shape[0]
    devices = arrived.shape[0]
    parts[...] = arrived[...].astype(jnp.float32).reshape(parts.shape)

    def rows_of(r):
        return parts[pl.ds(r, devices, stride=PER_DEST), :]

    ids = rows_of(ROW_IDS)
    number = lax.broadcasted_iota(jnp.int32, (devices, LANES), 1).astype(jnp.float32)
    nothing = jnp.zeros((devices, LANES), jnp.float32)
    chosen, lines = [], []
    for j in range(3 * CAP):
        chosen.append(jnp.where(ids[:, j : j + 1] == number, 1.0, 0.0).astype(jnp.bfloat16))
        first = rows_of(ROW_HEAT + j) if j < CAP else nothing
        lines.append(jnp.concatenate([first, rows_of(2 * j), rows_of(2 * j + 1)], axis=1))
    forcing = lax.dot_general(
        jnp.concatenate(chosen, axis=0),
        jnp.concatenate(lines, axis=0).astype(jnp.bfloat16),
        (((0,), (0,)), ((), ())),
        preferred_element_type=jnp.float32,
    )
    heat[...] = forcing[0:tiles, 0:LANES]
    half = (base[...] + WARMING_COEFF * forcing[0:tiles, 0:LANES]).astype(jnp.bfloat16)
    for j in range(CAP):
        answers[pl.ds(j, devices, stride=CAP), :] = jnp.dot(
            chosen[j][:, 0:tiles], half, preferred_element_type=jnp.float32
        )
    fu[...] = forcing[0:tiles, LANES : 2 * LANES]
    fv[...] = forcing[0:tiles, 2 * LANES : 3 * LANES]
    fside[0 : 2 * HALO] = forcing[tiles : tiles + 2 * HALO, LANES : 2 * LANES]
    fside[2 * HALO : 4 * HALO] = forcing[tiles : tiles + 2 * HALO, 2 * LANES : 3 * LANES]
    copy = pltpu.make_async_copy(answers, answers_hbm, sems.at[0])
    first = Received(first_far, first_near, odd)
    for side, part in ((0, first.prev), (1, first.next)):
        side_idx[side] = part(slice(ROW_IDX, ROW_IDX + 16)).astype(jnp.int32)
        side_w[side] = part(slice(ROW_W, ROW_W + 16))
        for n, row in ((0, ROW_U), (1, ROW_V)):
            at = HALO * (2 * n + side)
            sides[at : at + HALO] = first.rim(side, row)
    rows = (ROW_ETA, ROW_PX, ROW_PY)
    first_subcycle(
        gx, gy, eta, u, v, sides, fu, fv, fside, first.rims(0, rows), first.rims(1, rows), idx, w, side_idx, side_w, rim_idx, rim_w, flow, flow_pack, flow_scale, flow_outer,
        eta_new, u_new, v_new, sides_new, copy.start
    )
    send_rims(eta_new, eta_pack, eta_scale, rim_idx, rim_w, odd, far, near, up, dn)
    copy.wait()


def ocean_kernel(
    far, near, odd, eta, eta_part, u_part, v_part, sides, fside, idx, w, side_idx, side_w,
    rim_idx, rim_w, eta_new, eta_pack, eta_scale, u_new, v_new, sides_new, far_new, near_new,
    flow_outer, up, dn
):
    rows = (0, HALO, 2 * HALO)
    got = Received(far, near, odd)
    sides_new[...] = outer_subcycle(
        eta, eta_part, u_part, v_part, sides, fside, got.rims(0, rows), got.rims(1, rows), idx, w, side_idx, side_w, rim_idx, rim_w, flow_outer,
        eta_new, u_new, v_new
    )
    send_rims(
        eta_new, eta_pack, eta_scale, rim_idx, rim_w, odd, far_new, near_new, up, dn
    )


def last_ocean_kernel(
    far, near, odd, eta, eta_part, u_part, v_part, sides, fside, idx, w, side_idx, side_w,
    rim_idx, rim_w, base, heat, eta_new, velocity, warm, u_new, v_new, flow_outer
):
    warm[...] = base[...] + WARMING_COEFF * heat[...]
    rows = (0, HALO, 2 * HALO)
    got = Received(far, near, odd)
    outer_subcycle(
        eta, eta_part, u_part, v_part, sides, fside, got.rims(0, rows), got.rims(1, rows), idx, w, side_idx, side_w, rim_idx, rim_w, flow_outer,
        eta_new, u_new, v_new
    )
    for r in range(eta.shape[0]):
        cut = slice(r * LANES, (r + 1) * LANES)
        velocity[0:1, cut] = u_new[r : r + 1]
        velocity[1:2, cut] = v_new[r : r + 1]


def shards(
    air_warmth,
    eastern_breeze,
    northern_breeze,
    reciprocal_breadth,
    panel_neighbours,
    transfer_coefficients,
    transfer_across_tile,
    transfer_holder,
    transfer_down_tile,
    water_elevation,
    depth_mean_current,
    marine_skin_warmth,
    patch_neighbours,
    interface_span,
):
    devices = lax.axis_size(RING)
    points, levels, elements = air_warmth.shape
    cells = water_elevation.shape[0]
    tiles = cells // LANES
    blocks = transfer_holder.shape[0]
    cell_rows = shape_of(tiles, LANES)
    rim_rows = shape_of(4 * HALO, LANES)
    dma = pltpu.SemaphoreType.DMA
    air, eastern, northern, breadth_hbm, pn_hbm = in_hbm(
        air_warmth, eastern_breeze, northern_breeze, reciprocal_breadth.reshape(1, elements),
        panel_neighbours
    )

    pack_rows = shape_of(tiles // 2, LANES, dtype=jnp.int32)
    scale_rows = shape_of(8, LANES)
    cell_tables = in_hbm(
        marine_skin_warmth.reshape(tiles, LANES),
        depth_mean_current,
        patch_neighbours,
        interface_span,
    )
    rim_idx, rim_w, eta, eta_pack, eta_scale, far, near, odd = pl.pallas_call(
        prepare_kernel,
        in_specs=hbm(8),
        out_specs=vmem(8),
        out_shape=(
            shape_of(2, 16, LANES, dtype=jnp.int32),
            shape_of(2, 16, LANES),
            cell_rows,
            pack_rows,
            scale_rows,
            shape_of(ROWS_FIRST, LANES),
            shape_of(ROWS_FIRST, LANES),
            shape_of(8, elements, dtype=jnp.int32),
        ),
        scratch_shapes=[
            pltpu.VMEM((ROWS_FIRST, LANES), jnp.float32),
            pltpu.VMEM((ROWS_FIRST, LANES), jnp.float32),
            pltpu.VMEM((2, 4, 8, elements), jnp.float32),
            pltpu.VMEM((1, elements), jnp.float32),
            pltpu.VMEM((4, elements), jnp.int32),
            pltpu.VMEM((2, 8, LANES), jnp.float32),
            pltpu.VMEM((2, 2, OY), jnp.float32),
            pltpu.VMEM((2, 6, OY), jnp.int32),
            pltpu.VMEM((2, 6, OY), jnp.float32),
            dma((13,)),
        ],
        compiler_params=PARAMS,
        name="prepare",
    )(
        *in_hbm(air_warmth.reshape(4, 4, levels, elements)),
        breadth_hbm,
        pn_hbm,
        *in_hbm(water_elevation.reshape(tiles, LANES)),
        *cell_tables,
    )
    first_far, first_near = swap_both(far, near)

    low_wind = pltpu.VMEM((points, 16, elements), jnp.bfloat16)
    low_row = pltpu.VMEM((1, blocks), jnp.int32)
    flux, slots, breadth, pn, marks, idx, w, u, v, sst = pl.pallas_call(
        lambda *refs: plan_kernel(*refs, devices=devices, tiles=tiles),
        in_specs=hbm(12),
        out_specs=vmem(4) + smem(1) + vmem(5),
        out_shape=(
            shape_of(points, 8, elements), shape_of(devices, LANES), shape_of(1, elements),
            shape_of(4, elements, dtype=jnp.int32), pltpu.SMEM((8, blocks), jnp.int32),
            shape_of(6 * tiles, LANES, dtype=jnp.int32), shape_of(6 * tiles, LANES),
            cell_rows, cell_rows, cell_rows
        ),
        scratch_shapes=[
            pltpu.VMEM((points, 8, elements), jnp.float32), low_wind, low_wind,
            low_row, low_row, low_row, pltpu.VMEM((6, cells), jnp.int32),
            pltpu.VMEM((6, cells), jnp.float32), pltpu.VMEM((2, cells), jnp.float32),
            pltpu.VMEM((8, blocks), jnp.int32), dma((12,))
        ],
        compiler_params=PARAMS,
        name="plan",
    )(
        air,
        eastern,
        northern,
        breadth_hbm,
        pn_hbm,
        *in_hbm(
            transfer_holder.reshape(1, blocks),
            transfer_across_tile.reshape(1, blocks),
            transfer_down_tile.reshape(1, blocks),
        ),
        cell_tables[2],
        cell_tables[3],
        cell_tables[1],
        cell_tables[0],
    )

    home = pl.pallas_call(
        home_sums_kernel,
        in_specs=smem(1) + vmem(2),
        out_specs=pl.BlockSpec(memory_space=pltpu.VMEM),
        out_shape=shape_of(devices * 8, LANES),
        compiler_params=PARAMS,
        name="home_sums",
    )(marks, flux, transfer_coefficients)
    outgoing = pl.pallas_call(
        lambda *refs: forward_kernel(*refs, devices=devices),
        in_specs=smem(1) + vmem(9),
        out_specs=pl.BlockSpec(memory_space=pltpu.HBM),
        out_shape=pltpu.HBM((devices, PER_DEST, LANES), jnp.bfloat16),
        scratch_shapes=[
            pltpu.VMEM((devices, PER_DEST, LANES), jnp.bfloat16),
            pltpu.VMEM((devices * 8, LANES), jnp.float32),
            dma((4,)),
        ],
        compiler_params=PARAMS,
        name="forward_remap",
    )(
        marks, home, flux, slots, breadth, pn, first_far, first_near, odd, transfer_coefficients
    )
    outgoing, pn, gradient_eta = lax.optimization_barrier((outgoing, pn, eta))
    arrived = exchange(outgoing)
    gx, gy, base = pl.pallas_call(
        first_gradient_kernel,
        in_specs=vmem(11),
        out_specs=vmem(3),
        out_shape=(cell_rows,) * 3,
        scratch_shapes=[
            pltpu.VMEM((tiles // 2, LANES), jnp.int32), pltpu.VMEM((8, LANES), jnp.float32)
        ],
        compiler_params=PARAMS,
        name="first_gradient",
    )(
        idx, w, gradient_eta, eta_pack, eta_scale, sst, first_far, first_near, odd, rim_idx, rim_w
    )

    field = shape_of(points, levels, elements)
    edge = shape_of(4, levels, elements, dtype=jnp.bfloat16)
    swap_rows = shape_of(4 * HALO + 2 * levels, elements)
    wind = shape_of(points, levels, elements, dtype=jnp.bfloat16)
    loc, eastern, northern, east, west, far, near, edge_places = pl.pallas_call(
        local_step_kernel,
        in_specs=hbm(3) + vmem(3),
        out_specs=vmem(8),
        out_shape=(
            field, wind, wind, edge, edge, swap_rows, swap_rows,
            shape_of(8, elements, dtype=jnp.int32)
        ),
        scratch_shapes=[pltpu.VMEM((points, levels, elements), jnp.float32), dma((3,))],
        compiler_params=PARAMS,
        name="local_step",
    )(air, eastern, northern, breadth, pn, odd)

    rim_scratch = pltpu.VMEM((4 * HALO, LANES), jnp.float32)
    flow_scratch = [
        pltpu.VMEM((3, tiles, LANES), jnp.float32),
        pltpu.VMEM((3, tiles // 2, LANES), jnp.int32),
        pltpu.VMEM((3, 8, LANES), jnp.float32),
        pltpu.VMEM((3, 2 * HALO, LANES), jnp.float32),
    ]
    (
        eta, eta_pack, eta_scale, u, v, sides, far, near, fu, fv, fside, side_idx, side_w,
        heat, answers
    ) = pl.pallas_call(
        first_ocean_kernel,
        in_specs=vmem(16),
        out_specs=vmem(14) + hbm(1),
        out_shape=(
            cell_rows, pack_rows, scale_rows, cell_rows, cell_rows, rim_rows, swap_rows, swap_rows,
            cell_rows, cell_rows, rim_rows,
            shape_of(2, 16, LANES, dtype=jnp.int32), shape_of(2, 16, LANES),
            cell_rows, pltpu.HBM((devices * CAP, LANES), jnp.float32),
        ),
        scratch_shapes=flow_scratch + [rim_scratch] * 3 + [
            pltpu.VMEM((devices * PER_DEST, LANES), jnp.float32),
            pltpu.VMEM((devices * CAP, LANES), jnp.float32),
            dma((1,)),
        ],
        input_output_aliases={13: 6, 14: 7},
        compiler_params=PARAMS,
        name="first_ocean",
    )(
        arrived, first_far, first_near, odd, gx, gy, eta, u, v, idx, w, rim_idx, rim_w,
        far, near, base
    )
    far, near = swap_both(far, near)
    edges_far, edges_near = far, near

    for substep in range(1, NSUB):
        if substep == 1:
            u_part, v_part = pl.pallas_call(
                current_kernel,
                in_specs=vmem(9),
                out_specs=vmem(2),
                out_shape=(cell_rows,) * 2,
                compiler_params=PARAMS,
                name="current",
            )(idx, w, eta, eta_pack, eta_scale, u, v, fu, fv)
            answers, u_part = lax.optimization_barrier((answers, u_part))
            answered = exchange(answers.reshape(devices, CAP, LANES))
            eta_part = pl.pallas_call(
                height_kernel,
                in_specs=vmem(5),
                out_specs=pl.BlockSpec(memory_space=pltpu.VMEM),
                out_shape=cell_rows,
                scratch_shapes=flow_scratch[:3],
                compiler_params=PARAMS,
                name="height",
            )(idx, w, eta, u_part, v_part)
        else:
            eta_part, u_part, v_part = pl.pallas_call(
                inner_kernel,
                in_specs=vmem(9),
                out_specs=vmem(3),
                out_shape=(cell_rows,) * 3,
                scratch_shapes=flow_scratch[:3],
                compiler_params=PARAMS,
                name="inner",
            )(idx, w, eta, eta_pack, eta_scale, u, v, fu, fv)
        if substep == 2:
            eta_part, answered = lax.optimization_barrier((eta_part, answered))
            surface = pl.pallas_call(
                back_kernel,
                in_specs=smem(1) + vmem(2),
                out_specs=pl.BlockSpec(memory_space=pltpu.VMEM),
                out_shape=shape_of(points, LANES),
                scratch_shapes=[
                    pltpu.VMEM((devices * CAP, LANES), jnp.float32),
                    pltpu.VMEM((blocks, 8, LANES), jnp.float32),
                ],
                compiler_params=PARAMS,
                name="back_remap",
            )(marks, answered, transfer_coefficients)
            eta_part, surface = lax.optimization_barrier((eta_part, surface))
        operands = (
            far, near, odd, eta, eta_part, u_part, v_part, sides, fside, idx, w, side_idx, side_w, rim_idx, rim_w
        )
        outer_scratch = [pltpu.VMEM((3, 4 * HALO, LANES), jnp.float32)]
        if substep + 1 < NSUB:
            eta, eta_pack, eta_scale, u, v, sides, far, near = pl.pallas_call(
                ocean_kernel,
                in_specs=vmem(15),
                out_specs=vmem(8),
                out_shape=(cell_rows, pack_rows, scale_rows) + (cell_rows,) * 2 + (rim_rows,) * 3,
                scratch_shapes=outer_scratch + [rim_scratch] * 2,
                compiler_params=PARAMS,
                name="ocean",
            )(*operands)
            far, near = swap_both(far, near)
        else:
            eta, velocity, warm = pl.pallas_call(
                last_ocean_kernel,
                in_specs=vmem(17),
                out_specs=vmem(3),
                out_shape=(cell_rows, shape_of(2, cells), cell_rows),
                scratch_shapes=[pltpu.VMEM((tiles, LANES), jnp.float32)] * 2 + outer_scratch,
                compiler_params=PARAMS,
                name="last_ocean",
            )(*operands, base, heat)

    closing = pl.pallas_call(
        second_step_kernel,
        in_specs=vmem(14),
        out_specs=pl.BlockSpec(memory_space=pltpu.HBM),
        out_shape=pltpu.HBM((points, levels, elements), jnp.float32),
        scratch_shapes=[
            pltpu.VMEM((points, levels, elements), jnp.float32), dma((levels // 16,))
        ],
        compiler_params=PARAMS,
        name="second_step",
    )(
        loc, eastern, northern, breadth, pn, east, west, edges_far, edges_near, edge_places,
        first_far, first_near, odd, surface
    )
    return closing, eta.reshape(cells), velocity, warm.reshape(cells)


def solution(mesh):
    split = P(RING)
    last = P(None, RING)
    field = P(None, None, RING)
    return jax.shard_map(
        shards,
        mesh=mesh,
        in_specs=(
            field,
            field,
            field,
            split,
            last,
            P(RING, None, None),
            split,
            P(RING, None),
            split,
            split,
            last,
            split,
            last,
            last,
        ),
        out_specs=(field, split, last, split),
        check_vma=False,
    )
```

```python
import math

import jax
import jax.numpy as jnp
import numpy as np
from jax import lax
from jax.experimental import pallas as pl
from jax.experimental.pallas import tpu as pltpu
from jax.sharding import PartitionSpec as P

OY = 256
NSUB = 4
CAP = 2

STEP_SIZE = 0.05
JUMP_WEIGHT = 4.0
NUDGING_SPEED = 0.5
DAMPING = 0.9
GRAVITY = 0.3
WIND_GAIN = 0.3
DEPTH_RATE = 0.3
WARMING_COEFF = 0.3
SPREADING_COEFF = 0.5

RING = ("comp", "dom")
LANES = 128
HALO = OY // LANES
COS = [math.cos(k * math.pi / 3.0) for k in range(6)]
SIN = [0.0 if k % 3 == 0 else math.sin(k * math.pi / 3.0) for k in range(6)]

ROW_EDGE, ROW_BREADTH, ROW_ETA, ROW_U, ROW_V, ROW_SST = 0, 4, 8, 10, 12, 14
ROW_PX, ROW_PY, ROW_IDX, ROW_W, ROWS_FIRST = 16, 18, 24, 40, 56
MARK_COLUMN, MARK_OWN, MARK_HEAT, MARK_ANSWER, MARK_PLACE, MARK_READER = range(6)
PER_DEST, ROW_HEAT, ROW_IDS = 16, 12, 14


def swapped(value, first):
    count = lax.axis_size(RING)
    pairs = []
    for i in range(first, count + first, 2):
        pairs += [(i % count, (i + 1) % count), ((i + 1) % count, i % count)]
    return lax.ppermute(value, RING, pairs)


def swap_both(far, near):
    got_far = swapped(far, 1)
    return got_far, swapped(near, 0)


class Received:
    def __init__(self, far, near, odd):
        self.far, self.near, self.odd = far, near, odd

    def flag(self, rows):
        return jnp.broadcast_to(self.odd[0:1], rows.shape) > 0

    def prev(self, *cut):
        far, near = self.far[cut], self.near[cut]
        return jnp.where(self.flag(far), near, far)

    def next(self, *cut):
        far, near = self.far[cut], self.near[cut]
        return jnp.where(self.flag(far), far, near)

    def rim(self, side, row):
        cut = slice(row, row + HALO)
        return self.prev(cut) if side == 0 else self.next(cut)

    def rims(self, side, rows):
        return tuple(self.rim(side, row) for row in rows)


def arrange(up, dn, odd, far, near):
    flag = jnp.broadcast_to(odd[0:1], up.shape) > 0
    far[...] = jnp.where(flag, up[...], dn[...])
    near[...] = jnp.where(flag, dn[...], up[...])


def exchange(value):
    return lax.all_to_all(value, RING, split_axis=0, concat_axis=0, tiled=True)


def gll_matrix():
    points = np.array([-1.0, -1.0 / np.sqrt(5.0), 1.0 / np.sqrt(5.0), 1.0])
    barycentric = [
        1.0 / np.prod([points[s] - points[o] for o in range(4) if o != s]) for s in range(4)
    ]
    table = np.zeros((4, 4))
    for t in range(4):
        for s in range(4):
            if t != s:
                table[t, s] = barycentric[s] / barycentric[t] / (points[t] - points[s])
    for t in (0, 3):
        table[t, t] = -np.sum(table[t])
    return [[float(np.float32(value)) for value in line] for line in table]


GLL = gll_matrix()


def vmem(count):
    return [pl.BlockSpec(memory_space=pltpu.VMEM)] * count


def hbm(count):
    return [pl.BlockSpec(memory_space=pltpu.HBM)] * count


def in_hbm(*arrays):
    return [pltpu.with_memory_space_constraint(array, pltpu.HBM) for array in arrays]


def smem(count):
    return [pl.BlockSpec(memory_space=pltpu.SMEM)] * count


def shape_of(*dims, dtype=jnp.float32):
    return jax.ShapeDtypeStruct(dims, dtype)


PARAMS = pltpu.CompilerParams(vmem_limit_bytes=24 * 1024 * 1024)


def lane_take(rows, ids):
    return jnp.take_along_axis(rows, ids, axis=1, mode="promise_in_bounds")


def wide(row, lines):
    return jnp.broadcast_to(row, (lines, row.shape[1]))


def side_ids(pn):
    count = pn.shape[1]
    bits = count.bit_length() - 1
    table = pn[...]
    ids = [table[k : k + 1] & (count - 1) for k in range(4)]
    home = lax.shift_right_logical(table[0:1], bits)
    near = [lax.shift_right_logical(table[k : k + 1], bits) == home for k in range(4)]
    return ids, near


def element_step(state, east_wind, north_wind, scale, facing):
    jumps = [None] * 16
    sides = (
        (0, 1, 2, 3),
        (3, 7, 11, 15),
        (12, 13, 14, 15),
        (0, 4, 8, 12),
    )
    for k in range(4):
        for n, p in enumerate(sides[k]):
            term = facing[k][n] - state[p]
            jumps[p] = term if jumps[p] is None else jumps[p] + term
    result = []
    for p in range(16):
        i, j = p % 4, p // 4
        grad_x = grad_y = None
        for m in range(4):
            if GLL[i][m] != 0.0:
                term = GLL[i][m] * state[m + 4 * j]
                grad_x = term if grad_x is None else grad_x + term
            if GLL[j][m] != 0.0:
                term = GLL[j][m] * state[i + 4 * m]
                grad_y = term if grad_y is None else grad_y + term
        change = -(east_wind(p) * grad_x + north_wind(p) * grad_y)
        if jumps[p] is not None:
            change = change + JUMP_WEIGHT * jumps[p]
        result.append(state[p] + scale * change)
    return result


def load(pairs, sems):
    copies = [
        pltpu.make_async_copy(source, target, sems.at[n])
        for n, (source, target) in enumerate(pairs)
    ]
    for copy in copies:
        copy.start()
    return copies


def as_column(row):
    count = row.shape[1]
    return jnp.transpose(jnp.broadcast_to(row, (count, count)))


def edge_tables(partner, remote):
    count = partner.shape[1]
    pack = count // 4
    lane = lax.broadcasted_iota(jnp.int32, (count, count), 1)
    line = lax.broadcasted_iota(jnp.int32, (count, count), 0)
    flag = jnp.where(remote, 1.0, 0.0)
    rank = jnp.sum(jnp.where(line < lane, as_column(flag), 0.0), axis=0, keepdims=True)
    rank = as_column(jnp.where(remote, rank, -1.0))
    slot = (lane & (pack - 1)).astype(jnp.float32)
    chosen = jnp.sum(
        jnp.where(rank == slot, line.astype(jnp.float32), 0.0), axis=0, keepdims=True
    ).astype(jnp.int32)
    key = jnp.where(remote, partner, 2 * count).astype(jnp.float32)
    before = jnp.where(as_column(key) < key, 1.0, 0.0)
    place = jnp.sum(before, axis=0, keepdims=True).astype(jnp.int32)
    return chosen, jnp.minimum(place, pack - 1)


def rank_among_equals(row, most):
    count = row.shape[1]
    earlier = lax.broadcasted_iota(jnp.int32, (count, count), 0) < lax.broadcasted_iota(
        jnp.int32, (count, count), 1
    )
    number = row.astype(jnp.float32)
    same = as_column(number) == number
    return jnp.minimum(jnp.sum(jnp.where(same & earlier, 1, 0), axis=0, keepdims=True), most)


def slot_rows(holder_row, rank, down_row, devices, tiles):
    blocks = holder_row.shape[1]
    target = lax.broadcasted_iota(jnp.int32, (devices, blocks), 0)
    after = jnp.where(holder_row + 1 == devices, 0, holder_row + 1)
    before = jnp.where(holder_row == 0, devices - 1, holder_row - 1)
    last = down_row - (tiles - HALO)
    lane = lax.broadcasted_iota(jnp.int32, (devices, LANES), 1)
    result = jnp.full((devices, LANES), -1.0, jnp.float32)
    for n, (owner, number) in enumerate(
        (
            (holder_row, down_row),
            (after, jnp.where(last >= 0, tiles + last, -1)),
            (before, jnp.where(down_row < HALO, tiles + HALO + down_row, -1)),
        )
    ):
        for slot in range(CAP):
            named = (target == owner) & (rank == slot)
            value = jnp.sum(
                jnp.where(named, (number + 1).astype(jnp.float32), 0.0), axis=1, keepdims=True
            )
            result = jnp.where(lane == CAP * n + slot, value - 1.0, result)
    return result


def home_facing(state, ids, near):
    return [
        [lane_take(state[12 + n], ids[0]) for n in range(4)],
        [jnp.where(near[1], lane_take(state[4 * n], ids[1]), 0.0) for n in range(4)],
        [lane_take(state[n], ids[2]) for n in range(4)],
        [jnp.where(near[3], lane_take(state[3 + 4 * n], ids[3]), 0.0) for n in range(4)],
    ]


def plan_kernel(
    air_hbm, eastern_hbm, northern_hbm, breadth_hbm, pn_hbm, holder_hbm, across_hbm, down_hbm,
    nb_hbm, span_hbm, flow_hbm, sst_hbm, flux, slots, breadth, pn, marks, idx, w, u, v, sst,
    air, eastern, northern, holder, across, down, nb, span, flow, lists, sems, *, devices, tiles
):
    copies = load(
        (
            (air_hbm.at[:, pl.ds(0, 8), :], air),
            (eastern_hbm.at[:, pl.ds(0, 16), :], eastern),
            (northern_hbm.at[:, pl.ds(0, 16), :], northern),
            (breadth_hbm, breadth),
            (pn_hbm, pn),
            (holder_hbm, holder),
            (across_hbm, across),
            (down_hbm, down),
            (nb_hbm, nb),
            (span_hbm, span),
            (flow_hbm, flow),
            (sst_hbm, sst),
        ),
        sems,
    )
    for copy in copies:
        copy.wait()
    rank = rank_among_equals(holder[...], CAP - 1)
    place = across[...] * 2 + rank_among_equals(across[...], 1)
    blocks = place.shape[1]
    line = lax.broadcasted_iota(jnp.int32, (blocks, blocks), 0).astype(jnp.float32)
    lane = lax.broadcasted_iota(jnp.int32, (blocks, blocks), 1).astype(jnp.float32)
    here = as_column(place.astype(jnp.float32)) == lane
    reader = jnp.sum(jnp.where(here, line, 0.0), axis=0, keepdims=True).astype(jnp.int32)
    lists[...] = jnp.zeros_like(lists)
    for mark, row in (
        (MARK_COLUMN, across[...]),
        (MARK_OWN, holder[...] * 8 + 2 * rank),
        (MARK_HEAT, holder[...] * 8 + 4 + rank),
        (MARK_ANSWER, holder[...] * CAP + rank),
        (MARK_PLACE, place),
        (MARK_READER, reader),
    ):
        lists[mark : mark + 1] = row
    copy = pltpu.make_async_copy(lists, marks, sems.at[0])
    copy.start()
    slots[...] = slot_rows(holder[...], rank, down[...], devices, tiles)
    fill_tables(nb, span, flow, idx, w, u, v)
    lines, count = air.shape[1], air.shape[2]
    ids, near = side_ids(pn)
    ids = [wide(line, lines) for line in ids]
    state = [air[p] for p in range(16)]
    u = [eastern[p].astype(jnp.float32)[0:lines] for p in range(16)]
    v = [northern[p].astype(jnp.float32)[0:lines] for p in range(16)]
    result = element_step(
        state, lambda p: u[p], lambda p: v[p], STEP_SIZE * breadth[...],
        home_facing(state, ids, near)
    )
    for p in range(16):
        speed = jnp.sqrt(u[p] * u[p] + v[p] * v[p] + 1.0)
        flux[p, 0:1] = (speed * result[p])[0:1]
        flux[p, 1:2] = (speed * u[p])[0:1]
        flux[p, 2:3] = (speed * v[p])[0:1]
        flux[p, 3:4] = speed[0:1]
        flux[p, 4:8] = jnp.zeros((4, count), jnp.float32)
    copy.wait()


def local_step_kernel(
    air_hbm, eastern_hbm, northern_hbm, breadth, pn, odd, loc, eastern, northern, east, west,
    far, near_swap, places, air, sems
):
    copies = load(((air_hbm, air), (eastern_hbm, eastern), (northern_hbm, northern)), sems)
    count = breadth.shape[1]
    lines = 16
    ids, near = side_ids(pn)
    chosen_east, place_east = edge_tables(ids[1], jnp.logical_not(near[1]))
    chosen_west, place_west = edge_tables(ids[3], jnp.logical_not(near[3]))
    places[...] = jnp.zeros_like(places)
    places[0:1] = place_east
    places[1:2] = place_west
    chosen_east, chosen_west = wide(chosen_east, lines), wide(chosen_west, lines)
    group = lax.broadcasted_iota(jnp.int32, (lines, count), 1) // (count // 4)
    scale = STEP_SIZE * breadth[...]
    ids = [wide(line, lines) for line in ids]

    def packed(values, chosen):
        result = jnp.zeros((lines, count), jnp.float32)
        for n in range(4):
            result = jnp.where(group == n, lane_take(values[n], chosen), result)
        return result

    for copy in copies:
        copy.wait()
    levels = air.shape[1]

    def chunk(c, carry):
        at = pl.multiple_of(c * lines, lines)
        rows = pl.ds(at, lines)
        state = [air[p, rows] for p in range(16)]
        result = element_step(
            state,
            lambda p: eastern[p, rows].astype(jnp.float32),
            lambda p: northern[p, rows].astype(jnp.float32),
            scale,
            home_facing(state, ids, near),
        )
        for p in range(16):
            loc[p, rows] = result[p]
        here = pl.ds(pl.multiple_of(4 * HALO + at, 8), lines)
        beyond = pl.ds(pl.multiple_of(4 * HALO + levels + at, 8), lines)
        for n in range(4):
            east[n, rows] = state[3 + 4 * n].astype(jnp.bfloat16)
            west[n, rows] = state[4 * n].astype(jnp.bfloat16)
        flag = jnp.broadcast_to(odd[0:1], (lines, count)) > 0
        for target, values in ((here, state), (beyond, result)):
            to_next = packed([values[3 + 4 * n] for n in range(4)], chosen_east)
            to_prev = packed([values[4 * n] for n in range(4)], chosen_west)
            far[target] = jnp.where(flag, to_next, to_prev)
            near_swap[target] = jnp.where(flag, to_prev, to_next)
        return carry

    lax.fori_loop(0, levels // lines, chunk, 0)


def second_step_kernel(
    loc, eastern, northern, breadth, pn, east, west, far, near_swap, places, first_far,
    first_near, odd, surface, out_hbm, out, sems
):
    ids, near = side_ids(pn)
    levels, count = loc.shape[1], loc.shape[2]
    lines = 16
    pack = count // 4
    scale = STEP_SIZE * breadth[...]
    jump = JUMP_WEIGHT * scale
    ids = [wide(line, lines) for line in ids]
    got = Received(far, near_swap, odd)
    first = Received(first_far, first_near, odd)
    row = slice(ROW_BREADTH, ROW_BREADTH + 1)
    factors = [
        JUMP_WEIGHT * STEP_SIZE * lane_take(wide(line, lines), ids[side])
        for side, line in ((1, first.next(row)), (3, first.prev(row)))
    ]
    spots = [
        [wide(places[n : n + 1] + m * pack, lines) for m in range(4)] for n in (0, 1)
    ]

    def copy_out(c):
        rows = pl.ds(pl.multiple_of(c * lines, lines), lines)
        return pltpu.make_async_copy(out.at[:, rows, :], out_hbm.at[:, rows, :], sems.at[c])

    def chunk(c, carry):
        at = pl.multiple_of(c * lines, lines)
        rows = pl.ds(at, lines)
        now = pl.ds(pl.multiple_of(4 * HALO + at, 8), lines)
        later = pl.ds(pl.multiple_of(4 * HALO + levels + at, 8), lines)
        state = [loc[p, rows] for p in range(16)]

        def across(own, there_now, there_next, side, factor, spot):
            values, beyond = [], []
            for n in range(4):
                values.append(jnp.where(near[side], 0.0, lane_take(there_now, spot[n])))
                beyond.append(
                    lane_take(there_next, spot[n]) + factor * own[n, rows].astype(jnp.float32)
                )
            return values, beyond

        east_now, east_beyond = across(
            east, got.next(now), got.next(later), 1, factors[0], spots[0]
        )
        west_now, west_beyond = across(
            west, got.prev(now), got.prev(later), 3, factors[1], spots[1]
        )
        for n in range(4):
            state[3 + 4 * n] = state[3 + 4 * n] + jump * east_now[n]
            state[4 * n] = state[4 * n] + jump * west_now[n]
        facing = home_facing(state, ids, near)
        facing[1] = [jnp.where(near[1], facing[1][n], east_beyond[n]) for n in range(4)]
        facing[3] = [jnp.where(near[3], facing[3][n], west_beyond[n]) for n in range(4)]
        result = element_step(
            state,
            lambda p: eastern[p, rows].astype(jnp.float32),
            lambda p: northern[p, rows].astype(jnp.float32),
            scale,
            facing,
        )
        for p in range(16):
            out[p, rows] = result[p]

        @pl.when(c == 0)
        def _():
            for p in range(16):
                lowest = out[p, 0:1]
                out[p, 0:1] = lowest + NUDGING_SPEED * (surface[p : p + 1] - lowest)

        copy_out(c).start()
        return carry

    lax.fori_loop(0, levels // lines, chunk, 0)

    def finish(c, carry):
        copy_out(c).wait()
        return carry

    lax.fori_loop(0, levels // lines, finish, 0)


def home_sums_kernel(marks, flux, weights, own):
    own[...] = jnp.zeros_like(own)
    for b in range(weights.shape[0]):
        sums = jnp.dot(
            flux[marks[MARK_COLUMN, b]].astype(jnp.bfloat16), weights[b], preferred_element_type=jnp.float32
        )
        row = marks[MARK_OWN, b]
        own[pl.ds(row, 1), :] = sums[1:2]
        own[pl.ds(row + 1, 1), :] = sums[2:3]
        own[pl.ds(marks[MARK_HEAT, b], 1), :] = sums[0:1]


def forward_kernel(
    marks, home, flux, slots, breadth, pn, first_far, first_near, odd, weights, out_hbm, out, extra,
    sems, *, devices
):
    ids, near = side_ids(pn)
    jump = (JUMP_WEIGHT * STEP_SIZE) * breadth[...]
    first = Received(first_far, first_near, odd)
    from_east = lane_take(first.next(slice(0, 8)), wide(ids[1], 8))
    from_west = lane_take(first.prev(slice(0, 8)), wide(ids[3], 8))
    from_east = jnp.where(near[1], 0.0, jump * from_east)
    from_west = jnp.where(near[3], 0.0, jump * from_west)
    extra[...] = jnp.zeros_like(extra)
    for n in range(4):
        for p, change in ((3 + 4 * n, from_east), (4 * n, from_west)):
            line = wide(flux[p, 3:4] * change[n : n + 1], 8).astype(jnp.bfloat16)
            for reader in range(2):
                b = marks[MARK_READER, 2 * p + reader]
                sums = jnp.dot(line, weights[b], preferred_element_type=jnp.float32)
                extra[pl.ds(marks[MARK_HEAT, b], 1), :] = sums[0:1]
    line = lax.broadcasted_iota(jnp.int32, (8, LANES), 0)
    part, copies = devices // 4, []
    for d in range(devices):
        mine, prev, following = (
            home[8 * (n % devices) : 8 * (n % devices) + 8] for n in (d, d - 1, d + 1)
        )
        top = jnp.concatenate([mine[0:4], prev[0:4]], axis=0)
        bottom = jnp.where(line < 4, following, mine + extra[8 * d : 8 * d + 8])
        bottom = jnp.where(line == ROW_IDS - 8, wide(slots[d : d + 1], 8), bottom)
        out[d] = jnp.concatenate([top, bottom], axis=0).astype(jnp.bfloat16)
        if (d + 1) % part == 0:
            copies.append(
                pltpu.make_async_copy(
                    out.at[pl.ds(d + 1 - part, part)],
                    out_hbm.at[pl.ds(d + 1 - part, part)],
                    sems.at[d // part],
                )
            )
            copies[-1].start()
    for copy in copies:
        copy.wait()


def back_kernel(marks, arrived, weights, surface, lines, share):
    lines[...] = arrived[...].reshape(lines.shape)
    for b in range(weights.shape[0]):
        line = lines[pl.ds(marks[MARK_ANSWER, b], 1), :]
        share[marks[MARK_PLACE, b]] = lax.dot_general(
            wide(line, 8).astype(jnp.bfloat16),
            weights[b],
            (((1,), (1,)), ((), ())),
            preferred_element_type=jnp.float32,
        )
    for p in range(surface.shape[0]):
        surface[p : p + 1] = share[2 * p, 0:1] + share[2 * p + 1, 0:1]


def split_index(idx):
    return lax.shift_right_arithmetic(idx, 7), idx & (LANES - 1)


def by_tiles(function, idx):
    if idx.shape[0] <= 8:
        return function(idx)
    return jnp.concatenate(
        [function(idx[at : at + 8]) for at in range(0, idx.shape[0], 8)], axis=0
    )


def pick(idx, sources):
    def one(idx):
        high, low = split_index(idx)
        result = jnp.zeros(idx.shape, jnp.float32)
        for number, line in sources:
            result = jnp.where(high == number, lane_take(wide(line, idx.shape[0]), low), result)
        return result

    return by_tiles(one, idx)


def fill_pack(values, packed, scales):
    half = values.shape[0] // 2
    numbers = []
    for n, part in enumerate((values[:half], values[half:])):
        top = jnp.max(part, axis=(0, 1), keepdims=True)
        bottom = jnp.min(part, axis=(0, 1), keepdims=True)
        middle = 0.5 * (top + bottom)
        reach = jnp.maximum(jnp.maximum(top - middle, middle - bottom), 1e-30)
        numbers.append(jnp.floor((part - middle) * (32767.0 / reach) + 0.5).astype(jnp.int32))
        scales[n : n + 1] = jnp.broadcast_to(reach * (1.0 / 32767.0), (1, LANES))
        scales[2 + n : 3 + n] = jnp.broadcast_to(middle, (1, LANES))
    packed[...] = (numbers[1] << 16) | (numbers[0] & 0xFFFF)


def pick_own(idx, packed, scales):
    half = packed.shape[0]

    def one(idx):
        lines = idx.shape[0]
        high, low = split_index(idx)
        own = high - HALO
        upper = own >= half
        row = jnp.where(upper, own - half, own)
        words = jnp.zeros(idx.shape, jnp.int32)
        for r in range(half):
            words = jnp.where(row == r, lane_take(wide(packed[r : r + 1], lines), low), words)
        number = jnp.where(upper, words >> 16, (words << 16) >> 16)
        scale = jnp.where(upper, wide(scales[1:2], lines), wide(scales[0:1], lines))
        middle = jnp.where(upper, wide(scales[3:4], lines), wide(scales[2:3], lines))
        inside = (own >= 0) & (own < 2 * half)
        return jnp.where(inside, number.astype(jnp.float32) * scale + middle, 0.0)

    return by_tiles(one, idx)


def combine(terms, factors):
    total = None
    for term, factor in zip(terms, factors):
        if factor != 0.0:
            total = factor * term if total is None else total + factor * term
    return total


def pair_sums(table):
    terms = [table[HALO * k : HALO * (k + 1)] for k in range(6)]
    return combine(terms, COS), combine(terms, SIN)


def rim_partial(rim_idx, rim_w, eta, packed, scales, first):
    rows = rim_idx.shape[0]
    found = pick_own(rim_idx, packed, scales)
    centre = eta[first : first + HALO]
    centre = jnp.concatenate([centre] * (rows // HALO), axis=0)
    return pair_sums(rim_w * (found - centre))


def prepare_kernel(
    air_hbm, breadth_hbm, pn_hbm, eta_hbm, sst_hbm, flow_hbm, nb_hbm, span_hbm,
    rim_idx, rim_w, eta, eta_pack, eta_scale, far, near, odd,
    up, dn, air, breadth, pn, sst, flow, nb, span, sems
):
    tiles, cells = eta.shape[0], nb_hbm.shape[1]
    pairs = [(air_hbm.at[:, 3 * side, pl.ds(0, 8), :], air.at[side]) for side in (0, 1)]
    pairs.append((eta_hbm, eta))
    for side, at in ((0, 0), (1, cells - OY)):
        cut = pl.ds(at, OY)
        pairs.append((nb_hbm.at[:, cut], nb.at[side]))
        pairs.append((span_hbm.at[:, cut], span.at[side]))
        pairs.append((flow_hbm.at[:, cut], flow.at[side]))
    for side, at in ((0, 0), (1, tiles - 8)):
        pairs.append((sst_hbm.at[pl.ds(at, 8)], sst.at[side]))
    pairs.append((breadth_hbm, breadth))
    pairs.append((pn_hbm, pn))
    copies = load(pairs, sems)
    for copy in copies:
        copy.wait()
    shard = lax.shift_right_logical(pn[0:1], pn.shape[1].bit_length() - 1)
    odd[...] = wide(shard & 1, 8)
    fill_pack(eta[...], eta_pack, eta_scale)
    for side, first in ((0, 0), (1, tiles - HALO)):
        rim_idx[side, 12:16] = jnp.full((4, LANES), -1, jnp.int32)
        rim_w[side, 12:16] = jnp.zeros((4, LANES), jnp.float32)
        for j in range(HALO):
            cut = slice(j * LANES, (j + 1) * LANES)
            links = nb[side, :, cut]
            factors = slot_factors(links, span[side, :, cut])
            for k in range(6):
                at = HALO * k + j
                rim_idx[side, at : at + 1] = links[k : k + 1]
                rim_w[side, at : at + 1] = factors[k : k + 1]
    for side, first, target in ((0, 0, dn), (1, tiles - HALO, up)):
        target[...] = jnp.zeros_like(target)
        for n in range(4):
            target[ROW_EDGE + n : ROW_EDGE + n + 1] = air[side, n, 0:1]
        target[ROW_BREADTH : ROW_BREADTH + 1] = breadth[...]
        part_x, part_y = rim_partial(
            rim_idx[side], rim_w[side], eta, eta_pack, eta_scale, first
        )
        cut = slice(first, first + HALO)
        target[ROW_ETA : ROW_ETA + HALO] = eta[cut]
        for j in range(HALO):
            here = slice(j * LANES, (j + 1) * LANES)
            target[ROW_U + j : ROW_U + j + 1] = flow[side, 0:1, here]
            target[ROW_V + j : ROW_V + j + 1] = flow[side, 1:2, here]
        start = first % 8
        target[ROW_SST : ROW_SST + HALO] = sst[side, start : start + HALO]
        target[ROW_PX : ROW_PX + HALO] = part_x
        target[ROW_PY : ROW_PY + HALO] = part_y
        target[ROW_IDX : ROW_IDX + 16] = rim_idx[side].astype(jnp.float32)
        target[ROW_W : ROW_W + 16] = rim_w[side]
    arrange(up, dn, odd, far, near)


def slot_factors(links, span):
    return jnp.where(links >= 0, span * (1.0 / 3.0), 0.0)


def fill_tables(nb, span, flow, idx, w, u, v):
    tiles = u.shape[0]
    for r in range(tiles):
        cut = slice(r * LANES, (r + 1) * LANES)
        links = nb[:, cut]
        factors = slot_factors(links, span[:, cut])
        for k in range(6):
            idx[k * tiles + r : k * tiles + r + 1] = links[k : k + 1]
            w[k * tiles + r : k * tiles + r + 1] = factors[k : k + 1]
        u[r : r + 1] = flow[0:1, cut]
        v[r : r + 1] = flow[1:2, cut]


def own_gradient(idx, w, eta, packed, scales, gx, gy):
    tiles = eta.shape[0]

    def chunk(at):
        centre = eta[pl.ds(at, 8)]
        terms = []
        for k in range(6):
            found = pick_own(idx[pl.ds(k * tiles + at, 8)], packed, scales)
            terms.append(w[pl.ds(k * tiles + at, 8)] * (found - centre))
        gx[pl.ds(at, 8)] = combine(terms, COS)
        gy[pl.ds(at, 8)] = combine(terms, SIN)

    for c in range(tiles // 8):
        chunk(c * 8)


def own_spread(at, idx, w, flow, packed, scales):
    tiles = flow.shape[1]
    total = jnp.zeros((8, LANES), jnp.float32)
    for kk in range(3):
        centre = flow[kk, pl.ds(at, 8)]
        for k, sign in ((kk, 1.0), (kk + 3, -1.0)):
            rows = pl.ds(k * tiles + at, 8)
            found = pick_own(idx[rows], packed.at[kk], scales.at[kk])
            total = total + sign * w[rows] * (found - centre)
    return total


def inner_kernel(
    idx, w, eta, eta_pack, eta_scale, u, v, fu, fv, eta_part, u_part, v_part,
    flow, flow_pack, flow_scale
):
    current_kernel(idx, w, eta, eta_pack, eta_scale, u, v, fu, fv, u_part, v_part)
    height_kernel(idx, w, eta, u_part, v_part, eta_part, flow, flow_pack, flow_scale)


def current_kernel(idx, w, eta, eta_pack, eta_scale, u, v, fu, fv, u_part, v_part):
    own_gradient(idx, w, eta, eta_pack, eta_scale, u_part, v_part)
    u_part[...] = DAMPING * u[...] - GRAVITY * u_part[...] + WIND_GAIN * fu[...]
    v_part[...] = DAMPING * v[...] - GRAVITY * v_part[...] + WIND_GAIN * fv[...]


def height_kernel(idx, w, eta, u_part, v_part, eta_part, flow, flow_pack, flow_scale):
    tiles = eta.shape[0]
    fill_flow(flow, u_part[...], v_part[...])
    for kk in range(3):
        fill_pack(flow[kk], flow_pack.at[kk], flow_scale.at[kk])

    def chunk(at):
        total = own_spread(at, idx, w, flow, flow_pack, flow_scale)
        eta_part[pl.ds(at, 8)] = eta[pl.ds(at, 8)] - DEPTH_RATE * total

    for c in range(tiles // 8):
        chunk(c * 8)


def first_gradient_kernel(
    idx, w, eta, eta_pack, eta_scale, sst, first_far, first_near, odd, rim_idx, rim_w,
    gx, gy, base, sst_pack, sst_scale
):
    own_gradient(idx, w, eta, eta_pack, eta_scale, gx, gy)
    tiles = eta.shape[0]
    fill_pack(sst[...], sst_pack, sst_scale)

    def chunk(at):
        centre = sst[pl.ds(at, 8)]
        total = jnp.zeros_like(centre)
        for k in range(6):
            found = pick_own(idx[pl.ds(k * tiles + at, 8)], sst_pack, sst_scale)
            total = total + w[pl.ds(k * tiles + at, 8)] * (found - centre)
        base[pl.ds(at, 8)] = centre + (0.5 * SPREADING_COEFF) * total

    for c in range(tiles // 8):
        chunk(c * 8)
    first = Received(first_far, first_near, odd)
    for side, start, offset in ((0, 0, 0), (1, tiles - HALO, tiles + HALO)):
        rim = first.rim(side, ROW_SST)
        sources = [(offset + q, rim[q : q + 1]) for q in range(HALO)]
        found = rim_w[side] * pick(rim_idx[side], sources)
        total = combine([found[HALO * k : HALO * (k + 1)] for k in range(6)], [1.0] * 6)
        rows = slice(start, start + HALO)
        base[rows] = base[rows] + (0.5 * SPREADING_COEFF) * total


def fill_flow(flow, u, v):
    flow[0] = u
    for kk in (1, 2):
        flow[kk] = COS[kk] * u + SIN[kk] * v


def side_currents(eta, sides, fside, before, after, side_idx, side_w):
    tiles = eta.shape[0]
    slopes = []
    for side, offset, first, part in (
        (0, tiles + HALO, 0, before),
        (1, 0, tiles - HALO, after),
    ):
        sources = [(offset + q, eta[first + q : first + q + 1]) for q in range(HALO)]
        add_x, add_y = pair_sums(side_w[side] * pick(side_idx[side], sources))
        slopes.append((part[1] + add_x, part[2] + add_y))
    slope = jnp.concatenate([slopes[0][0], slopes[1][0], slopes[0][1], slopes[1][1]], axis=0)
    return DAMPING * sides[...] - GRAVITY * slope + WIND_GAIN * fside[...]


def rim_slopes(rim_idx, rim_w, before, after, tiles):
    result = []
    for side, offset, part in ((0, 0, before), (1, tiles + HALO, after)):
        sources = [(offset + q, part[0][q : q + 1]) for q in range(HALO)]
        result.append(pair_sums(rim_w[side] * pick(rim_idx[side], sources)))
    return result


def send_rims(eta, eta_pack, eta_scale, rim_idx, rim_w, odd, far, near, up, dn):
    tiles = eta.shape[0]
    fill_pack(eta[...], eta_pack, eta_scale)
    for side, first, target in ((0, 0, dn), (1, tiles - HALO, up)):
        part_x, part_y = rim_partial(
            rim_idx[side], rim_w[side], eta, eta_pack, eta_scale, first
        )
        target[0:HALO] = eta[first : first + HALO]
        target[HALO : 2 * HALO] = part_x
        target[2 * HALO : 3 * HALO] = part_y
        target[3 * HALO : 4 * HALO] = jnp.zeros((HALO, LANES), jnp.float32)
    rows = pl.ds(0, 4 * HALO)
    arrange(up, dn, odd, far.at[rows], near.at[rows])


def first_subcycle(
    gx, gy, eta, u, v, sides, fu, fv, fside, before, after, idx, w, side_idx, side_w,
    rim_idx, rim_w, flow, flow_pack, flow_scale, flow_outer, eta_new, u_new, v_new, sides_new,
    midway
):
    tiles = eta.shape[0]
    u_new[...] = DAMPING * u[...] - GRAVITY * gx[...] + WIND_GAIN * fu[...]
    v_new[...] = DAMPING * v[...] - GRAVITY * gy[...] + WIND_GAIN * fv[...]
    slopes = rim_slopes(rim_idx, rim_w, before, after, tiles)
    for first, (add_x, add_y) in zip((0, tiles - HALO), slopes):
        rows = slice(first, first + HALO)
        u_new[rows] = u_new[rows] - GRAVITY * add_x
        v_new[rows] = v_new[rows] - GRAVITY * add_y
    sides_next = side_currents(eta, sides, fside, before, after, side_idx, side_w)
    sides_new[...] = sides_next
    fill_flow(flow, u_new[...], v_new[...])
    fill_flow(flow_outer, sides_next[0 : 2 * HALO], sides_next[2 * HALO : 4 * HALO])
    for kk in range(3):
        fill_pack(flow[kk], flow_pack.at[kk], flow_scale.at[kk])

    def chunk(at):
        total = own_spread(at, idx, w, flow, flow_pack, flow_scale)
        eta_new[pl.ds(at, 8)] = eta[pl.ds(at, 8)] - DEPTH_RATE * total

    for c in range(tiles // 8):
        if c == tiles // 16:
            midway()
        chunk(c * 8)
    for side, first, offset in ((0, 0, 0), (1, tiles - HALO, tiles + HALO)):
        total = jnp.zeros((HALO, LANES), jnp.float32)
        for kk in range(3):
            at = side * HALO
            sources = [(offset + q, flow_outer[kk, at + q : at + q + 1]) for q in range(HALO)]
            found = rim_w[side] * pick(rim_idx[side], sources)
            total = (
                total
                + found[HALO * kk : HALO * (kk + 1)]
                - found[HALO * (kk + 3) : HALO * (kk + 4)]
            )
        rows = slice(first, first + HALO)
        eta_new[rows] = eta_new[rows] - DEPTH_RATE * total


def outer_subcycle(
    eta, eta_part, u_part, v_part, sides, fside, before, after, idx, w, side_idx, side_w,
    rim_idx, rim_w, flow_outer, eta_new, u_new, v_new
):
    tiles = eta.shape[0]
    slopes = rim_slopes(rim_idx, rim_w, before, after, tiles)
    sides_next = side_currents(eta, sides, fside, before, after, side_idx, side_w)
    u_new[...] = u_part[...]
    v_new[...] = v_part[...]
    changes_u = [-GRAVITY * slopes[side][0] for side in (0, 1)]
    changes_v = [-GRAVITY * slopes[side][1] for side in (0, 1)]
    for side, first in ((0, 0), (1, tiles - HALO)):
        rows = slice(first, first + HALO)
        u_new[rows] = u_new[rows] + changes_u[side]
        v_new[rows] = v_new[rows] + changes_v[side]
    fill_flow(
        flow_outer,
        jnp.concatenate([sides_next[0 : 2 * HALO]] + changes_u, axis=0),
        jnp.concatenate([sides_next[2 * HALO : 4 * HALO]] + changes_v, axis=0),
    )
    for c in range(tiles // 8):
        at = c * 8
        total = jnp.zeros((8, LANES), jnp.float32)
        for kk in range(3):
            line = lambda n: flow_outer[kk, n : n + 1]
            sources = [(HALO + q, line(2 * HALO + q)) for q in range(HALO)]
            sources += [(tiles + q, line(3 * HALO + q)) for q in range(HALO)]
            if at == 0:
                sources += [(q, line(q)) for q in range(HALO)]
            if at + 8 == tiles:
                sources += [(tiles + HALO + q, line(HALO + q)) for q in range(HALO)]
            total = (
                total
                + w[kk * tiles + at : kk * tiles + at + 8]
                * pick(idx[kk * tiles + at : kk * tiles + at + 8], sources)
                - w[(kk + 3) * tiles + at : (kk + 3) * tiles + at + 8]
                * pick(idx[(kk + 3) * tiles + at : (kk + 3) * tiles + at + 8], sources)
            )
        eta_new[at : at + 8] = eta_part[at : at + 8] - DEPTH_RATE * total
    for side, first in ((0, 0), (1, tiles - HALO)):
        centre = jnp.zeros((HALO, LANES), jnp.float32)
        for kk in range(3):
            factor = (
                rim_w[side, HALO * kk : HALO * (kk + 1)]
                - rim_w[side, HALO * (kk + 3) : HALO * (kk + 4)]
            )
            start = (2 + side) * HALO
            centre = centre + factor * flow_outer[kk, start : start + HALO]
        rows = slice(first, first + HALO)
        eta_new[rows] = eta_new[rows] + DEPTH_RATE * centre
    return sides_next


def first_ocean_kernel(
    arrived, first_far, first_near, odd, gx, gy, eta, u, v, idx, w, rim_idx, rim_w,
    far_old, near_old, base, eta_new, eta_pack, eta_scale, u_new, v_new, sides_new, far, near,
    fu, fv, fside, side_idx, side_w, heat, answers_hbm,
    flow, flow_pack, flow_scale, flow_outer, sides, up, dn, parts, answers, sems
):
    tiles = eta.shape[0]
    devices = arrived.shape[0]
    parts[...] = arrived[...].astype(jnp.float32).reshape(parts.shape)

    def rows_of(r):
        return parts[pl.ds(r, devices, stride=PER_DEST), :]

    ids = rows_of(ROW_IDS)
    number = lax.broadcasted_iota(jnp.int32, (devices, LANES), 1).astype(jnp.float32)
    nothing = jnp.zeros((devices, LANES), jnp.float32)
    chosen, lines = [], []
    for j in range(3 * CAP):
        chosen.append(jnp.where(ids[:, j : j + 1] == number, 1.0, 0.0).astype(jnp.bfloat16))
        first = rows_of(ROW_HEAT + j) if j < CAP else nothing
        lines.append(jnp.concatenate([first, rows_of(2 * j), rows_of(2 * j + 1)], axis=1))
    forcing = lax.dot_general(
        jnp.concatenate(chosen, axis=0),
        jnp.concatenate(lines, axis=0).astype(jnp.bfloat16),
        (((0,), (0,)), ((), ())),
        preferred_element_type=jnp.float32,
    )
    heat[...] = forcing[0:tiles, 0:LANES]
    half = (base[...] + WARMING_COEFF * forcing[0:tiles, 0:LANES]).astype(jnp.bfloat16)
    for j in range(CAP):
        answers[pl.ds(j, devices, stride=CAP), :] = jnp.dot(
            chosen[j][:, 0:tiles], half, preferred_element_type=jnp.float32
        )
    fu[...] = forcing[0:tiles, LANES : 2 * LANES]
    fv[...] = forcing[0:tiles, 2 * LANES : 3 * LANES]
    fside[0 : 2 * HALO] = forcing[tiles : tiles + 2 * HALO, LANES : 2 * LANES]
    fside[2 * HALO : 4 * HALO] = forcing[tiles : tiles + 2 * HALO, 2 * LANES : 3 * LANES]
    copy = pltpu.make_async_copy(answers, answers_hbm, sems.at[0])
    first = Received(first_far, first_near, odd)
    for side, part in ((0, first.prev), (1, first.next)):
        side_idx[side] = part(slice(ROW_IDX, ROW_IDX + 16)).astype(jnp.int32)
        side_w[side] = part(slice(ROW_W, ROW_W + 16))
        for n, row in ((0, ROW_U), (1, ROW_V)):
            at = HALO * (2 * n + side)
            sides[at : at + HALO] = first.rim(side, row)
    rows = (ROW_ETA, ROW_PX, ROW_PY)
    first_subcycle(
        gx, gy, eta, u, v, sides, fu, fv, fside, first.rims(0, rows), first.rims(1, rows), idx, w, side_idx, side_w, rim_idx, rim_w, flow, flow_pack, flow_scale, flow_outer,
        eta_new, u_new, v_new, sides_new, copy.start
    )
    send_rims(eta_new, eta_pack, eta_scale, rim_idx, rim_w, odd, far, near, up, dn)
    copy.wait()


def ocean_kernel(
    far, near, odd, eta, eta_part, u_part, v_part, sides, fside, idx, w, side_idx, side_w,
    rim_idx, rim_w, eta_new, eta_pack, eta_scale, u_new, v_new, sides_new, far_new, near_new,
    flow_outer, up, dn
):
    rows = (0, HALO, 2 * HALO)
    got = Received(far, near, odd)
    sides_new[...] = outer_subcycle(
        eta, eta_part, u_part, v_part, sides, fside, got.rims(0, rows), got.rims(1, rows), idx, w, side_idx, side_w, rim_idx, rim_w, flow_outer,
        eta_new, u_new, v_new
    )
    send_rims(
        eta_new, eta_pack, eta_scale, rim_idx, rim_w, odd, far_new, near_new, up, dn
    )


def last_ocean_kernel(
    far, near, odd, eta, eta_part, u_part, v_part, sides, fside, idx, w, side_idx, side_w,
    rim_idx, rim_w, base, heat, eta_new, velocity, warm, u_new, v_new, flow_outer
):
    warm[...] = base[...] + WARMING_COEFF * heat[...]
    rows = (0, HALO, 2 * HALO)
    got = Received(far, near, odd)
    outer_subcycle(
        eta, eta_part, u_part, v_part, sides, fside, got.rims(0, rows), got.rims(1, rows), idx, w, side_idx, side_w, rim_idx, rim_w, flow_outer,
        eta_new, u_new, v_new
    )
    for r in range(eta.shape[0]):
        cut = slice(r * LANES, (r + 1) * LANES)
        velocity[0:1, cut] = u_new[r : r + 1]
        velocity[1:2, cut] = v_new[r : r + 1]


def shards(
    air_warmth,
    eastern_breeze,
    northern_breeze,
    reciprocal_breadth,
    panel_neighbours,
    transfer_coefficients,
    transfer_across_tile,
    transfer_holder,
    transfer_down_tile,
    water_elevation,
    depth_mean_current,
    marine_skin_warmth,
    patch_neighbours,
    interface_span,
):
    devices = lax.axis_size(RING)
    points, levels, elements = air_warmth.shape
    cells = water_elevation.shape[0]
    tiles = cells // LANES
    blocks = transfer_holder.shape[0]
    cell_rows = shape_of(tiles, LANES)
    rim_rows = shape_of(4 * HALO, LANES)
    dma = pltpu.SemaphoreType.DMA
    air, eastern, northern, breadth_hbm, pn_hbm = in_hbm(
        air_warmth, eastern_breeze, northern_breeze, reciprocal_breadth.reshape(1, elements),
        panel_neighbours
    )

    pack_rows = shape_of(tiles // 2, LANES, dtype=jnp.int32)
    scale_rows = shape_of(8, LANES)
    cell_tables = in_hbm(
        marine_skin_warmth.reshape(tiles, LANES),
        depth_mean_current,
        patch_neighbours,
        interface_span,
    )
    rim_idx, rim_w, eta, eta_pack, eta_scale, far, near, odd = pl.pallas_call(
        prepare_kernel,
        in_specs=hbm(8),
        out_specs=vmem(8),
        out_shape=(
            shape_of(2, 16, LANES, dtype=jnp.int32),
            shape_of(2, 16, LANES),
            cell_rows,
            pack_rows,
            scale_rows,
            shape_of(ROWS_FIRST, LANES),
            shape_of(ROWS_FIRST, LANES),
            shape_of(8, elements, dtype=jnp.int32),
        ),
        scratch_shapes=[
            pltpu.VMEM((ROWS_FIRST, LANES), jnp.float32),
            pltpu.VMEM((ROWS_FIRST, LANES), jnp.float32),
            pltpu.VMEM((2, 4, 8, elements), jnp.float32),
            pltpu.VMEM((1, elements), jnp.float32),
            pltpu.VMEM((4, elements), jnp.int32),
            pltpu.VMEM((2, 8, LANES), jnp.float32),
            pltpu.VMEM((2, 2, OY), jnp.float32),
            pltpu.VMEM((2, 6, OY), jnp.int32),
            pltpu.VMEM((2, 6, OY), jnp.float32),
            dma((13,)),
        ],
        compiler_params=PARAMS,
        name="prepare",
    )(
        *in_hbm(air_warmth.reshape(4, 4, levels, elements)),
        breadth_hbm,
        pn_hbm,
        *in_hbm(water_elevation.reshape(tiles, LANES)),
        *cell_tables,
    )
    first_far, first_near = swap_both(far, near)

    low_wind = pltpu.VMEM((points, 16, elements), jnp.bfloat16)
    low_row = pltpu.VMEM((1, blocks), jnp.int32)
    flux, slots, breadth, pn, marks, idx, w, u, v, sst = pl.pallas_call(
        lambda *refs: plan_kernel(*refs, devices=devices, tiles=tiles),
        in_specs=hbm(12),
        out_specs=vmem(4) + smem(1) + vmem(5),
        out_shape=(
            shape_of(points, 8, elements), shape_of(devices, LANES), shape_of(1, elements),
            shape_of(4, elements, dtype=jnp.int32), pltpu.SMEM((8, blocks), jnp.int32),
            shape_of(6 * tiles, LANES, dtype=jnp.int32), shape_of(6 * tiles, LANES),
            cell_rows, cell_rows, cell_rows
        ),
        scratch_shapes=[
            pltpu.VMEM((points, 8, elements), jnp.float32), low_wind, low_wind,
            low_row, low_row, low_row, pltpu.VMEM((6, cells), jnp.int32),
            pltpu.VMEM((6, cells), jnp.float32), pltpu.VMEM((2, cells), jnp.float32),
            pltpu.VMEM((8, blocks), jnp.int32), dma((12,))
        ],
        compiler_params=PARAMS,
        name="plan",
    )(
        air,
        eastern,
        northern,
        breadth_hbm,
        pn_hbm,
        *in_hbm(
            transfer_holder.reshape(1, blocks),
            transfer_across_tile.reshape(1, blocks),
            transfer_down_tile.reshape(1, blocks),
        ),
        cell_tables[2],
        cell_tables[3],
        cell_tables[1],
        cell_tables[0],
    )

    home = pl.pallas_call(
        home_sums_kernel,
        in_specs=smem(1) + vmem(2),
        out_specs=pl.BlockSpec(memory_space=pltpu.VMEM),
        out_shape=shape_of(devices * 8, LANES),
        compiler_params=PARAMS,
        name="home_sums",
    )(marks, flux, transfer_coefficients)
    outgoing = pl.pallas_call(
        lambda *refs: forward_kernel(*refs, devices=devices),
        in_specs=smem(1) + vmem(9),
        out_specs=pl.BlockSpec(memory_space=pltpu.HBM),
        out_shape=pltpu.HBM((devices, PER_DEST, LANES), jnp.bfloat16),
        scratch_shapes=[
            pltpu.VMEM((devices, PER_DEST, LANES), jnp.bfloat16),
            pltpu.VMEM((devices * 8, LANES), jnp.float32),
            dma((4,)),
        ],
        compiler_params=PARAMS,
        name="forward_remap",
    )(
        marks, home, flux, slots, breadth, pn, first_far, first_near, odd, transfer_coefficients
    )
    outgoing, pn, gradient_eta = lax.optimization_barrier((outgoing, pn, eta))
    arrived = exchange(outgoing)
    gx, gy, base = pl.pallas_call(
        first_gradient_kernel,
        in_specs=vmem(11),
        out_specs=vmem(3),
        out_shape=(cell_rows,) * 3,
        scratch_shapes=[
            pltpu.VMEM((tiles // 2, LANES), jnp.int32), pltpu.VMEM((8, LANES), jnp.float32)
        ],
        compiler_params=PARAMS,
        name="first_gradient",
    )(
        idx, w, gradient_eta, eta_pack, eta_scale, sst, first_far, first_near, odd, rim_idx, rim_w
    )

    field = shape_of(points, levels, elements)
    edge = shape_of(4, levels, elements, dtype=jnp.bfloat16)
    swap_rows = shape_of(4 * HALO + 2 * levels, elements)
    wind = shape_of(points, levels, elements, dtype=jnp.bfloat16)
    loc, eastern, northern, east, west, far, near, edge_places = pl.pallas_call(
        local_step_kernel,
        in_specs=hbm(3) + vmem(3),
        out_specs=vmem(8),
        out_shape=(
            field, wind, wind, edge, edge, swap_rows, swap_rows,
            shape_of(8, elements, dtype=jnp.int32)
        ),
        scratch_shapes=[pltpu.VMEM((points, levels, elements), jnp.float32), dma((3,))],
        compiler_params=PARAMS,
        name="local_step",
    )(air, eastern, northern, breadth, pn, odd)

    rim_scratch = pltpu.VMEM((4 * HALO, LANES), jnp.float32)
    flow_scratch = [
        pltpu.VMEM((3, tiles, LANES), jnp.float32),
        pltpu.VMEM((3, tiles // 2, LANES), jnp.int32),
        pltpu.VMEM((3, 8, LANES), jnp.float32),
        pltpu.VMEM((3, 2 * HALO, LANES), jnp.float32),
    ]
    (
        eta, eta_pack, eta_scale, u, v, sides, far, near, fu, fv, fside, side_idx, side_w,
        heat, answers
    ) = pl.pallas_call(
        first_ocean_kernel,
        in_specs=vmem(16),
        out_specs=vmem(14) + hbm(1),
        out_shape=(
            cell_rows, pack_rows, scale_rows, cell_rows, cell_rows, rim_rows, swap_rows, swap_rows,
            cell_rows, cell_rows, rim_rows,
            shape_of(2, 16, LANES, dtype=jnp.int32), shape_of(2, 16, LANES),
            cell_rows, pltpu.HBM((devices * CAP, LANES), jnp.float32),
        ),
        scratch_shapes=flow_scratch + [rim_scratch] * 3 + [
            pltpu.VMEM((devices * PER_DEST, LANES), jnp.float32),
            pltpu.VMEM((devices * CAP, LANES), jnp.float32),
            dma((1,)),
        ],
        input_output_aliases={13: 6, 14: 7},
        compiler_params=PARAMS,
        name="first_ocean",
    )(
        arrived, first_far, first_near, odd, gx, gy, eta, u, v, idx, w, rim_idx, rim_w,
        far, near, base
    )
    far, near = swap_both(far, near)
    edges_far, edges_near = far, near

    for substep in range(1, NSUB):
        if substep == 1:
            u_part, v_part = pl.pallas_call(
                current_kernel,
                in_specs=vmem(9),
                out_specs=vmem(2),
                out_shape=(cell_rows,) * 2,
                compiler_params=PARAMS,
                name="current",
            )(idx, w, eta, eta_pack, eta_scale, u, v, fu, fv)
            answers, u_part = lax.optimization_barrier((answers, u_part))
            answered = exchange(answers.reshape(devices, CAP, LANES))
            eta_part = pl.pallas_call(
                height_kernel,
                in_specs=vmem(5),
                out_specs=pl.BlockSpec(memory_space=pltpu.VMEM),
                out_shape=cell_rows,
                scratch_shapes=flow_scratch[:3],
                compiler_params=PARAMS,
                name="height",
            )(idx, w, eta, u_part, v_part)
        else:
            eta_part, u_part, v_part = pl.pallas_call(
                inner_kernel,
                in_specs=vmem(9),
                out_specs=vmem(3),
                out_shape=(cell_rows,) * 3,
                scratch_shapes=flow_scratch[:3],
                compiler_params=PARAMS,
                name="inner",
            )(idx, w, eta, eta_pack, eta_scale, u, v, fu, fv)
        if substep == 2:
            eta_part, answered = lax.optimization_barrier((eta_part, answered))
            surface = pl.pallas_call(
                back_kernel,
                in_specs=smem(1) + vmem(2),
                out_specs=pl.BlockSpec(memory_space=pltpu.VMEM),
                out_shape=shape_of(points, LANES),
                scratch_shapes=[
                    pltpu.VMEM((devices * CAP, LANES), jnp.float32),
                    pltpu.VMEM((blocks, 8, LANES), jnp.float32),
                ],
                compiler_params=PARAMS,
                name="back_remap",
            )(marks, answered, transfer_coefficients)
            eta_part, surface = lax.optimization_barrier((eta_part, surface))
        operands = (
            far, near, odd, eta, eta_part, u_part, v_part, sides, fside, idx, w, side_idx, side_w, rim_idx, rim_w
        )
        outer_scratch = [pltpu.VMEM((3, 4 * HALO, LANES), jnp.float32)]
        if substep + 1 < NSUB:
            eta, eta_pack, eta_scale, u, v, sides, far, near = pl.pallas_call(
                ocean_kernel,
                in_specs=vmem(15),
                out_specs=vmem(8),
                out_shape=(cell_rows, pack_rows, scale_rows) + (cell_rows,) * 2 + (rim_rows,) * 3,
                scratch_shapes=outer_scratch + [rim_scratch] * 2,
                compiler_params=PARAMS,
                name="ocean",
            )(*operands)
            far, near = swap_both(far, near)
        else:
            eta, velocity, warm = pl.pallas_call(
                last_ocean_kernel,
                in_specs=vmem(17),
                out_specs=vmem(3),
                out_shape=(cell_rows, shape_of(2, cells), cell_rows),
                scratch_shapes=[pltpu.VMEM((tiles, LANES), jnp.float32)] * 2 + outer_scratch,
                compiler_params=PARAMS,
                name="last_ocean",
            )(*operands, base, heat)

    closing = pl.pallas_call(
        second_step_kernel,
        in_specs=vmem(14),
        out_specs=pl.BlockSpec(memory_space=pltpu.HBM),
        out_shape=pltpu.HBM((points, levels, elements), jnp.float32),
        scratch_shapes=[
            pltpu.VMEM((points, levels, elements), jnp.float32), dma((levels // 16,))
        ],
        compiler_params=PARAMS,
        name="second_step",
    )(
        loc, eastern, northern, breadth, pn, east, west, edges_far, edges_near, edge_places,
        first_far, first_near, odd, surface
    )
    return closing, eta.reshape(cells), velocity, warm.reshape(cells)


def solution(mesh):
    split = P(RING)
    last = P(None, RING)
    field = P(None, None, RING)
    return jax.shard_map(
        shards,
        mesh=mesh,
        in_specs=(
            field,
            field,
            field,
            split,
            last,
            P(RING, None, None),
            split,
            P(RING, None),
            split,
            split,
            last,
            split,
            last,
            last,
        ),
        out_specs=(field, split, last, split),
        check_vma=False,
    )
```

```python
import math

import jax
import jax.numpy as jnp
import numpy as np
from jax import lax
from jax.experimental import pallas as pl
from jax.experimental.pallas import tpu as pltpu
from jax.sharding import PartitionSpec as P

OY = 256
NSUB = 4
CAP = 2

STEP_SIZE = 0.05
JUMP_WEIGHT = 4.0
NUDGING_SPEED = 0.5
DAMPING = 0.9
GRAVITY = 0.3
WIND_GAIN = 0.3
DEPTH_RATE = 0.3
WARMING_COEFF = 0.3
SPREADING_COEFF = 0.5

RING = ("comp", "dom")
LANES = 128
HALO = OY // LANES
COS = [math.cos(k * math.pi / 3.0) for k in range(6)]
SIN = [0.0 if k % 3 == 0 else math.sin(k * math.pi / 3.0) for k in range(6)]

ROW_EDGE, ROW_BREADTH, ROW_ETA, ROW_U, ROW_V, ROW_SST = 0, 4, 8, 10, 12, 14
ROW_PX, ROW_PY, ROW_IDX, ROW_W, ROWS_FIRST = 16, 18, 24, 40, 56
MARK_COLUMN, MARK_OWN, MARK_HEAT, MARK_ANSWER, MARK_PLACE, MARK_READER = range(6)
PER_DEST, ROW_HEAT, ROW_IDS = 16, 12, 14


def swapped(value, first):
    count = lax.axis_size(RING)
    pairs = []
    for i in range(first, count + first, 2):
        pairs += [(i % count, (i + 1) % count), ((i + 1) % count, i % count)]
    return lax.ppermute(value, RING, pairs)


def swap_both(far, near):
    got_far = swapped(far, 1)
    return got_far, swapped(near, 0)


class Received:
    def __init__(self, far, near, odd):
        self.far, self.near, self.odd = far, near, odd

    def flag(self, rows):
        return jnp.broadcast_to(self.odd[0:1], rows.shape) > 0

    def prev(self, *cut):
        far, near = self.far[cut], self.near[cut]
        return jnp.where(self.flag(far), near, far)

    def next(self, *cut):
        far, near = self.far[cut], self.near[cut]
        return jnp.where(self.flag(far), far, near)

    def rim(self, side, row):
        cut = slice(row, row + HALO)
        return self.prev(cut) if side == 0 else self.next(cut)

    def rims(self, side, rows):
        return tuple(self.rim(side, row) for row in rows)


def arrange(up, dn, odd, far, near):
    flag = jnp.broadcast_to(odd[0:1], up.shape) > 0
    far[...] = jnp.where(flag, up[...], dn[...])
    near[...] = jnp.where(flag, dn[...], up[...])


def exchange(value):
    return lax.all_to_all(value, RING, split_axis=0, concat_axis=0, tiled=True)


def gll_matrix():
    points = np.array([-1.0, -1.0 / np.sqrt(5.0), 1.0 / np.sqrt(5.0), 1.0])
    barycentric = [
        1.0 / np.prod([points[s] - points[o] for o in range(4) if o != s]) for s in range(4)
    ]
    table = np.zeros((4, 4))
    for t in range(4):
        for s in range(4):
            if t != s:
                table[t, s] = barycentric[s] / barycentric[t] / (points[t] - points[s])
    for t in (0, 3):
        table[t, t] = -np.sum(table[t])
    return [[float(np.float32(value)) for value in line] for line in table]


GLL = gll_matrix()


def vmem(count):
    return [pl.BlockSpec(memory_space=pltpu.VMEM)] * count


def hbm(count):
    return [pl.BlockSpec(memory_space=pltpu.HBM)] * count


def in_hbm(*arrays):
    return [pltpu.with_memory_space_constraint(array, pltpu.HBM) for array in arrays]


def smem(count):
    return [pl.BlockSpec(memory_space=pltpu.SMEM)] * count


def shape_of(*dims, dtype=jnp.float32):
    return jax.ShapeDtypeStruct(dims, dtype)


PARAMS = pltpu.CompilerParams(vmem_limit_bytes=24 * 1024 * 1024)


def lane_take(rows, ids):
    return jnp.take_along_axis(rows, ids, axis=1, mode="promise_in_bounds")


def wide(row, lines):
    return jnp.broadcast_to(row, (lines, row.shape[1]))


def side_ids(pn):
    count = pn.shape[1]
    bits = count.bit_length() - 1
    table = pn[...]
    ids = [table[k : k + 1] & (count - 1) for k in range(4)]
    home = lax.shift_right_logical(table[0:1], bits)
    near = [lax.shift_right_logical(table[k : k + 1], bits) == home for k in range(4)]
    return ids, near


def element_step(state, east_wind, north_wind, scale, facing):
    jumps = [None] * 16
    sides = (
        (0, 1, 2, 3),
        (3, 7, 11, 15),
        (12, 13, 14, 15),
        (0, 4, 8, 12),
    )
    for k in range(4):
        for n, p in enumerate(sides[k]):
            term = facing[k][n] - state[p]
            jumps[p] = term if jumps[p] is None else jumps[p] + term
    result = []
    for p in range(16):
        i, j = p % 4, p // 4
        grad_x = grad_y = None
        for m in range(4):
            if GLL[i][m] != 0.0:
                term = GLL[i][m] * state[m + 4 * j]
                grad_x = term if grad_x is None else grad_x + term
            if GLL[j][m] != 0.0:
                term = GLL[j][m] * state[i + 4 * m]
                grad_y = term if grad_y is None else grad_y + term
        change = -(east_wind(p) * grad_x + north_wind(p) * grad_y)
        if jumps[p] is not None:
            change = change + JUMP_WEIGHT * jumps[p]
        result.append(state[p] + scale * change)
    return result


def load(pairs, sems):
    copies = [
        pltpu.make_async_copy(source, target, sems.at[n])
        for n, (source, target) in enumerate(pairs)
    ]
    for copy in copies:
        copy.start()
    return copies


def as_column(row):
    count = row.shape[1]
    return jnp.transpose(jnp.broadcast_to(row, (count, count)))


def edge_tables(partner, remote):
    count = partner.shape[1]
    pack = count // 4
    lane = lax.broadcasted_iota(jnp.int32, (count, count), 1)
    line = lax.broadcasted_iota(jnp.int32, (count, count), 0)
    flag = jnp.where(remote, 1.0, 0.0)
    rank = jnp.sum(jnp.where(line < lane, as_column(flag), 0.0), axis=0, keepdims=True)
    rank = as_column(jnp.where(remote, rank, -1.0))
    slot = (lane & (pack - 1)).astype(jnp.float32)
    chosen = jnp.sum(
        jnp.where(rank == slot, line.astype(jnp.float32), 0.0), axis=0, keepdims=True
    ).astype(jnp.int32)
    key = jnp.where(remote, partner, 2 * count).astype(jnp.float32)
    before = jnp.where(as_column(key) < key, 1.0, 0.0)
    place = jnp.sum(before, axis=0, keepdims=True).astype(jnp.int32)
    return chosen, jnp.minimum(place, pack - 1)


def rank_among_equals(row, most):
    count = row.shape[1]
    earlier = lax.broadcasted_iota(jnp.int32, (count, count), 0) < lax.broadcasted_iota(
        jnp.int32, (count, count), 1
    )
    number = row.astype(jnp.float32)
    same = as_column(number) == number
    return jnp.minimum(jnp.sum(jnp.where(same & earlier, 1, 0), axis=0, keepdims=True), most)


def slot_rows(holder_row, rank, down_row, devices, tiles):
    blocks = holder_row.shape[1]
    target = lax.broadcasted_iota(jnp.int32, (devices, blocks), 0)
    after = jnp.where(holder_row + 1 == devices, 0, holder_row + 1)
    before = jnp.where(holder_row == 0, devices - 1, holder_row - 1)
    last = down_row - (tiles - HALO)
    lane = lax.broadcasted_iota(jnp.int32, (devices, LANES), 1)
    result = jnp.full((devices, LANES), -1.0, jnp.float32)
    for n, (owner, number) in enumerate(
        (
            (holder_row, down_row),
            (after, jnp.where(last >= 0, tiles + last, -1)),
            (before, jnp.where(down_row < HALO, tiles + HALO + down_row, -1)),
        )
    ):
        for slot in range(CAP):
            named = (target == owner) & (rank == slot)
            value = jnp.sum(
                jnp.where(named, (number + 1).astype(jnp.float32), 0.0), axis=1, keepdims=True
            )
            result = jnp.where(lane == CAP * n + slot, value - 1.0, result)
    return result


def home_facing(state, ids, near):
    return [
        [lane_take(state[12 + n], ids[0]) for n in range(4)],
        [jnp.where(near[1], lane_take(state[4 * n], ids[1]), 0.0) for n in range(4)],
        [lane_take(state[n], ids[2]) for n in range(4)],
        [jnp.where(near[3], lane_take(state[3 + 4 * n], ids[3]), 0.0) for n in range(4)],
    ]


def plan_kernel(
    air_hbm, eastern_hbm, northern_hbm, breadth_hbm, pn_hbm, holder_hbm, across_hbm, down_hbm,
    nb_hbm, span_hbm, flow_hbm, sst_hbm, flux, slots, breadth, pn, marks, idx, w, u, v, sst,
    air, eastern, northern, holder, across, down, nb, span, flow, lists, sems, *, devices, tiles
):
    copies = load(
        (
            (air_hbm.at[:, pl.ds(0, 8), :], air),
            (eastern_hbm.at[:, pl.ds(0, 16), :], eastern),
            (northern_hbm.at[:, pl.ds(0, 16), :], northern),
            (breadth_hbm, breadth),
            (pn_hbm, pn),
            (holder_hbm, holder),
            (across_hbm, across),
            (down_hbm, down),
            (nb_hbm, nb),
            (span_hbm, span),
            (flow_hbm, flow),
            (sst_hbm, sst),
        ),
        sems,
    )
    for copy in copies:
        copy.wait()
    rank = rank_among_equals(holder[...], CAP - 1)
    place = across[...] * 2 + rank_among_equals(across[...], 1)
    blocks = place.shape[1]
    line = lax.broadcasted_iota(jnp.int32, (blocks, blocks), 0).astype(jnp.float32)
    lane = lax.broadcasted_iota(jnp.int32, (blocks, blocks), 1).astype(jnp.float32)
    here = as_column(place.astype(jnp.float32)) == lane
    reader = jnp.sum(jnp.where(here, line, 0.0), axis=0, keepdims=True).astype(jnp.int32)
    lists[...] = jnp.zeros_like(lists)
    for mark, row in (
        (MARK_COLUMN, across[...]),
        (MARK_OWN, holder[...] * 8 + 2 * rank),
        (MARK_HEAT, holder[...] * 8 + 4 + rank),
        (MARK_ANSWER, holder[...] * CAP + rank),
        (MARK_PLACE, place),
        (MARK_READER, reader),
    ):
        lists[mark : mark + 1] = row
    copy = pltpu.make_async_copy(lists, marks, sems.at[0])
    copy.start()
    slots[...] = slot_rows(holder[...], rank, down[...], devices, tiles)
    fill_tables(nb, span, flow, idx, w, u, v)
    lines, count = air.shape[1], air.shape[2]
    ids, near = side_ids(pn)
    ids = [wide(line, lines) for line in ids]
    state = [air[p] for p in range(16)]
    u = [eastern[p].astype(jnp.float32)[0:lines] for p in range(16)]
    v = [northern[p].astype(jnp.float32)[0:lines] for p in range(16)]
    result = element_step(
        state, lambda p: u[p], lambda p: v[p], STEP_SIZE * breadth[...],
        home_facing(state, ids, near)
    )
    for p in range(16):
        speed = jnp.sqrt(u[p] * u[p] + v[p] * v[p] + 1.0)
        flux[p, 0:1] = (speed * result[p])[0:1]
        flux[p, 1:2] = (speed * u[p])[0:1]
        flux[p, 2:3] = (speed * v[p])[0:1]
        flux[p, 3:4] = speed[0:1]
        flux[p, 4:8] = jnp.zeros((4, count), jnp.float32)
    copy.wait()


def local_step_kernel(
    air_hbm, eastern_hbm, northern_hbm, breadth, pn, odd, loc, eastern, northern, east, west,
    far, near_swap, places, air, sems
):
    copies = load(((air_hbm, air), (eastern_hbm, eastern), (northern_hbm, northern)), sems)
    count = breadth.shape[1]
    lines = 16
    ids, near = side_ids(pn)
    chosen_east, place_east = edge_tables(ids[1], jnp.logical_not(near[1]))
    chosen_west, place_west = edge_tables(ids[3], jnp.logical_not(near[3]))
    places[...] = jnp.zeros_like(places)
    places[0:1] = place_east
    places[1:2] = place_west
    chosen_east, chosen_west = wide(chosen_east, lines), wide(chosen_west, lines)
    group = lax.broadcasted_iota(jnp.int32, (lines, count), 1) // (count // 4)
    scale = STEP_SIZE * breadth[...]
    ids = [wide(line, lines) for line in ids]

    def packed(values, chosen):
        result = jnp.zeros((lines, count), jnp.float32)
        for n in range(4):
            result = jnp.where(group == n, lane_take(values[n], chosen), result)
        return result

    for copy in copies:
        copy.wait()
    levels = air.shape[1]

    def chunk(c, carry):
        at = pl.multiple_of(c * lines, lines)
        rows = pl.ds(at, lines)
        state = [air[p, rows] for p in range(16)]
        result = element_step(
            state,
            lambda p: eastern[p, rows].astype(jnp.float32),
            lambda p: northern[p, rows].astype(jnp.float32),
            scale,
            home_facing(state, ids, near),
        )
        for p in range(16):
            loc[p, rows] = result[p]
        here = pl.ds(pl.multiple_of(4 * HALO + at, 8), lines)
        beyond = pl.ds(pl.multiple_of(4 * HALO + levels + at, 8), lines)
        for n in range(4):
            east[n, rows] = state[3 + 4 * n].astype(jnp.bfloat16)
            west[n, rows] = state[4 * n].astype(jnp.bfloat16)
        flag = jnp.broadcast_to(odd[0:1], (lines, count)) > 0
        for target, values in ((here, state), (beyond, result)):
            to_next = packed([values[3 + 4 * n] for n in range(4)], chosen_east)
            to_prev = packed([values[4 * n] for n in range(4)], chosen_west)
            far[target] = jnp.where(flag, to_next, to_prev)
            near_swap[target] = jnp.where(flag, to_prev, to_next)
        return carry

    lax.fori_loop(0, levels // lines, chunk, 0)


def second_step_kernel(
    loc, eastern, northern, breadth, pn, east, west, far, near_swap, places, first_far,
    first_near, odd, surface, out_hbm, out, sems
):
    ids, near = side_ids(pn)
    levels, count = loc.shape[1], loc.shape[2]
    lines = 16
    pack = count // 4
    scale = STEP_SIZE * breadth[...]
    jump = JUMP_WEIGHT * scale
    ids = [wide(line, lines) for line in ids]
    got = Received(far, near_swap, odd)
    first = Received(first_far, first_near, odd)
    row = slice(ROW_BREADTH, ROW_BREADTH + 1)
    factors = [
        JUMP_WEIGHT * STEP_SIZE * lane_take(wide(line, lines), ids[side])
        for side, line in ((1, first.next(row)), (3, first.prev(row)))
    ]
    spots = [
        [wide(places[n : n + 1] + m * pack, lines) for m in range(4)] for n in (0, 1)
    ]

    def copy_out(c):
        rows = pl.ds(pl.multiple_of(c * lines, lines), lines)
        return pltpu.make_async_copy(out.at[:, rows, :], out_hbm.at[:, rows, :], sems.at[c])

    def chunk(c, carry):
        at = pl.multiple_of(c * lines, lines)
        rows = pl.ds(at, lines)
        now = pl.ds(pl.multiple_of(4 * HALO + at, 8), lines)
        later = pl.ds(pl.multiple_of(4 * HALO + levels + at, 8), lines)
        state = [loc[p, rows] for p in range(16)]

        def across(own, there_now, there_next, side, factor, spot):
            values, beyond = [], []
            for n in range(4):
                values.append(jnp.where(near[side], 0.0, lane_take(there_now, spot[n])))
                beyond.append(
                    lane_take(there_next, spot[n]) + factor * own[n, rows].astype(jnp.float32)
                )
            return values, beyond

        east_now, east_beyond = across(
            east, got.next(now), got.next(later), 1, factors[0], spots[0]
        )
        west_now, west_beyond = across(
            west, got.prev(now), got.prev(later), 3, factors[1], spots[1]
        )
        for n in range(4):
            state[3 + 4 * n] = state[3 + 4 * n] + jump * east_now[n]
            state[4 * n] = state[4 * n] + jump * west_now[n]
        facing = home_facing(state, ids, near)
        facing[1] = [jnp.where(near[1], facing[1][n], east_beyond[n]) for n in range(4)]
        facing[3] = [jnp.where(near[3], facing[3][n], west_beyond[n]) for n in range(4)]
        result = element_step(
            state,
            lambda p: eastern[p, rows].astype(jnp.float32),
            lambda p: northern[p, rows].astype(jnp.float32),
            scale,
            facing,
        )
        for p in range(16):
            out[p, rows] = result[p]

        @pl.when(c == 0)
        def _():
            for p in range(16):
                lowest = out[p, 0:1]
                out[p, 0:1] = lowest + NUDGING_SPEED * (surface[p : p + 1] - lowest)

        copy_out(c).start()
        return carry

    lax.fori_loop(0, levels // lines, chunk, 0)

    def finish(c, carry):
        copy_out(c).wait()
        return carry

    lax.fori_loop(0, levels // lines, finish, 0)


def home_sums_kernel(marks, flux, weights, own):
    own[...] = jnp.zeros_like(own)
    for b in range(weights.shape[0]):
        sums = jnp.dot(
            flux[marks[MARK_COLUMN, b]].astype(jnp.bfloat16), weights[b], preferred_element_type=jnp.float32
        )
        row = marks[MARK_OWN, b]
        own[pl.ds(row, 1), :] = sums[1:2]
        own[pl.ds(row + 1, 1), :] = sums[2:3]
        own[pl.ds(marks[MARK_HEAT, b], 1), :] = sums[0:1]


def forward_kernel(
    marks, home, flux, slots, breadth, pn, first_far, first_near, odd, weights, out_hbm, out, extra,
    sems, *, devices
):
    ids, near = side_ids(pn)
    jump = (JUMP_WEIGHT * STEP_SIZE) * breadth[...]
    first = Received(first_far, first_near, odd)
    from_east = lane_take(first.next(slice(0, 8)), wide(ids[1], 8))
    from_west = lane_take(first.prev(slice(0, 8)), wide(ids[3], 8))
    from_east = jnp.where(near[1], 0.0, jump * from_east)
    from_west = jnp.where(near[3], 0.0, jump * from_west)
    extra[...] = jnp.zeros_like(extra)
    for n in range(4):
        for p, change in ((3 + 4 * n, from_east), (4 * n, from_west)):
            line = wide(flux[p, 3:4] * change[n : n + 1], 8).astype(jnp.bfloat16)
            for reader in range(2):
                b = marks[MARK_READER, 2 * p + reader]
                sums = jnp.dot(line, weights[b], preferred_element_type=jnp.float32)
                extra[pl.ds(marks[MARK_HEAT, b], 1), :] = sums[0:1]
    line = lax.broadcasted_iota(jnp.int32, (8, LANES), 0)
    part, copies = devices, []
    for d in range(devices):
        mine, prev, following = (
            home[8 * (n % devices) : 8 * (n % devices) + 8] for n in (d, d - 1, d + 1)
        )
        top = jnp.concatenate([mine[0:4], prev[0:4]], axis=0)
        bottom = jnp.where(line < 4, following, mine + extra[8 * d : 8 * d + 8])
        bottom = jnp.where(line == ROW_IDS - 8, wide(slots[d : d + 1], 8), bottom)
        out[d] = jnp.concatenate([top, bottom], axis=0).astype(jnp.bfloat16)
        if (d + 1) % part == 0:
            copies.append(
                pltpu.make_async_copy(
                    out.at[pl.ds(d + 1 - part, part)],
                    out_hbm.at[pl.ds(d + 1 - part, part)],
                    sems.at[d // part],
                )
            )
            copies[-1].start()
    for copy in copies:
        copy.wait()


def back_kernel(marks, arrived, weights, surface, lines, share):
    lines[...] = arrived[...].reshape(lines.shape)
    for b in range(weights.shape[0]):
        line = lines[pl.ds(marks[MARK_ANSWER, b], 1), :]
        share[marks[MARK_PLACE, b]] = lax.dot_general(
            wide(line, 8).astype(jnp.bfloat16),
            weights[b],
            (((1,), (1,)), ((), ())),
            preferred_element_type=jnp.float32,
        )
    for p in range(surface.shape[0]):
        surface[p : p + 1] = share[2 * p, 0:1] + share[2 * p + 1, 0:1]


def split_index(idx):
    return lax.shift_right_arithmetic(idx, 7), idx & (LANES - 1)


def by_tiles(function, idx):
    if idx.shape[0] <= 8:
        return function(idx)
    return jnp.concatenate(
        [function(idx[at : at + 8]) for at in range(0, idx.shape[0], 8)], axis=0
    )


def pick(idx, sources):
    def one(idx):
        high, low = split_index(idx)
        result = jnp.zeros(idx.shape, jnp.float32)
        for number, line in sources:
            result = jnp.where(high == number, lane_take(wide(line, idx.shape[0]), low), result)
        return result

    return one(idx)


def fill_pack(values, packed, scales):
    half = values.shape[0] // 2
    numbers = []
    for n, part in enumerate((values[:half], values[half:])):
        top = jnp.max(part, axis=(0, 1), keepdims=True)
        bottom = jnp.min(part, axis=(0, 1), keepdims=True)
        middle = 0.5 * (top + bottom)
        reach = jnp.maximum(jnp.maximum(top - middle, middle - bottom), 1e-30)
        numbers.append(jnp.floor((part - middle) * (32767.0 / reach) + 0.5).astype(jnp.int32))
        scales[n : n + 1] = jnp.broadcast_to(reach * (1.0 / 32767.0), (1, LANES))
        scales[2 + n : 3 + n] = jnp.broadcast_to(middle, (1, LANES))
    packed[...] = (numbers[1] << 16) | (numbers[0] & 0xFFFF)


def pick_own(idx, packed, scales):
    half = packed.shape[0]

    def one(idx):
        lines = idx.shape[0]
        high, low = split_index(idx)
        own = high - HALO
        upper = own >= half
        row = jnp.where(upper, own - half, own)
        words = jnp.zeros(idx.shape, jnp.int32)
        for r in range(half):
            words = jnp.where(row == r, lane_take(wide(packed[r : r + 1], lines), low), words)
        number = jnp.where(upper, words >> 16, (words << 16) >> 16)
        scale = jnp.where(upper, wide(scales[1:2], lines), wide(scales[0:1], lines))
        middle = jnp.where(upper, wide(scales[3:4], lines), wide(scales[2:3], lines))
        inside = (own >= 0) & (own < 2 * half)
        return jnp.where(inside, number.astype(jnp.float32) * scale + middle, 0.0)

    return by_tiles(one, idx)


def combine(terms, factors):
    total = None
    for term, factor in zip(terms, factors):
        if factor != 0.0:
            total = factor * term if total is None else total + factor * term
    return total


def pair_sums(table):
    terms = [table[HALO * k : HALO * (k + 1)] for k in range(6)]
    return combine(terms, COS), combine(terms, SIN)


def rim_partial(rim_idx, rim_w, eta, packed, scales, first):
    rows = rim_idx.shape[0]
    found = pick_own(rim_idx, packed, scales)
    centre = eta[first : first + HALO]
    centre = jnp.concatenate([centre] * (rows // HALO), axis=0)
    return pair_sums(rim_w * (found - centre))


def prepare_kernel(
    air_hbm, breadth_hbm, pn_hbm, eta_hbm, sst_hbm, flow_hbm, nb_hbm, span_hbm,
    rim_idx, rim_w, eta, eta_pack, eta_scale, far, near, odd,
    up, dn, air, breadth, pn, sst, flow, nb, span, sems
):
    tiles, cells = eta.shape[0], nb_hbm.shape[1]
    pairs = [(air_hbm.at[:, 3 * side, pl.ds(0, 8), :], air.at[side]) for side in (0, 1)]
    pairs.append((eta_hbm, eta))
    for side, at in ((0, 0), (1, cells - OY)):
        cut = pl.ds(at, OY)
        pairs.append((nb_hbm.at[:, cut], nb.at[side]))
        pairs.append((span_hbm.at[:, cut], span.at[side]))
        pairs.append((flow_hbm.at[:, cut], flow.at[side]))
    for side, at in ((0, 0), (1, tiles - 8)):
        pairs.append((sst_hbm.at[pl.ds(at, 8)], sst.at[side]))
    pairs.append((breadth_hbm, breadth))
    pairs.append((pn_hbm, pn))
    copies = load(pairs, sems)
    for copy in copies:
        copy.wait()
    shard = lax.shift_right_logical(pn[0:1], pn.shape[1].bit_length() - 1)
    odd[...] = wide(shard & 1, 8)
    fill_pack(eta[...], eta_pack, eta_scale)
    for side, first in ((0, 0), (1, tiles - HALO)):
        rim_idx[side, 12:16] = jnp.full((4, LANES), -1, jnp.int32)
        rim_w[side, 12:16] = jnp.zeros((4, LANES), jnp.float32)
        for j in range(HALO):
            cut = slice(j * LANES, (j + 1) * LANES)
            links = nb[side, :, cut]
            factors = slot_factors(links, span[side, :, cut])
            for k in range(6):
                at = HALO * k + j
                rim_idx[side, at : at + 1] = links[k : k + 1]
                rim_w[side, at : at + 1] = factors[k : k + 1]
    for side, first, target in ((0, 0, dn), (1, tiles - HALO, up)):
        target[...] = jnp.zeros_like(target)
        for n in range(4):
            target[ROW_EDGE + n : ROW_EDGE + n + 1] = air[side, n, 0:1]
        target[ROW_BREADTH : ROW_BREADTH + 1] = breadth[...]
        part_x, part_y = rim_partial(
            rim_idx[side], rim_w[side], eta, eta_pack, eta_scale, first
        )
        cut = slice(first, first + HALO)
        target[ROW_ETA : ROW_ETA + HALO] = eta[cut]
        for j in range(HALO):
            here = slice(j * LANES, (j + 1) * LANES)
            target[ROW_U + j : ROW_U + j + 1] = flow[side, 0:1, here]
            target[ROW_V + j : ROW_V + j + 1] = flow[side, 1:2, here]
        start = first % 8
        target[ROW_SST : ROW_SST + HALO] = sst[side, start : start + HALO]
        target[ROW_PX : ROW_PX + HALO] = part_x
        target[ROW_PY : ROW_PY + HALO] = part_y
        target[ROW_IDX : ROW_IDX + 16] = rim_idx[side].astype(jnp.float32)
        target[ROW_W : ROW_W + 16] = rim_w[side]
    arrange(up, dn, odd, far, near)


def slot_factors(links, span):
    return jnp.where(links >= 0, span * (1.0 / 3.0), 0.0)


def fill_tables(nb, span, flow, idx, w, u, v):
    tiles = u.shape[0]
    for r in range(tiles):
        cut = slice(r * LANES, (r + 1) * LANES)
        links = nb[:, cut]
        factors = slot_factors(links, span[:, cut])
        for k in range(6):
            idx[k * tiles + r : k * tiles + r + 1] = links[k : k + 1]
            w[k * tiles + r : k * tiles + r + 1] = factors[k : k + 1]
        u[r : r + 1] = flow[0:1, cut]
        v[r : r + 1] = flow[1:2, cut]


def own_gradient(idx, w, eta, packed, scales, gx, gy):
    tiles = eta.shape[0]

    def chunk(at):
        centre = eta[pl.ds(at, 8)]
        terms = []
        for k in range(6):
            found = pick_own(idx[pl.ds(k * tiles + at, 8)], packed, scales)
            terms.append(w[pl.ds(k * tiles + at, 8)] * (found - centre))
        gx[pl.ds(at, 8)] = combine(terms, COS)
        gy[pl.ds(at, 8)] = combine(terms, SIN)

    for c in range(tiles // 8):
        chunk(c * 8)


def own_spread(at, idx, w, flow, packed, scales):
    tiles = flow.shape[1]
    total = jnp.zeros((8, LANES), jnp.float32)
    for kk in range(3):
        centre = flow[kk, pl.ds(at, 8)]
        for k, sign in ((kk, 1.0), (kk + 3, -1.0)):
            rows = pl.ds(k * tiles + at, 8)
            found = pick_own(idx[rows], packed.at[kk], scales.at[kk])
            total = total + sign * w[rows] * (found - centre)
    return total


def inner_kernel(
    idx, w, eta, eta_pack, eta_scale, u, v, fu, fv, eta_part, u_part, v_part,
    flow, flow_pack, flow_scale
):
    current_kernel(idx, w, eta, eta_pack, eta_scale, u, v, fu, fv, u_part, v_part)
    height_kernel(idx, w, eta, u_part, v_part, eta_part, flow, flow_pack, flow_scale)


def current_kernel(idx, w, eta, eta_pack, eta_scale, u, v, fu, fv, u_part, v_part):
    own_gradient(idx, w, eta, eta_pack, eta_scale, u_part, v_part)
    u_part[...] = DAMPING * u[...] - GRAVITY * u_part[...] + WIND_GAIN * fu[...]
    v_part[...] = DAMPING * v[...] - GRAVITY * v_part[...] + WIND_GAIN * fv[...]


def height_kernel(idx, w, eta, u_part, v_part, eta_part, flow, flow_pack, flow_scale):
    tiles = eta.shape[0]
    fill_flow(flow, u_part[...], v_part[...])
    for kk in range(3):
        fill_pack(flow[kk], flow_pack.at[kk], flow_scale.at[kk])

    def chunk(at):
        total = own_spread(at, idx, w, flow, flow_pack, flow_scale)
        eta_part[pl.ds(at, 8)] = eta[pl.ds(at, 8)] - DEPTH_RATE * total

    for c in range(tiles // 8):
        chunk(c * 8)


def first_gradient_kernel(
    idx, w, eta, eta_pack, eta_scale, sst, first_far, first_near, odd, rim_idx, rim_w,
    gx, gy, base, sst_pack, sst_scale
):
    own_gradient(idx, w, eta, eta_pack, eta_scale, gx, gy)
    tiles = eta.shape[0]
    fill_pack(sst[...], sst_pack, sst_scale)

    def chunk(at):
        centre = sst[pl.ds(at, 8)]
        total = jnp.zeros_like(centre)
        for k in range(6):
            found = pick_own(idx[pl.ds(k * tiles + at, 8)], sst_pack, sst_scale)
            total = total + w[pl.ds(k * tiles + at, 8)] * (found - centre)
        base[pl.ds(at, 8)] = centre + (0.5 * SPREADING_COEFF) * total

    for c in range(tiles // 8):
        chunk(c * 8)
    first = Received(first_far, first_near, odd)
    for side, start, offset in ((0, 0, 0), (1, tiles - HALO, tiles + HALO)):
        rim = first.rim(side, ROW_SST)
        sources = [(offset + q, rim[q : q + 1]) for q in range(HALO)]
        found = rim_w[side] * pick(rim_idx[side], sources)
        total = combine([found[HALO * k : HALO * (k + 1)] for k in range(6)], [1.0] * 6)
        rows = slice(start, start + HALO)
        base[rows] = base[rows] + (0.5 * SPREADING_COEFF) * total


def fill_flow(flow, u, v):
    flow[0] = u
    for kk in (1, 2):
        flow[kk] = COS[kk] * u + SIN[kk] * v


def side_currents(eta, sides, fside, before, after, side_idx, side_w):
    tiles = eta.shape[0]
    slopes = []
    for side, offset, first, part in (
        (0, tiles + HALO, 0, before),
        (1, 0, tiles - HALO, after),
    ):
        sources = [(offset + q, eta[first + q : first + q + 1]) for q in range(HALO)]
        add_x, add_y = pair_sums(side_w[side] * pick(side_idx[side], sources))
        slopes.append((part[1] + add_x, part[2] + add_y))
    slope = jnp.concatenate([slopes[0][0], slopes[1][0], slopes[0][1], slopes[1][1]], axis=0)
    return DAMPING * sides[...] - GRAVITY * slope + WIND_GAIN * fside[...]


def rim_slopes(rim_idx, rim_w, before, after, tiles):
    result = []
    for side, offset, part in ((0, 0, before), (1, tiles + HALO, after)):
        sources = [(offset + q, part[0][q : q + 1]) for q in range(HALO)]
        result.append(pair_sums(rim_w[side] * pick(rim_idx[side], sources)))
    return result


def send_rims(eta, eta_pack, eta_scale, rim_idx, rim_w, odd, far, near, up, dn):
    tiles = eta.shape[0]
    fill_pack(eta[...], eta_pack, eta_scale)
    for side, first, target in ((0, 0, dn), (1, tiles - HALO, up)):
        part_x, part_y = rim_partial(
            rim_idx[side], rim_w[side], eta, eta_pack, eta_scale, first
        )
        target[0:HALO] = eta[first : first + HALO]
        target[HALO : 2 * HALO] = part_x
        target[2 * HALO : 3 * HALO] = part_y
        target[3 * HALO : 4 * HALO] = jnp.zeros((HALO, LANES), jnp.float32)
    rows = pl.ds(0, 4 * HALO)
    arrange(up, dn, odd, far.at[rows], near.at[rows])


def first_subcycle(
    gx, gy, eta, u, v, sides, fu, fv, fside, before, after, idx, w, side_idx, side_w,
    rim_idx, rim_w, flow, flow_pack, flow_scale, flow_outer, eta_new, u_new, v_new, sides_new,
    midway
):
    tiles = eta.shape[0]
    u_new[...] = DAMPING * u[...] - GRAVITY * gx[...] + WIND_GAIN * fu[...]
    v_new[...] = DAMPING * v[...] - GRAVITY * gy[...] + WIND_GAIN * fv[...]
    slopes = rim_slopes(rim_idx, rim_w, before, after, tiles)
    for first, (add_x, add_y) in zip((0, tiles - HALO), slopes):
        rows = slice(first, first + HALO)
        u_new[rows] = u_new[rows] - GRAVITY * add_x
        v_new[rows] = v_new[rows] - GRAVITY * add_y
    sides_next = side_currents(eta, sides, fside, before, after, side_idx, side_w)
    sides_new[...] = sides_next
    fill_flow(flow, u_new[...], v_new[...])
    fill_flow(flow_outer, sides_next[0 : 2 * HALO], sides_next[2 * HALO : 4 * HALO])
    for kk in range(3):
        fill_pack(flow[kk], flow_pack.at[kk], flow_scale.at[kk])

    def chunk(at):
        total = own_spread(at, idx, w, flow, flow_pack, flow_scale)
        eta_new[pl.ds(at, 8)] = eta[pl.ds(at, 8)] - DEPTH_RATE * total

    for c in range(tiles // 8):
        if c == tiles // 16:
            midway()
        chunk(c * 8)
    for side, first, offset in ((0, 0, 0), (1, tiles - HALO, tiles + HALO)):
        total = jnp.zeros((HALO, LANES), jnp.float32)
        for kk in range(3):
            at = side * HALO
            sources = [(offset + q, flow_outer[kk, at + q : at + q + 1]) for q in range(HALO)]
            found = rim_w[side] * pick(rim_idx[side], sources)
            total = (
                total
                + found[HALO * kk : HALO * (kk + 1)]
                - found[HALO * (kk + 3) : HALO * (kk + 4)]
            )
        rows = slice(first, first + HALO)
        eta_new[rows] = eta_new[rows] - DEPTH_RATE * total


def outer_subcycle(
    eta, eta_part, u_part, v_part, sides, fside, before, after, idx, w, side_idx, side_w,
    rim_idx, rim_w, flow_outer, eta_new, u_new, v_new
):
    tiles = eta.shape[0]
    slopes = rim_slopes(rim_idx, rim_w, before, after, tiles)
    sides_next = side_currents(eta, sides, fside, before, after, side_idx, side_w)
    u_new[...] = u_part[...]
    v_new[...] = v_part[...]
    changes_u = [-GRAVITY * slopes[side][0] for side in (0, 1)]
    changes_v = [-GRAVITY * slopes[side][1] for side in (0, 1)]
    for side, first in ((0, 0), (1, tiles - HALO)):
        rows = slice(first, first + HALO)
        u_new[rows] = u_new[rows] + changes_u[side]
        v_new[rows] = v_new[rows] + changes_v[side]
    fill_flow(
        flow_outer,
        jnp.concatenate([sides_next[0 : 2 * HALO]] + changes_u, axis=0),
        jnp.concatenate([sides_next[2 * HALO : 4 * HALO]] + changes_v, axis=0),
    )
    for c in range(tiles // 8):
        at = c * 8
        total = jnp.zeros((8, LANES), jnp.float32)
        for kk in range(3):
            line = lambda n: flow_outer[kk, n : n + 1]
            sources = [(HALO + q, line(2 * HALO + q)) for q in range(HALO)]
            sources += [(tiles + q, line(3 * HALO + q)) for q in range(HALO)]
            if at == 0:
                sources += [(q, line(q)) for q in range(HALO)]
            if at + 8 == tiles:
                sources += [(tiles + HALO + q, line(HALO + q)) for q in range(HALO)]
            total = (
                total
                + w[kk * tiles + at : kk * tiles + at + 8]
                * pick(idx[kk * tiles + at : kk * tiles + at + 8], sources)
                - w[(kk + 3) * tiles + at : (kk + 3) * tiles + at + 8]
                * pick(idx[(kk + 3) * tiles + at : (kk + 3) * tiles + at + 8], sources)
            )
        eta_new[at : at + 8] = eta_part[at : at + 8] - DEPTH_RATE * total
    for side, first in ((0, 0), (1, tiles - HALO)):
        centre = jnp.zeros((HALO, LANES), jnp.float32)
        for kk in range(3):
            factor = (
                rim_w[side, HALO * kk : HALO * (kk + 1)]
                - rim_w[side, HALO * (kk + 3) : HALO * (kk + 4)]
            )
            start = (2 + side) * HALO
            centre = centre + factor * flow_outer[kk, start : start + HALO]
        rows = slice(first, first + HALO)
        eta_new[rows] = eta_new[rows] + DEPTH_RATE * centre
    return sides_next


def first_ocean_kernel(
    arrived, first_far, first_near, odd, gx, gy, eta, u, v, idx, w, rim_idx, rim_w,
    far_old, near_old, base, eta_new, eta_pack, eta_scale, u_new, v_new, sides_new, far, near,
    fu, fv, fside, side_idx, side_w, heat, answers_hbm,
    flow, flow_pack, flow_scale, flow_outer, sides, up, dn, parts, answers, sems
):
    tiles = eta.shape[0]
    devices = arrived.shape[0]
    parts[...] = arrived[...].astype(jnp.float32).reshape(parts.shape)

    def rows_of(r):
        return parts[pl.ds(r, devices, stride=PER_DEST), :]

    ids = rows_of(ROW_IDS)
    number = lax.broadcasted_iota(jnp.int32, (devices, LANES), 1).astype(jnp.float32)
    nothing = jnp.zeros((devices, LANES), jnp.float32)
    chosen, lines = [], []
    for j in range(3 * CAP):
        chosen.append(jnp.where(ids[:, j : j + 1] == number, 1.0, 0.0).astype(jnp.bfloat16))
        first = rows_of(ROW_HEAT + j) if j < CAP else nothing
        lines.append(jnp.concatenate([first, rows_of(2 * j), rows_of(2 * j + 1)], axis=1))
    forcing = lax.dot_general(
        jnp.concatenate(chosen, axis=0),
        jnp.concatenate(lines, axis=0).astype(jnp.bfloat16),
        (((0,), (0,)), ((), ())),
        preferred_element_type=jnp.float32,
    )
    heat[...] = forcing[0:tiles, 0:LANES]
    half = (base[...] + WARMING_COEFF * forcing[0:tiles, 0:LANES]).astype(jnp.bfloat16)
    for j in range(CAP):
        answers[pl.ds(j, devices, stride=CAP), :] = jnp.dot(
            chosen[j][:, 0:tiles], half, preferred_element_type=jnp.float32
        )
    fu[...] = forcing[0:tiles, LANES : 2 * LANES]
    fv[...] = forcing[0:tiles, 2 * LANES : 3 * LANES]
    fside[0 : 2 * HALO] = forcing[tiles : tiles + 2 * HALO, LANES : 2 * LANES]
    fside[2 * HALO : 4 * HALO] = forcing[tiles : tiles + 2 * HALO, 2 * LANES : 3 * LANES]
    copy = pltpu.make_async_copy(answers, answers_hbm, sems.at[0])
    first = Received(first_far, first_near, odd)
    for side, part in ((0, first.prev), (1, first.next)):
        side_idx[side] = part(slice(ROW_IDX, ROW_IDX + 16)).astype(jnp.int32)
        side_w[side] = part(slice(ROW_W, ROW_W + 16))
        for n, row in ((0, ROW_U), (1, ROW_V)):
            at = HALO * (2 * n + side)
            sides[at : at + HALO] = first.rim(side, row)
    rows = (ROW_ETA, ROW_PX, ROW_PY)
    first_subcycle(
        gx, gy, eta, u, v, sides, fu, fv, fside, first.rims(0, rows), first.rims(1, rows), idx, w, side_idx, side_w, rim_idx, rim_w, flow, flow_pack, flow_scale, flow_outer,
        eta_new, u_new, v_new, sides_new, copy.start
    )
    send_rims(eta_new, eta_pack, eta_scale, rim_idx, rim_w, odd, far, near, up, dn)
    copy.wait()


def ocean_kernel(
    far, near, odd, eta, eta_part, u_part, v_part, sides, fside, idx, w, side_idx, side_w,
    rim_idx, rim_w, eta_new, eta_pack, eta_scale, u_new, v_new, sides_new, far_new, near_new,
    flow_outer, up, dn
):
    rows = (0, HALO, 2 * HALO)
    got = Received(far, near, odd)
    sides_new[...] = outer_subcycle(
        eta, eta_part, u_part, v_part, sides, fside, got.rims(0, rows), got.rims(1, rows), idx, w, side_idx, side_w, rim_idx, rim_w, flow_outer,
        eta_new, u_new, v_new
    )
    send_rims(
        eta_new, eta_pack, eta_scale, rim_idx, rim_w, odd, far_new, near_new, up, dn
    )


def last_ocean_kernel(
    far, near, odd, eta, eta_part, u_part, v_part, sides, fside, idx, w, side_idx, side_w,
    rim_idx, rim_w, base, heat, eta_new, velocity, warm, u_new, v_new, flow_outer
):
    warm[...] = base[...] + WARMING_COEFF * heat[...]
    rows = (0, HALO, 2 * HALO)
    got = Received(far, near, odd)
    outer_subcycle(
        eta, eta_part, u_part, v_part, sides, fside, got.rims(0, rows), got.rims(1, rows), idx, w, side_idx, side_w, rim_idx, rim_w, flow_outer,
        eta_new, u_new, v_new
    )
    for r in range(eta.shape[0]):
        cut = slice(r * LANES, (r + 1) * LANES)
        velocity[0:1, cut] = u_new[r : r + 1]
        velocity[1:2, cut] = v_new[r : r + 1]


def shards(
    air_warmth,
    eastern_breeze,
    northern_breeze,
    reciprocal_breadth,
    panel_neighbours,
    transfer_coefficients,
    transfer_across_tile,
    transfer_holder,
    transfer_down_tile,
    water_elevation,
    depth_mean_current,
    marine_skin_warmth,
    patch_neighbours,
    interface_span,
):
    devices = lax.axis_size(RING)
    points, levels, elements = air_warmth.shape
    cells = water_elevation.shape[0]
    tiles = cells // LANES
    blocks = transfer_holder.shape[0]
    cell_rows = shape_of(tiles, LANES)
    rim_rows = shape_of(4 * HALO, LANES)
    dma = pltpu.SemaphoreType.DMA
    air, eastern, northern, breadth_hbm, pn_hbm = in_hbm(
        air_warmth, eastern_breeze, northern_breeze, reciprocal_breadth.reshape(1, elements),
        panel_neighbours
    )

    pack_rows = shape_of(tiles // 2, LANES, dtype=jnp.int32)
    scale_rows = shape_of(8, LANES)
    cell_tables = in_hbm(
        marine_skin_warmth.reshape(tiles, LANES),
        depth_mean_current,
        patch_neighbours,
        interface_span,
    )
    rim_idx, rim_w, eta, eta_pack, eta_scale, far, near, odd = pl.pallas_call(
        prepare_kernel,
        in_specs=hbm(8),
        out_specs=vmem(8),
        out_shape=(
            shape_of(2, 16, LANES, dtype=jnp.int32),
            shape_of(2, 16, LANES),
            cell_rows,
            pack_rows,
            scale_rows,
            shape_of(ROWS_FIRST, LANES),
            shape_of(ROWS_FIRST, LANES),
            shape_of(8, elements, dtype=jnp.int32),
        ),
        scratch_shapes=[
            pltpu.VMEM((ROWS_FIRST, LANES), jnp.float32),
            pltpu.VMEM((ROWS_FIRST, LANES), jnp.float32),
            pltpu.VMEM((2, 4, 8, elements), jnp.float32),
            pltpu.VMEM((1, elements), jnp.float32),
            pltpu.VMEM((4, elements), jnp.int32),
            pltpu.VMEM((2, 8, LANES), jnp.float32),
            pltpu.VMEM((2, 2, OY), jnp.float32),
            pltpu.VMEM((2, 6, OY), jnp.int32),
            pltpu.VMEM((2, 6, OY), jnp.float32),
            dma((13,)),
        ],
        compiler_params=PARAMS,
        name="prepare",
    )(
        *in_hbm(air_warmth.reshape(4, 4, levels, elements)),
        breadth_hbm,
        pn_hbm,
        *in_hbm(water_elevation.reshape(tiles, LANES)),
        *cell_tables,
    )
    first_far, first_near = swap_both(far, near)

    low_wind = pltpu.VMEM((points, 16, elements), jnp.bfloat16)
    low_row = pltpu.VMEM((1, blocks), jnp.int32)
    flux, slots, breadth, pn, marks, idx, w, u, v, sst = pl.pallas_call(
        lambda *refs: plan_kernel(*refs, devices=devices, tiles=tiles),
        in_specs=hbm(12),
        out_specs=vmem(4) + smem(1) + vmem(5),
        out_shape=(
            shape_of(points, 8, elements), shape_of(devices, LANES), shape_of(1, elements),
            shape_of(4, elements, dtype=jnp.int32), pltpu.SMEM((8, blocks), jnp.int32),
            shape_of(6 * tiles, LANES, dtype=jnp.int32), shape_of(6 * tiles, LANES),
            cell_rows, cell_rows, cell_rows
        ),
        scratch_shapes=[
            pltpu.VMEM((points, 8, elements), jnp.float32), low_wind, low_wind,
            low_row, low_row, low_row, pltpu.VMEM((6, cells), jnp.int32),
            pltpu.VMEM((6, cells), jnp.float32), pltpu.VMEM((2, cells), jnp.float32),
            pltpu.VMEM((8, blocks), jnp.int32), dma((12,))
        ],
        compiler_params=PARAMS,
        name="plan",
    )(
        air,
        eastern,
        northern,
        breadth_hbm,
        pn_hbm,
        *in_hbm(
            transfer_holder.reshape(1, blocks),
            transfer_across_tile.reshape(1, blocks),
            transfer_down_tile.reshape(1, blocks),
        ),
        cell_tables[2],
        cell_tables[3],
        cell_tables[1],
        cell_tables[0],
    )

    home = pl.pallas_call(
        home_sums_kernel,
        in_specs=smem(1) + vmem(2),
        out_specs=pl.BlockSpec(memory_space=pltpu.VMEM),
        out_shape=shape_of(devices * 8, LANES),
        compiler_params=PARAMS,
        name="home_sums",
    )(marks, flux, transfer_coefficients)
    outgoing = pl.pallas_call(
        lambda *refs: forward_kernel(*refs, devices=devices),
        in_specs=smem(1) + vmem(9),
        out_specs=pl.BlockSpec(memory_space=pltpu.HBM),
        out_shape=pltpu.HBM((devices, PER_DEST, LANES), jnp.bfloat16),
        scratch_shapes=[
            pltpu.VMEM((devices, PER_DEST, LANES), jnp.bfloat16),
            pltpu.VMEM((devices * 8, LANES), jnp.float32),
            dma((4,)),
        ],
        compiler_params=PARAMS,
        name="forward_remap",
    )(
        marks, home, flux, slots, breadth, pn, first_far, first_near, odd, transfer_coefficients
    )
    outgoing, pn, gradient_eta = lax.optimization_barrier((outgoing, pn, eta))
    arrived = exchange(outgoing)
    gx, gy, base = pl.pallas_call(
        first_gradient_kernel,
        in_specs=vmem(11),
        out_specs=vmem(3),
        out_shape=(cell_rows,) * 3,
        scratch_shapes=[
            pltpu.VMEM((tiles // 2, LANES), jnp.int32), pltpu.VMEM((8, LANES), jnp.float32)
        ],
        compiler_params=PARAMS,
        name="first_gradient",
    )(
        idx, w, gradient_eta, eta_pack, eta_scale, sst, first_far, first_near, odd, rim_idx, rim_w
    )

    field = shape_of(points, levels, elements)
    edge = shape_of(4, levels, elements, dtype=jnp.bfloat16)
    swap_rows = shape_of(4 * HALO + 2 * levels, elements)
    wind = shape_of(points, levels, elements, dtype=jnp.bfloat16)
    loc, eastern, northern, east, west, far, near, edge_places = pl.pallas_call(
        local_step_kernel,
        in_specs=hbm(3) + vmem(3),
        out_specs=vmem(8),
        out_shape=(
            field, wind, wind, edge, edge, swap_rows, swap_rows,
            shape_of(8, elements, dtype=jnp.int32)
        ),
        scratch_shapes=[pltpu.VMEM((points, levels, elements), jnp.float32), dma((3,))],
        compiler_params=PARAMS,
        name="local_step",
    )(air, eastern, northern, breadth, pn, odd)

    rim_scratch = pltpu.VMEM((4 * HALO, LANES), jnp.float32)
    flow_scratch = [
        pltpu.VMEM((3, tiles, LANES), jnp.float32),
        pltpu.VMEM((3, tiles // 2, LANES), jnp.int32),
        pltpu.VMEM((3, 8, LANES), jnp.float32),
        pltpu.VMEM((3, 2 * HALO, LANES), jnp.float32),
    ]
    (
        eta, eta_pack, eta_scale, u, v, sides, far, near, fu, fv, fside, side_idx, side_w,
        heat, answers
    ) = pl.pallas_call(
        first_ocean_kernel,
        in_specs=vmem(16),
        out_specs=vmem(14) + hbm(1),
        out_shape=(
            cell_rows, pack_rows, scale_rows, cell_rows, cell_rows, rim_rows, swap_rows, swap_rows,
            cell_rows, cell_rows, rim_rows,
            shape_of(2, 16, LANES, dtype=jnp.int32), shape_of(2, 16, LANES),
            cell_rows, pltpu.HBM((devices * CAP, LANES), jnp.float32),
        ),
        scratch_shapes=flow_scratch + [rim_scratch] * 3 + [
            pltpu.VMEM((devices * PER_DEST, LANES), jnp.float32),
            pltpu.VMEM((devices * CAP, LANES), jnp.float32),
            dma((1,)),
        ],
        input_output_aliases={13: 6, 14: 7},
        compiler_params=PARAMS,
        name="first_ocean",
    )(
        arrived, first_far, first_near, odd, gx, gy, eta, u, v, idx, w, rim_idx, rim_w,
        far, near, base
    )
    far, near = swap_both(far, near)
    edges_far, edges_near = far, near

    for substep in range(1, NSUB):
        if substep == 1:
            u_part, v_part = pl.pallas_call(
                current_kernel,
                in_specs=vmem(9),
                out_specs=vmem(2),
                out_shape=(cell_rows,) * 2,
                compiler_params=PARAMS,
                name="current",
            )(idx, w, eta, eta_pack, eta_scale, u, v, fu, fv)
            answers, u_part = lax.optimization_barrier((answers, u_part))
            answered = exchange(answers.reshape(devices, CAP, LANES))
            eta_part = pl.pallas_call(
                height_kernel,
                in_specs=vmem(5),
                out_specs=pl.BlockSpec(memory_space=pltpu.VMEM),
                out_shape=cell_rows,
                scratch_shapes=flow_scratch[:3],
                compiler_params=PARAMS,
                name="height",
            )(idx, w, eta, u_part, v_part)
        else:
            eta_part, u_part, v_part = pl.pallas_call(
                inner_kernel,
                in_specs=vmem(9),
                out_specs=vmem(3),
                out_shape=(cell_rows,) * 3,
                scratch_shapes=flow_scratch[:3],
                compiler_params=PARAMS,
                name="inner",
            )(idx, w, eta, eta_pack, eta_scale, u, v, fu, fv)
        if substep == 2:
            eta_part, answered = lax.optimization_barrier((eta_part, answered))
            surface = pl.pallas_call(
                back_kernel,
                in_specs=smem(1) + vmem(2),
                out_specs=pl.BlockSpec(memory_space=pltpu.VMEM),
                out_shape=shape_of(points, LANES),
                scratch_shapes=[
                    pltpu.VMEM((devices * CAP, LANES), jnp.float32),
                    pltpu.VMEM((blocks, 8, LANES), jnp.float32),
                ],
                compiler_params=PARAMS,
                name="back_remap",
            )(marks, answered, transfer_coefficients)
            eta_part, surface = lax.optimization_barrier((eta_part, surface))
        operands = (
            far, near, odd, eta, eta_part, u_part, v_part, sides, fside, idx, w, side_idx, side_w, rim_idx, rim_w
        )
        outer_scratch = [pltpu.VMEM((3, 4 * HALO, LANES), jnp.float32)]
        if substep + 1 < NSUB:
            eta, eta_pack, eta_scale, u, v, sides, far, near = pl.pallas_call(
                ocean_kernel,
                in_specs=vmem(15),
                out_specs=vmem(8),
                out_shape=(cell_rows, pack_rows, scale_rows) + (cell_rows,) * 2 + (rim_rows,) * 3,
                scratch_shapes=outer_scratch + [rim_scratch] * 2,
                compiler_params=PARAMS,
                name="ocean",
            )(*operands)
            far, near = swap_both(far, near)
        else:
            eta, velocity, warm = pl.pallas_call(
                last_ocean_kernel,
                in_specs=vmem(17),
                out_specs=vmem(3),
                out_shape=(cell_rows, shape_of(2, cells), cell_rows),
                scratch_shapes=[pltpu.VMEM((tiles, LANES), jnp.float32)] * 2 + outer_scratch,
                compiler_params=PARAMS,
                name="last_ocean",
            )(*operands, base, heat)

    closing = pl.pallas_call(
        second_step_kernel,
        in_specs=vmem(14),
        out_specs=pl.BlockSpec(memory_space=pltpu.HBM),
        out_shape=pltpu.HBM((points, levels, elements), jnp.float32),
        scratch_shapes=[
            pltpu.VMEM((points, levels, elements), jnp.float32), dma((levels // 16,))
        ],
        compiler_params=PARAMS,
        name="second_step",
    )(
        loc, eastern, northern, breadth, pn, east, west, edges_far, edges_near, edge_places,
        first_far, first_near, odd, surface
    )
    return closing, eta.reshape(cells), velocity, warm.reshape(cells)


def solution(mesh):
    split = P(RING)
    last = P(None, RING)
    field = P(None, None, RING)
    return jax.shard_map(
        shards,
        mesh=mesh,
        in_specs=(
            field,
            field,
            field,
            split,
            last,
            P(RING, None, None),
            split,
            P(RING, None),
            split,
            split,
            last,
            split,
            last,
            last,
        ),
        out_specs=(field, split, last, split),
        check_vma=False,
    )
```
